32 devices in a mesh: seq: 8 (over z, core), dp: 4 (over y, x).
Axes of the slice: x: 2, y: 2, z: 4, core: 2. Of those that a mesh axis runs over, the one named last changes fastest.
Arguments:
- tokens: bfloat16 [4, 2048, 1536], P('dp', 'seq'), may hold values from -6 to 6
- cotangent: bfloat16 [4, 2048, 1536], P('dp', 'seq'), may hold values from -6 to 6
- positions: int32 [4, 2048], P('dp'), may hold values from 0 to 2047, as said below
- qkv_master: float32 [1536, 2048], P(('seq', 'dp')), may hold values from -0.21875 to 0.21875
- qkv_first: float32 [1536, 2048], P(('seq', 'dp')), may hold values from -192 to 192
- qkv_second: float32 [1536, 2048], P(('seq', 'dp')), may hold values from 3850.24 to 15564.8
- out_master: float32 [1536, 1536], P(('seq', 'dp')), may hold values from -0.4375 to 0.4375
- out_first: float32 [1536, 1536], P(('seq', 'dp')), may hold values from -16 to 16
- out_second: float32 [1536, 1536], P(('seq', 'dp')), may hold values from 39.3216 to 155.648
- gate_up_master: float32 [2, 1536, 8960], P(None, ('seq', 'dp')), may hold values from -0.15625 to 0.15625
- gate_up_first: float32 [2, 1536, 8960], P(None, ('seq', 'dp')), may hold values from -14 to 14
- gate_up_second: float32 [2, 1536, 8960], P(None, ('seq', 'dp')), may hold values from 21.2992 to 83.5584
- down_master: float32 [8960, 1536], P(('seq', 'dp')), may hold values from -0.0625 to 0.0625
- down_first: float32 [8960, 1536], P(('seq', 'dp')), may hold values from -32 to 32
- down_second: float32 [8960, 1536], P(('seq', 'dp')), may hold values from 155.648 to 622.592
- small_master: float32 [5120], P(('seq', 'dp')), as said below
- small_first: float32 [5120], P(('seq', 'dp'))
- small_second: float32 [5120], P(('seq', 'dp')), as said below
Outputs:
- layer_out: bfloat16 [4, 2048, 1536], P('dp', 'seq')
- input_grad: float32 [4, 2048, 1536], P('dp', 'seq')
- qkv_first_new: float32 [1536, 2048], P(('seq', 'dp'))
- qkv_second_new: float32 [1536, 2048], P(('seq', 'dp'))
- qkv_master_new: float32 [1536, 2048], P(('seq', 'dp'))
- out_first_new: float32 [1536, 1536], P(('seq', 'dp'))
- out_second_new: float32 [1536, 1536], P(('seq', 'dp'))
- out_master_new: float32 [1536, 1536], P(('seq', 'dp'))
- gate_up_first_new: float32 [2, 1536, 8960], P(None, ('seq', 'dp'))
- gate_up_second_new: float32 [2, 1536, 8960], P(None, ('seq', 'dp'))
- gate_up_master_new: float32 [2, 1536, 8960], P(None, ('seq', 'dp'))
- down_first_new: float32 [8960, 1536], P(('seq', 'dp'))
- down_second_new: float32 [8960, 1536], P(('seq', 'dp'))
- down_master_new: float32 [8960, 1536], P(('seq', 'dp'))
- small_first_new: float32 [5120], P(('seq', 'dp'))
- small_second_new: float32 [5120], P(('seq', 'dp'))
- small_master_new: float32 [5120], P(('seq', 'dp'))
The draws below stay inside these ranges and needn't reach their ends.
Inputs may be any that keep to these rules, and one draw needn't show every extreme that they name: Each row is a permutation of 0 to 2047 made of runs of 128 consecutive positions, in rising order within a run; runs start at multiples of 128. `small_master`: gains first, bias last. `small_second`: Positive.
All inputs are finite; a program needn't handle non-finite values.
Results may differ from the reference program's by a relative error of at most 0.018.
The reference program's roundings to bfloat16 on the way count: a program that leaves them out, or rounds other values in their place, can miss the bound.
Values may be sent and summed in bfloat16 or wider, within the bound.
No kernel may reach another device: no remote copies, remote signals or barrier semaphores. Data moves between devices by JAX's collectives and lax.ppermute only.
A program may use at most 576 MiB of HBM per device.

```python
import math
import jax
import jax.numpy as jnp
from jax import lax

D = 1536
HEADS = 12
KVH = 2
HD = 128
FF = 8960
STEP = 10
QKVW = 2048
SMALL = 5120
LEN = 2048
SEQS = 4
PIECE = 128
TOK_ALL = 8192


def draw_positions(key, part):
    key = jax.random.fold_in(key, 11)
    sequence_keys = jax.random.split(key, SEQS)
    piece_count = LEN // PIECE
    orders = jax.vmap(lambda one_key: jax.random.permutation(one_key, piece_count))(sequence_keys)
    offsets = jnp.arange(LEN, dtype=jnp.int32)
    return (orders[:, offsets // PIECE] * PIECE + offsets % PIECE).astype(jnp.int32)


def segment_scales():
    pieces = [jnp.full((D,), 5.0, jnp.float32), jnp.full((D,), 0.75, jnp.float32), jnp.full((QKVW,), 3.0, jnp.float32)]
    return jnp.concatenate(pieces) * TOK_ALL ** 0.5


def draw_small_master(key, part):
    key = jax.random.fold_in(key, 21)
    gain_key, bias_key = jax.random.split(key)
    gains = 1.0 + 0.4 * jax.random.uniform(gain_key, (2 * D,), jnp.float32, -1.0, 1.0)
    biases = 0.5 * jax.random.normal(bias_key, (QKVW,), jnp.float32)
    return jnp.concatenate([gains, biases])


def draw_small_first(key, part):
    key = jax.random.fold_in(key, 22)
    return 0.11 * segment_scales() * jax.random.normal(key, (SMALL,), jnp.float32)


def draw_small_second(key, part):
    key = jax.random.fold_in(key, 23)
    spread = jax.random.uniform(key, (SMALL,), jnp.float32, jnp.log(0.053), jnp.log(0.21))
    scales = segment_scales()
    return jnp.exp(spread) * scales * scales


def steps_of(stream_key, extent, cuts, low, top_value):
    def one(axis_at, shards_of):
        draws = jax.random.uniform(jax.random.fold_in(jax.random.fold_in(stream_key, 6), axis_at), (shards_of,), jnp.float32, low / len(cuts), top_value / len(cuts))
        return jnp.repeat(jnp.exp(draws), extent[axis_at] // shards_of).reshape((-1,) + (1,) * (len(extent) - axis_at - 1))

    level = one(*cuts[0])
    for cut in cuts[1:]:
        level = level * one(*cut)
    return level


def normal_values(key, dims, width, limit, cuts=(), kind=jnp.bfloat16):
    values = jax.random.normal(key, dims, jnp.float32) * width
    if len(cuts) > 0:
        values = steps_of(key, dims, cuts, -0.22, 0.18) * values
    return jnp.clip(values, min=-limit, max=limit).astype(kind)


def setup_inputs(seed: int = 0) -> dict:
    streams_of = jax.random.split(jax.random.key(seed), 19)
    return {
        "tokens": normal_values(streams_of[0], (SEQS, LEN, D), 1.0, 6.0, ((0, 4), (1, 8))),
        "cotangent": normal_values(streams_of[1], (SEQS, LEN, D), 1.0, 6.0, ((0, 4), (1, 8))),
        "positions": draw_positions(jax.random.fold_in(streams_of[18], 71), 0),
        "qkv_master": normal_values(streams_of[3], (D, QKVW), (D // 2) ** -0.5, 0.21875, ((0, 32),), jnp.float32),
        "qkv_first": normal_values(streams_of[4], (D, QKVW), (0.33 * TOK_ALL ** 0.5), 192.0, ((0, 32),), jnp.float32),
        "qkv_second": jnp.clip(jnp.exp(math.log(15564.8) - 1.3968765 * jax.random.uniform(streams_of[5], (D, QKVW), jnp.float32) ** steps_of(streams_of[5], (D, QKVW), ((0, 32),), -0.2, 0.2)), 3850.24, 15564.8),
        "out_master": normal_values(streams_of[6], (D, D), (D // 8) ** -0.5, 0.4375, ((0, 32),), jnp.float32),
        "out_first": normal_values(streams_of[7], (D, D), (0.033 * TOK_ALL ** 0.5), 16.0, ((0, 32),), jnp.float32),
        "out_second": jnp.clip(jnp.exp(math.log(155.648) - 1.375823 * jax.random.uniform(streams_of[8], (D, D), jnp.float32) ** steps_of(streams_of[8], (D, D), ((0, 32),), -0.2, 0.2)), 39.3216, 155.648),
        "gate_up_master": normal_values(streams_of[9], (2, D, FF), D ** -0.5, 0.15625, ((1, 32),), jnp.float32),
        "gate_up_first": normal_values(streams_of[10], (2, D, FF), (0.024 * TOK_ALL ** 0.5), 14.0, ((1, 32),), jnp.float32),
        "gate_up_second": jnp.clip(jnp.exp(math.log(83.5584) - 1.36687631 * jax.random.uniform(streams_of[11], (2, D, FF), jnp.float32) ** steps_of(streams_of[11], (2, D, FF), ((1, 32),), -0.2, 0.2)), 21.2992, 83.5584),
        "down_master": normal_values(streams_of[12], (FF, D), FF ** -0.5, 0.0625, ((0, 32),), jnp.float32),
        "down_first": normal_values(streams_of[13], (FF, D), (0.066 * TOK_ALL ** 0.5), 32.0, ((0, 32),), jnp.float32),
        "down_second": jnp.clip(jnp.exp(math.log(622.592) - 1.3862944 * jax.random.uniform(streams_of[14], (FF, D), jnp.float32) ** steps_of(streams_of[14], (FF, D), ((0, 32),), -0.2, 0.2)), 155.648, 622.592),
        "small_master": draw_small_master(jax.random.fold_in(streams_of[18], 71), 0),
        "small_first": draw_small_first(jax.random.fold_in(streams_of[18], 71), 0),
        "small_second": draw_small_second(jax.random.fold_in(streams_of[18], 71), 0),
    }


norm_eps = 1e-06
rope_base = 1000000.0
beta_one = 0.9
beta_two = 0.95
adam_eps = 1e-08
masked_score = -1e+30

@jax.custom_vjp
def low(v):
    return lax.optimization_barrier(v.astype(jnp.bfloat16)).astype(jnp.float32)

@jax.custom_vjp
def low_back(v):
    return v

def low_keep(v):
    return (low(v), None)

def low_pass(kept, grad):
    return (grad,)

def back_keep(v):
    return (v, None)

def back_low(kept, grad):
    return (low(grad),)
low.defvjp(low_keep, low_pass)
low_back.defvjp(back_keep, back_low)

def matmul(left_side, right_side):
    return jnp.dot(left_side, right_side, precision=lax.Precision.HIGHEST, preferred_element_type=jnp.float32)

def rotary_tables(places):
    half_size = HD // 2
    freqs = rope_base ** (-(jnp.arange(half_size).astype(jnp.float32) * (2.0 / HD)))
    angles = places.astype(jnp.float32)[:, None] * freqs[None, :]
    return (jnp.cos(angles), jnp.sin(angles))

def rotate(values, cosine, sine_table):
    half_size = values.shape[-1] // 2
    first_half = values[..., :half_size]
    second_half = values[..., half_size:]
    cosine = cosine[:, None, :]
    sine_table = sine_table[:, None, :]
    return jnp.concatenate([first_half * cosine - second_half * sine_table, second_half * cosine + first_half * sine_table], axis=-1)

def attention(queries, key_rows, value_rows, places):
    length = queries.shape[0]
    block_rows = min(512, length)
    block_count = length // block_rows
    score_scale = HD ** (-0.5)
    grouped = queries.reshape(block_count, block_rows, KVH, HEADS // KVH, HD)
    query_places = places.reshape(block_count, block_rows)

    def one_block(block_items):
        query_block, block_places = block_items
        scores = jnp.einsum('qkgd,tkd->kgqt', query_block, key_rows, precision=lax.Precision.HIGHEST) * score_scale
        scores = low_back(scores)
        visible = block_places[:, None] >= places[None, :]
        scores = jnp.where(visible, scores, masked_score)
        weights = jax.nn.softmax(scores, axis=-1)
        mixture = jnp.einsum('kgqt,tkd->qkgd', low(weights), value_rows, precision=lax.Precision.HIGHEST)
        return mixture.reshape(block_rows, HEADS * HD)
    outputs = lax.map(jax.checkpoint(one_block), (grouped, query_places))
    return outputs.reshape(length, HEADS * HD)

def rms_scale(values):
    return lax.rsqrt(lax.optimization_barrier(jnp.mean(values * values, axis=-1, keepdims=True)) + norm_eps)

def layer_forward(inputs, w_qkv, w_out, w_gate_up, w_down, small_params, cosine, sine_table, places):
    length = inputs.shape[0]
    gain_one = small_params[:D]
    gain_two = small_params[D:2 * D]
    qkv_bias = small_params[2 * D:]
    normed_one = low(inputs * rms_scale(inputs) * gain_one)
    projected = low_back(matmul(normed_one, w_qkv) + qkv_bias)
    queries = rotate(projected[:, :D].reshape(length, HEADS, HD), cosine, sine_table)
    key_rows = rotate(projected[:, D:D + KVH * HD].reshape(length, KVH, HD), cosine, sine_table)
    value_rows = projected[:, D + KVH * HD:].reshape(length, KVH, HD)
    attended = attention(low(queries), low(key_rows), low(value_rows), places)
    attended = low(low_back(attended))
    residual = inputs + low_back(matmul(attended, w_out))
    normed_two = low(residual * rms_scale(residual) * gain_two)
    gate_rows = low_back(matmul(normed_two, w_gate_up[0]))
    up_rows = low_back(matmul(normed_two, w_gate_up[1]))
    hidden = low(jax.nn.silu(gate_rows) * up_rows)
    return residual + low_back(matmul(hidden, w_down))

def adamw_update(master, moment_one, moment_two, gradient, step_rate, decay_weight):
    first_new = beta_one * moment_one + (1.0 - beta_one) * gradient
    second_new = beta_two * moment_two + (1.0 - beta_two) * gradient * gradient
    first_hat = first_new / (1.0 - beta_one ** STEP)
    second_hat = second_new / (1.0 - beta_two ** STEP)
    master_new = master - step_rate * (first_hat / (jnp.sqrt(second_hat) + adam_eps) + decay_weight * master)
    return (first_new, second_new, master_new)

def reference(tokens, cotangent, positions, qkv_master, qkv_first, qkv_second, out_master, out_first, out_second, gate_up_master, gate_up_first, gate_up_second, down_master, down_first, down_second, small_master, small_first, small_second):
    masters = (qkv_master, out_master, gate_up_master, down_master, small_master)
    weights = tuple((lax.optimization_barrier(master.astype(jnp.bfloat16)).astype(jnp.float32) for master in masters))

    def per_sequence(totals, sequence_items):
        inputs, upstream, places = sequence_items
        cosine, sine_table = rotary_tables(places)

        def forward(values, *params):
            return layer_forward(values, *params, cosine, sine_table, places)
        outputs, pullback = jax.vjp(forward, inputs.astype(jnp.float32), *weights)
        gradients = pullback(upstream.astype(jnp.float32))
        totals = tuple((running_total + gradient for running_total, gradient in zip(totals, gradients[1:])))
        return (totals, (outputs.astype(jnp.bfloat16), gradients[0]))
    zero_sums = tuple((jnp.zeros(weight.shape, jnp.float32) for weight in weights))
    totals, (layer_out, input_grad) = lax.scan(per_sequence, zero_sums, (tokens, cotangent, positions))
    qkv_new = adamw_update(qkv_master, qkv_first, qkv_second, totals[0], 0.09, 0.1)
    out_new = adamw_update(out_master, out_first, out_second, totals[1], 0.18, 0.1)
    gate_up_new = adamw_update(gate_up_master, gate_up_first, gate_up_second, totals[2], 0.064, 0.1)
    down_new = adamw_update(down_master, down_first, down_second, totals[3], 0.026, 0.1)
    small_new = adamw_update(small_master, small_first, small_second, totals[4], 0.6, 0.0)
    return (layer_out, input_grad, qkv_new[0], qkv_new[1], qkv_new[2], out_new[0], out_new[1], out_new[2], gate_up_new[0], gate_up_new[1], gate_up_new[2], down_new[0], down_new[1], down_new[2], small_new[0], small_new[1], small_new[2])
```

```python
import jax
import jax.numpy as jnp
from jax import lax
from jax.sharding import PartitionSpec as P

D = 1536
HEADS = 12
KVH = 2
HD = 128
STEP = 10


norm_eps = 1e-06
rope_base = 1000000.0
beta_one = 0.9
beta_two = 0.95
adam_eps = 1e-08
masked_score = -1e30


def rotary_tables(places):
    half_size = HD // 2
    freqs = rope_base ** (-(jnp.arange(half_size).astype(jnp.float32) * (2.0 / HD)))
    angles = places.astype(jnp.float32)[:, None] * freqs[None, :]
    return (jnp.cos(angles), jnp.sin(angles))


def rotate(values, cosine, sine_table):
    half_size = values.shape[-1] // 2
    first_half = values[..., :half_size]
    second_half = values[..., half_size:]
    cosine = cosine[:, None, :]
    sine_table = sine_table[:, None, :]
    return jnp.concatenate(
        [
            first_half * cosine - second_half * sine_table,
            second_half * cosine + first_half * sine_table,
        ],
        axis=-1,
    )


def unrotate(gradients, cosine, sine_table):
    half_size = gradients.shape[-1] // 2
    first_half = gradients[..., :half_size]
    second_half = gradients[..., half_size:]
    cosine = cosine[:, None, :]
    sine_table = sine_table[:, None, :]
    return jnp.concatenate(
        [
            first_half * cosine + second_half * sine_table,
            second_half * cosine - first_half * sine_table,
        ],
        axis=-1,
    )


def over_blocks(carried, key_rows, value_rows, key_places, visit_block):
    total_rows = key_rows.shape[0]
    block_rows = 512

    def advance(block_index, carried):
        offset = block_index * block_rows
        key_block = lax.dynamic_slice_in_dim(key_rows, offset, block_rows, 0)
        value_block = lax.dynamic_slice_in_dim(value_rows, offset, block_rows, 0)
        place_block = lax.dynamic_slice_in_dim(key_places, offset, block_rows, 0)
        return visit_block(carried, key_block, value_block, place_block, offset)

    return lax.fori_loop(0, total_rows // block_rows, advance, carried)


def forward_visit(queries, query_places):
    score_scale = HD ** (-0.5)

    def visit_block(carried, key_block, value_block, place_block, offset):

        def compute_block(carried):
            running_max, running_sum, running_out = carried
            scores = (
                jnp.einsum("qkgd,tkd->kgqt", queries, key_block, preferred_element_type=jnp.float32)
                * score_scale
            )
            visible = query_places[:, None] >= place_block[None, :]
            scores = jnp.where(visible, scores, masked_score)
            new_max = jnp.maximum(running_max, jnp.max(scores, axis=-1))
            weights = jnp.where(visible, jnp.exp(scores - new_max[..., None]), 0.0)
            factor = jnp.exp(running_max - new_max)
            running_sum = running_sum * factor + jnp.sum(weights, axis=-1)
            update = jnp.einsum(
                "kgqt,tkd->qkgd",
                weights.astype(jnp.bfloat16),
                value_block,
                preferred_element_type=jnp.float32,
            )
            running_out = running_out * jnp.transpose(factor, (2, 0, 1))[..., None] + update
            return (new_max, running_sum, running_out)

        return lax.cond(
            jnp.min(place_block) <= jnp.max(query_places),
            compute_block,
            lambda unchanged: unchanged,
            carried,
        )

    return visit_block


def backward_visit(queries, query_places, out_grads, logsum, row_delta):
    score_scale = HD ** (-0.5)

    def visit_block(carried, key_block, value_block, place_block, offset):

        def compute_block(carried):
            query_grads, key_grads, value_grads = carried
            block_rows = key_block.shape[0]
            scores = (
                jnp.einsum("qkgd,tkd->kgqt", queries, key_block, preferred_element_type=jnp.float32)
                * score_scale
            )
            visible = query_places[:, None] >= place_block[None, :]
            probabilities = jnp.where(visible, jnp.exp(scores - logsum[..., None]), 0.0)
            prob_grads = jnp.einsum(
                "qkgd,tkd->kgqt", out_grads, value_block, preferred_element_type=jnp.float32
            )
            score_grads = (probabilities * (prob_grads - row_delta[..., None])).astype(jnp.bfloat16)
            query_grads = (
                query_grads
                + jnp.einsum(
                    "kgqt,tkd->qkgd", score_grads, key_block, preferred_element_type=jnp.float32
                )
                * score_scale
            )
            key_part = (
                jnp.einsum(
                    "kgqt,qkgd->tkd", score_grads, queries, preferred_element_type=jnp.float32
                )
                * score_scale
            )
            value_part = jnp.einsum(
                "kgqt,qkgd->tkd",
                probabilities.astype(jnp.bfloat16),
                out_grads,
                preferred_element_type=jnp.float32,
            )
            key_old = lax.dynamic_slice_in_dim(key_grads, offset, block_rows, 0)
            value_old = lax.dynamic_slice_in_dim(value_grads, offset, block_rows, 0)
            key_grads = lax.dynamic_update_slice_in_dim(key_grads, key_old + key_part, offset, 0)
            value_grads = lax.dynamic_update_slice_in_dim(
                value_grads, value_old + value_part, offset, 0
            )
            return (query_grads, key_grads, value_grads)

        return lax.cond(
            jnp.min(place_block) <= jnp.max(query_places),
            compute_block,
            lambda unchanged: unchanged,
            carried,
        )

    return visit_block


def core_swap(values):
    count = lax.axis_size("seq")
    return lax.ppermute(values, "seq", [(i, i ^ 1) for i in range(count)])


def chip_shift(values):
    count = lax.axis_size("seq")
    return lax.ppermute(values, "seq", [(i, (i + 2) % count) for i in range(count)])


def ring_pieces(values):
    pieces = [values]
    for _ in range(lax.axis_size("seq") // 2 - 1):
        pieces.append(chip_shift(pieces[-1]))
    return pieces


def ring_pairs(values):
    return [(piece, core_swap(piece)) for piece in ring_pieces(values)]


def ring_sum(parts):
    summed = [
        own.astype(jnp.float32) + core_swap(other.astype(jnp.bfloat16)).astype(jnp.float32)
        for own, other in parts
    ]
    if len(summed) == 1:
        return summed[0]
    running = summed[1].astype(jnp.bfloat16)
    for t in list(range(2, len(summed))) + [0]:
        running = chip_shift(running).astype(jnp.float32) + summed[t]
        if t:
            running = running.astype(jnp.bfloat16)
    return running


def adamw_update(master, moment_one, moment_two, gradient, step_rate, decay_weight):
    first_new = beta_one * moment_one + (1.0 - beta_one) * gradient
    second_new = beta_two * moment_two + (1.0 - beta_two) * gradient * gradient
    first_hat = first_new / (1.0 - beta_one**STEP)
    second_hat = second_new / (1.0 - beta_two**STEP)
    master_new = master - step_rate * (
        first_hat / (jnp.sqrt(second_hat) + adam_eps) + decay_weight * master
    )
    return (first_new, second_new, master_new)


def shards(
    tokens,
    cotangent,
    positions,
    qkv_master,
    qkv_first,
    qkv_second,
    out_master,
    out_first,
    out_second,
    gate_up_master,
    gate_up_first,
    gate_up_second,
    down_master,
    down_first,
    down_second,
    small_master,
    small_first,
    small_second,
):
    n_seq = lax.axis_size("seq")
    n_dp = lax.axis_size("dp")
    n_all = n_seq * n_dp
    chips = n_seq // 2
    seq_at = lax.axis_index("seq")
    chip_at, core_at = seq_at // 2, seq_at % 2
    groups = HEADS // KVH
    ff = down_master.shape[0] * n_all
    ff_own = ff // n_seq
    rows_own = qkv_master.shape[0]
    qkv_width = qkv_master.shape[1]
    small_own = small_master.shape[0]
    bf16 = jnp.bfloat16
    f32 = jnp.float32

    small_block = jnp.pad(small_master.astype(bf16), (0, rows_own * HD - small_own)).reshape(rows_own, HD)
    packed = jnp.concatenate([qkv_master.astype(bf16), small_block], axis=1)
    packed = lax.all_gather(packed, ("seq", "dp"), axis=0, tiled=True)
    w_qkv = packed[:, :qkv_width]
    small_params = packed[:, qkv_width:].reshape(n_all, rows_own * HD)[:, :small_own].reshape(-1)
    w_out = lax.all_gather(out_master.astype(bf16), ("seq", "dp"), axis=0, tiled=True)

    gate_up_send = gate_up_master.astype(bf16).reshape(2, rows_own, n_seq, ff_own).transpose(2, 0, 1, 3)
    gate_up_got = lax.all_to_all(gate_up_send, "seq", split_axis=0, concat_axis=0, tiled=True)
    gate_up_all = lax.all_gather(gate_up_got, "dp", axis=0, tiled=False)
    w_gate_up = gate_up_all.transpose(2, 1, 0, 3, 4).reshape(2, n_all * rows_own, ff_own)
    w_down = lax.all_gather(down_master.astype(bf16), "dp", axis=0, tiled=True)

    small_params = small_params.astype(f32)
    gain_one = small_params[:D]
    gain_two = small_params[D : 2 * D]
    qkv_bias = small_params[2 * D :]
    inputs = tokens[0].astype(f32)
    upstream = cotangent[0].astype(f32)
    tok_rows = inputs.shape[0]
    all_places = positions[0]
    seq_length = all_places.shape[0]
    own_places = lax.dynamic_slice_in_dim(all_places, seq_at * tok_rows, tok_rows, 0)
    chip_order = (chip_at - jnp.arange(chips)) % chips
    core_order = jnp.stack([core_at, 1 - core_at])
    ring_places = jnp.take(
        jnp.take(all_places.reshape(chips, 2, tok_rows), chip_order, axis=0), core_order, axis=1
    ).reshape(seq_length)

    cosine, sine_table = rotary_tables(own_places)
    scale_one = lax.rsqrt(jnp.mean(inputs * inputs, axis=-1, keepdims=True) + norm_eps)
    unit_one = inputs * scale_one
    normed_one = (unit_one * gain_one).astype(bf16)
    projected = jnp.dot(normed_one, w_qkv, preferred_element_type=f32) + qkv_bias
    queries = (
        rotate(projected[:, :D].reshape(tok_rows, HEADS, HD), cosine, sine_table)
        .astype(bf16)
        .reshape(tok_rows, KVH, groups, HD)
    )
    key_rows = rotate(
        projected[:, D : D + KVH * HD].reshape(tok_rows, KVH, HD), cosine, sine_table
    ).astype(bf16)
    value_rows = projected[:, D + KVH * HD :].reshape(tok_rows, KVH, HD).astype(bf16)

    key_value = jnp.concatenate(
        [key_rows.reshape(tok_rows, KVH * HD), value_rows.reshape(tok_rows, KVH * HD)], axis=1
    )
    key_value_all = jnp.concatenate([x for pair in ring_pairs(key_value) for x in pair], axis=0)
    keys_all = key_value_all[:, : KVH * HD].reshape(seq_length, KVH, HD)
    values_all = key_value_all[:, KVH * HD :].reshape(seq_length, KVH, HD)

    start_state = (
        jnp.full((KVH, groups, tok_rows), masked_score, f32),
        jnp.zeros((KVH, groups, tok_rows), f32),
        jnp.zeros((tok_rows, KVH, groups, HD), f32),
    )
    visit_forward = forward_visit(queries, own_places)
    fold_state = over_blocks(start_state, keys_all, values_all, ring_places, visit_forward)
    running_max, running_sum, running_out = fold_state
    attended = running_out / jnp.transpose(running_sum, (2, 0, 1))[..., None]
    logsum = running_max + jnp.log(running_sum)
    attended_low = attended.reshape(tok_rows, D).astype(bf16)
    residual = inputs + jnp.dot(attended_low, w_out, preferred_element_type=f32)
    scale_two = lax.rsqrt(jnp.mean(residual * residual, axis=-1, keepdims=True) + norm_eps)
    unit_two = residual * scale_two
    normed_two = (unit_two * gain_two).astype(bf16)

    upstream_pairs = ring_pairs(cotangent[0])
    normed_pairs = ring_pairs(normed_two)
    out_parts, grad_parts = [], []
    kept = []
    for (up_own, up_other), (normed_own, normed_other) in zip(upstream_pairs, normed_pairs):
        ffn_grads = jnp.concatenate([up_own, up_other], axis=0)
        normed = jnp.concatenate([normed_own, normed_other], axis=0)
        gate_rows = jnp.dot(normed, w_gate_up[0], preferred_element_type=f32)
        up_rows = jnp.dot(normed, w_gate_up[1], preferred_element_type=f32)
        sigmoid_gate = jax.nn.sigmoid(gate_rows)
        silu_gate = gate_rows * sigmoid_gate
        hidden = (silu_gate * up_rows).astype(bf16)
        partial_out = jnp.dot(hidden, w_down, preferred_element_type=f32)
        out_parts.append((partial_out[:tok_rows], partial_out[tok_rows:]))
        hidden_grads = jnp.einsum("td,fd->tf", ffn_grads, w_down, preferred_element_type=f32)
        gate_grads = (
            hidden_grads * up_rows * sigmoid_gate * (1.0 + gate_rows * (1.0 - sigmoid_gate))
        ).astype(bf16)
        up_grads = (hidden_grads * silu_gate).astype(bf16)
        partial_grad = jnp.einsum(
            "tf,df->td", gate_grads, w_gate_up[0], preferred_element_type=f32
        ) + jnp.einsum("tf,df->td", up_grads, w_gate_up[1], preferred_element_type=f32)
        grad_parts.append((partial_grad[:tok_rows], partial_grad[tok_rows:]))
        kept.append((ffn_grads, normed, hidden, gate_grads, up_grads))
    normed_two_grads = ring_sum(grad_parts)
    outputs = residual + ring_sum(out_parts)
    ffn_all, normed_all, hidden_all, gate_grads_all, up_grads_all = (
        jnp.concatenate([entry[k] for entry in kept], axis=0) for k in range(5)
    )
    down_grad = jnp.einsum("tf,td->fd", hidden_all, ffn_all, preferred_element_type=f32)
    down_owned = lax.psum_scatter(
        down_grad.astype(bf16), "dp", scatter_dimension=0, tiled=True
    ).astype(f32)
    gate_up_grad = jnp.stack(
        [
            jnp.einsum("td,tf->df", normed_all, gate_grads_all, preferred_element_type=f32).astype(bf16),
            jnp.einsum("td,tf->df", normed_all, up_grads_all, preferred_element_type=f32).astype(bf16),
        ]
    )
    gate_up_grad = gate_up_grad.reshape(2, n_seq, n_dp, rows_own, ff_own).transpose(2, 1, 0, 3, 4)
    gate_up_grad = lax.psum_scatter(
        gate_up_grad.reshape(-1, ff_own), "dp", scatter_dimension=0, tiled=True
    ).reshape(n_seq, 2, rows_own, ff_own)
    gate_up_owned = lax.all_to_all(gate_up_grad, "seq", split_axis=0, concat_axis=0, tiled=True)
    gate_up_owned = gate_up_owned.transpose(1, 2, 0, 3).reshape(2, rows_own, ff).astype(f32)

    gain_two_grad = jnp.sum(normed_two_grads * unit_two, axis=0)
    weighted_two = normed_two_grads * gain_two
    residual_grads = upstream + scale_two * (
        weighted_two - unit_two * jnp.mean(weighted_two * unit_two, axis=-1, keepdims=True)
    )
    branch_grads = residual_grads.astype(bf16)
    out_grad = jnp.einsum("td,te->de", attended_low, branch_grads, preferred_element_type=f32)
    out_owned = lax.psum_scatter(
        out_grad.astype(bf16), ("seq", "dp"), scatter_dimension=0, tiled=True
    ).astype(f32)
    attended_grads = (
        jnp.einsum("te,de->td", branch_grads, w_out, preferred_element_type=f32)
        .astype(bf16)
        .reshape(tok_rows, KVH, groups, HD)
    )
    row_delta = jnp.transpose(jnp.sum(attended_grads.astype(f32) * attended, axis=-1), (1, 2, 0))
    back_start = (
        jnp.zeros((tok_rows, KVH, groups, HD), f32),
        jnp.zeros((seq_length, KVH, HD), f32),
        jnp.zeros((seq_length, KVH, HD), f32),
    )
    visit_backward = backward_visit(queries, own_places, attended_grads, logsum, row_delta)
    back_state = over_blocks(back_start, keys_all, values_all, ring_places, visit_backward)
    query_grads, key_grads, value_grads = back_state
    key_value_grads = jnp.concatenate(
        [key_grads.reshape(seq_length, KVH * HD), value_grads.reshape(seq_length, KVH * HD)], axis=1
    ).reshape(chips, 2, tok_rows, 2 * KVH * HD)
    key_value_owned = ring_sum([(key_value_grads[t, 0], key_value_grads[t, 1]) for t in range(chips)])
    key_owned = key_value_owned[:, : KVH * HD].reshape(tok_rows, KVH, HD)
    value_owned = key_value_owned[:, KVH * HD :]
    query_pre = unrotate(query_grads.reshape(tok_rows, HEADS, HD), cosine, sine_table).reshape(
        tok_rows, D
    )
    key_pre = unrotate(key_owned, cosine, sine_table).reshape(tok_rows, KVH * HD)
    projected_grads = jnp.concatenate([query_pre, key_pre, value_owned], axis=1).astype(bf16)
    bias_grad = jnp.sum(projected_grads.astype(f32), axis=0)
    qkv_grad = jnp.einsum("td,tf->df", normed_one, projected_grads, preferred_element_type=f32)
    normed_one_grads = jnp.einsum("tf,df->td", projected_grads, w_qkv, preferred_element_type=f32)
    gain_one_grad = jnp.sum(normed_one_grads * unit_one, axis=0)
    weighted_one = normed_one_grads * gain_one
    input_grads = residual_grads + scale_one * (
        weighted_one - unit_one * jnp.mean(weighted_one * unit_one, axis=-1, keepdims=True)
    )
    small_grad = jnp.concatenate([gain_one_grad, gain_two_grad, bias_grad]).astype(bf16)
    small_grad = jnp.pad(
        small_grad.reshape(n_all, small_own), ((0, 0), (0, rows_own * HD - small_own))
    ).reshape(n_all * rows_own, HD)
    packed_grad = jnp.concatenate([qkv_grad.astype(bf16), small_grad], axis=1)
    packed_owned = lax.psum_scatter(
        packed_grad, ("seq", "dp"), scatter_dimension=0, tiled=True
    ).astype(f32)
    qkv_owned = packed_owned[:, :qkv_width]
    small_owned = packed_owned[:, qkv_width:].reshape(-1)[:small_own]
    qkv_new = adamw_update(qkv_master, qkv_first, qkv_second, qkv_owned, 0.09, 0.1)
    out_new = adamw_update(out_master, out_first, out_second, out_owned, 0.18, 0.1)
    gate_up_new = adamw_update(
        gate_up_master, gate_up_first, gate_up_second, gate_up_owned, 0.064, 0.1
    )
    down_new = adamw_update(down_master, down_first, down_second, down_owned, 0.026, 0.1)
    small_new = adamw_update(small_master, small_first, small_second, small_owned, 0.6, 0.0)
    return (
        outputs.astype(bf16)[None],
        input_grads[None],
        *qkv_new,
        *out_new,
        *gate_up_new,
        *down_new,
        *small_new,
    )


def solution(mesh):
    in_specs = (
        P("dp", "seq", None),
        P("dp", "seq", None),
        P("dp", None),
        P(("seq", "dp"), None),
        P(("seq", "dp"), None),
        P(("seq", "dp"), None),
        P(("seq", "dp"), None),
        P(("seq", "dp"), None),
        P(("seq", "dp"), None),
        P(None, ("seq", "dp"), None),
        P(None, ("seq", "dp"), None),
        P(None, ("seq", "dp"), None),
        P(("seq", "dp"), None),
        P(("seq", "dp"), None),
        P(("seq", "dp"), None),
        P(("seq", "dp")),
        P(("seq", "dp")),
        P(("seq", "dp")),
    )
    out_specs = (
        P("dp", "seq", None),
        P("dp", "seq", None),
        P(("seq", "dp"), None),
        P(("seq", "dp"), None),
        P(("seq", "dp"), None),
        P(("seq", "dp"), None),
        P(("seq", "dp"), None),
        P(("seq", "dp"), None),
        P(None, ("seq", "dp"), None),
        P(None, ("seq", "dp"), None),
        P(None, ("seq", "dp"), None),
        P(("seq", "dp"), None),
        P(("seq", "dp"), None),
        P(("seq", "dp"), None),
        P(("seq", "dp")),
        P(("seq", "dp")),
        P(("seq", "dp")),
    )
    return jax.shard_map(shards, mesh=mesh, in_specs=in_specs, out_specs=out_specs, check_vma=False)
```

```python
import functools

import jax
import jax.numpy as jnp
from jax import lax
from jax.experimental import pallas as pl
from jax.experimental.pallas import tpu as pltpu
from jax.sharding import PartitionSpec as P

D = 1536
HEADS = 12
KVH = 2
HD = 128
STEP = 10


norm_eps = 1e-06
rope_base = 1000000.0
beta_one = 0.9
beta_two = 0.95
adam_eps = 1e-08
masked_score = -1e30
log2_e = 1.4426950408889634
bf16 = jnp.bfloat16
f32 = jnp.float32


def rotary_tables(places):
    half_size = HD // 2
    freqs = rope_base ** (-(jnp.arange(half_size).astype(jnp.float32) * (2.0 / HD)))
    angles = places.astype(jnp.float32)[:, None] * freqs[None, :]
    return (jnp.cos(angles), jnp.sin(angles))


def rotate(values, cosine, sine_table):
    half_size = values.shape[-1] // 2
    first_half = values[..., :half_size]
    second_half = values[..., half_size:]
    cosine = cosine[:, None, :]
    sine_table = sine_table[:, None, :]
    return jnp.concatenate(
        [
            first_half * cosine - second_half * sine_table,
            second_half * cosine + first_half * sine_table,
        ],
        axis=-1,
    )


def unrotate(gradients, cosine, sine_table):
    half_size = gradients.shape[-1] // 2
    first_half = gradients[..., :half_size]
    second_half = gradients[..., half_size:]
    cosine = cosine[:, None, :]
    sine_table = sine_table[:, None, :]
    return jnp.concatenate(
        [
            first_half * cosine + second_half * sine_table,
            second_half * cosine - first_half * sine_table,
        ],
        axis=-1,
    )


def attend_kernel(q_ref, kv_ref, query_places, key_places, out_ref, lse_ref):
    groups = HEADS // KVH
    scale = HD**-0.5 * log2_e
    visible = key_places[...] <= query_places[...]
    for kv in range(KVH):
        keys = kv_ref[:, kv * HD : (kv + 1) * HD]
        values = kv_ref[:, (KVH + kv) * HD : (KVH + kv + 1) * HD].T
        for h in range(kv * groups, (kv + 1) * groups):
            columns = slice(h * HD, (h + 1) * HD)
            scores = lax.dot_general(
                keys, q_ref[:, columns], (((1,), (1,)), ((), ())), preferred_element_type=f32
            )
            scores = jnp.where(visible, scores, masked_score)
            top = jnp.max(scores, axis=0, keepdims=True)
            weights = jnp.exp2((scores - top) * scale)
            total = jnp.sum(weights, axis=0, keepdims=True)
            mixed = jnp.dot(values, weights.astype(bf16), preferred_element_type=f32)
            out_ref[:, columns] = (mixed / total).T
            lse_ref[h : h + 1, :] = top * scale + jnp.log2(total)


def attend(queries, key_value, query_places, key_places):
    rows, total = queries.shape[0], key_value.shape[0]
    return pl.pallas_call(
        attend_kernel,
        out_shape=(
            jax.ShapeDtypeStruct((rows, HEADS * HD), f32),
            jax.ShapeDtypeStruct((HEADS, rows), f32),
        ),
        compiler_params=pltpu.CompilerParams(vmem_limit_bytes=48 << 20),
        cost_estimate=pl.CostEstimate(
            flops=4 * rows * total * HD * HEADS,
            bytes_accessed=8 * rows * HEADS * HD,
            transcendentals=rows * total * HEADS,
        ),
        name="attend",
    )(queries, key_value, query_places.reshape(1, rows), key_places.reshape(total, 1))


def attend_back_kernel(
    q_ref,
    kv_ref,
    grad_ref,
    out_ref,
    lse_ref,
    query_places,
    key_places,
    q_grad_ref,
    kv_grad_ref,
    q_rows,
    grad_rows,
    deltas,
    q_sums,
    *,
    block,
):
    rows = q_ref.shape[0]
    groups = HEADS // KVH
    scale = HD**-0.5
    for kv in range(KVH):
        for j in range(groups):
            part = slice(j * rows, (j + 1) * rows)
            columns = slice((kv * groups + j) * HD, (kv * groups + j + 1) * HD)
            q_rows[part, :] = q_ref[:, columns]
            grads = grad_ref[:, columns]
            grad_rows[part, :] = grads
            product = grads.astype(f32) * out_ref[:, columns]
            deltas[:, part] = jnp.sum(product.T, axis=0, keepdims=True)
        q_sums[...] = jnp.zeros_like(q_sums)

        @pl.loop(0, kv_ref.shape[0] // block)
        def _(step):
            at = pl.ds(pl.multiple_of(step * block, block), block)
            visible = key_places[at, :] <= query_places[...]
            keys = kv_ref[at, kv * HD : (kv + 1) * HD]
            values = kv_ref[at, (KVH + kv) * HD : (KVH + kv + 1) * HD]
            key_sum = value_sum = None
            for j in range(groups):
                part = slice(j * rows, (j + 1) * rows)
                h = kv * groups + j
                queries, grads = q_rows[part, :], grad_rows[part, :]
                scores = lax.dot_general(
                    keys, queries, (((1,), (1,)), ((), ())), preferred_element_type=f32
                )
                weights = jnp.where(
                    visible, jnp.exp2(scores * (scale * log2_e) - lse_ref[h : h + 1, :]), 0.0
                )
                weight_grads = lax.dot_general(
                    values, grads, (((1,), (1,)), ((), ())), preferred_element_type=f32
                )
                score_grads = (weights * (weight_grads - deltas[:, part])).astype(bf16)
                value_part = jnp.dot(weights.astype(bf16), grads, preferred_element_type=f32)
                key_part = jnp.dot(score_grads, queries, preferred_element_type=f32)
                key_sum = key_part if key_sum is None else key_sum + key_part
                value_sum = value_part if value_sum is None else value_sum + value_part
                q_sums[part, :] += lax.dot_general(
                    score_grads, keys, (((0,), (0,)), ((), ())), preferred_element_type=f32
                )
            kv_grad_ref[at, kv * HD : (kv + 1) * HD] = (key_sum * scale).astype(bf16)
            kv_grad_ref[at, (KVH + kv) * HD : (KVH + kv + 1) * HD] = value_sum.astype(bf16)

        for j in range(groups):
            columns = slice((kv * groups + j) * HD, (kv * groups + j + 1) * HD)
            q_grad_ref[:, columns] = q_sums[j * rows : (j + 1) * rows, :] * scale


def attend_back(queries, key_value, grads, attended, lse, query_places, key_places):
    rows, total = queries.shape[0], key_value.shape[0]
    groups = HEADS // KVH
    return pl.pallas_call(
        functools.partial(attend_back_kernel, block=512),
        out_shape=(
            jax.ShapeDtypeStruct((rows, HEADS * HD), f32),
            jax.ShapeDtypeStruct((total, 2 * KVH * HD), bf16),
        ),
        scratch_shapes=[
            pltpu.VMEM((groups * rows, HD), bf16),
            pltpu.VMEM((groups * rows, HD), bf16),
            pltpu.VMEM((1, groups * rows), f32),
            pltpu.VMEM((groups * rows, HD), f32),
        ],
        compiler_params=pltpu.CompilerParams(vmem_limit_bytes=48 << 20),
        cost_estimate=pl.CostEstimate(
            flops=10 * rows * total * HD * HEADS,
            bytes_accessed=16 * rows * HEADS * HD,
            transcendentals=rows * total * HEADS,
        ),
        name="attend_back",
    )(
        queries,
        key_value,
        grads,
        attended,
        lse,
        query_places.reshape(1, rows),
        key_places.reshape(total, 1),
    )


def seq_perm(values, chips, flip):
    count = lax.axis_size("seq")
    return lax.ppermute(
        values, "seq", [(i, ((i + 2 * chips) % count) ^ flip) for i in range(count)]
    )


def dp_perm(values, bit):
    return lax.ppermute(values, "dp", [(i, i ^ bit) for i in range(lax.axis_size("dp"))])


def dp_bits():
    return [1 << i for i in range(lax.axis_size("dp").bit_length() - 1)]


def dp_gather(values, bits):
    have = [(values, 0)]
    for bit in bits:
        have += [(dp_perm(piece, bit), k ^ bit) for piece, k in have]
    return have


def pick(values, index, axis):
    return lax.dynamic_index_in_dim(values, index, axis, keepdims=False)


def assemble_kernel(where, *refs, splits, counts):
    ins, outs, sems = refs[: len(counts)], refs[len(counts) : -1], refs[-1]
    copies = []
    entry = 0
    for ref, (column, count) in zip(ins, counts):
        for i in range(count):
            for out, start, width in splits[column]:
                copies.append(
                    pltpu.make_async_copy(
                        ref.at[i, :, pl.ds(start, width)],
                        outs[out[0]].at[where[entry], :, pl.ds(out[1], width)],
                        sems.at[len(copies)],
                    )
                )
            entry += 1
    for copy in copies:
        copy.start()
    for copy in copies:
        copy.wait()


def assemble(pieces, where, splits, out_widths):
    counts = [(column, array.shape[0]) for array, column in pieces]
    rows = pieces[0][0].shape[1]
    blocks = sum(count for column, count in counts if column == 0)
    n_copies = sum(count * len(splits[column]) for column, count in counts)
    return pl.pallas_call(
        functools.partial(assemble_kernel, splits=splits, counts=counts),
        out_shape=tuple(jax.ShapeDtypeStruct((blocks, rows, w), bf16) for w in out_widths),
        in_specs=[pl.BlockSpec(memory_space=pltpu.SMEM)]
        + [pl.BlockSpec(memory_space=pl.ANY)] * len(pieces),
        out_specs=tuple(pl.BlockSpec(memory_space=pltpu.VMEM) for _ in out_widths),
        scratch_shapes=[pltpu.SemaphoreType.DMA((n_copies,))],
        compiler_params=pltpu.CompilerParams(vmem_limit_bytes=48 << 20),
        cost_estimate=pl.CostEstimate(
            flops=0, bytes_accessed=4 * blocks * rows * sum(out_widths), transcendentals=0
        ),
        name="assemble",
    )(where.astype(jnp.int32), *[array for array, _ in pieces])


def places_of():
    n_chips = lax.axis_size("seq") // 2
    seq_at = lax.axis_index("seq")
    return n_chips, seq_at // 2, seq_at % 2, lax.axis_size("dp"), lax.axis_index("dp")


def gather_rows(values, cut, splits, out_widths):
    n_chips, chip, core, n_dp, dp_at = places_of()
    ring = [values] + [seq_perm(values, t, 0) for t in range(1, n_chips)]
    pieces, where = [], []
    for column, (lo, hi) in enumerate(((0, cut), (cut, values.shape[1]))):
        bits = dp_bits()[:: 1 if column == 0 else -1]
        for piece, k in dp_gather(jnp.stack([r[:, lo:hi] for r in ring]), bits):
            for flip, array in ((0, piece), (1, seq_perm(piece, 0, 1))):
                pieces.append((array, column))
                where += [
                    (((chip - t) % n_chips) * 2 + (core ^ flip)) * n_dp + (dp_at ^ k)
                    for t in range(n_chips)
                ]
    return assemble(pieces, jnp.stack(where), splits, out_widths)


def halve(values, axes, bits):
    dp_at = lax.axis_index("dp")
    axes = dict(axes)
    for bit in bits:
        axis = axes.pop(bit)
        mine = (dp_at // bit) % 2
        got = dp_perm(pick(values, 1 - mine, axis), bit)
        values = (pick(values, mine, axis).astype(f32) + got.astype(f32)).astype(bf16)
        axes = {b: x - (x > axis) for b, x in axes.items()}
    return values


def sum_rows(values, cut):
    n_chips, chip, core, n_dp, dp_at = places_of()
    rows, width = values.shape[1:]
    values = values.reshape(n_chips, 2, n_dp, rows, width)
    got = seq_perm(pick(values, 1 - core, 1), 0, 1)
    values = (pick(values, core, 1).astype(f32) + got.astype(f32)).astype(bf16)
    bits = dp_bits()
    parts = []
    for lo, hi, order in ((0, cut, bits), (cut, width, bits[::-1])):
        part = values[..., lo:hi].reshape((n_chips,) + (2,) * len(bits) + (rows, hi - lo))
        part = halve(part, {b: len(bits) - i for i, b in enumerate(bits)}, order)
        total = pick(part, chip, 0).astype(f32)
        for t in range(1, n_chips):
            total = total + seq_perm(pick(part, (chip + t) % n_chips, 0), t, 0).astype(f32)
        parts.append(total)
    return jnp.concatenate(parts, axis=1)


def exchange(values):
    n_chips, chip, core, _, _ = places_of()
    values = values.reshape((n_chips, 2) + values.shape[1:])
    kept = pick(values, core, 1)
    got = seq_perm(pick(values, 1 - core, 1), 0, 1)
    pairs = jnp.stack([kept, got], axis=1)
    out = [pick(pairs, chip, 0)]
    for t in range(1, n_chips):
        out.append(seq_perm(pick(pairs, (chip + t) % n_chips, 0), t, 0))
    return out


def ring_pairs(values):
    pieces = [values]
    for _ in range(lax.axis_size("seq") // 2 - 1):
        pieces.append(seq_perm(pieces[-1], 1, 0))
    return [(piece, seq_perm(piece, 0, 1)) for piece in pieces]


def sent_pairs(values):
    pieces = [values] + [seq_perm(values, t, 0) for t in range(1, lax.axis_size("seq") // 2)]
    return [(piece, seq_perm(piece, 0, 1)) for piece in pieces]


def ring_sum(parts):
    summed = [
        own.astype(f32) + seq_perm(other.astype(bf16), 0, 1).astype(f32) for own, other in parts
    ]
    if len(summed) == 1:
        return summed[0]
    running = summed[1].astype(bf16)
    for t in list(range(2, len(summed))) + [0]:
        running = seq_perm(running, 1, 0).astype(f32) + summed[t]
        if t:
            running = running.astype(bf16)
    return running


def adamw_update(master, moment_one, moment_two, gradient, step_rate, decay_weight):
    first_new = beta_one * moment_one + (1.0 - beta_one) * gradient
    second_new = beta_two * moment_two + (1.0 - beta_two) * gradient * gradient
    first_hat = first_new / (1.0 - beta_one**STEP)
    second_hat = second_new / (1.0 - beta_two**STEP)
    master_new = master - step_rate * (
        first_hat / (jnp.sqrt(second_hat) + adam_eps) + decay_weight * master
    )
    return (first_new, second_new, master_new)


def shards(
    tokens,
    cotangent,
    positions,
    qkv_master,
    qkv_first,
    qkv_second,
    out_master,
    out_first,
    out_second,
    gate_up_master,
    gate_up_first,
    gate_up_second,
    down_master,
    down_first,
    down_second,
    small_master,
    small_first,
    small_second,
):
    n_seq = lax.axis_size("seq")
    n_dp = lax.axis_size("dp")
    n_all = n_seq * n_dp
    chips = n_seq // 2
    seq_at = lax.axis_index("seq")
    dp_at = lax.axis_index("dp")
    chip_at, core_at = seq_at // 2, seq_at % 2
    ff = down_master.shape[0] * n_all
    ff_own = ff // n_seq
    rows_own = qkv_master.shape[0]
    qkv_width = qkv_master.shape[1]
    small_own = small_master.shape[0]

    half = qkv_width // 2
    small_block = jnp.pad(
        small_master.astype(bf16), (0, rows_own * HD - small_own)
    ).reshape(rows_own, HD)
    packed = jnp.concatenate([small_block, qkv_master.astype(bf16)], axis=1)
    w_qkv, small_blocks = gather_rows(
        packed,
        HD + half,
        ((((1, 0), 0, HD), ((0, 0), HD, half)), (((0, half), 0, half),)),
        (qkv_width, HD),
    )
    w_qkv = w_qkv.reshape(D, qkv_width)
    small_params = small_blocks.reshape(n_all, rows_own * HD)[:, :small_own].reshape(-1)
    (w_out,) = gather_rows(
        out_master.astype(bf16),
        D // 2,
        ((((0, 0), 0, D // 2),), (((0, D // 2), 0, D // 2),)),
        (D,),
    )
    w_out = w_out.reshape(D, D)

    gate_up_send = (
        gate_up_master.astype(bf16).reshape(2, rows_own, n_seq, ff_own).transpose(2, 0, 1, 3)
    )
    gate_up_got = jnp.concatenate(exchange(gate_up_send), axis=0)
    ring_order = [
        ((chip_at - t) % chips) * 2 + (core_at ^ flip) for t in range(chips) for flip in range(2)
    ]
    w_gate, w_up = (
        assemble(
            [(piece, 0) for piece, _ in gathered],
            jnp.stack([s * n_dp + (dp_at ^ k) for _, k in gathered for s in ring_order]),
            ((((0, 0), 0, ff_own),),),
            (ff_own,),
        )[0].reshape(D, ff_own)
        for gathered in (
            dp_gather(gate_up_got[:, 0], dp_bits()),
            dp_gather(gate_up_got[:, 1], dp_bits()[::-1]),
        )
    )
    w_down = lax.all_gather(down_master.astype(bf16), "dp", axis=0, tiled=True)

    small_params = small_params.astype(f32)
    gain_one = small_params[:D]
    gain_two = small_params[D : 2 * D]
    qkv_bias = small_params[2 * D :]
    inputs = tokens[0].astype(f32)
    upstream = cotangent[0].astype(f32)
    tok_rows = inputs.shape[0]
    all_places = positions[0]
    seq_length = all_places.shape[0]
    own_places = lax.dynamic_slice_in_dim(all_places, seq_at * tok_rows, tok_rows, 0)
    chip_order = (chip_at - jnp.arange(chips)) % chips
    core_order = jnp.stack([core_at, 1 - core_at])
    ring_places = jnp.take(
        jnp.take(all_places.reshape(chips, 2, tok_rows), chip_order, axis=0), core_order, axis=1
    )
    ring_places = ring_places.transpose(1, 0, 2).reshape(seq_length)

    cosine, sine_table = rotary_tables(own_places)
    scale_one = lax.rsqrt(jnp.mean(inputs * inputs, axis=-1, keepdims=True) + norm_eps)
    unit_one = inputs * scale_one
    normed_one = (unit_one * gain_one).astype(bf16)
    projected = jnp.dot(normed_one, w_qkv, preferred_element_type=f32) + qkv_bias
    queries = (
        rotate(projected[:, :D].reshape(tok_rows, HEADS, HD), cosine, sine_table)
        .astype(bf16)
        .reshape(tok_rows, D)
    )
    key_rows = rotate(
        projected[:, D : D + KVH * HD].reshape(tok_rows, KVH, HD), cosine, sine_table
    ).astype(bf16)
    value_rows = projected[:, D + KVH * HD :].reshape(tok_rows, KVH, HD).astype(bf16)

    key_value = jnp.concatenate(
        [key_rows.reshape(tok_rows, KVH * HD), value_rows.reshape(tok_rows, KVH * HD)], axis=1
    )
    key_value_own = jnp.concatenate(
        [key_value] + [seq_perm(key_value, t, 0) for t in range(1, chips)], axis=0
    )
    key_value_all = jnp.concatenate([key_value_own, seq_perm(key_value_own, 0, 1)], axis=0)
    attended, logsum = attend(queries, key_value_all, own_places, ring_places)
    attended_low = attended.astype(bf16)
    residual = inputs + jnp.dot(attended_low, w_out, preferred_element_type=f32)
    scale_two = lax.rsqrt(jnp.mean(residual * residual, axis=-1, keepdims=True) + norm_eps)
    unit_two = residual * scale_two
    normed_two = (unit_two * gain_two).astype(bf16)

    upstream_pairs = sent_pairs(cotangent[0])
    normed_pairs = ring_pairs(normed_two)
    out_parts, grad_parts = [], []
    kept = []
    for (up_own, up_other), (normed_own, normed_other) in zip(upstream_pairs, normed_pairs):
        ffn_grads = jnp.concatenate([up_own, up_other], axis=0)
        normed = jnp.concatenate([normed_own, normed_other], axis=0)
        gate_rows = jnp.dot(normed, w_gate, preferred_element_type=f32)
        up_rows = jnp.dot(normed, w_up, preferred_element_type=f32)
        sigmoid_gate = jax.nn.sigmoid(gate_rows)
        silu_gate = gate_rows * sigmoid_gate
        hidden = (silu_gate * up_rows).astype(bf16)
        partial_out = jnp.dot(hidden, w_down, preferred_element_type=f32)
        out_parts.append((partial_out[:tok_rows], partial_out[tok_rows:]))
        hidden_grads = jnp.einsum("td,fd->tf", ffn_grads, w_down, preferred_element_type=f32)
        gate_grads = (
            hidden_grads * up_rows * sigmoid_gate * (1.0 + gate_rows * (1.0 - sigmoid_gate))
        ).astype(bf16)
        up_grads = (hidden_grads * silu_gate).astype(bf16)
        partial_grad = jnp.einsum(
            "tf,df->td", gate_grads, w_gate, preferred_element_type=f32
        ) + jnp.einsum("tf,df->td", up_grads, w_up, preferred_element_type=f32)
        grad_parts.append((partial_grad[:tok_rows], partial_grad[tok_rows:]))
        kept.append((ffn_grads, normed, hidden, gate_grads, up_grads))
    normed_two_grads = ring_sum(grad_parts)
    outputs = residual + ring_sum(out_parts)
    ffn_all, normed_all, hidden_all, gate_grads_all, up_grads_all = (
        jnp.concatenate([entry[k] for entry in kept], axis=0) for k in range(5)
    )
    down_grad = jnp.einsum("tf,td->fd", hidden_all, ffn_all, preferred_element_type=f32)
    down_owned = lax.psum_scatter(
        down_grad.astype(bf16), "dp", scatter_dimension=0, tiled=True
    ).astype(f32)
    gate_up_sums = []
    for grads, order in ((gate_grads_all, dp_bits()), (up_grads_all, dp_bits()[::-1])):
        part = jnp.einsum("td,tf->df", normed_all, grads, preferred_element_type=f32).astype(bf16)
        part = part.reshape((n_seq,) + (2,) * len(order) + (rows_own, ff_own))
        axes = {bit: len(order) - i for i, bit in enumerate(dp_bits())}
        gate_up_sums.append(halve(part, axes, order))
    gate_up_pieces = jnp.concatenate(exchange(jnp.stack(gate_up_sums, axis=1)), axis=0)
    gate_up_owned = jnp.take(gate_up_pieces, jnp.argsort(jnp.stack(ring_order)), axis=0)
    gate_up_owned = gate_up_owned.transpose(1, 2, 0, 3).reshape(2, rows_own, ff).astype(f32)

    gain_two_grad = jnp.sum(normed_two_grads * unit_two, axis=0)
    weighted_two = normed_two_grads * gain_two
    residual_grads = upstream + scale_two * (
        weighted_two - unit_two * jnp.mean(weighted_two * unit_two, axis=-1, keepdims=True)
    )
    branch_grads = residual_grads.astype(bf16)
    out_grad = jnp.einsum("td,te->de", attended_low, branch_grads, preferred_element_type=f32)
    out_owned = sum_rows(out_grad.astype(bf16).reshape(n_all, rows_own, D), D // 2)
    attended_grads = jnp.einsum(
        "te,de->td", branch_grads, w_out, preferred_element_type=f32
    ).astype(bf16)
    query_grads, key_value_grads = attend_back(
        queries, key_value_all, attended_grads, attended, logsum, own_places, ring_places
    )
    key_value_grads = key_value_grads.reshape(2, chips, tok_rows, 2 * KVH * HD)
    others = seq_perm(key_value_grads[1], 0, 1)
    both = (key_value_grads[0].astype(f32) + others.astype(f32)).astype(bf16)
    key_value_owned = both[0].astype(f32)
    for t in range(1, chips):
        key_value_owned = key_value_owned + seq_perm(both[t], chips - t, 0).astype(f32)
    key_owned = key_value_owned[:, : KVH * HD].reshape(tok_rows, KVH, HD)
    value_owned = key_value_owned[:, KVH * HD :]
    query_pre = unrotate(query_grads.reshape(tok_rows, HEADS, HD), cosine, sine_table).reshape(
        tok_rows, D
    )
    key_pre = unrotate(key_owned, cosine, sine_table).reshape(tok_rows, KVH * HD)
    projected_grads = jnp.concatenate([query_pre, key_pre, value_owned], axis=1).astype(bf16)
    bias_grad = jnp.sum(projected_grads.astype(f32), axis=0)
    qkv_grad = jnp.einsum("td,tf->df", normed_one, projected_grads, preferred_element_type=f32)
    normed_one_grads = jnp.einsum("tf,df->td", projected_grads, w_qkv, preferred_element_type=f32)
    gain_one_grad = jnp.sum(normed_one_grads * unit_one, axis=0)
    weighted_one = normed_one_grads * gain_one
    input_grads = residual_grads + scale_one * (
        weighted_one - unit_one * jnp.mean(weighted_one * unit_one, axis=-1, keepdims=True)
    )
    small_grad = jnp.concatenate([gain_one_grad, gain_two_grad, bias_grad]).astype(bf16)
    small_grad = jnp.pad(
        small_grad.reshape(n_all, small_own), ((0, 0), (0, rows_own * HD - small_own))
    ).reshape(n_all * rows_own, HD)
    packed_grad = jnp.concatenate([small_grad, qkv_grad.astype(bf16)], axis=1)
    packed_owned = sum_rows(packed_grad.reshape(n_all, rows_own, HD + qkv_width), HD + half)
    qkv_owned = packed_owned[:, HD:]
    small_owned = packed_owned[:, :HD].reshape(-1)[:small_own]
    qkv_new = adamw_update(qkv_master, qkv_first, qkv_second, qkv_owned, 0.09, 0.1)
    out_new = adamw_update(out_master, out_first, out_second, out_owned, 0.18, 0.1)
    gate_up_new = adamw_update(
        gate_up_master, gate_up_first, gate_up_second, gate_up_owned, 0.064, 0.1
    )
    down_new = adamw_update(down_master, down_first, down_second, down_owned, 0.026, 0.1)
    small_new = adamw_update(small_master, small_first, small_second, small_owned, 0.6, 0.0)
    return (
        outputs.astype(bf16)[None],
        input_grads[None],
        *qkv_new,
        *out_new,
        *gate_up_new,
        *down_new,
        *small_new,
    )


def solution(mesh):
    in_specs = (
        P("dp", "seq", None),
        P("dp", "seq", None),
        P("dp", None),
        P(("seq", "dp"), None),
        P(("seq", "dp"), None),
        P(("seq", "dp"), None),
        P(("seq", "dp"), None),
        P(("seq", "dp"), None),
        P(("seq", "dp"), None),
        P(None, ("seq", "dp"), None),
        P(None, ("seq", "dp"), None),
        P(None, ("seq", "dp"), None),
        P(("seq", "dp"), None),
        P(("seq", "dp"), None),
        P(("seq", "dp"), None),
        P(("seq", "dp")),
        P(("seq", "dp")),
        P(("seq", "dp")),
    )
    out_specs = (
        P("dp", "seq", None),
        P("dp", "seq", None),
        P(("seq", "dp"), None),
        P(("seq", "dp"), None),
        P(("seq", "dp"), None),
        P(("seq", "dp"), None),
        P(("seq", "dp"), None),
        P(("seq", "dp"), None),
        P(None, ("seq", "dp"), None),
        P(None, ("seq", "dp"), None),
        P(None, ("seq", "dp"), None),
        P(("seq", "dp"), None),
        P(("seq", "dp"), None),
        P(("seq", "dp"), None),
        P(("seq", "dp")),
        P(("seq", "dp")),
        P(("seq", "dp")),
    )
    return jax.shard_map(shards, mesh=mesh, in_specs=in_specs, out_specs=out_specs, check_vma=False)
```

```python
import functools

import jax
import jax.numpy as jnp
from jax import lax
from jax.experimental import pallas as pl
from jax.experimental.pallas import tpu as pltpu
from jax.sharding import PartitionSpec as P

D = 1536
HEADS = 12
KVH = 2
HD = 128
STEP = 10


norm_eps = 1e-06
rope_base = 1000000.0
beta_one = 0.9
beta_two = 0.95
adam_eps = 1e-08
masked_score = -1e30
log2_e = 1.4426950408889634
bf16 = jnp.bfloat16
f32 = jnp.float32


def rotary_tables(places):
    half_size = HD // 2
    freqs = rope_base ** (-(jnp.arange(half_size).astype(jnp.float32) * (2.0 / HD)))
    angles = places.astype(jnp.float32)[:, None] * freqs[None, :]
    return (jnp.cos(angles), jnp.sin(angles))


def rotate(values, cosine, sine_table):
    half_size = values.shape[-1] // 2
    first_half = values[..., :half_size]
    second_half = values[..., half_size:]
    cosine = cosine[:, None, :]
    sine_table = sine_table[:, None, :]
    return jnp.concatenate(
        [
            first_half * cosine - second_half * sine_table,
            second_half * cosine + first_half * sine_table,
        ],
        axis=-1,
    )


def unrotate(gradients, cosine, sine_table):
    half_size = gradients.shape[-1] // 2
    first_half = gradients[..., :half_size]
    second_half = gradients[..., half_size:]
    cosine = cosine[:, None, :]
    sine_table = sine_table[:, None, :]
    return jnp.concatenate(
        [
            first_half * cosine + second_half * sine_table,
            second_half * cosine - first_half * sine_table,
        ],
        axis=-1,
    )


small_cost = pl.CostEstimate(flops=10**6, bytes_accessed=10**6, transcendentals=0)


def after(values, *others):
    return lax.optimization_barrier((values,) + others)[0]


def attend_kernel(q_ref, kv_ref, query_places, key_places, out_ref, lse_ref):
    groups = HEADS // KVH
    scale = HD**-0.5 * log2_e
    visible = key_places[...] <= query_places[...]
    for kv in range(KVH):
        keys = kv_ref[:, kv * HD : (kv + 1) * HD]
        values = kv_ref[:, (KVH + kv) * HD : (KVH + kv + 1) * HD].T
        for h in range(kv * groups, (kv + 1) * groups):
            columns = slice(h * HD, (h + 1) * HD)
            scores = lax.dot_general(
                keys, q_ref[:, columns], (((1,), (1,)), ((), ())), preferred_element_type=f32
            )
            scores = jnp.where(visible, scores, masked_score)
            top = jnp.max(scores, axis=0, keepdims=True)
            weights = jnp.exp2((scores - top) * scale)
            total = jnp.sum(weights, axis=0, keepdims=True)
            mixed = jnp.dot(values, weights.astype(bf16), preferred_element_type=f32)
            out_ref[:, columns] = (mixed / total).T
            lse_ref[h : h + 1, :] = top * scale + jnp.log2(total)


def attend(queries, key_value, query_places, key_places):
    rows, total = queries.shape[0], key_value.shape[0]
    return pl.pallas_call(
        attend_kernel,
        out_shape=(
            jax.ShapeDtypeStruct((rows, HEADS * HD), f32),
            jax.ShapeDtypeStruct((HEADS, rows), f32),
        ),
        compiler_params=pltpu.CompilerParams(vmem_limit_bytes=48 << 20),
        cost_estimate=small_cost,
        name="attend",
    )(queries, key_value, query_places.reshape(1, rows), key_places.reshape(total, 1))


def attend_back_kernel(
    q_ref,
    kv_ref,
    grad_ref,
    out_ref,
    lse_ref,
    query_places,
    key_places,
    q_grad_ref,
    kv_grad_ref,
    q_rows,
    grad_rows,
    deltas,
    q_sums,
    *,
    block,
):
    rows = q_ref.shape[0]
    groups = HEADS // KVH
    scale = HD**-0.5
    for kv in range(KVH):
        for j in range(groups):
            part = slice(j * rows, (j + 1) * rows)
            columns = slice((kv * groups + j) * HD, (kv * groups + j + 1) * HD)
            q_rows[part, :] = q_ref[:, columns]
            grads = grad_ref[:, columns]
            grad_rows[part, :] = grads
            product = grads.astype(f32) * out_ref[:, columns]
            deltas[:, part] = jnp.sum(product.T, axis=0, keepdims=True)
        q_sums[...] = jnp.zeros_like(q_sums)

        @pl.loop(0, kv_ref.shape[0] // block)
        def _(step):
            at = pl.ds(pl.multiple_of(step * block, block), block)
            visible = key_places[at, :] <= query_places[...]
            keys = kv_ref[at, kv * HD : (kv + 1) * HD]
            values = kv_ref[at, (KVH + kv) * HD : (KVH + kv + 1) * HD]
            key_sum = value_sum = None
            for j in range(groups):
                part = slice(j * rows, (j + 1) * rows)
                h = kv * groups + j
                queries, grads = q_rows[part, :], grad_rows[part, :]
                scores = lax.dot_general(
                    keys, queries, (((1,), (1,)), ((), ())), preferred_element_type=f32
                )
                weights = jnp.where(
                    visible, jnp.exp2(scores * (scale * log2_e) - lse_ref[h : h + 1, :]), 0.0
                )
                weight_grads = lax.dot_general(
                    values, grads, (((1,), (1,)), ((), ())), preferred_element_type=f32
                )
                score_grads = (weights * (weight_grads - deltas[:, part])).astype(bf16)
                value_part = jnp.dot(weights.astype(bf16), grads, preferred_element_type=f32)
                key_part = jnp.dot(score_grads, queries, preferred_element_type=f32)
                key_sum = key_part if key_sum is None else key_sum + key_part
                value_sum = value_part if value_sum is None else value_sum + value_part
                q_sums[part, :] += lax.dot_general(
                    score_grads, keys, (((0,), (0,)), ((), ())), preferred_element_type=f32
                )
            kv_grad_ref[at, kv * HD : (kv + 1) * HD] = (key_sum * scale).astype(bf16)
            kv_grad_ref[at, (KVH + kv) * HD : (KVH + kv + 1) * HD] = value_sum.astype(bf16)

        for j in range(groups):
            columns = slice((kv * groups + j) * HD, (kv * groups + j + 1) * HD)
            q_grad_ref[:, columns] = q_sums[j * rows : (j + 1) * rows, :] * scale


def attend_back(queries, key_value, grads, attended, lse, query_places, key_places):
    rows, total = queries.shape[0], key_value.shape[0]
    groups = HEADS // KVH
    return pl.pallas_call(
        functools.partial(attend_back_kernel, block=512),
        out_shape=(
            jax.ShapeDtypeStruct((rows, HEADS * HD), f32),
            jax.ShapeDtypeStruct((total, 2 * KVH * HD), bf16),
        ),
        scratch_shapes=[
            pltpu.VMEM((groups * rows, HD), bf16),
            pltpu.VMEM((groups * rows, HD), bf16),
            pltpu.VMEM((1, groups * rows), f32),
            pltpu.VMEM((groups * rows, HD), f32),
        ],
        compiler_params=pltpu.CompilerParams(vmem_limit_bytes=48 << 20),
        cost_estimate=small_cost,
        name="attend_back",
    )(
        queries,
        key_value,
        grads,
        attended,
        lse,
        query_places.reshape(1, rows),
        key_places.reshape(total, 1),
    )


def seq_perm(values, chips, flip):
    count = lax.axis_size("seq")
    return lax.ppermute(
        values, "seq", [(i, ((i + 2 * chips) % count) ^ flip) for i in range(count)]
    )


def dp_perm(values, bit):
    return lax.ppermute(values, "dp", [(i, i ^ bit) for i in range(lax.axis_size("dp"))])


def dp_bits():
    return [1 << i for i in range(lax.axis_size("dp").bit_length() - 1)]


def dp_gather(values, bits):
    have = [(values, 0)]
    for bit in bits:
        have += [(dp_perm(piece, bit), k ^ bit) for piece, k in have]
    return have


def pick(values, index, axis):
    return lax.dynamic_index_in_dim(values, index, axis, keepdims=False)


def assemble_kernel(where, *refs, splits, counts):
    ins, outs, sems = refs[: len(counts)], refs[len(counts) : -1], refs[-1]
    copies = []
    entry = 0
    for ref, (column, count) in zip(ins, counts):
        for i in range(count):
            for out, start, width in splits[column]:
                copies.append(
                    pltpu.make_async_copy(
                        ref.at[i, :, pl.ds(start, width)],
                        outs[out[0]].at[where[entry], :, pl.ds(out[1], width)],
                        sems.at[len(copies)],
                    )
                )
            entry += 1
    for copy in copies:
        copy.start()
    for copy in copies:
        copy.wait()


def assemble(pieces, where, splits, out_widths):
    counts = [(column, array.shape[0]) for array, column in pieces]
    rows = pieces[0][0].shape[1]
    blocks = sum(count for column, count in counts if column == 0)
    n_copies = sum(count * len(splits[column]) for column, count in counts)
    return pl.pallas_call(
        functools.partial(assemble_kernel, splits=splits, counts=counts),
        out_shape=tuple(jax.ShapeDtypeStruct((blocks, rows, w), bf16) for w in out_widths),
        in_specs=[pl.BlockSpec(memory_space=pltpu.SMEM)]
        + [pl.BlockSpec(memory_space=pl.ANY)] * len(pieces),
        out_specs=tuple(pl.BlockSpec(memory_space=pltpu.VMEM) for _ in out_widths),
        scratch_shapes=[pltpu.SemaphoreType.DMA((n_copies,))],
        compiler_params=pltpu.CompilerParams(vmem_limit_bytes=48 << 20),
        cost_estimate=small_cost,
        name="assemble",
    )(where.astype(jnp.int32), *[array for array, _ in pieces])


def places_of():
    n_chips = lax.axis_size("seq") // 2
    seq_at = lax.axis_index("seq")
    return n_chips, seq_at // 2, seq_at % 2, lax.axis_size("dp"), lax.axis_index("dp")


def gather_rows(values, cut, splits, out_widths):
    n_chips, chip, core, n_dp, dp_at = places_of()
    ring = [values] + [seq_perm(values, t, 0) for t in range(1, n_chips)]
    pieces, where = [], []
    for column, (lo, hi) in enumerate(((0, cut), (cut, values.shape[1]))):
        bits = dp_bits()[:: 1 if column == 0 else -1]
        for piece, k in dp_gather(jnp.stack([r[:, lo:hi] for r in ring]), bits):
            for flip, array in ((0, piece), (1, seq_perm(piece, 0, 1))):
                pieces.append((array, column))
                where += [
                    (((chip - t) % n_chips) * 2 + (core ^ flip)) * n_dp + (dp_at ^ k)
                    for t in range(n_chips)
                ]
    return assemble(pieces, jnp.stack(where), splits, out_widths), ring[1:]


def halve(values, axes, bits):
    dp_at = lax.axis_index("dp")
    axes = dict(axes)
    for bit in bits:
        axis = axes.pop(bit)
        mine = (dp_at // bit) % 2
        got = dp_perm(pick(values, 1 - mine, axis), bit)
        values = (pick(values, mine, axis).astype(f32) + got.astype(f32)).astype(bf16)
        axes = {b: x - (x > axis) for b, x in axes.items()}
    return values


def sum_rows(values, cut):
    n_chips, chip, core, n_dp, dp_at = places_of()
    rows, width = values.shape[1:]
    values = values.reshape(n_chips, 2, n_dp, rows, width)
    got = seq_perm(pick(values, 1 - core, 1), 0, 1)
    values = (pick(values, core, 1).astype(f32) + got.astype(f32)).astype(bf16)
    bits = dp_bits()
    parts = []
    for lo, hi, order in ((0, cut, bits), (cut, width, bits[::-1])):
        part = values[..., lo:hi].reshape((n_chips,) + (2,) * len(bits) + (rows, hi - lo))
        part = halve(part, {b: len(bits) - i for i, b in enumerate(bits)}, order)
        total = pick(part, chip, 0).astype(f32)
        for t in range(1, n_chips):
            total = total + seq_perm(pick(part, (chip + t) % n_chips, 0), t, 0).astype(f32)
        parts.append(total)
    return jnp.concatenate(parts, axis=1)


def exchange(values, *earlier):
    n_chips, chip, core, _, _ = places_of()
    values = values.reshape((n_chips, 2) + values.shape[1:])
    kept = pick(values, core, 1)
    got = seq_perm(pick(values, 1 - core, 1), 0, 1)
    pairs = after(jnp.stack([kept, got], axis=1), *earlier)
    out = [pick(pairs, chip, 0)]
    for t in range(1, n_chips):
        out.append(seq_perm(pick(pairs, (chip + t) % n_chips, 0), t, 0))
    return out


def ffn_kernel(
    normed_own,
    normed_other,
    grad_own,
    grad_other,
    w_gate,
    w_up,
    w_down,
    *refs,
    earlier,
):
    out_refs, grad_refs, kept_refs = refs[earlier : earlier + 2], refs[earlier + 2 : earlier + 4], refs[earlier + 4 :]
    normed_ref, ffn_grad_ref, hidden_ref, gate_ref, up_ref = kept_refs
    rows = normed_own.shape[0]

    def dot(left, right):
        return jnp.dot(left, right[...], preferred_element_type=f32)

    def dot_transposed(left, right):
        return lax.dot_general(
            left, right[...], (((1,), (1,)), ((), ())), preferred_element_type=f32
        )

    for i, (normed_in, grad_in) in enumerate(((normed_own, grad_own), (normed_other, grad_other))):
        to = slice(i * rows, (i + 1) * rows)
        normed, ffn_grad = normed_in[...], grad_in[...]
        normed_ref[0, to, :] = normed
        ffn_grad_ref[0, to, :] = ffn_grad
        gate = dot(normed, w_gate)
        up = dot(normed, w_up)
        sigmoid = 1.0 / (1.0 + jnp.exp(-gate))
        silu = gate * sigmoid
        hidden = (silu * up).astype(bf16)
        hidden_ref[0, to, :] = hidden
        out_refs[i][...] = dot(hidden, w_down).astype(bf16)
        hidden_grad = dot_transposed(ffn_grad, w_down)
        gate_grad = (hidden_grad * up * sigmoid * (1.0 + gate * (1.0 - sigmoid))).astype(bf16)
        up_grad = (hidden_grad * silu).astype(bf16)
        gate_ref[0, to, :] = gate_grad
        up_ref[0, to, :] = up_grad
        grad_refs[i][...] = (
            dot_transposed(gate_grad, w_gate) + dot_transposed(up_grad, w_up)
        ).astype(bf16)


def feed_forward(normed, grads, w_gate, w_up, w_down, slot, slots, kept):
    rows, width = normed[0].shape
    ff_own = w_gate.shape[1]
    token = jax.ShapeDtypeStruct((rows, width), bf16)
    widths = (width, width, ff_own, ff_own, ff_own)
    operands = [*normed, *grads, w_gate, w_up, w_down]
    whole = [pl.BlockSpec(memory_space=pltpu.VMEM)]
    n = len(operands)
    return pl.pallas_call(
        functools.partial(ffn_kernel, earlier=len(kept)),
        grid=(1,),
        out_shape=(token,) * 4
        + tuple(jax.ShapeDtypeStruct((slots, 2 * rows, w), bf16) for w in widths),
        in_specs=whole * n + [pl.BlockSpec(memory_space=pl.ANY)] * len(kept),
        out_specs=tuple(whole * 4)
        + tuple(pl.BlockSpec((1, 2 * rows, w), lambda i: (slot, 0, 0)) for w in widths),
        input_output_aliases={n + i: 4 + i for i in range(len(kept))},
        compiler_params=pltpu.CompilerParams(vmem_limit_bytes=58 << 20),
        cost_estimate=small_cost,
        name="feed_forward",
    )(*operands, *kept)


def ring_pairs(values):
    pieces = [values]
    for _ in range(lax.axis_size("seq") // 2 - 1):
        pieces.append(seq_perm(pieces[-1], 1, 0))
    return [(piece, seq_perm(piece, 0, 1)) for piece in pieces]


def sent_pairs(values):
    pieces = [values] + [seq_perm(values, t, 0) for t in range(1, lax.axis_size("seq") // 2)]
    return [(piece, seq_perm(piece, 0, 1)) for piece in pieces]


def ring_sum(parts):
    summed = [
        own.astype(f32) + seq_perm(other.astype(bf16), 0, 1).astype(f32) for own, other in parts
    ]
    if len(summed) == 1:
        return summed[0]
    running = summed[1].astype(bf16)
    for t in list(range(2, len(summed))) + [0]:
        running = seq_perm(running, 1, 0).astype(f32) + summed[t]
        if t:
            running = running.astype(bf16)
    return running


def adamw_update(master, moment_one, moment_two, gradient, step_rate, decay_weight):
    first_new = beta_one * moment_one + (1.0 - beta_one) * gradient
    second_new = beta_two * moment_two + (1.0 - beta_two) * gradient * gradient
    first_hat = first_new / (1.0 - beta_one**STEP)
    second_hat = second_new / (1.0 - beta_two**STEP)
    master_new = master - step_rate * (
        first_hat / (jnp.sqrt(second_hat) + adam_eps) + decay_weight * master
    )
    return (first_new, second_new, master_new)


def shards(
    tokens,
    cotangent,
    positions,
    qkv_master,
    qkv_first,
    qkv_second,
    out_master,
    out_first,
    out_second,
    gate_up_master,
    gate_up_first,
    gate_up_second,
    down_master,
    down_first,
    down_second,
    small_master,
    small_first,
    small_second,
):
    n_seq = lax.axis_size("seq")
    n_dp = lax.axis_size("dp")
    n_all = n_seq * n_dp
    chips = n_seq // 2
    seq_at = lax.axis_index("seq")
    dp_at = lax.axis_index("dp")
    chip_at, core_at = seq_at // 2, seq_at % 2
    ff = down_master.shape[0] * n_all
    ff_dev = down_master.shape[0]
    ff_pad = -(-ff_dev // 16) * 16
    ff_own = n_dp * ff_pad
    rows_own = qkv_master.shape[0]
    qkv_width = qkv_master.shape[1]
    small_own = small_master.shape[0]

    half = qkv_width // 2
    small_block = jnp.pad(
        small_master.astype(bf16), (0, rows_own * HD - small_own)
    ).reshape(rows_own, HD)
    packed = jnp.concatenate([small_block, qkv_master.astype(bf16)], axis=1)
    (w_qkv, small_blocks), qkv_ring = gather_rows(
        packed,
        HD + half,
        ((((1, 0), 0, HD), ((0, 0), HD, half)), (((0, half), 0, half),)),
        (qkv_width, HD),
    )
    w_qkv = w_qkv.reshape(D, qkv_width)
    small_params = small_blocks.reshape(n_all, rows_own * HD)[:, :small_own].reshape(-1)
    w_out = lax.all_gather(
        after(out_master.astype(bf16), *qkv_ring), ("seq", "dp"), axis=0, tiled=True
    )

    gate_up_send = jnp.pad(
        gate_up_master.astype(bf16).reshape(2, rows_own, n_seq, n_dp, ff_dev),
        ((0, 0), (0, 0), (0, 0), (0, 0), (0, ff_pad - ff_dev)),
    )
    gate_up_send = gate_up_send.reshape(2, rows_own, n_seq, ff_own).transpose(2, 0, 1, 3)
    gate_up_pieces = exchange(gate_up_send, *qkv_ring)
    gate_up_got = jnp.concatenate(gate_up_pieces, axis=0)
    ring_order = [
        ((chip_at - t) % chips) * 2 + (core_at ^ flip) for t in range(chips) for flip in range(2)
    ]
    w_gate, w_up = (
        assemble(
            [(piece, 0) for piece, _ in gathered],
            jnp.stack([s * n_dp + (dp_at ^ k) for _, k in gathered for s in ring_order]),
            ((((0, 0), 0, ff_own),),),
            (ff_own,),
        )[0].reshape(D, ff_own)
        for gathered in (
            dp_gather(gate_up_got[:, 0], dp_bits()),
            dp_gather(gate_up_got[:, 1], dp_bits()[::-1]),
        )
    )
    down_share = jnp.pad(down_master.astype(bf16), ((0, ff_pad - ff_dev), (0, 0)))
    w_down = lax.all_gather(after(down_share, w_qkv), "dp", axis=0, tiled=True)

    small_params = small_params.astype(f32)
    gain_one = small_params[:D]
    gain_two = small_params[D : 2 * D]
    qkv_bias = small_params[2 * D :]
    inputs = tokens[0].astype(f32)
    upstream = cotangent[0].astype(f32)
    tok_rows = inputs.shape[0]
    all_places = positions[0]
    seq_length = all_places.shape[0]
    own_places = lax.dynamic_slice_in_dim(all_places, seq_at * tok_rows, tok_rows, 0)
    chip_order = (chip_at - jnp.arange(chips)) % chips
    core_order = jnp.stack([core_at, 1 - core_at])
    ring_places = jnp.take(
        jnp.take(all_places.reshape(chips, 2, tok_rows), chip_order, axis=0), core_order, axis=1
    )
    ring_places = ring_places.transpose(1, 0, 2).reshape(seq_length)

    cosine, sine_table = rotary_tables(own_places)
    scale_one = lax.rsqrt(jnp.mean(inputs * inputs, axis=-1, keepdims=True) + norm_eps)
    unit_one = inputs * scale_one
    normed_one = after((unit_one * gain_one).astype(bf16), *gate_up_pieces)
    projected = jnp.dot(normed_one, w_qkv, preferred_element_type=f32) + qkv_bias
    queries = (
        rotate(projected[:, :D].reshape(tok_rows, HEADS, HD), cosine, sine_table)
        .astype(bf16)
        .reshape(tok_rows, D)
    )
    key_rows = rotate(
        projected[:, D : D + KVH * HD].reshape(tok_rows, KVH, HD), cosine, sine_table
    ).astype(bf16)
    value_rows = projected[:, D + KVH * HD :].reshape(tok_rows, KVH, HD).astype(bf16)

    key_value = jnp.concatenate(
        [key_rows.reshape(tok_rows, KVH * HD), value_rows.reshape(tok_rows, KVH * HD)], axis=1
    )
    key_value_own = jnp.concatenate(
        [key_value] + [seq_perm(key_value, t, 0) for t in range(1, chips)], axis=0
    )
    key_value_all = jnp.concatenate([key_value_own, seq_perm(key_value_own, 0, 1)], axis=0)
    attended, logsum = attend(queries, key_value_all, own_places, ring_places)
    attended_low = attended.astype(bf16)
    residual = inputs + jnp.dot(attended_low, w_out, preferred_element_type=f32)
    scale_two = lax.rsqrt(jnp.mean(residual * residual, axis=-1, keepdims=True) + norm_eps)
    unit_two = residual * scale_two
    normed_two = (unit_two * gain_two).astype(bf16)

    upstream_pairs = sent_pairs(after(cotangent[0], key_value_own))
    normed_pairs = ring_pairs(normed_two)
    out_parts, grad_parts = [], []
    kept = ()
    for slot in range(chips):
        out_own, out_other, grad_own, grad_other, *kept = feed_forward(
            normed_pairs[slot], upstream_pairs[slot], w_gate, w_up, w_down, slot, chips, kept
        )
        out_parts.append((out_own, out_other))
        grad_parts.append((grad_own, grad_other))
    normed_two_grads = ring_sum(grad_parts)
    outputs = residual + ring_sum(
        [(after(own, normed_two_grads), other) for own, other in out_parts]
    )
    normed_all, ffn_all, hidden_all, gate_grads_all, up_grads_all = (
        entry.reshape(seq_length, -1) for entry in kept
    )
    gate_up_sums = []
    for grads, order in ((gate_grads_all, dp_bits()), (up_grads_all, dp_bits()[::-1])):
        part = jnp.einsum("td,tf->df", normed_all, grads, preferred_element_type=f32).astype(bf16)
        part = part.reshape((n_seq,) + (2,) * len(order) + (rows_own, ff_own))
        axes = {bit: len(order) - i for i, bit in enumerate(dp_bits())}
        gate_up_sums.append(halve(part, axes, order))
    gate_up_pieces = jnp.concatenate(exchange(jnp.stack(gate_up_sums, axis=1)), axis=0)
    gate_up_owned = jnp.take(gate_up_pieces, jnp.argsort(jnp.stack(ring_order)), axis=0)
    gate_up_owned = gate_up_owned.reshape(n_seq, 2, rows_own, n_dp, ff_pad)[..., :ff_dev]
    gate_up_owned = gate_up_owned.transpose(1, 2, 0, 3, 4).reshape(2, rows_own, ff).astype(f32)
    down_grad = jnp.einsum("tf,td->fd", hidden_all, ffn_all, preferred_element_type=f32)
    down_owned = lax.psum_scatter(
        down_grad.astype(bf16), "dp", scatter_dimension=0, tiled=True
    )[:ff_dev].astype(f32)

    gain_two_grad = jnp.sum(normed_two_grads * unit_two, axis=0)
    weighted_two = normed_two_grads * gain_two
    residual_grads = upstream + scale_two * (
        weighted_two - unit_two * jnp.mean(weighted_two * unit_two, axis=-1, keepdims=True)
    )
    branch_grads = residual_grads.astype(bf16)
    out_grad = jnp.einsum("td,te->de", attended_low, branch_grads, preferred_element_type=f32)
    out_owned = sum_rows(out_grad.astype(bf16).reshape(n_all, rows_own, D), D // 2)
    attended_grads = jnp.einsum(
        "te,de->td", branch_grads, w_out, preferred_element_type=f32
    ).astype(bf16)
    query_grads, key_value_grads = attend_back(
        queries, key_value_all, attended_grads, attended, logsum, own_places, ring_places
    )
    key_value_grads = key_value_grads.reshape(2, chips, tok_rows, 2 * KVH * HD)
    others = seq_perm(key_value_grads[1], 0, 1)
    both = (key_value_grads[0].astype(f32) + others.astype(f32)).astype(bf16)
    key_value_owned = both[0].astype(f32)
    for t in range(1, chips):
        key_value_owned = key_value_owned + seq_perm(both[t], chips - t, 0).astype(f32)
    key_owned = key_value_owned[:, : KVH * HD].reshape(tok_rows, KVH, HD)
    value_owned = key_value_owned[:, KVH * HD :]
    query_pre = unrotate(query_grads.reshape(tok_rows, HEADS, HD), cosine, sine_table).reshape(
        tok_rows, D
    )
    key_pre = unrotate(key_owned, cosine, sine_table).reshape(tok_rows, KVH * HD)
    query_pre = query_pre.astype(bf16)
    key_value_pre = jnp.concatenate([key_pre, value_owned], axis=1).astype(bf16)
    query_grad = jnp.einsum("td,tf->df", normed_one, query_pre, preferred_element_type=f32)
    query_owned = sum_rows(query_grad.astype(bf16).reshape(n_all, rows_own, D), D // 2)
    key_value_grad = jnp.einsum(
        "td,tf->df", normed_one, key_value_pre, preferred_element_type=f32
    )
    normed_one_grads = jnp.einsum(
        "tf,df->td", query_pre, w_qkv[:, :D], preferred_element_type=f32
    ) + jnp.einsum("tf,df->td", key_value_pre, w_qkv[:, D:], preferred_element_type=f32)
    bias_grad = jnp.concatenate(
        [jnp.sum(query_pre.astype(f32), axis=0), jnp.sum(key_value_pre.astype(f32), axis=0)]
    )
    gain_one_grad = jnp.sum(normed_one_grads * unit_one, axis=0)
    weighted_one = normed_one_grads * gain_one
    input_grads = residual_grads + scale_one * (
        weighted_one - unit_one * jnp.mean(weighted_one * unit_one, axis=-1, keepdims=True)
    )
    small_grad = jnp.concatenate([gain_one_grad, gain_two_grad, bias_grad]).astype(bf16)
    small_grad = jnp.pad(
        small_grad.reshape(n_all, small_own), ((0, 0), (0, rows_own * HD - small_own))
    ).reshape(n_all * rows_own, HD)
    packed_grad = jnp.concatenate([small_grad, key_value_grad.astype(bf16)], axis=1)
    packed_owned = sum_rows(
        packed_grad.reshape(n_all, rows_own, HD + 2 * KVH * HD), HD + KVH * HD
    )
    qkv_owned = jnp.concatenate([query_owned, packed_owned[:, HD:]], axis=1)
    small_owned = packed_owned[:, :HD].reshape(-1)[:small_own]
    qkv_new = adamw_update(qkv_master, qkv_first, qkv_second, qkv_owned, 0.09, 0.1)
    out_new = adamw_update(out_master, out_first, out_second, out_owned, 0.18, 0.1)
    gate_up_new = adamw_update(
        gate_up_master, gate_up_first, gate_up_second, gate_up_owned, 0.064, 0.1
    )
    down_new = adamw_update(down_master, down_first, down_second, down_owned, 0.026, 0.1)
    small_new = adamw_update(small_master, small_first, small_second, small_owned, 0.6, 0.0)
    return (
        outputs.astype(bf16)[None],
        input_grads[None],
        *qkv_new,
        *out_new,
        *gate_up_new,
        *down_new,
        *small_new,
    )


def solution(mesh):
    in_specs = (
        P("dp", "seq", None),
        P("dp", "seq", None),
        P("dp", None),
        P(("seq", "dp"), None),
        P(("seq", "dp"), None),
        P(("seq", "dp"), None),
        P(("seq", "dp"), None),
        P(("seq", "dp"), None),
        P(("seq", "dp"), None),
        P(None, ("seq", "dp"), None),
        P(None, ("seq", "dp"), None),
        P(None, ("seq", "dp"), None),
        P(("seq", "dp"), None),
        P(("seq", "dp"), None),
        P(("seq", "dp"), None),
        P(("seq", "dp")),
        P(("seq", "dp")),
        P(("seq", "dp")),
    )
    out_specs = (
        P("dp", "seq", None),
        P("dp", "seq", None),
        P(("seq", "dp"), None),
        P(("seq", "dp"), None),
        P(("seq", "dp"), None),
        P(("seq", "dp"), None),
        P(("seq", "dp"), None),
        P(("seq", "dp"), None),
        P(None, ("seq", "dp"), None),
        P(None, ("seq", "dp"), None),
        P(None, ("seq", "dp"), None),
        P(("seq", "dp"), None),
        P(("seq", "dp"), None),
        P(("seq", "dp"), None),
        P(("seq", "dp")),
        P(("seq", "dp")),
        P(("seq", "dp")),
    )
    return jax.shard_map(shards, mesh=mesh, in_specs=in_specs, out_specs=out_specs, check_vma=False)
```

```python
import functools

import jax
import jax.numpy as jnp
from jax import lax
from jax.experimental import pallas as pl
from jax.experimental.pallas import tpu as pltpu
from jax.sharding import PartitionSpec as P

D = 1536
HEADS = 12
KVH = 2
HD = 128
STEP = 10
KVW = KVH * HD


norm_eps = 1e-06
rope_base = 1000000.0
beta_one = 0.9
beta_two = 0.95
adam_eps = 1e-08
masked_score = -1e30
log2_e = 1.4426950408889634
bf16 = jnp.bfloat16
f32 = jnp.float32
vmem = pl.BlockSpec(memory_space=pltpu.VMEM)
smem = pl.BlockSpec(memory_space=pltpu.SMEM)
anywhere = pl.BlockSpec(memory_space=pl.ANY)


def shape_of(dims, kind):
    return jax.ShapeDtypeStruct(dims, kind)


def kernel_call(kernel, name, out_shape, operands, **options):
    return pl.pallas_call(
        kernel,
        name=name,
        out_shape=out_shape,
        compiler_params=pltpu.CompilerParams(vmem_limit_bytes=58 << 20),
        cost_estimate=pl.CostEstimate(flops=10**6, bytes_accessed=10**6, transcendentals=0),
        **options,
    )(*operands)


def after(values, *others):
    return lax.optimization_barrier((values,) + others)[0]


def dot(left, right):
    return jnp.dot(left, right, preferred_element_type=f32)


def dot_transposed(left, right):
    return lax.dot_general(left, right, (((1,), (1,)), ((), ())), preferred_element_type=f32)


def rotary_tables(places):
    half_size = HD // 2
    freqs = rope_base ** (-(jnp.arange(half_size).astype(f32) * (2.0 / HD)))
    angles = places.astype(f32)[:, None] * freqs[None, :]
    cosine, sine = jnp.cos(angles), jnp.sin(angles)
    return jnp.concatenate([cosine, cosine], axis=1), jnp.concatenate([-sine, sine], axis=1)


def rms_scale(values):
    return lax.rsqrt(jnp.mean(values * values, axis=-1, keepdims=True) + norm_eps)


def swap_halves(values):
    return pltpu.roll(values, HD // 2, 1)


def head(index):
    return slice(index * HD, (index + 1) * HD)


def project_kernel(tokens, w_qkv, gain, bias, cosine, sine, normed_ref, query_ref, kv_ref):
    inputs = tokens[...].astype(f32)
    normed = (inputs * rms_scale(inputs) * gain[...]).astype(bf16)
    normed_ref[...] = normed
    cos, sin = cosine[...], sine[...]
    rows_kv = dot(normed, w_qkv[:, D:]) + bias[:, D:]
    for j in range(KVH):
        part = rows_kv[:, head(j)]
        kv_ref[:, head(j)] = (part * cos + swap_halves(part) * sin).astype(bf16)
    kv_ref[:, KVW:] = rows_kv[:, KVW:].astype(bf16)
    rows_q = dot(normed, w_qkv[:, :D]) + bias[:, :D]
    for j in range(HEADS):
        part = rows_q[:, head(j)]
        query_ref[:, head(j)] = (part * cos + swap_halves(part) * sin).astype(bf16)


def project(tokens, w_qkv, gain, bias, cosine, sine):
    rows = tokens.shape[0]
    return kernel_call(
        project_kernel,
        "project",
        (shape_of((rows, D), bf16), shape_of((rows, D), bf16), shape_of((rows, 2 * KVW), bf16)),
        (tokens, w_qkv, gain, bias, cosine, sine),
    )


def attend_kernel(q_ref, query_places, key_places, *refs):
    pieces, (out_ref, lse_ref, kv_ref) = refs[:-3], refs[-3:]
    rows = q_ref.shape[0]
    for i, piece in enumerate(pieces):
        kv_ref[i * rows : (i + 1) * rows, :] = piece[...]
    groups = HEADS // KVH
    scale = HD**-0.5 * log2_e
    visible = key_places[...] <= query_places[...]
    for kv in range(KVH):
        keys = kv_ref[:, head(kv)]
        values = kv_ref[:, head(KVH + kv)].T
        for h in range(kv * groups, (kv + 1) * groups):
            scores = dot_transposed(keys, q_ref[:, head(h)])
            scores = jnp.where(visible, scores, masked_score)
            top = jnp.max(scores, axis=0, keepdims=True)
            weights = jnp.exp2((scores - top) * scale)
            total = jnp.sum(weights, axis=0, keepdims=True)
            mixed = dot(values, weights.astype(bf16))
            out_ref[:, head(h)] = (mixed / total).T
            lse_ref[h : h + 1, :] = top * scale + jnp.log2(total)


def attend(queries, pieces, query_places, key_places):
    rows, total = queries.shape[0], key_places.shape[0]
    return kernel_call(
        attend_kernel,
        "attend",
        (
            shape_of((rows, D), f32),
            shape_of((HEADS, rows), f32),
            shape_of((total, 2 * KVW), bf16),
        ),
        (queries, query_places, key_places, *pieces),
    )


def out_kernel(tokens, attended, w_out, gain, residual_ref, normed_ref, low_ref):
    low = attended[...].astype(bf16)
    low_ref[...] = low
    residual = tokens[...].astype(f32) + dot(low, w_out[...])
    residual_ref[...] = residual
    normed_ref[...] = (residual * rms_scale(residual) * gain[...]).astype(bf16)


def out_project(tokens, attended, w_out, gain):
    dims = tokens.shape
    return kernel_call(
        out_kernel,
        "out_project",
        (shape_of(dims, f32), shape_of(dims, bf16), shape_of(dims, bf16)),
        (tokens, attended, w_out, gain),
    )


def ffn_kernel(
    normed_own, normed_other, grad_own, grad_other, w_gate, w_up, w_down, *refs, earlier
):
    refs = refs[earlier:]
    out_refs, grad_refs = refs[:2], refs[2:4]
    normed_ref, ffn_grad_ref, hidden_ref, gate_ref, up_ref = refs[4:]
    rows = normed_own.shape[0]
    for i, (normed_in, grad_in) in enumerate(((normed_own, grad_own), (normed_other, grad_other))):
        to = slice(i * rows, (i + 1) * rows)
        normed, ffn_grad = normed_in[...], grad_in[...]
        normed_ref[0, to, :] = normed
        ffn_grad_ref[0, to, :] = ffn_grad
        gate = dot(normed, w_gate[...])
        up = dot(normed, w_up[...])
        sigmoid = 1.0 / (1.0 + jnp.exp(-gate))
        silu = gate * sigmoid
        hidden = (silu * up).astype(bf16)
        hidden_ref[0, to, :] = hidden
        out_refs[i][...] = dot(hidden, w_down[...]).astype(bf16)
        hidden_grad = dot_transposed(ffn_grad, w_down[...])
        gate_grad = (hidden_grad * up * sigmoid * (1.0 + gate * (1.0 - sigmoid))).astype(bf16)
        up_grad = (hidden_grad * silu).astype(bf16)
        gate_ref[0, to, :] = gate_grad
        up_ref[0, to, :] = up_grad
        grad_refs[i][...] = (
            dot_transposed(gate_grad, w_gate[...]) + dot_transposed(up_grad, w_up[...])
        ).astype(bf16)


def feed_forward(normed, grads, w_gate, w_up, w_down, slot, slots, kept):
    rows, width = normed[0].shape
    ff_own = w_gate.shape[1]
    token = shape_of((rows, width), bf16)
    widths = (width, width, ff_own, ff_own, ff_own)
    operands = (*normed, *grads, w_gate, w_up, w_down)
    return kernel_call(
        functools.partial(ffn_kernel, earlier=len(kept)),
        "feed_forward",
        (token,) * 4 + tuple(shape_of((slots, 2 * rows, w), bf16) for w in widths),
        (*operands, *kept),
        grid=(1,),
        in_specs=[vmem] * len(operands) + [anywhere] * len(kept),
        out_specs=(vmem,) * 4
        + tuple(pl.BlockSpec((1, 2 * rows, w), lambda i: (slot, 0, 0)) for w in widths),
        input_output_aliases={len(operands) + i: 4 + i for i in range(len(kept))},
    )


def norm_back_kernel(
    got, own, other, residual_ref, cotangent, gain, w_out, grad_ref, low_ref, back_ref, gain_ref
):
    normed_grad = got[...].astype(f32) + own[...].astype(f32) + other[...].astype(f32)
    residual = residual_ref[...]
    scale = rms_scale(residual)
    unit = residual * scale
    gain_ref[...] = jnp.sum(normed_grad * unit, axis=0, keepdims=True)
    weighted = normed_grad * gain[...]
    grad = cotangent[...].astype(f32) + scale * (
        weighted - unit * jnp.mean(weighted * unit, axis=-1, keepdims=True)
    )
    grad_ref[...] = grad
    low = grad.astype(bf16)
    low_ref[...] = low
    back_ref[...] = dot_transposed(low, w_out[...]).astype(bf16)


def norm_back(got, own, other, residual, cotangent, gain, w_out):
    dims = residual.shape
    return kernel_call(
        norm_back_kernel,
        "norm_back",
        (shape_of(dims, f32), shape_of(dims, bf16), shape_of(dims, bf16), shape_of((1, D), f32)),
        (got, own, other, residual, cotangent, gain, w_out),
    )


def attend_back_kernel(
    q_ref,
    kv_ref,
    grad_ref,
    out_ref,
    lse_ref,
    query_places,
    key_places,
    cosine,
    sine,
    q_grad_ref,
    kv_own_ref,
    kv_other_ref,
    q_rows,
    grad_rows,
    deltas,
    q_sums,
):
    rows = q_ref.shape[0]
    groups = HEADS // KVH
    scale = HD**-0.5
    for kv in range(KVH):
        for j in range(groups):
            part = slice(j * rows, (j + 1) * rows)
            columns = head(kv * groups + j)
            q_rows[part, :] = q_ref[:, columns]
            grads = grad_ref[:, columns]
            grad_rows[part, :] = grads
            product = grads.astype(f32) * out_ref[:, columns]
            deltas[:, part] = jnp.sum(product.T, axis=0, keepdims=True)
        q_sums[...] = jnp.zeros_like(q_sums)

        @pl.loop(0, kv_ref.shape[0] // (2 * rows))
        def _(step):
            at = pl.ds(pl.multiple_of(step * (2 * rows), 2 * rows), 2 * rows)
            visible = key_places[at, :] <= query_places[...]
            keys = kv_ref[at, head(kv)]
            values = kv_ref[at, head(KVH + kv)]
            key_sum = value_sum = None
            for j in range(groups):
                part = slice(j * rows, (j + 1) * rows)
                h = kv * groups + j
                queries, grads = q_rows[part, :], grad_rows[part, :]
                scores = dot_transposed(keys, queries)
                weights = jnp.where(
                    visible, jnp.exp2(scores * (scale * log2_e) - lse_ref[h : h + 1, :]), 0.0
                )
                weight_grads = dot_transposed(values, grads)
                score_grads = (weights * (weight_grads - deltas[:, part])).astype(bf16)
                value_part = dot(weights.astype(bf16), grads)
                key_part = dot(score_grads, queries)
                key_sum = key_part if key_sum is None else key_sum + key_part
                value_sum = value_part if value_sum is None else value_sum + value_part
                q_sums[part, :] += lax.dot_general(
                    score_grads, keys, (((0,), (0,)), ((), ())), preferred_element_type=f32
                )
            key_sum = (key_sum * scale).astype(bf16)
            value_sum = value_sum.astype(bf16)
            to = pl.ds(pl.multiple_of(step * rows, rows), rows)
            for ref, mine in ((kv_own_ref, slice(0, rows)), (kv_other_ref, slice(rows, 2 * rows))):
                ref[to, head(kv)] = key_sum[mine, :]
                ref[to, head(KVH + kv)] = value_sum[mine, :]

        for j in range(groups):
            part = q_sums[j * rows : (j + 1) * rows, :] * scale
            q_grad_ref[:, head(kv * groups + j)] = (
                part * cosine[...] - swap_halves(part) * sine[...]
            ).astype(bf16)


def attend_back(queries, key_value, grads, attended, lse, query_places, key_places, cosine, sine):
    rows, total = queries.shape[0], key_value.shape[0]
    groups = HEADS // KVH
    return kernel_call(
        attend_back_kernel,
        "attend_back",
        (
            shape_of((rows, D), bf16),
            shape_of((total // 2, 2 * KVW), bf16),
            shape_of((total // 2, 2 * KVW), bf16),
        ),
        (queries, key_value, grads, attended, lse, query_places, key_places, cosine, sine),
        scratch_shapes=[
            pltpu.VMEM((groups * rows, HD), bf16),
            pltpu.VMEM((groups * rows, HD), bf16),
            pltpu.VMEM((1, groups * rows), f32),
            pltpu.VMEM((groups * rows, HD), f32),
        ],
    )


def input_kernel(
    tokens, gain, w_qkv, query_grad, cosine, sine, residual_grad, own, *refs
):
    got, (kv_ref, input_ref, gain_ref, bias_ref) = refs[:-4], refs[-4:]
    rows = own[...].astype(f32)
    for piece in got:
        rows = rows + piece[...].astype(f32)
    for j in range(KVH):
        part = rows[:, head(j)]
        kv_ref[:, head(j)] = (part * cosine[...] - swap_halves(part) * sine[...]).astype(bf16)
    kv_ref[:, KVW:] = rows[:, KVW:].astype(bf16)
    kv_grad = kv_ref[...]
    q_grad = query_grad[...]
    bias_ref[:, :D] = jnp.sum(q_grad.astype(f32), axis=0, keepdims=True)
    bias_ref[:, D:] = jnp.sum(kv_grad.astype(f32), axis=0, keepdims=True)
    normed_grad = dot_transposed(q_grad, w_qkv[:, :D]) + dot_transposed(kv_grad, w_qkv[:, D:])
    inputs = tokens[...].astype(f32)
    scale = rms_scale(inputs)
    unit = inputs * scale
    gain_ref[...] = jnp.sum(normed_grad * unit, axis=0, keepdims=True)
    weighted = normed_grad * gain[...]
    input_ref[...] = residual_grad[...] + scale * (
        weighted - unit * jnp.mean(weighted * unit, axis=-1, keepdims=True)
    )


def input_back(tokens, gain, w_qkv, query_grad, cosine, sine, residual_grad, own, got):
    rows = tokens.shape[0]
    return kernel_call(
        input_kernel,
        "input_back",
        (
            shape_of((rows, 2 * KVW), bf16),
            shape_of((rows, D), f32),
            shape_of((1, D), f32),
            shape_of((1, D + 2 * KVW), f32),
        ),
        (tokens, gain, w_qkv, query_grad, cosine, sine, residual_grad, own, *got),
    )


def cut_kernel(values, out_ref, *, n_dp, own, padded):
    out_ref[...] = jnp.zeros_like(out_ref)
    for s in range(out_ref.shape[0]):
        for d in range(n_dp):
            start = (s * n_dp + d) * own
            out_ref[s, 0, :, d * padded : d * padded + own] = values[
                0, :, start : start + own
            ].astype(bf16)


def cut_hidden(values, n_seq, n_dp, padded):
    two, rows, ff = values.shape
    own = ff // (n_seq * n_dp)
    return kernel_call(
        functools.partial(cut_kernel, n_dp=n_dp, own=own, padded=padded),
        "cut_hidden",
        shape_of((n_seq, two, rows, n_dp * padded), bf16),
        (values,),
        grid=(two,),
        in_specs=[pl.BlockSpec((1, rows, ff), lambda g: (g, 0, 0))],
        out_specs=pl.BlockSpec((n_seq, 1, rows, n_dp * padded), lambda g: (0, g, 0, 0)),
    )


def adamw_update(master, moment_one, moment_two, gradient, step_rate, decay_weight):
    first_new = beta_one * moment_one + (1.0 - beta_one) * gradient
    second_new = beta_two * moment_two + (1.0 - beta_two) * gradient * gradient
    first_hat = first_new / (1.0 - beta_one**STEP)
    second_hat = second_new / (1.0 - beta_two**STEP)
    master_new = master - step_rate * (
        first_hat / (jnp.sqrt(second_hat) + adam_eps) + decay_weight * master
    )
    return (first_new, second_new, master_new)


def adamw_kernel(where, master, first, second, *refs, n_dp, own, padded, rate, decay):
    pieces, (first_ref, second_ref, master_ref, slots, joined) = refs[:-5], refs[-5:]
    for t, piece in enumerate(pieces):
        for o in range(2):
            slots[where[2 * t + o]] = piece[o, 0]
    for s in range(slots.shape[0]):
        for d in range(n_dp):
            start = (s * n_dp + d) * own
            joined[:, start : start + own] = slots[
                s, :, d * padded : d * padded + own
            ].astype(f32)
    first_ref[0], second_ref[0], master_ref[0] = adamw_update(
        master[0], first[0], second[0], joined[...], rate, decay
    )


def adamw_hidden(master, first, second, pieces, where, n_dp, padded, rate, decay):
    two, rows, ff = master.shape
    n_seq = 2 * len(pieces)
    own = ff // (n_seq * n_dp)
    block = pl.BlockSpec((1, rows, ff), lambda g: (g, 0, 0))
    part = pl.BlockSpec((2, 1, rows, n_dp * padded), lambda g: (0, g, 0, 0))
    return kernel_call(
        functools.partial(
            adamw_kernel, n_dp=n_dp, own=own, padded=padded, rate=rate, decay=decay
        ),
        "adamw_hidden",
        (shape_of(master.shape, f32),) * 3,
        (where, master, first, second, *pieces),
        grid=(two,),
        in_specs=[smem] + [block] * 3 + [part] * len(pieces),
        out_specs=(block,) * 3,
        scratch_shapes=[
            pltpu.VMEM((n_seq, rows, n_dp * padded), bf16),
            pltpu.VMEM((rows, ff), f32),
        ],
    )


def assemble_kernel(where, *refs, splits, counts):
    ins, outs, sems = refs[: len(counts)], refs[len(counts) : -1], refs[-1]
    copies = []
    entry = 0
    for ref, (column, count) in zip(ins, counts):
        for i in range(count):
            for out, start, width in splits[column]:
                copies.append(
                    pltpu.make_async_copy(
                        ref.at[i, :, pl.ds(start, width)],
                        outs[out[0]].at[where[entry], :, pl.ds(out[1], width)],
                        sems.at[len(copies)],
                    )
                )
            entry += 1
    for copy in copies:
        copy.start()
    for copy in copies:
        copy.wait()


def assemble(pieces, where, splits, out_widths):
    counts = [(column, array.shape[0]) for array, column in pieces]
    rows = pieces[0][0].shape[1]
    blocks = sum(count for column, count in counts if column == 0)
    n_copies = sum(count * len(splits[column]) for column, count in counts)
    return kernel_call(
        functools.partial(assemble_kernel, splits=splits, counts=counts),
        "assemble",
        tuple(shape_of((blocks, rows, w), bf16) for w in out_widths),
        (where.astype(jnp.int32), *[array for array, _ in pieces]),
        in_specs=[smem] + [anywhere] * len(pieces),
        out_specs=(vmem,) * len(out_widths),
        scratch_shapes=[pltpu.SemaphoreType.DMA((n_copies,))],
    )


def seq_perm(values, chips, flip):
    count = lax.axis_size("seq")
    return lax.ppermute(
        values, "seq", [(i, ((i + 2 * chips) % count) ^ flip) for i in range(count)]
    )


def dp_perm(values, bit):
    return lax.ppermute(values, "dp", [(i, i ^ bit) for i in range(lax.axis_size("dp"))])


def dp_bits():
    return [1 << i for i in range(lax.axis_size("dp").bit_length() - 1)]


def dp_gather(values, bits, *milestones):
    have = [(values, 0)]
    for i, bit in enumerate(bits):
        if i and milestones:
            have = have[:1] + [(after(piece, *milestones), k) for piece, k in have[1:]]
        have += [(dp_perm(piece, bit), k ^ bit) for piece, k in have]
    return have


def pick(values, index, axis):
    return lax.dynamic_index_in_dim(values, index, axis, keepdims=False)


def places_of():
    n_chips = lax.axis_size("seq") // 2
    seq_at = lax.axis_index("seq")
    return n_chips, seq_at // 2, seq_at % 2, lax.axis_size("dp"), lax.axis_index("dp")


def sent_pieces(values):
    return [values] + [seq_perm(values, t, 0) for t in range(1, lax.axis_size("seq") // 2)]


def gather_rows(ring, cut, splits, out_widths):
    n_chips, chip, core, n_dp, dp_at = places_of()
    pieces, where = [], []
    for column, (lo, hi) in enumerate(((0, cut), (cut, ring[0].shape[1]))):
        bits = dp_bits()[:: 1 if column == 0 else -1]
        for piece, k in dp_gather(jnp.stack([r[:, lo:hi] for r in ring]), bits):
            for flip, array in ((0, piece), (1, seq_perm(piece, 0, 1))):
                pieces.append((array, column))
                where += [
                    (((chip - t) % n_chips) * 2 + (core ^ flip)) * n_dp + (dp_at ^ k)
                    for t in range(n_chips)
                ]
    return assemble(pieces, jnp.stack(where), splits, out_widths)


def halve(values, axes, bits, *milestones):
    dp_at = lax.axis_index("dp")
    axes = dict(axes)
    for i, bit in enumerate(bits):
        axis = axes.pop(bit)
        mine = (dp_at // bit) % 2
        sent = pick(values, 1 - mine, axis)
        got = dp_perm(after(sent, *milestones) if i and milestones else sent, bit)
        values = (pick(values, mine, axis).astype(f32) + got.astype(f32)).astype(bf16)
        axes = {b: x - (x > axis) for b, x in axes.items()}
    return values


def sum_rows(values, cut, start=(), last=()):
    n_chips, chip, core, n_dp, dp_at = places_of()
    rows, width = values.shape[1:]
    values = values.reshape(n_chips, 2, n_dp, rows, width)
    got = seq_perm(pick(values, 1 - core, 1), 0, 1)
    values = (pick(values, core, 1).astype(f32) + got.astype(f32)).astype(bf16)
    if start:
        values = after(values, *start)
    bits = dp_bits()
    parts = []
    for lo, hi, order in ((0, cut, bits), (cut, width, bits[::-1])):
        part = values[..., lo:hi].reshape((n_chips,) + (2,) * len(bits) + (rows, hi - lo))
        part = halve(part, {b: len(bits) - i for i, b in enumerate(bits)}, order)
        if last:
            part = after(part, *last)
        total = pick(part, chip, 0).astype(f32)
        for t in range(1, n_chips):
            total = total + seq_perm(pick(part, (chip + t) % n_chips, 0), t, 0).astype(f32)
        parts.append(total)
    return jnp.concatenate(parts, axis=1)


def exchange(values, *earlier):
    n_chips, chip, core, _, _ = places_of()
    values = values.reshape((n_chips, 2) + values.shape[1:])
    kept = pick(values, core, 1)
    got = seq_perm(pick(values, 1 - core, 1), 0, 1)
    pairs = jnp.stack([kept, got], axis=1)
    if earlier:
        pairs = after(pairs, *earlier)
    return [pick(pairs, chip, 0)] + [
        seq_perm(pick(pairs, (chip + t) % n_chips, 0), t, 0) for t in range(1, n_chips)
    ]


def ring_pieces(values):
    pieces = [values]
    for _ in range(lax.axis_size("seq") // 2 - 1):
        pieces.append(seq_perm(pieces[-1], 1, 0))
    return pieces


def with_swapped(pieces):
    return [(piece, seq_perm(piece, 0, 1)) for piece in pieces]


def ring_sum(parts, milestones=()):
    swapped = [seq_perm(other, 0, 1) for _, other in parts]
    if len(parts) == 1:
        return jnp.zeros_like(parts[0][0]), parts[0][0], swapped[0]
    running = None
    for t in range(1, len(parts)):
        total = parts[t][0].astype(f32) + swapped[t].astype(f32)
        if running is not None:
            total = total + running.astype(f32)
        total = total.astype(bf16)
        if t <= len(milestones):
            total = after(total, *milestones[t - 1])
        running = seq_perm(total, 1, 0)
    return running, parts[0][0], swapped[0]


def shards(
    tokens,
    cotangent,
    positions,
    qkv_master,
    qkv_first,
    qkv_second,
    out_master,
    out_first,
    out_second,
    gate_up_master,
    gate_up_first,
    gate_up_second,
    down_master,
    down_first,
    down_second,
    small_master,
    small_first,
    small_second,
):
    n_chips, chip_at, core_at, n_dp, dp_at = places_of()
    n_seq = 2 * n_chips
    n_all = n_seq * n_dp
    rows_own, qkv_width = qkv_master.shape
    half = qkv_width // 2
    small_own = small_master.shape[0]
    ff_dev = down_master.shape[0]
    ff_pad = -(-ff_dev // 16) * 16
    ff_own = n_dp * ff_pad
    inputs = tokens[0]
    upstream = cotangent[0]
    tok_rows = inputs.shape[0]
    all_places = positions[0]
    seq_length = all_places.shape[0]

    ring_order = jnp.stack(
        [
            ((chip_at - t) % n_chips) * 2 + (core_at ^ flip)
            for t in range(n_chips)
            for flip in range(2)
        ]
    ).astype(jnp.int32)
    by_device = all_places.reshape(n_seq, tok_rows)
    query_places = lax.dynamic_slice_in_dim(by_device, chip_at * 2 + core_at, 1, 0)
    key_places = jnp.take(by_device, ring_order, axis=0).reshape(seq_length, 1)
    cosine, sine = rotary_tables(query_places[0])

    small_block = jnp.pad(
        small_master.astype(bf16), (0, rows_own * HD - small_own)
    ).reshape(rows_own, HD)
    packed = jnp.concatenate([small_block, qkv_master.astype(bf16)], axis=1)
    qkv_ring = sent_pieces(packed)
    gate_up_send = cut_hidden(gate_up_master, n_seq, n_dp, ff_pad)
    gate_up_pieces = exchange(gate_up_send, *qkv_ring[1:])
    w_out = lax.all_gather(
        after(out_master.astype(bf16), *qkv_ring[1:]), ("seq", "dp"), axis=0, tiled=True
    )
    w_qkv, small_blocks = gather_rows(
        qkv_ring,
        HD + half,
        ((((1, 0), 0, HD), ((0, 0), HD, half)), (((0, half), 0, half),)),
        (qkv_width, HD),
    )
    w_qkv = w_qkv.reshape(D, qkv_width)
    down_share = jnp.pad(down_master.astype(bf16), ((0, ff_pad - ff_dev), (0, 0)))
    w_down = lax.all_gather(after(down_share, w_qkv), "dp", axis=0, tiled=True)
    small_params = small_blocks.reshape(n_all, rows_own * HD)[:, :small_own].reshape(1, -1)
    small_params = small_params.astype(f32)
    gain_one = small_params[:, :D]
    gain_two = small_params[:, D : 2 * D]
    qkv_bias = small_params[:, 2 * D :]

    normed_one, queries, key_value = project(
        inputs, after(w_qkv, *gate_up_pieces), gain_one, qkv_bias, cosine, sine
    )
    kv_ring = sent_pieces(key_value)
    kv_pairs = with_swapped(kv_ring)
    gate_up_got = after(jnp.concatenate(gate_up_pieces, axis=0), key_value)
    gate_gathered = dp_gather(gate_up_got[:, 0], dp_bits(), *kv_ring[1:])
    up_gathered = dp_gather(gate_up_got[:, 1], dp_bits()[::-1], *kv_ring[1:])
    upstream_ring = sent_pieces(after(upstream, *kv_ring[1:]))
    attended, logsum, key_value_all = attend(
        queries, [piece for pair in kv_pairs for piece in pair], query_places, key_places
    )
    residual, normed_two, attended_low = out_project(inputs, attended, w_out, gain_two)

    w_gate, w_up = (
        assemble(
            [(piece, 0) for piece, _ in gathered],
            jnp.concatenate([ring_order * n_dp + (dp_at ^ k) for _, k in gathered]),
            ((((0, 0), 0, ff_own),),),
            (ff_own,),
        )[0].reshape(D, ff_own)
        for gathered in (gate_gathered, up_gathered)
    )
    normed_pairs = with_swapped(ring_pieces(normed_two))
    upstream_pairs = with_swapped(upstream_ring)
    out_parts, grad_parts = [], []
    kept = ()
    for slot in range(n_chips):
        out_own, out_other, grad_own, grad_other, *kept = feed_forward(
            normed_pairs[slot], upstream_pairs[slot], w_gate, w_up, w_down, slot, n_chips, kept
        )
        out_parts.append((out_own, out_other))
        grad_parts.append((grad_own, grad_other))
    normed_all, ffn_all, hidden_all, gate_grads_all, up_grads_all = (
        entry.reshape(seq_length, -1) for entry in kept
    )
    gate_up_grads = [
        jnp.einsum("td,tf->df", normed_all, grads, preferred_element_type=f32)
        .astype(bf16)
        .reshape((n_seq,) + (2,) * len(dp_bits()) + (rows_own, ff_own))
        for grads in (gate_grads_all, up_grads_all)
    ]
    down_grad = jnp.einsum("tf,td->fd", hidden_all, ffn_all, preferred_element_type=f32)
    down_owned = lax.psum_scatter(
        down_grad.astype(bf16), "dp", scatter_dimension=0, tiled=True
    )[:ff_dev].astype(f32)

    grad_ring, grad_own, grad_other = ring_sum(grad_parts)
    residual_grads, branch_grads, attended_grads, gain_two_grad = norm_back(
        grad_ring, grad_own, grad_other, residual, upstream, gain_two, w_out
    )
    query_pre, kv_grad_own, kv_grad_other = attend_back(
        queries,
        key_value_all,
        attended_grads,
        attended,
        logsum,
        query_places,
        key_places,
        cosine,
        sine,
    )
    kv_swapped = seq_perm(kv_grad_other, 0, 1)
    kv_sum = (kv_grad_own.astype(f32) + kv_swapped.astype(f32)).astype(bf16)
    kv_sum = kv_sum.reshape(n_chips, tok_rows, 2 * KVW)
    kv_got = [seq_perm(kv_sum[t], n_chips - t, 0) for t in range(1, n_chips)]

    out_ring, out_own, out_other = ring_sum(
        [(after(own, grad_ring), after(other, grad_ring)) for own, other in out_parts],
        [(), (query_pre,), (kv_got[0],)] + [(kv_got[0],)] * n_chips,
    )
    outputs = (
        residual + out_ring.astype(f32) + out_own.astype(f32) + out_other.astype(f32)
    ).astype(bf16)

    axes = {bit: len(dp_bits()) - i for i, bit in enumerate(dp_bits())}
    gate_up_sums = [
        halve(grads, axes, order, query_pre)
        for grads, order in zip(gate_up_grads, (dp_bits(), dp_bits()[::-1]))
    ]
    gate_up_owned = exchange(jnp.stack(gate_up_sums, axis=1), *kv_got)
    out_grad = jnp.einsum("td,te->de", attended_low, branch_grads, preferred_element_type=f32)
    out_owned = sum_rows(
        out_grad.astype(bf16).reshape(n_all, rows_own, D), D // 2, (query_pre,), tuple(kv_got)
    )
    query_grad = jnp.einsum("td,tf->df", normed_one, query_pre, preferred_element_type=f32)
    query_owned = sum_rows(
        query_grad.astype(bf16).reshape(n_all, rows_own, D), D // 2, (), tuple(kv_got)
    )
    key_value_pre, input_grads, gain_one_grad, bias_grad = input_back(
        inputs,
        gain_one,
        w_qkv,
        query_pre,
        cosine,
        sine,
        residual_grads,
        kv_sum[0],
        kv_got,
    )
    key_value_grad = jnp.einsum(
        "td,tf->df", normed_one, key_value_pre, preferred_element_type=f32
    )
    small_grad = jnp.concatenate([gain_one_grad, gain_two_grad, bias_grad], axis=1).astype(bf16)
    small_grad = jnp.pad(
        small_grad.reshape(n_all, small_own), ((0, 0), (0, rows_own * HD - small_own))
    ).reshape(n_all * rows_own, HD)
    packed_grad = jnp.concatenate([small_grad, key_value_grad.astype(bf16)], axis=1)
    packed_owned = sum_rows(packed_grad.reshape(n_all, rows_own, HD + 2 * KVW), HD + KVW)
    qkv_owned = jnp.concatenate([query_owned, packed_owned[:, HD:]], axis=1)
    small_owned = packed_owned[:, :HD].reshape(-1)[:small_own]

    qkv_new = adamw_update(qkv_master, qkv_first, qkv_second, qkv_owned, 0.09, 0.1)
    out_new = adamw_update(out_master, out_first, out_second, out_owned, 0.18, 0.1)
    gate_up_new = adamw_hidden(
        gate_up_master,
        gate_up_first,
        gate_up_second,
        gate_up_owned,
        ring_order,
        n_dp,
        ff_pad,
        0.064,
        0.1,
    )
    down_new = adamw_update(down_master, down_first, down_second, down_owned, 0.026, 0.1)
    small_new = adamw_update(small_master, small_first, small_second, small_owned, 0.6, 0.0)
    return (
        outputs[None],
        input_grads[None],
        *qkv_new,
        *out_new,
        *gate_up_new,
        *down_new,
        *small_new,
    )


def solution(mesh):
    in_specs = (
        P("dp", "seq", None),
        P("dp", "seq", None),
        P("dp", None),
        P(("seq", "dp"), None),
        P(("seq", "dp"), None),
        P(("seq", "dp"), None),
        P(("seq", "dp"), None),
        P(("seq", "dp"), None),
        P(("seq", "dp"), None),
        P(None, ("seq", "dp"), None),
        P(None, ("seq", "dp"), None),
        P(None, ("seq", "dp"), None),
        P(("seq", "dp"), None),
        P(("seq", "dp"), None),
        P(("seq", "dp"), None),
        P(("seq", "dp")),
        P(("seq", "dp")),
        P(("seq", "dp")),
    )
    out_specs = (
        P("dp", "seq", None),
        P("dp", "seq", None),
        P(("seq", "dp"), None),
        P(("seq", "dp"), None),
        P(("seq", "dp"), None),
        P(("seq", "dp"), None),
        P(("seq", "dp"), None),
        P(("seq", "dp"), None),
        P(None, ("seq", "dp"), None),
        P(None, ("seq", "dp"), None),
        P(None, ("seq", "dp"), None),
        P(("seq", "dp"), None),
        P(("seq", "dp"), None),
        P(("seq", "dp"), None),
        P(("seq", "dp")),
        P(("seq", "dp")),
        P(("seq", "dp")),
    )
    return jax.shard_map(shards, mesh=mesh, in_specs=in_specs, out_specs=out_specs, check_vma=False)
```

```python
import functools

import jax
import jax.numpy as jnp
from jax import lax
from jax.experimental import pallas as pl
from jax.experimental.pallas import tpu as pltpu
from jax.sharding import PartitionSpec as P

D = 1536
HEADS = 12
KVH = 2
HD = 128
STEP = 10
KVW = KVH * HD
PIECE = 128


norm_eps = 1e-06
rope_base = 1000000.0
beta_one = 0.9
beta_two = 0.95
adam_eps = 1e-08
masked_score = -1e30
log2_e = 1.4426950408889634
bf16 = jnp.bfloat16
f32 = jnp.float32
vmem = pl.BlockSpec(memory_space=pltpu.VMEM)
smem = pl.BlockSpec(memory_space=pltpu.SMEM)
anywhere = pl.BlockSpec(memory_space=pl.ANY)


def shape_of(dims, kind):
    return jax.ShapeDtypeStruct(dims, kind)


def kernel_call(kernel, name, out_shape, operands, megabytes=32, **options):
    return pl.pallas_call(
        kernel,
        name=name,
        out_shape=out_shape,
        compiler_params=pltpu.CompilerParams(vmem_limit_bytes=megabytes << 20),
        cost_estimate=pl.CostEstimate(flops=10**6, bytes_accessed=10**6, transcendentals=0),
        **options,
    )(*operands)


def after(values, *others):
    return lax.optimization_barrier((values,) + others)[0]


def fence(*groups):
    flat, tree = jax.tree.flatten(groups)
    return jax.tree.unflatten(tree, lax.optimization_barrier(tuple(flat)))


def dot(left, right):
    return jnp.dot(left, right, preferred_element_type=f32)


def dot_transposed(left, right):
    return lax.dot_general(left, right, (((1,), (1,)), ((), ())), preferred_element_type=f32)


def rotary_tables(places):
    half_size = HD // 2
    freqs = rope_base ** (-(jnp.arange(half_size).astype(f32) * (2.0 / HD)))
    angles = places.astype(f32)[:, None] * freqs[None, :]
    cosine, sine = jnp.cos(angles), jnp.sin(angles)
    return jnp.concatenate([cosine, cosine], axis=1), jnp.concatenate([-sine, sine], axis=1)


def rms_scale(values):
    return lax.rsqrt(jnp.mean(values * values, axis=-1, keepdims=True) + norm_eps)


def swap_halves(values):
    return pltpu.roll(values, HD // 2, 1)


def head(index):
    return slice(index * HD, (index + 1) * HD)


def project_kv_kernel(tokens, w_qkv, gain, bias, cosine, sine, normed_ref, kv_ref):
    inputs = tokens[...].astype(f32)
    normed = (inputs * rms_scale(inputs) * gain[...]).astype(bf16)
    normed_ref[...] = normed
    rows = dot(normed, w_qkv[:, D:]) + bias[:, D:]
    for j in range(KVH):
        part = rows[:, head(j)]
        kv_ref[:, head(j)] = (part * cosine[...] + swap_halves(part) * sine[...]).astype(bf16)
    kv_ref[:, KVW:] = rows[:, KVW:].astype(bf16)


def project_q_kernel(normed, w_qkv, bias, cosine, sine, query_ref):
    rows = dot(normed[...], w_qkv[:, :D]) + bias[:, :D]
    for j in range(HEADS):
        part = rows[:, head(j)]
        query_ref[:, head(j)] = (part * cosine[...] + swap_halves(part) * sine[...]).astype(bf16)


def project_kv(tokens, w_qkv, gain, bias, cosine, sine):
    rows = tokens.shape[0]
    return kernel_call(
        project_kv_kernel,
        "project_kv",
        (shape_of((rows, D), bf16), shape_of((rows, 2 * KVW), bf16)),
        (tokens, w_qkv, gain, bias, cosine, sine),
    )


def project_q(normed, w_qkv, bias, cosine, sine):
    return kernel_call(
        project_q_kernel,
        "project_q",
        shape_of(normed.shape, bf16),
        (normed, w_qkv, bias, cosine, sine),
    )


def visible_block(query_bases, key_bases, first_run, runs):
    down = lax.broadcasted_iota(jnp.int32, (PIECE, PIECE), 0)
    across = lax.broadcasted_iota(jnp.int32, (PIECE, PIECE), 1)
    later = down - across
    return jnp.concatenate(
        [
            jnp.concatenate(
                [
                    later <= query_bases[q] - key_bases[first_run + r]
                    for q in range(query_bases.shape[0])
                ],
                axis=1,
            )
            for r in range(runs)
        ],
        axis=0,
    )


def attend_kernel(query_bases, key_bases, q_ref, *refs):
    pieces, (out_ref, lse_ref, kv_ref) = refs[:-3], refs[-3:]
    rows = q_ref.shape[0]
    for i, piece in enumerate(pieces):
        kv_ref[i * rows : (i + 1) * rows, :] = piece[...]
    groups = HEADS // KVH
    scale = HD**-0.5 * log2_e
    visible = visible_block(query_bases, key_bases, 0, key_bases.shape[0])
    for kv in range(KVH):
        keys = kv_ref[:, head(kv)]
        values = kv_ref[:, head(KVH + kv)].T
        for h in range(kv * groups, (kv + 1) * groups):
            scores = dot_transposed(keys, q_ref[:, head(h)])
            scores = jnp.where(visible, scores, masked_score)
            top = jnp.max(scores, axis=0, keepdims=True)
            weights = jnp.exp2((scores - top) * scale)
            total = jnp.sum(weights, axis=0, keepdims=True)
            mixed = dot(values, weights.astype(bf16))
            out_ref[:, head(h)] = (mixed / total).T
            lse_ref[h : h + 1, :] = top * scale + jnp.log2(total)


def attend(queries, pieces, query_bases, key_bases):
    rows, total = queries.shape[0], key_bases.shape[0] * PIECE
    return kernel_call(
        attend_kernel,
        "attend",
        (
            shape_of((rows, D), f32),
            shape_of((HEADS, rows), f32),
            shape_of((total, 2 * KVW), bf16),
        ),
        (query_bases, key_bases, queries, *pieces),
        in_specs=[smem] * 2 + [vmem] * (1 + len(pieces)),
    )


def out_kernel(tokens, attended, w_out, gain, residual_ref, normed_ref, low_ref):
    low = attended[...].astype(bf16)
    low_ref[...] = low
    residual = tokens[...].astype(f32) + dot(low, w_out[...])
    residual_ref[...] = residual
    normed_ref[...] = (residual * rms_scale(residual) * gain[...]).astype(bf16)


def out_project(tokens, attended, w_out, gain):
    dims = tokens.shape
    return kernel_call(
        out_kernel,
        "out_project",
        (shape_of(dims, f32), shape_of(dims, bf16), shape_of(dims, bf16)),
        (tokens, attended, w_out, gain),
    )


def ffn_kernel(
    normed_own, normed_other, grad_own, grad_other, w_gate_up, w_down, *refs, earlier
):
    refs = refs[earlier:]
    out_refs, grad_refs = refs[:2], refs[2:4]
    normed_ref, ffn_grad_ref, hidden_ref, gate_ref, up_ref = refs[4:]
    rows = normed_own.shape[0]
    for i, (normed_in, grad_in) in enumerate(((normed_own, grad_own), (normed_other, grad_other))):
        to = slice(i * rows, (i + 1) * rows)
        normed, ffn_grad = normed_in[...], grad_in[...]
        normed_ref[0, to, :] = normed
        ffn_grad_ref[0, to, :] = ffn_grad
        gate = dot(normed, w_gate_up[0])
        up = dot(normed, w_gate_up[1])
        sigmoid = 1.0 / (1.0 + jnp.exp(-gate))
        silu = gate * sigmoid
        hidden = (silu * up).astype(bf16)
        hidden_ref[0, to, :] = hidden
        out_refs[i][...] = dot(hidden, w_down[...]).astype(bf16)
        hidden_grad = dot_transposed(ffn_grad, w_down[...])
        gate_grad = (hidden_grad * up * sigmoid * (1.0 + gate * (1.0 - sigmoid))).astype(bf16)
        up_grad = (hidden_grad * silu).astype(bf16)
        gate_ref[0, to, :] = gate_grad
        up_ref[0, to, :] = up_grad
        grad_refs[i][...] = (
            dot_transposed(gate_grad, w_gate_up[0]) + dot_transposed(up_grad, w_gate_up[1])
        ).astype(bf16)


def feed_forward(normed, grads, w_gate_up, w_down, slot, slots, kept):
    rows, width = normed[0].shape
    ff_own = w_down.shape[0]
    token = shape_of((rows, width), bf16)
    widths = (width, width, ff_own, ff_own, ff_own)
    operands = (*normed, *grads, w_gate_up, w_down)
    return kernel_call(
        functools.partial(ffn_kernel, earlier=len(kept)),
        "feed_forward",
        (token,) * 4 + tuple(shape_of((slots, 2 * rows, w), bf16) for w in widths),
        (*operands, *kept),
        grid=(1,),
        in_specs=[vmem] * len(operands) + [anywhere] * len(kept),
        out_specs=(vmem,) * 4
        + tuple(pl.BlockSpec((1, 2 * rows, w), lambda i: (slot, 0, 0)) for w in widths),
        input_output_aliases={len(operands) + i: 4 + i for i in range(len(kept))},
    )


def norm_back_kernel(
    got, own, other, residual_ref, cotangent, gain, w_out, grad_ref, low_ref, back_ref, gain_ref
):
    normed_grad = got[...].astype(f32) + own[...].astype(f32) + other[...].astype(f32)
    residual = residual_ref[...]
    scale = rms_scale(residual)
    unit = residual * scale
    gain_ref[...] = jnp.sum(normed_grad * unit, axis=0, keepdims=True)
    weighted = normed_grad * gain[...]
    grad = cotangent[...].astype(f32) + scale * (
        weighted - unit * jnp.mean(weighted * unit, axis=-1, keepdims=True)
    )
    grad_ref[...] = grad
    low = grad.astype(bf16)
    low_ref[...] = low
    back_ref[...] = dot_transposed(low, w_out[...]).astype(bf16)


def norm_back(got, own, other, residual, cotangent, gain, w_out):
    dims = residual.shape
    return kernel_call(
        norm_back_kernel,
        "norm_back",
        (shape_of(dims, f32), shape_of(dims, bf16), shape_of(dims, bf16), shape_of((1, D), f32)),
        (got, own, other, residual, cotangent, gain, w_out),
    )


def attend_back_kernel(
    query_bases,
    key_bases,
    q_ref,
    kv_ref,
    grad_ref,
    out_ref,
    lse_ref,
    cosine,
    sine,
    q_grad_ref,
    kv_own_ref,
    kv_other_ref,
    q_rows,
    grad_rows,
    deltas,
    q_sums,
):
    rows = q_ref.shape[0]
    groups = HEADS // KVH
    scale = HD**-0.5
    for kv in range(KVH):
        for j in range(groups):
            part = slice(j * rows, (j + 1) * rows)
            columns = head(kv * groups + j)
            q_rows[part, :] = q_ref[:, columns]
            grads = grad_ref[:, columns]
            grad_rows[part, :] = grads
            product = grads.astype(f32) * out_ref[:, columns]
            deltas[:, part] = jnp.sum(product.T, axis=0, keepdims=True)
        q_sums[...] = jnp.zeros_like(q_sums)

        @pl.loop(0, kv_ref.shape[0] // (2 * rows))
        def _(step):
            at = pl.ds(pl.multiple_of(step * (2 * rows), 2 * rows), 2 * rows)
            runs = 2 * rows // PIECE
            visible = visible_block(query_bases, key_bases, step * runs, runs)
            keys = kv_ref[at, head(kv)]
            values = kv_ref[at, head(KVH + kv)]
            key_sum = value_sum = None
            for j in range(groups):
                part = slice(j * rows, (j + 1) * rows)
                h = kv * groups + j
                queries, grads = q_rows[part, :], grad_rows[part, :]
                scores = dot_transposed(keys, queries)
                weights = jnp.where(
                    visible, jnp.exp2(scores * (scale * log2_e) - lse_ref[h : h + 1, :]), 0.0
                )
                weight_grads = dot_transposed(values, grads)
                score_grads = (weights * (weight_grads - deltas[:, part])).astype(bf16)
                value_part = dot(weights.astype(bf16), grads)
                key_part = dot(score_grads, queries)
                key_sum = key_part if key_sum is None else key_sum + key_part
                value_sum = value_part if value_sum is None else value_sum + value_part
                q_sums[part, :] += lax.dot_general(
                    score_grads, keys, (((0,), (0,)), ((), ())), preferred_element_type=f32
                )
            key_sum = (key_sum * scale).astype(bf16)
            value_sum = value_sum.astype(bf16)
            to = pl.ds(pl.multiple_of(step * rows, rows), rows)
            for ref, mine in ((kv_own_ref, slice(0, rows)), (kv_other_ref, slice(rows, 2 * rows))):
                ref[to, head(kv)] = key_sum[mine, :]
                ref[to, head(KVH + kv)] = value_sum[mine, :]

        for j in range(groups):
            part = q_sums[j * rows : (j + 1) * rows, :] * scale
            q_grad_ref[:, head(kv * groups + j)] = (
                part * cosine[...] - swap_halves(part) * sine[...]
            ).astype(bf16)


def attend_back(queries, key_value, grads, attended, lse, query_bases, key_bases, cosine, sine):
    rows, total = queries.shape[0], key_value.shape[0]
    groups = HEADS // KVH
    return kernel_call(
        attend_back_kernel,
        "attend_back",
        (
            shape_of((rows, D), bf16),
            shape_of((total // 2, 2 * KVW), bf16),
            shape_of((total // 2, 2 * KVW), bf16),
        ),
        (query_bases, key_bases, queries, key_value, grads, attended, lse, cosine, sine),
        in_specs=[smem] * 2 + [vmem] * 7,
        scratch_shapes=[
            pltpu.VMEM((groups * rows, HD), bf16),
            pltpu.VMEM((groups * rows, HD), bf16),
            pltpu.VMEM((1, groups * rows), f32),
            pltpu.VMEM((groups * rows, HD), f32),
        ],
    )


def input_kernel(
    tokens, gain, w_qkv, query_grad, cosine, sine, residual_grad, own, *refs
):
    got, (kv_ref, input_ref, gain_ref, bias_ref) = refs[:-4], refs[-4:]
    rows = own[...].astype(f32)
    for piece in got:
        rows = rows + piece[...].astype(f32)
    for j in range(KVH):
        part = rows[:, head(j)]
        kv_ref[:, head(j)] = (part * cosine[...] - swap_halves(part) * sine[...]).astype(bf16)
    kv_ref[:, KVW:] = rows[:, KVW:].astype(bf16)
    kv_grad = kv_ref[...]
    q_grad = query_grad[...]
    bias_ref[:, :D] = jnp.sum(q_grad.astype(f32), axis=0, keepdims=True)
    bias_ref[:, D:] = jnp.sum(kv_grad.astype(f32), axis=0, keepdims=True)
    normed_grad = dot_transposed(q_grad, w_qkv[:, :D]) + dot_transposed(kv_grad, w_qkv[:, D:])
    inputs = tokens[...].astype(f32)
    scale = rms_scale(inputs)
    unit = inputs * scale
    gain_ref[...] = jnp.sum(normed_grad * unit, axis=0, keepdims=True)
    weighted = normed_grad * gain[...]
    input_ref[...] = residual_grad[...] + scale * (
        weighted - unit * jnp.mean(weighted * unit, axis=-1, keepdims=True)
    )


def input_back(tokens, gain, w_qkv, query_grad, cosine, sine, residual_grad, own, got):
    rows = tokens.shape[0]
    return kernel_call(
        input_kernel,
        "input_back",
        (
            shape_of((rows, 2 * KVW), bf16),
            shape_of((rows, D), f32),
            shape_of((1, D), f32),
            shape_of((1, D + 2 * KVW), f32),
        ),
        (tokens, gain, w_qkv, query_grad, cosine, sine, residual_grad, own, *got),
    )


def cut_kernel(values, out_ref, *, n_dp, own, padded):
    out_ref[...] = jnp.zeros_like(out_ref)
    for s in range(out_ref.shape[0]):
        for d in range(n_dp):
            start = (s * n_dp + d) * own
            out_ref[s, 0, :, d * padded : d * padded + own] = values[
                0, :, start : start + own
            ].astype(bf16)


def cut_hidden(values, n_seq, n_dp, padded):
    two, rows, ff = values.shape
    own = ff // (n_seq * n_dp)
    return kernel_call(
        functools.partial(cut_kernel, n_dp=n_dp, own=own, padded=padded),
        "cut_hidden",
        shape_of((n_seq, two, rows, n_dp * padded), bf16),
        (values,),
        grid=(two,),
        in_specs=[pl.BlockSpec((1, rows, ff), lambda g: (g, 0, 0))],
        out_specs=pl.BlockSpec((n_seq, 1, rows, n_dp * padded), lambda g: (0, g, 0, 0)),
    )


def adamw_update(master, moment_one, moment_two, gradient, step_rate, decay_weight):
    first_new = beta_one * moment_one + (1.0 - beta_one) * gradient
    second_new = beta_two * moment_two + (1.0 - beta_two) * gradient * gradient
    first_hat = first_new / (1.0 - beta_one**STEP)
    second_hat = second_new / (1.0 - beta_two**STEP)
    master_new = master - step_rate * (
        first_hat / (jnp.sqrt(second_hat) + adam_eps) + decay_weight * master
    )
    return (first_new, second_new, master_new)


def adamw_kernel(where, master, first, second, *refs, n_dp, own, padded, rate, decay):
    pieces, (first_ref, second_ref, master_ref, slots, joined) = refs[:-5], refs[-5:]
    for t, piece in enumerate(pieces):
        for o in range(2):
            slots[where[2 * t + o]] = piece[o, 0]
    for s in range(slots.shape[0]):
        for d in range(n_dp):
            start = (s * n_dp + d) * own
            joined[:, start : start + own] = slots[
                s, :, d * padded : d * padded + own
            ].astype(f32)
    first_ref[0], second_ref[0], master_ref[0] = adamw_update(
        master[0], first[0], second[0], joined[...], rate, decay
    )


def adamw_hidden(master, first, second, pieces, where, n_dp, padded, rate, decay):
    two, rows, ff = master.shape
    n_seq = 2 * len(pieces)
    own = ff // (n_seq * n_dp)
    block = pl.BlockSpec((1, rows, ff), lambda g: (g, 0, 0))
    part = pl.BlockSpec((2, 1, rows, n_dp * padded), lambda g: (0, g, 0, 0))
    return kernel_call(
        functools.partial(
            adamw_kernel, n_dp=n_dp, own=own, padded=padded, rate=rate, decay=decay
        ),
        "adamw_hidden",
        (shape_of(master.shape, f32),) * 3,
        (where, master, first, second, *pieces),
        megabytes=44,
        grid=(two,),
        in_specs=[smem] + [block] * 3 + [part] * len(pieces),
        out_specs=(block,) * 3,
        scratch_shapes=[
            pltpu.VMEM((n_seq, rows, n_dp * padded), bf16),
            pltpu.VMEM((rows, ff), f32),
        ],
    )


def assemble_kernel(where, *refs, splits, counts):
    ins, outs, sems = refs[: len(counts)], refs[len(counts) : -1], refs[-1]
    copies = []
    entry = 0
    for ref, (column, count) in zip(ins, counts):
        for i in range(count):
            for out, start, width in splits[column]:
                copies.append(
                    pltpu.make_async_copy(
                        ref.at[i, :, pl.ds(start, width)],
                        outs[out[0]].at[where[entry], :, pl.ds(out[1], width)],
                        sems.at[len(copies)],
                    )
                )
            entry += 1
    for copy in copies:
        copy.start()
    for copy in copies:
        copy.wait()


def assemble(pieces, where, splits, out_widths):
    counts = [(column, array.shape[0]) for array, column in pieces]
    rows = pieces[0][0].shape[1]
    blocks = sum(count for column, count in counts if column == 0)
    n_copies = sum(count * len(splits[column]) for column, count in counts)
    return kernel_call(
        functools.partial(assemble_kernel, splits=splits, counts=counts),
        "assemble",
        tuple(shape_of((blocks, rows, w), bf16) for w in out_widths),
        (where.astype(jnp.int32), *[array for array, _ in pieces]),
        in_specs=[smem] + [anywhere] * len(pieces),
        out_specs=(vmem,) * len(out_widths),
        scratch_shapes=[pltpu.SemaphoreType.DMA((n_copies,))],
    )


def seq_perm(values, chips, flip):
    count = lax.axis_size("seq")
    return lax.ppermute(
        values, "seq", [(i, ((i + 2 * chips) % count) ^ flip) for i in range(count)]
    )


def dp_perm(values, bit):
    return lax.ppermute(values, "dp", [(i, i ^ bit) for i in range(lax.axis_size("dp"))])


def dp_bits():
    return [1 << i for i in range(lax.axis_size("dp").bit_length() - 1)]


def pick(values, index, axis):
    return lax.dynamic_index_in_dim(values, index, axis, keepdims=False)


def places_of():
    n_chips = lax.axis_size("seq") // 2
    seq_at = lax.axis_index("seq")
    return n_chips, seq_at // 2, seq_at % 2, lax.axis_size("dp"), lax.axis_index("dp")


def swap(values):
    return seq_perm(values, 0, 1)


def sent_pieces(values):
    return [values] + [seq_perm(values, t, 0) for t in range(1, lax.axis_size("seq") // 2)]


def add(left, right):
    return (left.astype(f32) + right.astype(f32)).astype(bf16)


def halve(values, axis, bit):
    mine = (lax.axis_index("dp") // bit) % 2
    return pick(values, mine, axis), pick(values, 1 - mine, axis)


def bit_axes(first):
    bits = dp_bits()
    return {bit: first + len(bits) - 1 - i for i, bit in enumerate(bits)}


def drop_axis(axes, bit):
    return {b: x - (x > axes[bit]) for b, x in axes.items() if b != bit}


def halve_stage(values, axes, bit, *milestones):
    stays, goes = halve(values, axes[bit], bit)
    if milestones:
        goes = after(goes, *milestones)
    return stays, dp_perm(goes, bit), drop_axis(axes, bit)


def shards(
    tokens,
    cotangent,
    positions,
    qkv_master,
    qkv_first,
    qkv_second,
    out_master,
    out_first,
    out_second,
    gate_up_master,
    gate_up_first,
    gate_up_second,
    down_master,
    down_first,
    down_second,
    small_master,
    small_first,
    small_second,
):
    n_chips, chip_at, core_at, n_dp, dp_at = places_of()
    n_seq = 2 * n_chips
    n_all = n_seq * n_dp
    bits = dp_bits()
    rows_own, qkv_width = qkv_master.shape
    half = qkv_width // 2
    small_own = small_master.shape[0]
    ff_dev = down_master.shape[0]
    ff_pad = -(-ff_dev // 16) * 16
    ff_own = n_dp * ff_pad
    inputs = tokens[0]
    upstream = cotangent[0]
    tok_rows = inputs.shape[0]
    seq_length = positions.shape[1]
    shifts = list(range(1, n_chips))

    ring_chips = [(chip_at - t) % n_chips for t in range(n_chips)]
    ring_order = jnp.stack(
        [chip * 2 + (core_at ^ flip) for chip in ring_chips for flip in range(2)]
    ).astype(jnp.int32)
    bases = positions[0, ::PIECE].reshape(n_seq, tok_rows // PIECE)
    key_bases = jnp.take(bases, ring_order, axis=0)
    query_bases = key_bases[0]
    key_bases = key_bases.reshape(-1)
    own_places = lax.dynamic_slice_in_dim(
        positions[0], (chip_at * 2 + core_at) * tok_rows, tok_rows, 0
    )
    cosine, sine = rotary_tables(own_places)

    small_block = jnp.pad(
        small_master.astype(bf16), (0, rows_own * HD - small_own)
    ).reshape(rows_own, HD)
    packed = jnp.concatenate([small_block, qkv_master.astype(bf16)], axis=1)
    qkv_ring = sent_pieces(packed)
    cut = cut_hidden(gate_up_master, n_seq, n_dp, ff_pad)
    cut = cut.reshape((n_chips, 2) + cut.shape[1:])
    pairs = jnp.stack([pick(cut, core_at, 1), swap(pick(cut, 1 - core_at, 1))], axis=1)
    qkv_ring, pairs, cosine, sine = fence(qkv_ring, pairs, cosine, sine)

    def exchange(shift):
        return seq_perm(pick(pairs, (chip_at + shift) % n_chips, 0), shift, 0)

    w_out = lax.all_gather(
        after(out_master.astype(bf16), pairs), ("seq", "dp"), axis=0, tiled=True
    )

    columns = ((0, HD + half), (HD + half, HD + qkv_width))
    orders = (bits, bits[::-1])
    held = [jnp.stack([r[:, lo:hi] for r in qkv_ring]) for lo, hi in columns]
    flips = [[0], [0]]
    gate_up_pieces = {0: pick(pairs, chip_at, 0)}
    groups = [shifts[:1], shifts[1:-1], shifts[-1:]] if n_chips > 2 else [shifts, [], []]
    for stage in range(len(bits)):
        got = [dp_perm(h, order[stage]) for h, order in zip(held, orders)]
        if stage == len(bits) - 1:
            swapped = [swap(h) for h in held]
        for shift in groups[min(stage, 1)] if stage < 2 else []:
            gate_up_pieces[shift] = exchange(shift)
        got, held, gate_up_pieces = fence(got, held, gate_up_pieces)
        flips = [f + [k ^ order[stage] for k in f] for f, order in zip(flips, orders)]
        if stage < len(bits) - 1:
            held = [jnp.concatenate([h, g], axis=0) for h, g in zip(held, got)]
    (swapped,) = fence(swapped)
    down_share = jnp.pad(down_master.astype(bf16), ((0, ff_pad - ff_dev), (0, 0)))
    w_down = lax.all_gather(after(down_share, *got), "dp", axis=0, tiled=True)
    for shift in groups[2]:
        gate_up_pieces[shift] = exchange(shift)
    got_swapped = [swap(g) for g in got]
    pieces, where = [], []
    for column in range(2):
        for flip, part, ks in (
            (0, held[column], flips[column][: n_dp // 2]),
            (0, got[column], flips[column][n_dp // 2 :]),
            (1, swapped[column], flips[column][: n_dp // 2]),
            (1, got_swapped[column], flips[column][n_dp // 2 :]),
        ):
            pieces.append((part, column))
            where += [
                (chip * 2 + (core_at ^ flip)) * n_dp + (dp_at ^ k) for k in ks for chip in ring_chips
            ]
    w_qkv, small_blocks = assemble(
        pieces,
        jnp.stack(where),
        ((((1, 0), 0, HD), ((0, 0), HD, half)), (((0, half), 0, half),)),
        (qkv_width, HD),
    )
    w_qkv, small_blocks, gate_up_pieces = fence(w_qkv, small_blocks, gate_up_pieces)
    w_qkv = w_qkv.reshape(D, qkv_width)
    small_params = small_blocks.reshape(n_all, rows_own * HD)[:, :small_own].reshape(1, -1)
    small_params = small_params.astype(f32)
    gain_one = small_params[:, :D]
    gain_two = small_params[:, D : 2 * D]
    qkv_bias = small_params[:, 2 * D :]
    normed_one, key_value = project_kv(inputs, w_qkv, gain_one, qkv_bias, cosine, sine)
    gate_up_held = [
        jnp.concatenate([gate_up_pieces[t] for t in ts], axis=0)
        for ts in (range(n_chips // 2), range(n_chips // 2, n_chips))
    ]
    normed_one, key_value, gate_up_held = fence(normed_one, key_value, gate_up_held)

    kv_ring = sent_pieces(key_value)
    gate_up_parts = [
        [held, dp_perm(held, order[0])] for held, order in zip(gate_up_held, orders)
    ]
    gate_up_flips = [[0, order[0]] for order in orders]
    queries = project_q(normed_one, w_qkv, qkv_bias, cosine, sine)
    kv_swapped = [swap(kv_ring[0])] + [swap(after(piece, queries)) for piece in kv_ring[1:]]
    kv_ring, kv_swapped, gate_up_parts, queries, upstream = fence(
        kv_ring, kv_swapped, gate_up_parts, queries, upstream
    )

    def cross(start, stop, stage):
        for parts, flips_of, order in zip(gate_up_parts, gate_up_flips, orders):
            parts += [dp_perm(piece, order[stage]) for piece in parts[start:stop]]
            flips_of += [k ^ order[stage] for k in flips_of[start:stop]]

    upstream_ring = [upstream, seq_perm(upstream, 1, 0)]
    cross(0, 1 if len(bits) == 2 else 2, 1)
    attended, logsum, key_value_all = attend(
        queries, [piece for pair in zip(kv_ring, kv_swapped) for piece in pair], query_bases, key_bases
    )
    gate_up_parts, upstream_ring, attended, logsum, key_value_all = fence(
        gate_up_parts, upstream_ring, attended, logsum, key_value_all
    )

    def ring_step(pieces):
        return pieces + [seq_perm(pieces[-1], 1, 0)] if len(pieces) < n_chips else pieces

    upstream_ring = ring_step(upstream_ring)
    if len(bits) == 2:
        cross(1, 2, 1)
    else:
        cross(0, 4, 2)
    upstream_swapped = [swap(piece) for piece in upstream_ring[:2]]
    residual, normed_two, attended_low = out_project(inputs, attended, w_out, gain_two)
    normed_ring, normed_swapped = [normed_two], [swap(normed_two)]
    gate_up_parts, upstream_ring, upstream_swapped, normed_ring, normed_swapped, residual = fence(
        gate_up_parts, upstream_ring, upstream_swapped, normed_ring, normed_swapped, residual
    )

    pieces, where = [], []
    for column, (parts, flips_of) in enumerate(zip(gate_up_parts, gate_up_flips)):
        slots = ring_order[:n_chips] if column == 0 else ring_order[n_chips:]
        for part, k in zip(parts, flips_of):
            pieces.append((part.reshape(-1, rows_own, ff_own), 0))
            block = slots * n_dp + (dp_at ^ k)
            where.append(jnp.stack([block, n_all + block], axis=1).reshape(-1))
    (w_gate_up,) = assemble(
        pieces, jnp.concatenate(where), ((((0, 0), 0, ff_own),),), (ff_own,)
    )
    w_gate_up = w_gate_up.reshape(2, D, ff_own)
    out_parts, kept = [], ()
    running = None
    for slot in range(n_chips):
        sent = None if running is None else seq_perm(running, 1, 0)
        normed_ring = ring_step(normed_ring)
        upstream_ring = ring_step(upstream_ring)
        out_own, out_other, grad_own, grad_other, *kept = feed_forward(
            (normed_ring[slot], normed_swapped[slot]),
            (upstream_ring[slot], upstream_swapped[slot]),
            w_gate_up,
            w_down,
            slot,
            n_chips,
            kept,
        )
        out_parts.append((out_own, out_other))
        grad_swapped = swap(grad_other)
        if slot + 1 < n_chips:
            normed_swapped = normed_swapped + [swap(after(normed_ring[slot + 1], grad_own))]
        if slot + 2 < n_chips and len(upstream_swapped) < slot + 3:
            upstream_swapped = upstream_swapped + [swap(after(upstream_ring[slot + 2], grad_own))]
        if slot == 0:
            grad_first = (grad_own, grad_swapped)
        elif sent is None:
            running = add(grad_own, grad_swapped)
        else:
            running = add(add(grad_own, grad_swapped), after(sent, grad_own))
        running, normed_ring, normed_swapped, upstream_ring, upstream_swapped, out_parts, kept = fence(
            running, normed_ring, normed_swapped, upstream_ring, upstream_swapped, out_parts, kept
        )

    grad_ring = jnp.zeros_like(grad_first[0]) if running is None else seq_perm(running, 1, 0)
    normed_all, ffn_all, hidden_all, gate_grads_all, up_grads_all = (
        entry.reshape(seq_length, -1) for entry in kept
    )
    gate_up_grads = [
        jnp.einsum("td,tf->df", normed_all, grads, preferred_element_type=f32)
        .astype(bf16)
        .reshape((n_seq,) + (2,) * len(bits) + (rows_own, ff_own))
        for grads in (gate_grads_all, up_grads_all)
    ]
    out_pairs = [(own, swap(other)) for own, other in out_parts]
    out_total = [add(own, other) for own, other in out_pairs[1:]]
    grad_ring, gate_up_grads, out_pairs, out_total = fence(
        grad_ring, gate_up_grads, out_pairs, out_total
    )

    axes = bit_axes(1)
    stages = [
        halve_stage(grads, axes, order[0]) for grads, order in zip(gate_up_grads, orders)
    ]
    out_running = seq_perm(out_total[0], 1, 0) if n_chips > 1 else None
    residual_grads, branch_grads, attended_grads, gain_two_grad = norm_back(
        grad_ring, *grad_first, residual, upstream, gain_two, w_out
    )
    query_pre, kv_grad_own, kv_grad_other = attend_back(
        queries,
        key_value_all,
        attended_grads,
        attended,
        logsum,
        query_bases,
        key_bases,
        cosine,
        sine,
    )
    stages = [(add(stays, after(got, query_pre)), rest) for stays, got, rest in stages]
    kv_swapped = swap(kv_grad_other)
    kv_sum = add(kv_grad_own, kv_swapped).reshape(n_chips, tok_rows, 2 * KVW)
    sums = [values for values, _ in stages]
    axes_left = [rest for _, rest in stages]
    sums, kv_sum, query_pre, branch_grads, out_running, hidden_all, ffn_all = fence(
        sums, kv_sum, query_pre, branch_grads, out_running, hidden_all, ffn_all
    )

    kv_got = [seq_perm(kv_sum[t], n_chips - t, 0) for t in range(1, n_chips)]
    later = []
    for values, rest, order in zip(sums, axes_left, orders):
        for bit in order[1:]:
            stays, got, rest = halve_stage(values, rest, bit)
            values = add(stays, got)
        later.append(values)
    query_grad = jnp.einsum("td,tf->df", normed_one, query_pre, preferred_element_type=f32)
    out_grad = jnp.einsum("td,te->de", attended_low, branch_grads, preferred_element_type=f32)
    both = jnp.stack([query_grad.astype(bf16), out_grad.astype(bf16)])
    both = both.reshape(2, n_chips, 2, n_dp, rows_own, D)
    both_got = swap(pick(both, 1 - core_at, 2))
    both = add(pick(both, core_at, 2), both_got)
    both = both.reshape((2, n_chips) + (2,) * len(bits) + (rows_own, D))
    down_grad = jnp.einsum("tf,td->fd", hidden_all, ffn_all, preferred_element_type=f32)
    later, both, kv_got, kv_sum, out_running = fence(later, both, kv_got, kv_sum, out_running)
    down_owned = lax.psum_scatter(
        down_grad.astype(bf16), "dp", scatter_dimension=0, tiled=True
    )[:ff_dev].astype(f32)

    later = jnp.stack(later, axis=1)
    later = later.reshape((n_chips, 2) + later.shape[1:])
    later = jnp.stack([pick(later, core_at, 1), swap(pick(later, 1 - core_at, 1))], axis=1)

    def exchange_back(shift):
        return seq_perm(pick(later, (chip_at + shift) % n_chips, 0), shift, 0)

    query_side, out_side = both[0], both[1]
    query_stage = halve_stage(query_side, axes, bits[0])
    out_stage = halve_stage(out_side, axes, bits[-1])
    key_value_pre, input_grads, gain_one_grad, bias_grad = input_back(
        inputs,
        gain_one,
        w_qkv,
        query_pre,
        cosine,
        sine,
        residual_grads,
        kv_sum[0],
        kv_got,
    )
    key_value_grad = jnp.einsum(
        "td,tf->df", normed_one, key_value_pre, preferred_element_type=f32
    )
    small_grad = jnp.concatenate([gain_one_grad, gain_two_grad, bias_grad], axis=1).astype(bf16)
    small_grad = jnp.pad(
        small_grad.reshape(n_all, small_own), ((0, 0), (0, rows_own * HD - small_own))
    ).reshape(n_all * rows_own, HD)
    packed_grad = jnp.concatenate([small_grad, key_value_grad.astype(bf16)], axis=1)
    packed_grad = packed_grad.reshape(n_chips, 2, n_dp, rows_own, HD + 2 * KVW)
    packed_got = swap(pick(packed_grad, 1 - core_at, 1))
    packed_grad = add(pick(packed_grad, core_at, 1), packed_got)
    packed_grad = packed_grad.reshape((n_chips,) + (2,) * len(bits) + packed_grad.shape[2:])
    query_sum, query_axes = add(query_stage[0], query_stage[1]), query_stage[2]
    out_sum, out_axes = add(out_stage[0], out_stage[1]), out_stage[2]
    gate_up_owned = {0: pick(later, chip_at, 0)}
    for shift in groups[0]:
        gate_up_owned[shift] = exchange_back(shift)
    if n_chips > 2:
        out_running = add(out_running, out_total[1])
    packed_grad, query_sum, out_sum, gate_up_owned, out_running = fence(
        packed_grad, query_sum, out_sum, gate_up_owned, out_running
    )

    for shift in groups[1]:
        gate_up_owned[shift] = exchange_back(shift)
    for bit in bits[1:]:
        stays, got, query_axes = halve_stage(query_sum, query_axes, bit)
        query_sum = add(stays, got)
    for bit in bits[::-1][1:]:
        stays, got, out_axes = halve_stage(out_sum, out_axes, bit)
        out_sum = add(stays, got)
    packed_parts = []
    for lo, hi, order in ((0, HD + KVW, bits), (HD + KVW, HD + 2 * KVW, bits[::-1])):
        part, part_axes = packed_grad[..., lo:hi], axes
        for bit in order:
            stays, got, part_axes = halve_stage(part, part_axes, bit)
            part = add(stays, got)
        packed_parts.append(part)
    packed_sum = jnp.concatenate(packed_parts, axis=-1)
    if n_chips > 2:
        out_running = seq_perm(out_running, 1, 0)
        if n_chips > 3:
            out_running = add(out_running, out_total[2])
    packed_sum, query_sum, out_sum, gate_up_owned, out_running = fence(
        packed_sum, query_sum, out_sum, gate_up_owned, out_running
    )

    rest_sum = jnp.concatenate([packed_sum, query_sum, out_sum], axis=-1)
    total = pick(rest_sum, chip_at, 0).astype(f32)
    for shift in shifts:
        total = total + seq_perm(
            pick(rest_sum, (chip_at + shift) % n_chips, 0), shift, 0
        ).astype(f32)
    for shift in groups[2]:
        gate_up_owned[shift] = exchange_back(shift)
    for t in range(3, n_chips):
        out_running = seq_perm(out_running, 1, 0)
        if t + 1 < n_chips:
            out_running = add(out_running, out_total[t])
    outputs = residual + out_pairs[0][0].astype(f32) + out_pairs[0][1].astype(f32)
    if n_chips > 1:
        outputs = outputs + out_running.astype(f32)
    outputs = outputs.astype(bf16)
    gate_up_new = adamw_hidden(
        gate_up_master,
        gate_up_first,
        gate_up_second,
        [gate_up_owned[t] for t in range(n_chips)],
        ring_order,
        n_dp,
        ff_pad,
        0.064,
        0.1,
    )
    packed_owned, query_owned, out_owned = jnp.split(
        total, (HD + 2 * KVW, HD + 2 * KVW + D), axis=1
    )
    qkv_owned = jnp.concatenate([query_owned, packed_owned[:, HD:]], axis=1)
    small_owned = packed_owned[:, :HD].reshape(-1)[:small_own]

    qkv_new = adamw_update(qkv_master, qkv_first, qkv_second, qkv_owned, 0.09, 0.1)
    out_new = adamw_update(out_master, out_first, out_second, out_owned, 0.18, 0.1)
    down_new = adamw_update(down_master, down_first, down_second, down_owned, 0.026, 0.1)
    small_new = adamw_update(small_master, small_first, small_second, small_owned, 0.6, 0.0)
    return (
        outputs[None],
        input_grads[None],
        *qkv_new,
        *out_new,
        *gate_up_new,
        *down_new,
        *small_new,
    )


def solution(mesh):
    in_specs = (
        P("dp", "seq", None),
        P("dp", "seq", None),
        P("dp", None),
        P(("seq", "dp"), None),
        P(("seq", "dp"), None),
        P(("seq", "dp"), None),
        P(("seq", "dp"), None),
        P(("seq", "dp"), None),
        P(("seq", "dp"), None),
        P(None, ("seq", "dp"), None),
        P(None, ("seq", "dp"), None),
        P(None, ("seq", "dp"), None),
        P(("seq", "dp"), None),
        P(("seq", "dp"), None),
        P(("seq", "dp"), None),
        P(("seq", "dp")),
        P(("seq", "dp")),
        P(("seq", "dp")),
    )
    out_specs = (
        P("dp", "seq", None),
        P("dp", "seq", None),
        P(("seq", "dp"), None),
        P(("seq", "dp"), None),
        P(("seq", "dp"), None),
        P(("seq", "dp"), None),
        P(("seq", "dp"), None),
        P(("seq", "dp"), None),
        P(None, ("seq", "dp"), None),
        P(None, ("seq", "dp"), None),
        P(None, ("seq", "dp"), None),
        P(("seq", "dp"), None),
        P(("seq", "dp"), None),
        P(("seq", "dp"), None),
        P(("seq", "dp")),
        P(("seq", "dp")),
        P(("seq", "dp")),
    )
    return jax.shard_map(shards, mesh=mesh, in_specs=in_specs, out_specs=out_specs, check_vma=False)
```

```python
import functools

import jax
import jax.numpy as jnp
from jax import lax
from jax.experimental import pallas as pl
from jax.experimental.pallas import tpu as pltpu
from jax.sharding import PartitionSpec as P

D = 1536
HEADS = 12
KVH = 2
HD = 128
STEP = 10
KVW = KVH * HD
PIECE = 128


norm_eps = 1e-06
rope_base = 1000000.0
beta_one = 0.9
beta_two = 0.95
adam_eps = 1e-08
masked_score = -1e30
log2_e = 1.4426950408889634
bf16 = jnp.bfloat16
f32 = jnp.float32
vmem = pl.BlockSpec(memory_space=pltpu.VMEM)
smem = pl.BlockSpec(memory_space=pltpu.SMEM)
anywhere = pl.BlockSpec(memory_space=pl.ANY)


def shape_of(dims, kind):
    return jax.ShapeDtypeStruct(dims, kind)


def kernel_call(kernel, name, out_shape, operands, megabytes=32, **options):
    return pl.pallas_call(
        kernel,
        name=name,
        out_shape=out_shape,
        compiler_params=pltpu.CompilerParams(vmem_limit_bytes=megabytes << 20),
        cost_estimate=pl.CostEstimate(flops=10**6, bytes_accessed=10**6, transcendentals=0),
        **options,
    )(*operands)


def after(values, *others):
    return lax.optimization_barrier((values,) + others)[0]


def fence(*groups):
    flat, tree = jax.tree.flatten(groups)
    return jax.tree.unflatten(tree, lax.optimization_barrier(tuple(flat)))


def dot(left, right):
    return jnp.dot(left, right, preferred_element_type=f32)


def dot_transposed(left, right):
    return lax.dot_general(left, right, (((1,), (1,)), ((), ())), preferred_element_type=f32)


def rotary_tables(places):
    half_size = HD // 2
    freqs = rope_base ** (-(jnp.arange(half_size).astype(f32) * (2.0 / HD)))
    angles = places.astype(f32)[:, None] * freqs[None, :]
    cosine, sine = jnp.cos(angles), jnp.sin(angles)
    return jnp.concatenate([cosine, cosine], axis=1), jnp.concatenate([-sine, sine], axis=1)


def rms_scale(values):
    return lax.rsqrt(jnp.mean(values * values, axis=-1, keepdims=True) + norm_eps)


def swap_halves(values):
    return pltpu.roll(values, HD // 2, 1)


def head(index):
    return slice(index * HD, (index + 1) * HD)


def project_kv_kernel(tokens, w_qkv, gain, bias, cosine, sine, normed_ref, kv_ref):
    inputs = tokens[...].astype(f32)
    normed = (inputs * rms_scale(inputs) * gain[...]).astype(bf16)
    normed_ref[...] = normed
    rows = dot(normed, w_qkv[:, D:]) + bias[:, D:]
    for j in range(KVH):
        part = rows[:, head(j)]
        kv_ref[:, head(j)] = (part * cosine[...] + swap_halves(part) * sine[...]).astype(bf16)
    kv_ref[:, KVW:] = rows[:, KVW:].astype(bf16)


def project_q_kernel(normed, w_qkv, bias, cosine, sine, query_ref):
    rows = dot(normed[...], w_qkv[:, :D]) + bias[:, :D]
    for j in range(HEADS):
        part = rows[:, head(j)]
        query_ref[:, head(j)] = (part * cosine[...] + swap_halves(part) * sine[...]).astype(bf16)


def project_kv(tokens, w_qkv, gain, bias, cosine, sine):
    rows = tokens.shape[0]
    return kernel_call(
        project_kv_kernel,
        "project_kv",
        (shape_of((rows, D), bf16), shape_of((rows, 2 * KVW), bf16)),
        (tokens, w_qkv, gain, bias, cosine, sine),
    )


def project_q(normed, w_qkv, bias, cosine, sine):
    return kernel_call(
        project_q_kernel,
        "project_q",
        shape_of(normed.shape, bf16),
        (normed, w_qkv, bias, cosine, sine),
    )


def mask_keys(values, query_bases, key_bases, first_run, fill):
    later = lax.broadcasted_iota(jnp.int32, (PIECE, PIECE), 0) - lax.broadcasted_iota(
        jnp.int32, (PIECE, PIECE), 1
    )
    keys, queries = values.shape
    rows = []
    for r in range(keys // PIECE):
        down = slice(r * PIECE, (r + 1) * PIECE)
        row = []
        for q in range(queries // PIECE):
            gap = query_bases[q] - key_bases[first_run + r]
            row.append(jnp.where(later <= gap, values[down, q * PIECE : (q + 1) * PIECE], fill))
        rows.append(jnp.concatenate(row, axis=1))
    return jnp.concatenate(rows, axis=0)


def attend_kernel(query_bases, key_bases, q_ref, *refs):
    pieces, (out_ref, lse_ref, kv_ref) = refs[:-3], refs[-3:]
    rows = q_ref.shape[0]
    for i, piece in enumerate(pieces):
        kv_ref[i * rows : (i + 1) * rows, :] = piece[...]
    groups = HEADS // KVH
    scale = HD**-0.5 * log2_e
    for kv in range(KVH):
        values = kv_ref[:, head(KVH + kv)].T
        for h in range(kv * groups, (kv + 1) * groups):
            queries = q_ref[:, head(h)]
            scores = []
            for run in range(key_bases.shape[0]):
                keys = kv_ref[run * PIECE : (run + 1) * PIECE, head(kv)]
                part = dot_transposed(keys, queries)
                scores.append(mask_keys(part, query_bases, key_bases, run, masked_score))
            scores = jnp.concatenate(scores, axis=0)
            top = jnp.max(scores, axis=0, keepdims=True)
            weights = jnp.exp2((scores - top) * scale)
            total = jnp.sum(weights, axis=0, keepdims=True)
            mixed = dot(values, weights.astype(bf16))
            out_ref[:, head(h)] = (mixed / total).T
            lse_ref[h : h + 1, :] = top * scale + jnp.log2(total)


def attend(queries, pieces, query_bases, key_bases):
    rows, total = queries.shape[0], key_bases.shape[0] * PIECE
    return kernel_call(
        attend_kernel,
        "attend",
        (
            shape_of((rows, D), f32),
            shape_of((HEADS, rows), f32),
            shape_of((total, 2 * KVW), bf16),
        ),
        (query_bases, key_bases, queries, *pieces),
        in_specs=[smem] * 2 + [vmem] * (1 + len(pieces)),
    )


def out_kernel(tokens, attended, w_out, gain, residual_ref, normed_ref, low_ref):
    low = attended[...].astype(bf16)
    low_ref[...] = low
    residual = tokens[...].astype(f32) + dot(low, w_out[...])
    residual_ref[...] = residual
    normed_ref[...] = (residual * rms_scale(residual) * gain[...]).astype(bf16)


def out_project(tokens, attended, w_out, gain):
    dims = tokens.shape
    return kernel_call(
        out_kernel,
        "out_project",
        (shape_of(dims, f32), shape_of(dims, bf16), shape_of(dims, bf16)),
        (tokens, attended, w_out, gain),
    )


def ffn_kernel(
    normed_own, normed_other, grad_own, grad_other, w_gate_up, w_down, *refs, earlier
):
    refs = refs[earlier:]
    out_refs, grad_refs = refs[:2], refs[2:4]
    normed_ref, ffn_grad_ref, hidden_ref, gate_ref, up_ref = refs[4:]
    rows = normed_own.shape[0]
    for i, (normed_in, grad_in) in enumerate(((normed_own, grad_own), (normed_other, grad_other))):
        to = slice(i * rows, (i + 1) * rows)
        normed, ffn_grad = normed_in[...], grad_in[...]
        normed_ref[0, to, :] = normed
        ffn_grad_ref[0, to, :] = ffn_grad
        gate = dot(normed, w_gate_up[0])
        up = dot(normed, w_gate_up[1])
        sigmoid = 1.0 / (1.0 + jnp.exp(-gate))
        silu = gate * sigmoid
        hidden = (silu * up).astype(bf16)
        hidden_ref[0, to, :] = hidden
        out_refs[i][...] = dot(hidden, w_down[...]).astype(bf16)
        hidden_grad = dot_transposed(ffn_grad, w_down[...])
        gate_grad = (hidden_grad * up * sigmoid * (1.0 + gate * (1.0 - sigmoid))).astype(bf16)
        up_grad = (hidden_grad * silu).astype(bf16)
        gate_ref[0, to, :] = gate_grad
        up_ref[0, to, :] = up_grad
        grad_refs[i][...] = (
            dot_transposed(gate_grad, w_gate_up[0]) + dot_transposed(up_grad, w_gate_up[1])
        ).astype(bf16)


def feed_forward(normed, grads, w_gate_up, w_down, slot, slots, kept):
    rows, width = normed[0].shape
    ff_own = w_down.shape[0]
    token = shape_of((rows, width), bf16)
    widths = (width, width, ff_own, ff_own, ff_own)
    operands = (*normed, *grads, w_gate_up, w_down)
    return kernel_call(
        functools.partial(ffn_kernel, earlier=len(kept)),
        "feed_forward",
        (token,) * 4 + tuple(shape_of((slots, 2 * rows, w), bf16) for w in widths),
        (*operands, *kept),
        grid=(1,),
        in_specs=[vmem] * len(operands) + [anywhere] * len(kept),
        out_specs=(vmem,) * 4
        + tuple(pl.BlockSpec((1, 2 * rows, w), lambda i: (slot, 0, 0)) for w in widths),
        input_output_aliases={len(operands) + i: 4 + i for i in range(len(kept))},
    )


def norm_back_kernel(
    got, own, other, residual_ref, cotangent, gain, w_out, grad_ref, low_ref, back_ref, gain_ref
):
    normed_grad = got[...].astype(f32) + own[...].astype(f32) + other[...].astype(f32)
    residual = residual_ref[...]
    scale = rms_scale(residual)
    unit = residual * scale
    gain_ref[...] = jnp.sum(normed_grad * unit, axis=0, keepdims=True)
    weighted = normed_grad * gain[...]
    grad = cotangent[...].astype(f32) + scale * (
        weighted - unit * jnp.mean(weighted * unit, axis=-1, keepdims=True)
    )
    grad_ref[...] = grad
    low = grad.astype(bf16)
    low_ref[...] = low
    back_ref[...] = dot_transposed(low, w_out[...]).astype(bf16)


def norm_back(got, own, other, residual, cotangent, gain, w_out):
    dims = residual.shape
    return kernel_call(
        norm_back_kernel,
        "norm_back",
        (shape_of(dims, f32), shape_of(dims, bf16), shape_of(dims, bf16), shape_of((1, D), f32)),
        (got, own, other, residual, cotangent, gain, w_out),
    )


def attend_back_kernel(
    query_bases,
    key_bases,
    q_ref,
    kv_ref,
    grad_ref,
    out_ref,
    lse_ref,
    cosine,
    sine,
    q_grad_ref,
    kv_own_ref,
    kv_other_ref,
    q_rows,
    grad_rows,
    deltas,
    q_sums,
):
    rows = q_ref.shape[0]
    groups = HEADS // KVH
    scale = HD**-0.5
    for kv in range(KVH):
        for j in range(groups):
            part = slice(j * rows, (j + 1) * rows)
            columns = head(kv * groups + j)
            q_rows[part, :] = q_ref[:, columns]
            grads = grad_ref[:, columns]
            grad_rows[part, :] = grads
            product = grads.astype(f32) * out_ref[:, columns]
            deltas[:, part] = jnp.sum(product.T, axis=0, keepdims=True)
        q_sums[...] = jnp.zeros_like(q_sums)

        @pl.loop(0, kv_ref.shape[0] // (2 * rows), unroll=2)
        def _(step):
            at = pl.ds(pl.multiple_of(step * (2 * rows), 2 * rows), 2 * rows)
            runs = 2 * rows // PIECE
            keys = kv_ref[at, head(kv)]
            values = kv_ref[at, head(KVH + kv)]
            key_sum = value_sum = None
            for j in range(groups):
                part = slice(j * rows, (j + 1) * rows)
                h = kv * groups + j
                queries, grads = q_rows[part, :], grad_rows[part, :]
                scores = dot_transposed(keys, queries)
                weights = jnp.exp2(scores * (scale * log2_e) - lse_ref[h : h + 1, :])
                weights = mask_keys(weights, query_bases, key_bases, step * runs, 0.0)
                weight_grads = dot_transposed(values, grads)
                score_grads = (weights * (weight_grads - deltas[:, part])).astype(bf16)
                value_part = dot(weights.astype(bf16), grads)
                key_part = dot(score_grads, queries)
                key_sum = key_part if key_sum is None else key_sum + key_part
                value_sum = value_part if value_sum is None else value_sum + value_part
                q_sums[part, :] += lax.dot_general(
                    score_grads, keys, (((0,), (0,)), ((), ())), preferred_element_type=f32
                )
            key_sum = (key_sum * scale).astype(bf16)
            value_sum = value_sum.astype(bf16)
            to = pl.ds(pl.multiple_of(step * rows, rows), rows)
            for ref, mine in ((kv_own_ref, slice(0, rows)), (kv_other_ref, slice(rows, 2 * rows))):
                ref[to, head(kv)] = key_sum[mine, :]
                ref[to, head(KVH + kv)] = value_sum[mine, :]

        for j in range(groups):
            part = q_sums[j * rows : (j + 1) * rows, :] * scale
            q_grad_ref[:, head(kv * groups + j)] = (
                part * cosine[...] - swap_halves(part) * sine[...]
            ).astype(bf16)


def attend_back(queries, key_value, grads, attended, lse, query_bases, key_bases, cosine, sine):
    rows, total = queries.shape[0], key_value.shape[0]
    groups = HEADS // KVH
    return kernel_call(
        attend_back_kernel,
        "attend_back",
        (
            shape_of((rows, D), bf16),
            shape_of((total // 2, 2 * KVW), bf16),
            shape_of((total // 2, 2 * KVW), bf16),
        ),
        (query_bases, key_bases, queries, key_value, grads, attended, lse, cosine, sine),
        in_specs=[smem] * 2 + [vmem] * 7,
        scratch_shapes=[
            pltpu.VMEM((groups * rows, HD), bf16),
            pltpu.VMEM((groups * rows, HD), bf16),
            pltpu.VMEM((1, groups * rows), f32),
            pltpu.VMEM((groups * rows, HD), f32),
        ],
    )


def input_kernel(
    tokens, gain, w_qkv, query_grad, cosine, sine, residual_grad, own, *refs
):
    got, (kv_ref, input_ref, gain_ref, bias_ref) = refs[:-4], refs[-4:]
    rows = own[...].astype(f32)
    for piece in got:
        rows = rows + piece[...].astype(f32)
    for j in range(KVH):
        part = rows[:, head(j)]
        kv_ref[:, head(j)] = (part * cosine[...] - swap_halves(part) * sine[...]).astype(bf16)
    kv_ref[:, KVW:] = rows[:, KVW:].astype(bf16)
    kv_grad = kv_ref[...]
    q_grad = query_grad[...]
    bias_ref[:, :D] = jnp.sum(q_grad.astype(f32), axis=0, keepdims=True)
    bias_ref[:, D:] = jnp.sum(kv_grad.astype(f32), axis=0, keepdims=True)
    normed_grad = dot_transposed(q_grad, w_qkv[:, :D]) + dot_transposed(kv_grad, w_qkv[:, D:])
    inputs = tokens[...].astype(f32)
    scale = rms_scale(inputs)
    unit = inputs * scale
    gain_ref[...] = jnp.sum(normed_grad * unit, axis=0, keepdims=True)
    weighted = normed_grad * gain[...]
    input_ref[...] = residual_grad[...] + scale * (
        weighted - unit * jnp.mean(weighted * unit, axis=-1, keepdims=True)
    )


def input_back(tokens, gain, w_qkv, query_grad, cosine, sine, residual_grad, own, got):
    rows = tokens.shape[0]
    return kernel_call(
        input_kernel,
        "input_back",
        (
            shape_of((rows, 2 * KVW), bf16),
            shape_of((rows, D), f32),
            shape_of((1, D), f32),
            shape_of((1, D + 2 * KVW), f32),
        ),
        (tokens, gain, w_qkv, query_grad, cosine, sine, residual_grad, own, *got),
    )


def weight_grad_kernel(left, *refs):
    rights, outs = refs[: len(refs) // 2], refs[len(refs) // 2 :]
    turned = left[...].T
    for right, out in zip(rights, outs):
        out[...] = dot(turned, right[...]).astype(bf16)


def weight_grad_split_kernel(sides, left, *refs, inners):
    count = len(inners)
    rights, outs = refs[:count], refs[count:]
    turned = left[...].T
    for i, (right, inner) in enumerate(zip(rights, inners)):
        stays, goes = outs[2 * i], outs[2 * i + 1]
        rows = stays.shape[2]
        result = dot(turned, right[...]).astype(bf16)
        for side, refs_of in ((0, (stays, goes)), (1, (goes, stays))):

            @pl.when(sides[i] == side)
            def _():
                for o in range(stays.shape[0]):
                    for bit in range(2):
                        for j in range(inner):
                            block = (o * 2 + bit) * inner + j
                            refs_of[bit][o, j] = result[block * rows : (block + 1) * rows]


def weight_grad(left, rights, block=3 * HD):
    tokens, m = left.shape
    block = block if m % block == 0 else HD
    whole = pl.Buffered(buffer_count=1)
    return kernel_call(
        weight_grad_kernel,
        "weight_grad",
        tuple(shape_of((m, right.shape[1]), bf16) for right in rights),
        (left, *rights),
        megabytes=40,
        grid=(m // block,),
        in_specs=[pl.BlockSpec((tokens, block), lambda i: (0, i))]
        + [
            pl.BlockSpec(right.shape, lambda i: (0, 0), pipeline_mode=whole) for right in rights
        ],
        out_specs=tuple(
            pl.BlockSpec((block, right.shape[1]), lambda i: (i, 0)) for right in rights
        ),
    )


def weight_grad_split(left, rights, sides, inners, rows, block=3 * HD, part=(0, 1)):
    tokens, m = left.shape
    m = m // part[1]
    steps = m // block
    whole = pl.Buffered(buffer_count=1)
    out_shape, out_specs = [], []
    for right, inner in zip(rights, inners):
        n = right.shape[1]
        outer = block // (2 * inner * rows)
        for _ in range(2):
            out_shape.append(shape_of((steps * outer, inner, rows, n), bf16))
            out_specs.append(pl.BlockSpec((outer, inner, rows, n), lambda i: (i, 0, 0, 0)))
    outs = kernel_call(
        functools.partial(weight_grad_split_kernel, inners=inners),
        "weight_grad",
        tuple(out_shape),
        (sides, left, *rights),
        megabytes=44,
        grid=(steps,),
        in_specs=[smem, pl.BlockSpec((tokens, block), lambda i: (0, i + part[0] * steps))]
        + [
            pl.BlockSpec(right.shape, lambda i: (0, 0), pipeline_mode=whole) for right in rights
        ],
        out_specs=tuple(out_specs),
    )
    outs = [out.reshape((-1,) + out.shape[2:]) for out in outs]
    return [(outs[2 * i], outs[2 * i + 1]) for i in range(len(rights))]


def stack_kernel(*refs, cuts):
    pieces, outs = refs[: -len(cuts)], refs[-len(cuts) :]
    for i, piece in enumerate(pieces):
        for out, (lo, hi) in zip(outs, cuts):
            out[i] = piece[:, lo:hi]


def stack_columns(pieces, cuts):
    return kernel_call(
        functools.partial(stack_kernel, cuts=cuts),
        "stack_columns",
        tuple(shape_of((len(pieces), pieces[0].shape[0], hi - lo), bf16) for lo, hi in cuts),
        tuple(pieces),
    )


def cut_kernel(core, values, kept_ref, sent_ref, *, n_dp, own, padded):
    kept_ref[...] = jnp.zeros_like(kept_ref)
    sent_ref[...] = jnp.zeros_like(sent_ref)
    for side, refs in ((0, (kept_ref, sent_ref)), (1, (sent_ref, kept_ref))):

        @pl.when(core[0] == side)
        def _():
            for s in range(2 * kept_ref.shape[0]):
                for d in range(n_dp):
                    start = (s * n_dp + d) * own
                    refs[s % 2][s // 2, 0, :, d * padded : d * padded + own] = values[
                        0, :, start : start + own
                    ].astype(bf16)


def cut_hidden(values, core, n_chips, n_dp, padded):
    two, rows, ff = values.shape
    own = ff // (2 * n_chips * n_dp)
    dims = (n_chips, two, rows, n_dp * padded)
    return kernel_call(
        functools.partial(cut_kernel, n_dp=n_dp, own=own, padded=padded),
        "cut_hidden",
        (shape_of(dims, bf16),) * 2,
        (core, values),
        grid=(two,),
        in_specs=[smem, pl.BlockSpec((1, rows, ff), lambda g: (g, 0, 0))],
        out_specs=(pl.BlockSpec((n_chips, 1, rows, n_dp * padded), lambda g: (0, g, 0, 0)),) * 2,
    )


def turn_kernel(chip, *refs, n_chips, width):
    ins, outs = refs[: len(refs) - n_chips], refs[len(refs) - n_chips :]
    per_side = len(ins) // 2
    for t, out in enumerate(outs):
        at = lax.rem(chip[0] + t, n_chips)
        for side in range(2):
            parts = ins[side * per_side : (side + 1) * per_side]
            if per_side == 1:
                out[side] = parts[0][at]
                continue
            for half in range(2):
                for g in range(width):
                    part = parts[half * width + g]

                    @pl.when(at // part.shape[0] == half)
                    def _():
                        out[side, g] = part[lax.rem(at, part.shape[0])]


def turn_pairs(kept, got, chip, n_chips):
    rows, width = kept[0].shape[-2:]
    return kernel_call(
        functools.partial(turn_kernel, n_chips=n_chips, width=2),
        "turn_pairs",
        (shape_of((2, 2, rows, width), bf16),) * n_chips,
        (chip, *kept, *got),
        in_specs=[smem] + [vmem] * (len(kept) + len(got)),
    )


def add_kernel(*refs):
    *ins, out = refs
    total = ins[0][...].astype(f32)
    for ref in ins[1:]:
        total = total + ref[...].astype(f32)
    out[...] = total.astype(bf16)


def add(*arrays):
    return kernel_call(add_kernel, "add", shape_of(arrays[0].shape, bf16), arrays)


def add_turn_kernel(chip, kept, got, *outs):
    n = kept.shape[0]
    for t, out in enumerate(outs):
        at = lax.rem(chip[0] + t, n)
        out[...] = (kept[at].astype(f32) + got[at].astype(f32)).astype(bf16)


def add_turn(kept, got, chip):
    n = kept.shape[0]
    return kernel_call(
        add_turn_kernel,
        "add_turn",
        (shape_of(kept.shape[1:], bf16),) * n,
        (chip, kept, got),
        in_specs=[smem, vmem, vmem],
    )


def add_halve_kernel(mine, kept, got, stays, goes):
    for out, side in ((stays, mine[0]), (goes, 1 - mine[0])):
        for o in range(kept.shape[0]):
            out[o] = (kept[o, side].astype(f32) + got[o, side].astype(f32)).astype(bf16)


def add_halve(kept, got, mine, outer):
    blocks, rows, width = kept.shape
    dims = (outer, 2, blocks // (2 * outer), rows, width)
    half = (outer, blocks // (2 * outer), rows, width)
    stays, goes = kernel_call(
        add_halve_kernel,
        "add_halve",
        (shape_of(half, bf16),) * 2,
        (mine, kept.reshape(dims), got.reshape(dims)),
        in_specs=[smem, vmem, vmem],
        megabytes=40,
    )
    return stays.reshape(-1, rows, width), goes.reshape(-1, rows, width)


def adamw_update(master, moment_one, moment_two, gradient, step_rate, decay_weight):
    first_new = beta_one * moment_one + (1.0 - beta_one) * gradient
    second_new = beta_two * moment_two + (1.0 - beta_two) * gradient * gradient
    first_hat = first_new / (1.0 - beta_one**STEP)
    second_hat = second_new / (1.0 - beta_two**STEP)
    master_new = master - step_rate * (
        first_hat / (jnp.sqrt(second_hat) + adam_eps) + decay_weight * master
    )
    return (first_new, second_new, master_new)


def adamw_kernel(where, master, first, second, *refs, n_dp, own, padded, rate, decay):
    pieces, (first_ref, second_ref, master_ref, slots, joined) = refs[:-5], refs[-5:]
    for t, piece in enumerate(pieces):
        for o in range(2):
            slots[where[2 * t + o]] = piece[o, 0]
    for s in range(slots.shape[0]):
        for d in range(n_dp):
            start = (s * n_dp + d) * own
            joined[:, start : start + own] = slots[
                s, :, d * padded : d * padded + own
            ].astype(f32)
    first_ref[0], second_ref[0], master_ref[0] = adamw_update(
        master[0], first[0], second[0], joined[...], rate, decay
    )


def adamw_hidden(master, first, second, pieces, where, n_dp, padded, rate, decay):
    two, rows, ff = master.shape
    n_seq = 2 * len(pieces)
    own = ff // (n_seq * n_dp)
    block = pl.BlockSpec((1, rows, ff), lambda g: (g, 0, 0))
    part = pl.BlockSpec((2, 1, rows, n_dp * padded), lambda g: (0, g, 0, 0))
    return kernel_call(
        functools.partial(
            adamw_kernel, n_dp=n_dp, own=own, padded=padded, rate=rate, decay=decay
        ),
        "adamw_hidden",
        (shape_of(master.shape, f32),) * 3,
        (where, master, first, second, *pieces),
        megabytes=44,
        grid=(two,),
        in_specs=[smem] + [block] * 3 + [part] * len(pieces),
        out_specs=(block,) * 3,
        scratch_shapes=[
            pltpu.VMEM((n_seq, rows, n_dp * padded), bf16),
            pltpu.VMEM((rows, ff), f32),
        ],
    )


def assemble_kernel(where, *refs, splits, counts):
    ins, outs, sems = refs[: len(counts)], refs[len(counts) : -1], refs[-1]
    copies = []
    entry = 0
    for ref, (column, count) in zip(ins, counts):
        for i in range(count):
            for out, start, width in splits[column]:
                copies.append(
                    pltpu.make_async_copy(
                        ref.at[i, :, pl.ds(start, width)],
                        outs[out[0]].at[where[entry], :, pl.ds(out[1], width)],
                        sems.at[len(copies)],
                    )
                )
            entry += 1
    for copy in copies:
        copy.start()
    for copy in copies:
        copy.wait()


def assemble(pieces, where, splits, out_widths):
    counts = [(column, array.shape[0]) for array, column in pieces]
    rows = pieces[0][0].shape[1]
    blocks = sum(count for column, count in counts if column == 0)
    n_copies = sum(count * len(splits[column]) for column, count in counts)
    return kernel_call(
        functools.partial(assemble_kernel, splits=splits, counts=counts),
        "assemble",
        tuple(shape_of((blocks, rows, w), bf16) for w in out_widths),
        (where.astype(jnp.int32), *[array for array, _ in pieces]),
        in_specs=[smem] + [anywhere] * len(pieces),
        out_specs=(vmem,) * len(out_widths),
        scratch_shapes=[pltpu.SemaphoreType.DMA((n_copies,))],
    )


def seq_perm(values, chips, flip):
    count = lax.axis_size("seq")
    return lax.ppermute(
        values, "seq", [(i, ((i + 2 * chips) % count) ^ flip) for i in range(count)]
    )


def dp_perm(values, bit):
    return lax.ppermute(values, "dp", [(i, i ^ bit) for i in range(lax.axis_size("dp"))])


def dp_bits():
    return [1 << i for i in range(lax.axis_size("dp").bit_length() - 1)]


def pick(values, index, axis):
    return lax.dynamic_index_in_dim(values, index, axis, keepdims=False)


def places_of():
    n_chips = lax.axis_size("seq") // 2
    seq_at = lax.axis_index("seq")
    return n_chips, seq_at // 2, seq_at % 2, lax.axis_size("dp"), lax.axis_index("dp")


def swap(values):
    return seq_perm(values, 0, 1)


def sent_pieces(values):
    return [values] + [seq_perm(values, t, 0) for t in range(1, lax.axis_size("seq") // 2)]


def shards(
    tokens,
    cotangent,
    positions,
    qkv_master,
    qkv_first,
    qkv_second,
    out_master,
    out_first,
    out_second,
    gate_up_master,
    gate_up_first,
    gate_up_second,
    down_master,
    down_first,
    down_second,
    small_master,
    small_first,
    small_second,
):
    n_chips, chip_at, core_at, n_dp, dp_at = places_of()
    n_seq = 2 * n_chips
    n_all = n_seq * n_dp
    bits = dp_bits()
    rows_own, qkv_width = qkv_master.shape
    half = qkv_width // 2
    small_own = small_master.shape[0]
    ff_dev = down_master.shape[0]
    ff_pad = -(-ff_dev // 16) * 16
    ff_own = n_dp * ff_pad
    inputs = tokens[0]
    upstream = cotangent[0]
    tok_rows = inputs.shape[0]
    seq_length = positions.shape[1]
    shifts = list(range(1, n_chips))

    ring_chips = [(chip_at - t) % n_chips for t in range(n_chips)]
    ring_order = jnp.stack(
        [chip * 2 + (core_at ^ flip) for chip in ring_chips for flip in range(2)]
    ).astype(jnp.int32)
    bases = positions[0, ::PIECE].reshape(n_seq, tok_rows // PIECE)
    key_bases = jnp.take(bases, ring_order, axis=0)
    query_bases = key_bases[0]
    key_bases = key_bases.reshape(-1)
    own_places = lax.dynamic_slice_in_dim(
        positions[0], (chip_at * 2 + core_at) * tok_rows, tok_rows, 0
    )
    cosine, sine = rotary_tables(own_places)

    small_block = jnp.pad(
        small_master.astype(bf16), (0, rows_own * HD - small_own)
    ).reshape(rows_own, HD)
    packed = jnp.concatenate([small_block, qkv_master.astype(bf16)], axis=1)
    qkv_ring = sent_pieces(packed)
    core_side = core_at.reshape(1).astype(jnp.int32)
    chip_side = chip_at.reshape(1).astype(jnp.int32)
    bit_sides = {bit: ((dp_at // bit) % 2).reshape(1).astype(jnp.int32) for bit in bits}
    cut_kept, cut_sent = cut_hidden(gate_up_master, core_side, n_chips, n_dp, ff_pad)
    to_send = turn_pairs([cut_kept], [swap(cut_sent)], chip_side, n_chips)
    qkv_ring, to_send, cosine, sine = fence(qkv_ring, to_send, cosine, sine)

    def exchange(shift):
        return seq_perm(to_send[shift], shift, 0)

    w_out = lax.all_gather(
        after(out_master.astype(bf16), *to_send), ("seq", "dp"), axis=0, tiled=True
    )

    columns = ((0, HD + half), (HD + half, HD + qkv_width))
    orders = (bits, bits[::-1])
    held = list(stack_columns(qkv_ring, columns))
    flips = [[0], [0]]
    gate_up_pieces = {0: to_send[0]}
    groups = [shifts[:1], shifts[-1:], shifts[1:-1]] if n_chips > 2 else [shifts, [], []]
    for stage in range(len(bits)):
        got = [dp_perm(h, order[stage]) for h, order in zip(held, orders)]
        if stage == len(bits) - 1:
            swapped = [swap(h) for h in held]
        for shift in groups[min(stage, 1)] if stage < 2 else []:
            gate_up_pieces[shift] = exchange(shift)
        got, held, gate_up_pieces = fence(got, held, gate_up_pieces)
        flips = [f + [k ^ order[stage] for k in f] for f, order in zip(flips, orders)]
        if stage < len(bits) - 1:
            held = [jnp.concatenate([h, g], axis=0) for h, g in zip(held, got)]
    (swapped,) = fence(swapped)
    down_share = jnp.pad(down_master.astype(bf16), ((0, ff_pad - ff_dev), (0, 0)))
    w_down = lax.all_gather(after(down_share, *got), "dp", axis=0, tiled=True)
    for shift in groups[2]:
        gate_up_pieces[shift] = exchange(shift)
    got_swapped = [swap(g) for g in got]
    pieces, where = [], []
    for column in range(2):
        for flip, part, ks in (
            (0, held[column], flips[column][: n_dp // 2]),
            (0, got[column], flips[column][n_dp // 2 :]),
            (1, swapped[column], flips[column][: n_dp // 2]),
            (1, got_swapped[column], flips[column][n_dp // 2 :]),
        ):
            pieces.append((part, column))
            where += [
                (chip * 2 + (core_at ^ flip)) * n_dp + (dp_at ^ k) for k in ks for chip in ring_chips
            ]
    w_qkv, small_blocks = assemble(
        pieces,
        jnp.stack(where),
        ((((1, 0), 0, HD), ((0, 0), HD, half)), (((0, half), 0, half),)),
        (qkv_width, HD),
    )
    w_qkv = w_qkv.reshape(D, qkv_width)
    small_params = small_blocks.reshape(n_all, rows_own * HD)[:, :small_own].reshape(1, -1)
    small_params = small_params.astype(f32)
    gain_one = small_params[:, :D]
    gain_two = small_params[:, D : 2 * D]
    qkv_bias = small_params[:, 2 * D :]
    normed_one, key_value = project_kv(inputs, w_qkv, gain_one, qkv_bias, cosine, sine)
    gate_up_held = [
        jnp.concatenate([gate_up_pieces[t] for t in ts], axis=0)
        for ts in (range(n_chips // 2), range(n_chips // 2, n_chips))
    ]
    normed_one, key_value, gate_up_held = fence(normed_one, key_value, gate_up_held)

    kv_ring = sent_pieces(key_value)
    gate_up_parts = [
        [held, dp_perm(held, order[0])] for held, order in zip(gate_up_held, orders)
    ]
    gate_up_flips = [[0, order[0]] for order in orders]
    queries = project_q(normed_one, w_qkv, qkv_bias, cosine, sine)
    kv_swapped = [swap(kv_ring[0])] + [swap(after(piece, queries)) for piece in kv_ring[1:]]
    kv_ring, kv_swapped, gate_up_parts, queries, upstream = fence(
        kv_ring, kv_swapped, gate_up_parts, queries, upstream
    )

    def cross(start, stop, stage):
        for parts, flips_of, order in zip(gate_up_parts, gate_up_flips, orders):
            parts += [dp_perm(piece, order[stage]) for piece in parts[start:stop]]
            flips_of += [k ^ order[stage] for k in flips_of[start:stop]]

    upstream_ring = [upstream, seq_perm(upstream, 1, 0)]
    cross(0, 1 if len(bits) == 2 else 2, 1)
    attended, logsum, key_value_all = attend(
        queries, [piece for pair in zip(kv_ring, kv_swapped) for piece in pair], query_bases, key_bases
    )
    gate_up_parts, upstream_ring, attended, logsum, key_value_all = fence(
        gate_up_parts, upstream_ring, attended, logsum, key_value_all
    )

    def ring_step(pieces):
        return pieces + [seq_perm(pieces[-1], 1, 0)] if len(pieces) < n_chips else pieces

    upstream_ring = ring_step(upstream_ring)
    if len(bits) == 2:
        cross(1, 2, 1)
    else:
        cross(0, 4, 2)
    upstream_swapped = [swap(piece) for piece in upstream_ring[:2]]
    residual, normed_two, attended_low = out_project(inputs, attended, w_out, gain_two)
    normed_ring, normed_swapped = [normed_two], [swap(normed_two)]
    gate_up_parts, upstream_ring, upstream_swapped, normed_ring, normed_swapped, residual = fence(
        gate_up_parts, upstream_ring, upstream_swapped, normed_ring, normed_swapped, residual
    )

    pieces, where = [], []
    for column, (parts, flips_of) in enumerate(zip(gate_up_parts, gate_up_flips)):
        slots = ring_order[:n_chips] if column == 0 else ring_order[n_chips:]
        for part, k in zip(parts, flips_of):
            pieces.append((part.reshape(-1, rows_own, ff_own), 0))
            block = slots * n_dp + (dp_at ^ k)
            where.append(jnp.stack([block, n_all + block], axis=1).reshape(-1))
    (w_gate_up,) = assemble(
        pieces, jnp.concatenate(where), ((((0, 0), 0, ff_own),),), (ff_own,)
    )
    w_gate_up = w_gate_up.reshape(2, D, ff_own)
    out_parts, kept = [], ()
    running = None
    for slot in range(n_chips):
        sent = None if running is None else seq_perm(running, 1, 0)
        normed_ring = ring_step(normed_ring)
        upstream_ring = ring_step(upstream_ring)
        out_own, out_other, grad_own, grad_other, *kept = feed_forward(
            (normed_ring[slot], normed_swapped[slot]),
            (upstream_ring[slot], upstream_swapped[slot]),
            w_gate_up,
            w_down,
            slot,
            n_chips,
            kept,
        )
        out_parts.append((out_own, out_other))
        grad_swapped = swap(grad_other)
        if slot + 1 < n_chips:
            normed_swapped = normed_swapped + [swap(after(normed_ring[slot + 1], grad_own))]
        if slot + 2 < n_chips and len(upstream_swapped) < slot + 3:
            upstream_swapped = upstream_swapped + [swap(after(upstream_ring[slot + 2], grad_own))]
        if slot == 0:
            grad_first = (grad_own, grad_swapped)
        elif sent is None:
            running = add(grad_own, grad_swapped)
        else:
            running = add(grad_own, grad_swapped, after(sent, grad_own))
        running, normed_ring, normed_swapped, upstream_ring, upstream_swapped, out_parts, kept = fence(
            running, normed_ring, normed_swapped, upstream_ring, upstream_swapped, out_parts, kept
        )

    grad_ring = jnp.zeros_like(grad_first[0]) if running is None else seq_perm(running, 1, 0)
    normed_all, ffn_all, hidden_all, gate_grads_all, up_grads_all = (
        entry.reshape(seq_length, -1) for entry in kept
    )
    first_inner = [first_bit for first_bit in (orders[0][0], orders[1][0])]
    first_sides = jnp.concatenate([bit_sides[order[0]] for order in orders])
    halves = [
        weight_grad_split(
            normed_all,
            (gate_grads_all, up_grads_all),
            first_sides,
            first_inner,
            rows_own,
            part=(part, 2),
        )
        for part in range(2)
    ]
    out_pairs = [(own, swap(other)) for own, other in out_parts]
    out_total = [add(own, other) for own, other in out_pairs[1:]]
    grad_ring, halves, out_pairs, out_total, hidden_all, ffn_all = fence(
        grad_ring, halves, out_pairs, out_total, hidden_all, ffn_all
    )

    got_one = [dp_perm(goes, order[0]) for (_, goes), order in zip(halves[0], orders)]
    out_running = seq_perm(out_total[0], 1, 0) if n_chips > 1 else None
    residual_grads, branch_grads, attended_grads, gain_two_grad = norm_back(
        grad_ring, *grad_first, residual, upstream, gain_two, w_out
    )
    query_pre, kv_grad_own, kv_grad_other = attend_back(
        queries,
        key_value_all,
        attended_grads,
        attended,
        logsum,
        query_bases,
        key_bases,
        cosine,
        sine,
    )
    got_one, kv_grad_own, kv_grad_other, query_pre, branch_grads, out_running = fence(
        got_one, kv_grad_own, kv_grad_other, query_pre, branch_grads, out_running
    )
    own_parts = kv_grad_own.reshape(n_chips, tok_rows, 2 * KVW)
    other_parts = swap(kv_grad_other).reshape(n_chips, tok_rows, 2 * KVW)
    kv_sum = add_turn(own_parts, other_parts, jnp.zeros_like(chip_side))
    kv_sum, halves, hidden_all, ffn_all, query_pre, branch_grads = fence(
        kv_sum, halves, hidden_all, ffn_all, query_pre, branch_grads
    )

    def next_split(kept_part, got, done_bits, left_bits):
        rest = [bit for bit in bits[::-1] if bit not in done_bits]
        bit = left_bits[0]
        lead = kept_part.shape[0] // 2 ** len(rest)
        return add_halve(kept_part, got, bit_sides[bit], lead * 2 ** rest.index(bit))

    kv_got = [seq_perm(kv_sum[t], n_chips - t, 0) for t in range(1, n_chips)]
    got_two = [dp_perm(goes, order[0]) for (_, goes), order in zip(halves[1], orders)]
    split_one = [
        next_split(stays, got, order[:1], order[1:])
        for (stays, _), got, order in zip(halves[0], got_one, orders)
    ]
    got_one = [dp_perm(goes, order[1]) for (_, goes), order in zip(split_one, orders)]
    (query_split,) = weight_grad_split(
        normed_one, (query_pre,), core_side, [n_dp], rows_own
    )
    (out_split,) = weight_grad_split(
        attended_low, (branch_grads,), core_side, [n_dp], rows_own
    )
    (down_grad,) = weight_grad(hidden_all, (ffn_all,))
    kv_got, got_two, got_one, query_split, out_split, down_grad = fence(
        kv_got, got_two, got_one, query_split, out_split, down_grad
    )
    down_owned = lax.psum_scatter(down_grad, "dp", scatter_dimension=0, tiled=True)
    down_owned = down_owned[:ff_dev].astype(f32)

    def finish(split, got, order):
        kept_part = split[0]
        for i in range(2, len(order)):
            kept_part, goes = next_split(kept_part, got, order[:i], order[i:])
            got = dp_perm(goes, order[i])
        return kept_part, got

    if n_chips > 2:
        out_running = seq_perm(add(out_running, out_total[1]), 1, 0)
    split_two = [
        next_split(stays, got, order[:1], order[1:])
        for (stays, _), got, order in zip(halves[1], got_two, orders)
    ]
    got_two = [dp_perm(goes, order[1]) for (_, goes), order in zip(split_two, orders)]
    both = [(split[0], swap(split[1])) for split in (query_split, out_split)]
    key_value_pre, input_grads, gain_one_grad, bias_grad = input_back(
        inputs,
        gain_one,
        w_qkv,
        query_pre,
        cosine,
        sine,
        residual_grads,
        kv_sum[0],
        kv_got,
    )
    ((kv_stays, kv_goes),) = weight_grad_split(
        normed_one, (key_value_pre,), core_side, [n_dp], rows_own
    )
    split_two, got_two, both, input_grads, kv_stays, kv_goes, out_running, small_parts = fence(
        split_two,
        got_two,
        both,
        input_grads,
        kv_stays,
        kv_goes,
        out_running,
        (gain_one_grad, gain_two_grad, bias_grad),
    )

    both = [
        next_split(kept_part, got, [], order) for (kept_part, got), order in zip(both, orders)
    ]
    both_got = [dp_perm(goes, order[0]) for (_, goes), order in zip(both, orders)]
    ready = [finish(split, got, order) for split, got, order in zip(split_one, got_one, orders)]
    ready += [finish(split, got, order) for split, got, order in zip(split_two, got_two, orders)]
    ready = [
        add_halve(kept_part, got, core_side, kept_part.shape[0] // 2) for kept_part, got in ready
    ]
    to_send = turn_pairs(
        [kept_part for kept_part, _ in ready],
        [swap(sent) for _, sent in ready],
        chip_side,
        n_chips,
    )
    small_grad = jnp.concatenate(small_parts, axis=1).astype(bf16)
    small_grad = jnp.pad(
        small_grad.reshape(n_all, small_own), ((0, 0), (0, rows_own * HD - small_own))
    ).reshape(n_chips, 2, n_dp, rows_own, HD)
    kv_stays = jnp.concatenate(
        [pick(small_grad, core_at, 1).reshape(-1, rows_own, HD), kv_stays], axis=2
    )
    kv_goes = jnp.concatenate(
        [pick(small_grad, 1 - core_at, 1).reshape(-1, rows_own, HD), kv_goes], axis=2
    )
    kv_side = (kv_stays, swap(kv_goes))
    to_send, both, both_got, kv_side = fence(to_send, both, both_got, kv_side)

    gate_up_owned = {0: to_send[0]}
    for shift in groups[0] + groups[1] + groups[2]:
        gate_up_owned[shift] = exchange(shift)
    kv_split = next_split(*kv_side, [], orders[0])
    three = [(both[0], both_got[0], orders[0]), (both[1], both_got[1], orders[1])]
    three.append((kv_split, dp_perm(kv_split[1], orders[0][0]), orders[0]))
    rest_send = []
    for (kept_part, _), got, order in three:
        for i in range(1, len(order)):
            kept_part, goes = next_split(kept_part, got, order[:i], order[i:])
            got = dp_perm(goes, order[i])
        rest_send.append(add_turn(kept_part, got, chip_side))
    if n_chips > 3:
        out_running = add(out_running, out_total[2])
    gate_up_owned, rest_send, out_running = fence(gate_up_owned, rest_send, out_running)

    rest_send = [
        jnp.concatenate([parts[t] for parts in rest_send], axis=1) for t in range(n_chips)
    ]
    total = rest_send[0].astype(f32)
    for shift in shifts:
        total = total + seq_perm(rest_send[shift], shift, 0).astype(f32)
    for t in range(3, n_chips):
        if t > 3:
            out_running = add(out_running, out_total[t - 1])
        out_running = seq_perm(out_running, 1, 0)
    outputs = residual + out_pairs[0][0].astype(f32) + out_pairs[0][1].astype(f32)
    if n_chips > 1:
        outputs = outputs + out_running.astype(f32)
    outputs = outputs.astype(bf16)
    gate_up_new = adamw_hidden(
        gate_up_master,
        gate_up_first,
        gate_up_second,
        [gate_up_owned[t] for t in range(n_chips)],
        ring_order,
        n_dp,
        ff_pad,
        0.064,
        0.1,
    )
    query_owned, out_owned, small_owned, kv_owned = jnp.split(
        total, (D, 2 * D, 2 * D + HD), axis=1
    )
    qkv_owned = jnp.concatenate([query_owned, kv_owned], axis=1)
    small_owned = small_owned.reshape(-1)[:small_own]

    qkv_new = adamw_update(qkv_master, qkv_first, qkv_second, qkv_owned, 0.09, 0.1)
    out_new = adamw_update(out_master, out_first, out_second, out_owned, 0.18, 0.1)
    down_new = adamw_update(down_master, down_first, down_second, down_owned, 0.026, 0.1)
    small_new = adamw_update(small_master, small_first, small_second, small_owned, 0.6, 0.0)
    return (
        outputs[None],
        input_grads[None],
        *qkv_new,
        *out_new,
        *gate_up_new,
        *down_new,
        *small_new,
    )


def solution(mesh):
    in_specs = (
        P("dp", "seq", None),
        P("dp", "seq", None),
        P("dp", None),
        P(("seq", "dp"), None),
        P(("seq", "dp"), None),
        P(("seq", "dp"), None),
        P(("seq", "dp"), None),
        P(("seq", "dp"), None),
        P(("seq", "dp"), None),
        P(None, ("seq", "dp"), None),
        P(None, ("seq", "dp"), None),
        P(None, ("seq", "dp"), None),
        P(("seq", "dp"), None),
        P(("seq", "dp"), None),
        P(("seq", "dp"), None),
        P(("seq", "dp")),
        P(("seq", "dp")),
        P(("seq", "dp")),
    )
    out_specs = (
        P("dp", "seq", None),
        P("dp", "seq", None),
        P(("seq", "dp"), None),
        P(("seq", "dp"), None),
        P(("seq", "dp"), None),
        P(("seq", "dp"), None),
        P(("seq", "dp"), None),
        P(("seq", "dp"), None),
        P(None, ("seq", "dp"), None),
        P(None, ("seq", "dp"), None),
        P(None, ("seq", "dp"), None),
        P(("seq", "dp"), None),
        P(("seq", "dp"), None),
        P(("seq", "dp"), None),
        P(("seq", "dp")),
        P(("seq", "dp")),
        P(("seq", "dp")),
    )
    return jax.shard_map(shards, mesh=mesh, in_specs=in_specs, out_specs=out_specs, check_vma=False)
```

```python
import functools

import jax
import jax.numpy as jnp
from jax import lax
from jax.experimental import pallas as pl
from jax.experimental.pallas import tpu as pltpu
from jax.sharding import PartitionSpec as P

D = 1536
HEADS = 12
KVH = 2
HD = 128
STEP = 10
KVW = KVH * HD
PIECE = 128


norm_eps = 1e-06
rope_base = 1000000.0
beta_one = 0.9
beta_two = 0.95
adam_eps = 1e-08
masked_score = -1e30
log2_e = 1.4426950408889634
bf16 = jnp.bfloat16
f32 = jnp.float32
vmem = pl.BlockSpec(memory_space=pltpu.VMEM)
smem = pl.BlockSpec(memory_space=pltpu.SMEM)
anywhere = pl.BlockSpec(memory_space=pl.ANY)


def shape_of(dims, kind):
    return jax.ShapeDtypeStruct(dims, kind)


def kernel_call(kernel, name, out_shape, operands, megabytes=32, **options):
    return pl.pallas_call(
        kernel,
        name=name,
        out_shape=out_shape,
        compiler_params=pltpu.CompilerParams(vmem_limit_bytes=megabytes << 20),
        cost_estimate=pl.CostEstimate(flops=10**6, bytes_accessed=10**6, transcendentals=0),
        **options,
    )(*operands)


def after(values, *others):
    return lax.optimization_barrier((values,) + others)[0]


def fence(*groups):
    flat, tree = jax.tree.flatten(groups)
    return jax.tree.unflatten(tree, lax.optimization_barrier(tuple(flat)))


def dot(left, right):
    return jnp.dot(left, right, preferred_element_type=f32)


def dot_transposed(left, right):
    return lax.dot_general(left, right, (((1,), (1,)), ((), ())), preferred_element_type=f32)


def rotary_tables(places):
    half_size = HD // 2
    freqs = rope_base ** (-(jnp.arange(half_size).astype(f32) * (2.0 / HD)))
    angles = places.astype(f32)[:, None] * freqs[None, :]
    cosine, sine = jnp.cos(angles), jnp.sin(angles)
    return jnp.concatenate([cosine, cosine], axis=1), jnp.concatenate([-sine, sine], axis=1)


def rms_scale(values):
    return lax.rsqrt(jnp.mean(values * values, axis=-1, keepdims=True) + norm_eps)


def swap_halves(values):
    return pltpu.roll(values, HD // 2, 1)


def head(index):
    return slice(index * HD, (index + 1) * HD)


def project_kv_kernel(tokens, w_qkv, gain, bias, cosine, sine, normed_ref, kv_ref):
    inputs = tokens[...].astype(f32)
    normed = (inputs * rms_scale(inputs) * gain[...]).astype(bf16)
    normed_ref[...] = normed
    rows = dot(normed, w_qkv[:, D:]) + bias[:, D:]
    for j in range(KVH):
        part = rows[:, head(j)]
        kv_ref[:, head(j)] = (part * cosine[...] + swap_halves(part) * sine[...]).astype(bf16)
    kv_ref[:, KVW:] = rows[:, KVW:].astype(bf16)


def project_q_kernel(normed, w_qkv, bias, cosine, sine, query_ref):
    rows = dot(normed[...], w_qkv[:, :D]) + bias[:, :D]
    for j in range(HEADS):
        part = rows[:, head(j)]
        query_ref[:, head(j)] = (part * cosine[...] + swap_halves(part) * sine[...]).astype(bf16)


def project_kv(tokens, w_qkv, gain, bias, cosine, sine):
    rows = tokens.shape[0]
    return kernel_call(
        project_kv_kernel,
        "project_kv",
        (shape_of((rows, D), bf16), shape_of((rows, 2 * KVW), bf16)),
        (tokens, w_qkv, gain, bias, cosine, sine),
    )


def project_q(normed, w_qkv, bias, cosine, sine):
    return kernel_call(
        project_q_kernel,
        "project_q",
        shape_of(normed.shape, bf16),
        (normed, w_qkv, bias, cosine, sine),
    )


def mask_keys(values, query_bases, key_bases, first_run, fill):
    later = lax.broadcasted_iota(jnp.int32, (PIECE, PIECE), 0) - lax.broadcasted_iota(
        jnp.int32, (PIECE, PIECE), 1
    )
    keys, queries = values.shape
    rows = []
    for r in range(keys // PIECE):
        down = slice(r * PIECE, (r + 1) * PIECE)
        row = []
        for q in range(queries // PIECE):
            gap = query_bases[q] - key_bases[first_run + r]
            row.append(jnp.where(later <= gap, values[down, q * PIECE : (q + 1) * PIECE], fill))
        rows.append(jnp.concatenate(row, axis=1))
    return jnp.concatenate(rows, axis=0)


def attend_kernel(query_bases, key_bases, q_ref, *refs):
    pieces, (out_ref, lse_ref, kv_ref) = refs[:-3], refs[-3:]
    rows = q_ref.shape[0]
    for i, piece in enumerate(pieces):
        kv_ref[i * rows : (i + 1) * rows, :] = piece[...]
    groups = HEADS // KVH
    scale = HD**-0.5 * log2_e
    for kv in range(KVH):
        values = kv_ref[:, head(KVH + kv)].T
        for h in range(kv * groups, (kv + 1) * groups):
            queries = q_ref[:, head(h)]
            scores = []
            for run in range(key_bases.shape[0]):
                keys = kv_ref[run * PIECE : (run + 1) * PIECE, head(kv)]
                part = dot_transposed(keys, queries)
                scores.append(mask_keys(part, query_bases, key_bases, run, masked_score))
            scores = jnp.concatenate(scores, axis=0)
            top = jnp.max(scores, axis=0, keepdims=True)
            weights = jnp.exp2((scores - top) * scale)
            total = jnp.sum(weights, axis=0, keepdims=True)
            mixed = dot(values, weights.astype(bf16))
            out_ref[:, head(h)] = (mixed / total).T
            lse_ref[h : h + 1, :] = top * scale + jnp.log2(total)


def attend(queries, pieces, query_bases, key_bases):
    rows, total = queries.shape[0], key_bases.shape[0] * PIECE
    return kernel_call(
        attend_kernel,
        "attend",
        (
            shape_of((rows, D), f32),
            shape_of((HEADS, rows), f32),
            shape_of((total, 2 * KVW), bf16),
        ),
        (query_bases, key_bases, queries, *pieces),
        in_specs=[smem] * 2 + [vmem] * (1 + len(pieces)),
    )


def out_kernel(tokens, attended, w_out, gain, residual_ref, normed_ref, low_ref):
    low = attended[...].astype(bf16)
    low_ref[...] = low
    residual = tokens[...].astype(f32) + dot(low, w_out[...])
    residual_ref[...] = residual
    normed_ref[...] = (residual * rms_scale(residual) * gain[...]).astype(bf16)


def out_project(tokens, attended, w_out, gain):
    dims = tokens.shape
    return kernel_call(
        out_kernel,
        "out_project",
        (shape_of(dims, f32), shape_of(dims, bf16), shape_of(dims, bf16)),
        (tokens, attended, w_out, gain),
    )


def ffn_kernel(
    normed_own, normed_other, grad_own, grad_other, w_gate_up, w_down, *refs, earlier
):
    refs = refs[earlier:]
    out_refs, grad_refs = refs[:2], refs[2:4]
    normed_ref, ffn_grad_ref, hidden_ref, gate_ref, up_ref = refs[4:]
    rows = normed_own.shape[0]
    for i, (normed_in, grad_in) in enumerate(((normed_own, grad_own), (normed_other, grad_other))):
        to = slice(i * rows, (i + 1) * rows)
        normed, ffn_grad = normed_in[...], grad_in[...]
        normed_ref[0, to, :] = normed
        ffn_grad_ref[0, to, :] = ffn_grad
        gate = dot(normed, w_gate_up[0])
        up = dot(normed, w_gate_up[1])
        sigmoid = 1.0 / (1.0 + jnp.exp(-gate))
        silu = gate * sigmoid
        hidden = (silu * up).astype(bf16)
        hidden_ref[0, to, :] = hidden
        out_refs[i][...] = dot(hidden, w_down[...]).astype(bf16)
        hidden_grad = dot_transposed(ffn_grad, w_down[...])
        gate_grad = (hidden_grad * up * sigmoid * (1.0 + gate * (1.0 - sigmoid))).astype(bf16)
        up_grad = (hidden_grad * silu).astype(bf16)
        gate_ref[0, to, :] = gate_grad
        up_ref[0, to, :] = up_grad
        grad_refs[i][...] = (
            dot_transposed(gate_grad, w_gate_up[0]) + dot_transposed(up_grad, w_gate_up[1])
        ).astype(bf16)


def feed_forward(normed, grads, w_gate_up, w_down, slot, slots, kept):
    rows, width = normed[0].shape
    ff_own = w_down.shape[0]
    token = shape_of((rows, width), bf16)
    widths = (width, width, ff_own, ff_own, ff_own)
    operands = (*normed, *grads, w_gate_up, w_down)
    return kernel_call(
        functools.partial(ffn_kernel, earlier=len(kept)),
        "feed_forward",
        (token,) * 4 + tuple(shape_of((slots, 2 * rows, w), bf16) for w in widths),
        (*operands, *kept),
        grid=(1,),
        in_specs=[vmem] * len(operands) + [anywhere] * len(kept),
        out_specs=(vmem,) * 4
        + tuple(pl.BlockSpec((1, 2 * rows, w), lambda i: (slot, 0, 0)) for w in widths),
        input_output_aliases={len(operands) + i: 4 + i for i in range(len(kept))},
    )


def norm_back_kernel(
    got, own, other, residual_ref, cotangent, gain, w_out, grad_ref, low_ref, back_ref, gain_ref
):
    normed_grad = got[...].astype(f32) + own[...].astype(f32) + other[...].astype(f32)
    residual = residual_ref[...]
    scale = rms_scale(residual)
    unit = residual * scale
    gain_ref[...] = jnp.sum(normed_grad * unit, axis=0, keepdims=True)
    weighted = normed_grad * gain[...]
    grad = cotangent[...].astype(f32) + scale * (
        weighted - unit * jnp.mean(weighted * unit, axis=-1, keepdims=True)
    )
    grad_ref[...] = grad
    low = grad.astype(bf16)
    low_ref[...] = low
    back_ref[...] = dot_transposed(low, w_out[...]).astype(bf16)


def norm_back(got, own, other, residual, cotangent, gain, w_out):
    dims = residual.shape
    return kernel_call(
        norm_back_kernel,
        "norm_back",
        (shape_of(dims, f32), shape_of(dims, bf16), shape_of(dims, bf16), shape_of((1, D), f32)),
        (got, own, other, residual, cotangent, gain, w_out),
    )


def attend_back_kernel(
    query_bases,
    key_bases,
    q_ref,
    kv_ref,
    grad_ref,
    out_ref,
    lse_ref,
    cosine,
    sine,
    q_grad_ref,
    kv_own_ref,
    kv_other_ref,
    q_rows,
    grad_rows,
    deltas,
    q_sums,
):
    rows = q_ref.shape[0]
    groups = HEADS // KVH
    scale = HD**-0.5
    for kv in range(KVH):
        for j in range(groups):
            part = slice(j * rows, (j + 1) * rows)
            columns = head(kv * groups + j)
            q_rows[part, :] = q_ref[:, columns]
            grads = grad_ref[:, columns]
            grad_rows[part, :] = grads
            product = grads.astype(f32) * out_ref[:, columns]
            deltas[:, part] = jnp.sum(product.T, axis=0, keepdims=True)
        q_sums[...] = jnp.zeros_like(q_sums)

        @pl.loop(0, kv_ref.shape[0] // (2 * rows), unroll=2)
        def _(step):
            at = pl.ds(pl.multiple_of(step * (2 * rows), 2 * rows), 2 * rows)
            runs = 2 * rows // PIECE
            keys = kv_ref[at, head(kv)]
            values = kv_ref[at, head(KVH + kv)]
            key_sum = value_sum = None
            for j in range(groups):
                part = slice(j * rows, (j + 1) * rows)
                h = kv * groups + j
                queries, grads = q_rows[part, :], grad_rows[part, :]
                scores = dot_transposed(keys, queries)
                weights = jnp.exp2(scores * (scale * log2_e) - lse_ref[h : h + 1, :])
                weights = mask_keys(weights, query_bases, key_bases, step * runs, 0.0)
                weight_grads = dot_transposed(values, grads)
                score_grads = (weights * (weight_grads - deltas[:, part])).astype(bf16)
                value_part = dot(weights.astype(bf16), grads)
                key_part = dot(score_grads, queries)
                key_sum = key_part if key_sum is None else key_sum + key_part
                value_sum = value_part if value_sum is None else value_sum + value_part
                q_sums[part, :] += lax.dot_general(
                    score_grads, keys, (((0,), (0,)), ((), ())), preferred_element_type=f32
                )
            key_sum = (key_sum * scale).astype(bf16)
            value_sum = value_sum.astype(bf16)
            to = pl.ds(pl.multiple_of(step * rows, rows), rows)
            for ref, mine in ((kv_own_ref, slice(0, rows)), (kv_other_ref, slice(rows, 2 * rows))):
                ref[to, head(kv)] = key_sum[mine, :]
                ref[to, head(KVH + kv)] = value_sum[mine, :]

        for j in range(groups):
            part = q_sums[j * rows : (j + 1) * rows, :] * scale
            q_grad_ref[:, head(kv * groups + j)] = (
                part * cosine[...] - swap_halves(part) * sine[...]
            ).astype(bf16)


def attend_back(queries, key_value, grads, attended, lse, query_bases, key_bases, cosine, sine):
    rows, total = queries.shape[0], key_value.shape[0]
    groups = HEADS // KVH
    return kernel_call(
        attend_back_kernel,
        "attend_back",
        (
            shape_of((rows, D), bf16),
            shape_of((total // 2, 2 * KVW), bf16),
            shape_of((total // 2, 2 * KVW), bf16),
        ),
        (query_bases, key_bases, queries, key_value, grads, attended, lse, cosine, sine),
        in_specs=[smem] * 2 + [vmem] * 7,
        scratch_shapes=[
            pltpu.VMEM((groups * rows, HD), bf16),
            pltpu.VMEM((groups * rows, HD), bf16),
            pltpu.VMEM((1, groups * rows), f32),
            pltpu.VMEM((groups * rows, HD), f32),
        ],
    )


def input_kernel(
    tokens, gain, w_qkv, query_grad, cosine, sine, residual_grad, own, *refs
):
    got, (kv_ref, input_ref, gain_ref, bias_ref) = refs[:-4], refs[-4:]
    rows = own[...].astype(f32)
    for piece in got:
        rows = rows + piece[...].astype(f32)
    for j in range(KVH):
        part = rows[:, head(j)]
        kv_ref[:, head(j)] = (part * cosine[...] - swap_halves(part) * sine[...]).astype(bf16)
    kv_ref[:, KVW:] = rows[:, KVW:].astype(bf16)
    kv_grad = kv_ref[...]
    q_grad = query_grad[...]
    bias_ref[:, :D] = jnp.sum(q_grad.astype(f32), axis=0, keepdims=True)
    bias_ref[:, D:] = jnp.sum(kv_grad.astype(f32), axis=0, keepdims=True)
    normed_grad = dot_transposed(q_grad, w_qkv[:, :D]) + dot_transposed(kv_grad, w_qkv[:, D:])
    inputs = tokens[...].astype(f32)
    scale = rms_scale(inputs)
    unit = inputs * scale
    gain_ref[...] = jnp.sum(normed_grad * unit, axis=0, keepdims=True)
    weighted = normed_grad * gain[...]
    input_ref[...] = residual_grad[...] + scale * (
        weighted - unit * jnp.mean(weighted * unit, axis=-1, keepdims=True)
    )


def input_back(tokens, gain, w_qkv, query_grad, cosine, sine, residual_grad, own, got):
    rows = tokens.shape[0]
    return kernel_call(
        input_kernel,
        "input_back",
        (
            shape_of((rows, 2 * KVW), bf16),
            shape_of((rows, D), f32),
            shape_of((1, D), f32),
            shape_of((1, D + 2 * KVW), f32),
        ),
        (tokens, gain, w_qkv, query_grad, cosine, sine, residual_grad, own, *got),
        megabytes=58,
    )


def weight_grad_kernel(sides, left, *refs, count, inners, based):
    rights, refs = refs[:count], refs[count:]
    bases, outs = refs[: count * based], refs[count * based :]
    turned = left[...].reshape(-1, left.shape[-1]).T
    for i, right in enumerate(rights):
        result = dot(turned, right[...].reshape(-1, right.shape[-1]))
        if based:
            result = result + bases[i][...]
        if not inners:
            outs[i][...] = result.astype(outs[i].dtype)
            continue
        stays, goes = outs[2 * i], outs[2 * i + 1]
        rows = stays.shape[2]
        result = result.astype(bf16)
        for side, refs_of in ((0, (stays, goes)), (1, (goes, stays))):

            @pl.when(sides[i] == side)
            def _():
                for o in range(stays.shape[0]):
                    for bit in range(2):
                        for j in range(inners[i]):
                            block = (o * 2 + bit) * inners[i] + j
                            refs_of[bit][o, j] = result[block * rows : (block + 1) * rows]


def weight_grad(
    left, rights, slots=(0, 1), bases=(), split=None, rows=0, part=(0, 1), kind=bf16
):
    n_slots, tokens, m = left.shape
    n_slots = n_slots // slots[1]
    m = m // part[1]
    block = 3 * HD if m % (3 * HD) == 0 else HD
    steps = m // block
    first = part[0] * steps
    whole = pl.Buffered(buffer_count=1)
    sides, inners = split if split else (jnp.zeros((1,), jnp.int32), ())
    out_shape, out_specs = [], []
    for i, right in enumerate(rights):
        n = right.shape[-1]
        if not inners:
            out_shape.append(shape_of((m, n), kind))
            out_specs.append(pl.BlockSpec((block, n), lambda i: (i, 0)))
            continue
        outer = block // (2 * inners[i] * rows)
        for _ in range(2):
            out_shape.append(shape_of((steps * outer, inners[i], rows, n), bf16))
            out_specs.append(pl.BlockSpec((outer, inners[i], rows, n), lambda i: (i, 0, 0, 0)))
    outs = kernel_call(
        functools.partial(
            weight_grad_kernel, count=len(rights), inners=inners, based=int(bool(bases))
        ),
        "weight_grad",
        tuple(out_shape),
        (sides, left, *rights, *bases),
        megabytes=44,
        grid=(steps,),
        in_specs=[
            smem,
            pl.BlockSpec((n_slots, tokens, block), lambda i: (slots[0], 0, i + first)),
        ]
        + [
            pl.BlockSpec(
                (n_slots, tokens, right.shape[-1]),
                lambda i: (slots[0], 0, 0),
                pipeline_mode=whole,
            )
            for right in rights
        ]
        + [pl.BlockSpec((block, base.shape[1]), lambda i: (i + first, 0)) for base in bases],
        out_specs=tuple(out_specs),
    )
    if not inners:
        return outs
    outs = [out.reshape((-1,) + out.shape[2:]) for out in outs]
    return [(outs[2 * i], outs[2 * i + 1]) for i in range(len(rights))]


def stack_kernel(*refs, cuts):
    pieces, outs = refs[: -len(cuts)], refs[-len(cuts) :]
    for i, piece in enumerate(pieces):
        for out, (lo, hi) in zip(outs, cuts):
            out[i] = piece[:, lo:hi]


def stack_columns(pieces, cuts):
    return kernel_call(
        functools.partial(stack_kernel, cuts=cuts),
        "stack_columns",
        tuple(shape_of((len(pieces), pieces[0].shape[0], hi - lo), bf16) for lo, hi in cuts),
        tuple(pieces),
    )


def cut_kernel(core, values, kept_ref, sent_ref, *, n_dp, own, padded):
    kept_ref[...] = jnp.zeros_like(kept_ref)
    sent_ref[...] = jnp.zeros_like(sent_ref)
    for side, refs in ((0, (kept_ref, sent_ref)), (1, (sent_ref, kept_ref))):

        @pl.when(core[0] == side)
        def _():
            for s in range(2 * kept_ref.shape[0]):
                for d in range(n_dp):
                    start = (s * n_dp + d) * own
                    refs[s % 2][s // 2, 0, :, d * padded : d * padded + own] = values[
                        0, :, start : start + own
                    ].astype(bf16)


def cut_hidden(values, core, n_chips, n_dp, padded):
    two, rows, ff = values.shape
    own = ff // (2 * n_chips * n_dp)
    dims = (n_chips, two, rows, n_dp * padded)
    return kernel_call(
        functools.partial(cut_kernel, n_dp=n_dp, own=own, padded=padded),
        "cut_hidden",
        (shape_of(dims, bf16),) * 2,
        (core, values),
        grid=(two,),
        in_specs=[smem, pl.BlockSpec((1, rows, ff), lambda g: (g, 0, 0))],
        out_specs=(pl.BlockSpec((n_chips, 1, rows, n_dp * padded), lambda g: (0, g, 0, 0)),) * 2,
    )


def turn_kernel(chip, *refs, n_chips):
    ins, outs = refs[: len(refs) - n_chips], refs[len(refs) - n_chips :]
    per_side = len(ins) // 2
    for t, out in enumerate(outs):
        at = lax.rem(chip[0] + t, n_chips)
        for side in range(2):
            if per_side == 1:
                out[side] = ins[side][at]
            else:
                for g in range(2):
                    out[side, g] = ins[2 * side + g][at]


def turn_pairs(kept, got, chip, n_chips):
    rows, width = kept[0].shape[-2:]
    return kernel_call(
        functools.partial(turn_kernel, n_chips=n_chips),
        "turn_pairs",
        (shape_of((2, 2, rows, width), bf16),) * n_chips,
        (chip, *kept, *got),
        in_specs=[smem] + [vmem] * (len(kept) + len(got)),
    )


def add_kernel(*refs):
    *ins, out = refs
    total = ins[0][...].astype(f32)
    for ref in ins[1:]:
        total = total + ref[...].astype(f32)
    out[...] = total.astype(bf16)


def add(*arrays):
    return kernel_call(add_kernel, "add", shape_of(arrays[0].shape, bf16), arrays)


def add_turn_kernel(chip, kept, got, *outs):
    n = kept.shape[0]
    for t, out in enumerate(outs):
        at = lax.rem(chip[0] + t, n)
        out[...] = (kept[at].astype(f32) + got[at].astype(f32)).astype(bf16)


def add_turn(kept, got, chip):
    n = kept.shape[0]
    return kernel_call(
        add_turn_kernel,
        "add_turn",
        (shape_of(kept.shape[1:], bf16),) * n,
        (chip, kept, got),
        in_specs=[smem, vmem, vmem],
    )


def add_halve_kernel(mine, *refs):
    parts, (stays, goes) = refs[:-2], refs[-2:]
    count = len(parts) // 2
    at = 0
    for kept, got in zip(parts[:count], parts[count:]):
        for o in range(kept.shape[0]):
            for out, side in ((stays, mine[0]), (goes, 1 - mine[0])):
                out[at] = (kept[o, side].astype(f32) + got[o, side].astype(f32)).astype(bf16)
            at += 1


def add_halve(kept, got, mine, outer):
    rows, width = kept[0].shape[1:]
    blocks = sum(part.shape[0] for part in kept)
    inner = blocks // (2 * outer)
    half = shape_of((outer, inner, rows, width), bf16)
    stays, goes = kernel_call(
        add_halve_kernel,
        "add_halve",
        (half, half),
        (mine, *[part.reshape(-1, 2, inner, rows, width) for part in (*kept, *got)]),
        in_specs=[smem] + [vmem] * (len(kept) + len(got)),
        megabytes=40,
    )
    return stays.reshape(-1, rows, width), goes.reshape(-1, rows, width)


def adamw_update(master, moment_one, moment_two, gradient, step_rate, decay_weight):
    first_new = beta_one * moment_one + (1.0 - beta_one) * gradient
    second_new = beta_two * moment_two + (1.0 - beta_two) * gradient * gradient
    first_hat = first_new / (1.0 - beta_one**STEP)
    second_hat = second_new / (1.0 - beta_two**STEP)
    master_new = master - step_rate * (
        first_hat / (jnp.sqrt(second_hat) + adam_eps) + decay_weight * master
    )
    return (first_new, second_new, master_new)


def adamw_kernel(where, master, first, second, *refs, n_dp, own, padded, rate, decay):
    pieces, (first_ref, second_ref, master_ref, slots, joined) = refs[:-5], refs[-5:]
    for t, piece in enumerate(pieces):
        for o in range(2):
            slots[where[2 * t + o]] = piece[o, 0]
    for s in range(slots.shape[0]):
        for d in range(n_dp):
            start = (s * n_dp + d) * own
            joined[:, start : start + own] = slots[
                s, :, d * padded : d * padded + own
            ].astype(f32)
    first_ref[0], second_ref[0], master_ref[0] = adamw_update(
        master[0], first[0], second[0], joined[...], rate, decay
    )


def adamw_hidden(master, first, second, pieces, where, n_dp, padded, rate, decay):
    two, rows, ff = master.shape
    n_seq = 2 * len(pieces)
    own = ff // (n_seq * n_dp)
    block = pl.BlockSpec((1, rows, ff), lambda g: (g, 0, 0))
    part = pl.BlockSpec((2, 1, rows, n_dp * padded), lambda g: (0, g, 0, 0))
    return kernel_call(
        functools.partial(
            adamw_kernel, n_dp=n_dp, own=own, padded=padded, rate=rate, decay=decay
        ),
        "adamw_hidden",
        (shape_of(master.shape, f32),) * 3,
        (where, master, first, second, *pieces),
        megabytes=44,
        grid=(two,),
        in_specs=[smem] + [block] * 3 + [part] * len(pieces),
        out_specs=(block,) * 3,
        scratch_shapes=[
            pltpu.VMEM((n_seq, rows, n_dp * padded), bf16),
            pltpu.VMEM((rows, ff), f32),
        ],
    )


def assemble_kernel(where, *refs, splits, counts):
    ins, outs, sems = refs[: len(counts)], refs[len(counts) : -1], refs[-1]
    copies = []
    entry = 0
    for ref, (column, count) in zip(ins, counts):
        for i in range(count):
            for out, start, width in splits[column]:
                copies.append(
                    pltpu.make_async_copy(
                        ref.at[i, :, pl.ds(start, width)],
                        outs[out[0]].at[where[entry], :, pl.ds(out[1], width)],
                        sems.at[len(copies)],
                    )
                )
            entry += 1
    for copy in copies:
        copy.start()
    for copy in copies:
        copy.wait()


def assemble(pieces, where, splits, out_widths):
    counts = [(column, array.shape[0]) for array, column in pieces]
    rows = pieces[0][0].shape[1]
    blocks = sum(count for column, count in counts if column == 0)
    n_copies = sum(count * len(splits[column]) for column, count in counts)
    return kernel_call(
        functools.partial(assemble_kernel, splits=splits, counts=counts),
        "assemble",
        tuple(shape_of((blocks, rows, w), bf16) for w in out_widths),
        (where.astype(jnp.int32), *[array for array, _ in pieces]),
        in_specs=[smem] + [anywhere] * len(pieces),
        out_specs=(vmem,) * len(out_widths),
        scratch_shapes=[pltpu.SemaphoreType.DMA((n_copies,))],
    )


def seq_perm(values, chips, flip):
    count = lax.axis_size("seq")
    return lax.ppermute(
        values, "seq", [(i, ((i + 2 * chips) % count) ^ flip) for i in range(count)]
    )


def dp_perm(values, bit):
    return lax.ppermute(values, "dp", [(i, i ^ bit) for i in range(lax.axis_size("dp"))])


def dp_bits():
    return [1 << i for i in range(lax.axis_size("dp").bit_length() - 1)]


def pick(values, index, axis):
    return lax.dynamic_index_in_dim(values, index, axis, keepdims=False)


def places_of():
    n_chips = lax.axis_size("seq") // 2
    seq_at = lax.axis_index("seq")
    return n_chips, seq_at // 2, seq_at % 2, lax.axis_size("dp"), lax.axis_index("dp")


def swap(values):
    return seq_perm(values, 0, 1)


def sent_pieces(values):
    return [values] + [seq_perm(values, t, 0) for t in range(1, lax.axis_size("seq") // 2)]


def shards(
    tokens,
    cotangent,
    positions,
    qkv_master,
    qkv_first,
    qkv_second,
    out_master,
    out_first,
    out_second,
    gate_up_master,
    gate_up_first,
    gate_up_second,
    down_master,
    down_first,
    down_second,
    small_master,
    small_first,
    small_second,
):
    n_chips, chip_at, core_at, n_dp, dp_at = places_of()
    n_seq = 2 * n_chips
    n_all = n_seq * n_dp
    bits = dp_bits()
    rows_own, qkv_width = qkv_master.shape
    half = qkv_width // 2
    small_own = small_master.shape[0]
    ff_dev = down_master.shape[0]
    ff_pad = -(-ff_dev // 16) * 16
    ff_own = n_dp * ff_pad
    inputs = tokens[0]
    upstream = cotangent[0]
    tok_rows = inputs.shape[0]
    seq_length = positions.shape[1]
    shifts = list(range(1, n_chips))

    ring_chips = [(chip_at - t) % n_chips for t in range(n_chips)]
    ring_order = jnp.stack(
        [chip * 2 + (core_at ^ flip) for chip in ring_chips for flip in range(2)]
    ).astype(jnp.int32)
    bases = positions[0, ::PIECE].reshape(n_seq, tok_rows // PIECE)
    key_bases = jnp.take(bases, ring_order, axis=0)
    query_bases = key_bases[0]
    key_bases = key_bases.reshape(-1)
    own_places = lax.dynamic_slice_in_dim(
        positions[0], (chip_at * 2 + core_at) * tok_rows, tok_rows, 0
    )
    cosine, sine = rotary_tables(own_places)

    small_block = jnp.pad(
        small_master.astype(bf16), (0, rows_own * HD - small_own)
    ).reshape(rows_own, HD)
    packed = jnp.concatenate([small_block, qkv_master.astype(bf16)], axis=1)
    qkv_ring = sent_pieces(packed)
    core_side = core_at.reshape(1).astype(jnp.int32)
    chip_side = chip_at.reshape(1).astype(jnp.int32)
    bit_sides = {bit: ((dp_at // bit) % 2).reshape(1).astype(jnp.int32) for bit in bits}
    cut_kept, cut_sent = cut_hidden(gate_up_master, core_side, n_chips, n_dp, ff_pad)
    to_send = turn_pairs([cut_kept], [swap(cut_sent)], chip_side, n_chips)
    qkv_ring, to_send, cosine, sine = fence(qkv_ring, to_send, cosine, sine)

    def exchange(shift):
        return seq_perm(to_send[shift], shift, 0)

    w_out = lax.all_gather(
        after(out_master.astype(bf16), *to_send), ("seq", "dp"), axis=0, tiled=True
    )

    columns = ((0, HD + half), (HD + half, HD + qkv_width))
    orders = (bits, bits[::-1])
    held = list(stack_columns(qkv_ring, columns))
    flips = [[0], [0]]
    gate_up_pieces = {0: to_send[0]}
    groups = [shifts[:1], shifts[-1:], shifts[1:-1]] if n_chips > 2 else [shifts, [], []]
    for stage in range(len(bits)):
        got = [dp_perm(h, order[stage]) for h, order in zip(held, orders)]
        if stage == len(bits) - 1:
            swapped = [swap(h) for h in held]
        for shift in groups[min(stage, 1)] if stage < 2 else []:
            gate_up_pieces[shift] = exchange(shift)
        got, held, gate_up_pieces = fence(got, held, gate_up_pieces)
        flips = [f + [k ^ order[stage] for k in f] for f, order in zip(flips, orders)]
        if stage < len(bits) - 1:
            held = [jnp.concatenate([h, g], axis=0) for h, g in zip(held, got)]
    (swapped,) = fence(swapped)
    down_share = jnp.pad(down_master.astype(bf16), ((0, ff_pad - ff_dev), (0, 0)))
    w_down = lax.all_gather(after(down_share, *got), "dp", axis=0, tiled=True)
    for shift in groups[2]:
        gate_up_pieces[shift] = exchange(shift)
    got_swapped = [swap(g) for g in got]
    pieces, where = [], []
    for column in range(2):
        for flip, part, ks in (
            (0, held[column], flips[column][: n_dp // 2]),
            (0, got[column], flips[column][n_dp // 2 :]),
            (1, swapped[column], flips[column][: n_dp // 2]),
            (1, got_swapped[column], flips[column][n_dp // 2 :]),
        ):
            pieces.append((part, column))
            where += [
                (chip * 2 + (core_at ^ flip)) * n_dp + (dp_at ^ k) for k in ks for chip in ring_chips
            ]
    w_qkv, small_blocks = assemble(
        pieces,
        jnp.stack(where),
        ((((1, 0), 0, HD), ((0, 0), HD, half)), (((0, half), 0, half),)),
        (qkv_width, HD),
    )
    w_qkv = w_qkv.reshape(D, qkv_width)
    small_params = small_blocks.reshape(n_all, rows_own * HD)[:, :small_own].reshape(1, -1)
    small_params = small_params.astype(f32)
    gain_one = small_params[:, :D]
    gain_two = small_params[:, D : 2 * D]
    qkv_bias = small_params[:, 2 * D :]
    normed_one, key_value = project_kv(inputs, w_qkv, gain_one, qkv_bias, cosine, sine)
    gate_up_held = [
        jnp.concatenate([gate_up_pieces[t] for t in ts], axis=0)
        for ts in (range(n_chips // 2), range(n_chips // 2, n_chips))
    ]
    normed_one, key_value, gate_up_held = fence(normed_one, key_value, gate_up_held)

    kv_ring = sent_pieces(key_value)
    gate_up_parts = [
        [held, dp_perm(held, order[0])] for held, order in zip(gate_up_held, orders)
    ]
    gate_up_flips = [[0, order[0]] for order in orders]
    queries = project_q(normed_one, w_qkv, qkv_bias, cosine, sine)
    kv_swapped = [swap(kv_ring[0])] + [swap(after(piece, queries)) for piece in kv_ring[1:]]
    kv_ring, kv_swapped, gate_up_parts, queries, upstream = fence(
        kv_ring, kv_swapped, gate_up_parts, queries, upstream
    )

    def cross(start, stop, stage):
        for parts, flips_of, order in zip(gate_up_parts, gate_up_flips, orders):
            parts += [dp_perm(piece, order[stage]) for piece in parts[start:stop]]
            flips_of += [k ^ order[stage] for k in flips_of[start:stop]]

    upstream_ring = [upstream, seq_perm(upstream, 1, 0)]
    cross(0, 1 if len(bits) == 2 else 2, 1)
    attended, logsum, key_value_all = attend(
        queries, [piece for pair in zip(kv_ring, kv_swapped) for piece in pair], query_bases, key_bases
    )
    gate_up_parts, upstream_ring, attended, logsum, key_value_all = fence(
        gate_up_parts, upstream_ring, attended, logsum, key_value_all
    )

    def ring_step(pieces):
        return pieces + [seq_perm(pieces[-1], 1, 0)] if len(pieces) < n_chips else pieces

    upstream_ring = ring_step(upstream_ring)
    if len(bits) == 2:
        cross(1, 2, 1)
    else:
        cross(0, 4, 2)
    upstream_swapped = [swap(piece) for piece in upstream_ring[:2]]
    residual, normed_two, attended_low = out_project(inputs, attended, w_out, gain_two)
    normed_ring, normed_swapped = [normed_two], [swap(normed_two)]
    gate_up_parts, upstream_ring, upstream_swapped, normed_ring, normed_swapped, residual = fence(
        gate_up_parts, upstream_ring, upstream_swapped, normed_ring, normed_swapped, residual
    )

    pieces, where = [], []
    for column, (parts, flips_of) in enumerate(zip(gate_up_parts, gate_up_flips)):
        slots = ring_order[:n_chips] if column == 0 else ring_order[n_chips:]
        for part, k in zip(parts, flips_of):
            pieces.append((part.reshape(-1, rows_own, ff_own), 0))
            block = slots * n_dp + (dp_at ^ k)
            where.append(jnp.stack([block, n_all + block], axis=1).reshape(-1))
    (w_gate_up,) = assemble(
        pieces, jnp.concatenate(where), ((((0, 0), 0, ff_own),),), (ff_own,)
    )
    w_gate_up = w_gate_up.reshape(2, D, ff_own)
    out_parts, kept = [], ()
    running = None
    for slot in range(n_chips):
        sent = None if running is None else seq_perm(running, 1, 0)
        normed_ring = ring_step(normed_ring)
        upstream_ring = ring_step(upstream_ring)
        out_own, out_other, grad_own, grad_other, *kept = feed_forward(
            (normed_ring[slot], normed_swapped[slot]),
            (upstream_ring[slot], upstream_swapped[slot]),
            w_gate_up,
            w_down,
            slot,
            n_chips,
            kept,
        )
        out_parts.append((out_own, out_other))
        if slot == n_chips // 2:
            normed_all, ffn_all, hidden_all, gate_grads_all, up_grads_all = kept
            bases = weight_grad(normed_all, (gate_grads_all, up_grads_all), (0, 2), kind=f32)
            down_bases = weight_grad(hidden_all, (ffn_all,), (0, 2), kind=f32)
        grad_swapped = swap(grad_other)
        if slot + 1 < n_chips:
            normed_swapped = normed_swapped + [swap(after(normed_ring[slot + 1], grad_own))]
        if slot + 2 < n_chips and len(upstream_swapped) < slot + 3:
            upstream_swapped = upstream_swapped + [swap(after(upstream_ring[slot + 2], grad_own))]
        if slot == 0:
            grad_first = (grad_own, grad_swapped)
        elif sent is None:
            running = add(grad_own, grad_swapped)
        else:
            running = add(grad_own, grad_swapped, after(sent, grad_own))
        running, normed_ring, normed_swapped, upstream_ring, upstream_swapped, out_parts, kept = fence(
            running, normed_ring, normed_swapped, upstream_ring, upstream_swapped, out_parts, kept
        )
        if slot == n_chips // 2:
            bases, down_bases, kept = fence(bases, down_bases, kept)

    grad_ring = jnp.zeros_like(grad_first[0]) if running is None else seq_perm(running, 1, 0)
    normed_all, ffn_all, hidden_all, gate_grads_all, up_grads_all = kept
    (down_grad,) = weight_grad(hidden_all, (ffn_all,), (1, 2), down_bases)
    first_split = (
        jnp.concatenate([bit_sides[order[0]] for order in orders]),
        tuple(order[0] for order in orders),
    )
    halves = [
        weight_grad(
            normed_all,
            (gate_grads_all, up_grads_all),
            (1, 2),
            bases,
            first_split,
            rows_own,
            (part, 2),
        )
        for part in range(2)
    ]
    out_pairs = [(own, swap(other)) for own, other in out_parts]
    out_total = [add(own, other) for own, other in out_pairs[1:]]
    grad_ring, halves, out_pairs, out_total = fence(grad_ring, halves, out_pairs, out_total)
    down_owned = lax.psum_scatter(down_grad, "dp", scatter_dimension=0, tiled=True)
    down_owned = down_owned[:ff_dev].astype(f32)

    got_one = [dp_perm(goes, order[0]) for (_, goes), order in zip(halves[0], orders)]
    out_running = seq_perm(out_total[0], 1, 0) if n_chips > 1 else None
    residual_grads, branch_grads, attended_grads, gain_two_grad = norm_back(
        grad_ring, *grad_first, residual, upstream, gain_two, w_out
    )
    query_pre, kv_grad_own, kv_grad_other = attend_back(
        queries,
        key_value_all,
        attended_grads,
        attended,
        logsum,
        query_bases,
        key_bases,
        cosine,
        sine,
    )
    got_one, kv_grad_own, kv_grad_other, query_pre, branch_grads, out_running = fence(
        got_one, kv_grad_own, kv_grad_other, query_pre, branch_grads, out_running
    )
    own_parts = kv_grad_own.reshape(n_chips, tok_rows, 2 * KVW)
    other_parts = swap(kv_grad_other).reshape(n_chips, tok_rows, 2 * KVW)
    kv_sum = add_turn(own_parts, other_parts, jnp.zeros_like(chip_side))
    kv_sum, halves, query_pre, branch_grads = fence(kv_sum, halves, query_pre, branch_grads)

    def next_split(kept_parts, got, done_bits, left_bits):
        rest = [bit for bit in bits[::-1] if bit not in done_bits]
        bit = left_bits[0]
        lead = sum(part.shape[0] for part in kept_parts) // 2 ** len(rest)
        return add_halve(kept_parts, got, bit_sides[bit], lead * 2 ** rest.index(bit))

    kv_got = [seq_perm(kv_sum[t], n_chips - t, 0) for t in range(1, n_chips)]
    got_two = [dp_perm(goes, order[0]) for (_, goes), order in zip(halves[1], orders)]
    by_core = (core_side, (n_dp,))
    (query_split,) = weight_grad(normed_one[None], (query_pre[None],), split=by_core, rows=rows_own)
    (out_split,) = weight_grad(
        attended_low[None], (branch_grads[None],), split=by_core, rows=rows_own
    )
    kv_got, got_two, query_split, out_split, down_owned = fence(
        kv_got, got_two, query_split, out_split, down_owned
    )

    if n_chips > 2:
        out_running = seq_perm(add(out_running, out_total[1]), 1, 0)
    gate_up_split = [
        next_split([one[0], two[0]], [got, other], order[:1], order[1:])
        for one, two, got, other, order in zip(*halves, got_one, got_two, orders)
    ]
    gate_up_sums = [dp_perm(goes, order[1]) for (_, goes), order in zip(gate_up_split, orders)]
    both = [(split[0], swap(split[1])) for split in (query_split, out_split)]
    key_value_pre, input_grads, gain_one_grad, bias_grad = input_back(
        inputs,
        gain_one,
        w_qkv,
        query_pre,
        cosine,
        sine,
        residual_grads,
        kv_sum[0],
        kv_got,
    )
    ((kv_stays, kv_goes),) = weight_grad(
        normed_one[None], (key_value_pre[None],), split=by_core, rows=rows_own
    )
    gate_up_split, gate_up_sums, both, input_grads, kv_stays, kv_goes, out_running, small_parts = fence(
        gate_up_split,
        gate_up_sums,
        both,
        input_grads,
        kv_stays,
        kv_goes,
        out_running,
        (gain_one_grad, gain_two_grad, bias_grad),
    )

    if n_chips > 3:
        out_running = seq_perm(add(out_running, out_total[2]), 1, 0)
    ready = []
    for split, got, order in zip(gate_up_split, gate_up_sums, orders):
        kept_part = split[0]
        for i in range(2, len(order)):
            kept_part, goes = next_split([kept_part], [got], order[:i], order[i:])
            got = dp_perm(goes, order[i])
        ready.append(add_halve([kept_part], [got], core_side, n_chips))
    both = [
        next_split([kept_part], [got], [], order) for (kept_part, got), order in zip(both, orders)
    ]
    to_send = turn_pairs(
        [kept_part for kept_part, _ in ready],
        [swap(sent) for _, sent in ready],
        chip_side,
        n_chips,
    )
    small_grad = jnp.concatenate(small_parts, axis=1).astype(bf16)
    small_grad = jnp.pad(
        small_grad.reshape(n_all, small_own), ((0, 0), (0, rows_own * HD - small_own))
    ).reshape(n_chips, 2, n_dp, rows_own, HD)
    kv_stays = jnp.concatenate(
        [pick(small_grad, core_at, 1).reshape(-1, rows_own, HD), kv_stays], axis=2
    )
    kv_goes = jnp.concatenate(
        [pick(small_grad, 1 - core_at, 1).reshape(-1, rows_own, HD), kv_goes], axis=2
    )
    kv_side = (kv_stays, swap(kv_goes))
    to_send, both, kv_side, out_running = fence(to_send, both, kv_side, out_running)

    gate_up_owned = {0: to_send[0]}
    both_got = [dp_perm(goes, order[0]) for (_, goes), order in zip(both, orders)]
    for shift in groups[0] + groups[1]:
        gate_up_owned[shift] = exchange(shift)
    kv_split = next_split([kv_side[0]], [kv_side[1]], [], orders[0])
    kv_sums = dp_perm(kv_split[1], orders[0][0])
    gate_up_owned, both_got, kv_split, kv_sums = fence(gate_up_owned, both_got, kv_split, kv_sums)

    for shift in groups[2]:
        gate_up_owned[shift] = exchange(shift)
    three = [(both[0], both_got[0], orders[0]), (both[1], both_got[1], orders[1])]
    three.append((kv_split, kv_sums, orders[0]))
    rest_send = []
    for (kept_part, _), got, order in three:
        for i in range(1, len(order)):
            kept_part, goes = next_split([kept_part], [got], order[:i], order[i:])
            got = dp_perm(goes, order[i])
        rest_send.append(add_turn(kept_part, got, chip_side))
    gate_up_owned, rest_send = fence(gate_up_owned, rest_send)

    rest_send = [
        jnp.concatenate([parts[t] for parts in rest_send], axis=1) for t in range(n_chips)
    ]
    total = rest_send[0].astype(f32)
    for shift in shifts:
        total = total + seq_perm(rest_send[shift], shift, 0).astype(f32)
    for t in range(4, n_chips):
        out_running = seq_perm(add(out_running, out_total[t - 1]), 1, 0)
    outputs = residual + out_pairs[0][0].astype(f32) + out_pairs[0][1].astype(f32)
    if n_chips > 1:
        outputs = outputs + out_running.astype(f32)
    outputs = outputs.astype(bf16)
    gate_up_new = adamw_hidden(
        gate_up_master,
        gate_up_first,
        gate_up_second,
        [gate_up_owned[t] for t in range(n_chips)],
        ring_order,
        n_dp,
        ff_pad,
        0.064,
        0.1,
    )
    query_owned, out_owned, small_owned, kv_owned = jnp.split(
        total, (D, 2 * D, 2 * D + HD), axis=1
    )
    qkv_owned = jnp.concatenate([query_owned, kv_owned], axis=1)
    small_owned = small_owned.reshape(-1)[:small_own]

    qkv_new = adamw_update(qkv_master, qkv_first, qkv_second, qkv_owned, 0.09, 0.1)
    out_new = adamw_update(out_master, out_first, out_second, out_owned, 0.18, 0.1)
    down_new = adamw_update(down_master, down_first, down_second, down_owned, 0.026, 0.1)
    small_new = adamw_update(small_master, small_first, small_second, small_owned, 0.6, 0.0)
    return (
        outputs[None],
        input_grads[None],
        *qkv_new,
        *out_new,
        *gate_up_new,
        *down_new,
        *small_new,
    )


def solution(mesh):
    in_specs = (
        P("dp", "seq", None),
        P("dp", "seq", None),
        P("dp", None),
        P(("seq", "dp"), None),
        P(("seq", "dp"), None),
        P(("seq", "dp"), None),
        P(("seq", "dp"), None),
        P(("seq", "dp"), None),
        P(("seq", "dp"), None),
        P(None, ("seq", "dp"), None),
        P(None, ("seq", "dp"), None),
        P(None, ("seq", "dp"), None),
        P(("seq", "dp"), None),
        P(("seq", "dp"), None),
        P(("seq", "dp"), None),
        P(("seq", "dp")),
        P(("seq", "dp")),
        P(("seq", "dp")),
    )
    out_specs = (
        P("dp", "seq", None),
        P("dp", "seq", None),
        P(("seq", "dp"), None),
        P(("seq", "dp"), None),
        P(("seq", "dp"), None),
        P(("seq", "dp"), None),
        P(("seq", "dp"), None),
        P(("seq", "dp"), None),
        P(None, ("seq", "dp"), None),
        P(None, ("seq", "dp"), None),
        P(None, ("seq", "dp"), None),
        P(("seq", "dp"), None),
        P(("seq", "dp"), None),
        P(("seq", "dp"), None),
        P(("seq", "dp")),
        P(("seq", "dp")),
        P(("seq", "dp")),
    )
    return jax.shard_map(shards, mesh=mesh, in_specs=in_specs, out_specs=out_specs, check_vma=False)
```

```python
import functools

import jax
import jax.numpy as jnp
from jax import lax
from jax.experimental import pallas as pl
from jax.experimental.pallas import tpu as pltpu
from jax.sharding import PartitionSpec as P

D = 1536
HEADS = 12
KVH = 2
HD = 128
STEP = 10
KVW = KVH * HD
PIECE = 128


norm_eps = 1e-06
rope_base = 1000000.0
beta_one = 0.9
beta_two = 0.95
adam_eps = 1e-08
masked_score = -1e30
log2_e = 1.4426950408889634
bf16 = jnp.bfloat16
f32 = jnp.float32
vmem = pl.BlockSpec(memory_space=pltpu.VMEM)
smem = pl.BlockSpec(memory_space=pltpu.SMEM)
anywhere = pl.BlockSpec(memory_space=pl.ANY)


def shape_of(dims, kind):
    return jax.ShapeDtypeStruct(dims, kind)


def kernel_call(kernel, name, out_shape, operands, megabytes=32, **options):
    return pl.pallas_call(
        kernel,
        name=name,
        out_shape=out_shape,
        compiler_params=pltpu.CompilerParams(vmem_limit_bytes=megabytes << 20),
        cost_estimate=pl.CostEstimate(flops=10**6, bytes_accessed=10**6, transcendentals=0),
        **options,
    )(*operands)


def after(values, *others):
    return lax.optimization_barrier((values,) + others)[0]


def fence(*groups):
    flat, tree = jax.tree.flatten(groups)
    return jax.tree.unflatten(tree, lax.optimization_barrier(tuple(flat)))


def dot(left, right):
    return jnp.dot(left, right, preferred_element_type=f32)


def dot_transposed(left, right):
    return lax.dot_general(left, right, (((1,), (1,)), ((), ())), preferred_element_type=f32)


def rotary_tables(places):
    half_size = HD // 2
    freqs = rope_base ** (-(jnp.arange(half_size).astype(f32) * (2.0 / HD)))
    angles = places.astype(f32)[:, None] * freqs[None, :]
    cosine, sine = jnp.cos(angles), jnp.sin(angles)
    return jnp.concatenate([cosine, cosine], axis=1), jnp.concatenate([-sine, sine], axis=1)


def rms_scale(values):
    return lax.rsqrt(jnp.mean(values * values, axis=-1, keepdims=True) + norm_eps)


def swap_halves(values):
    return pltpu.roll(values, HD // 2, 1)


def head(index):
    return slice(index * HD, (index + 1) * HD)


def project_kv_kernel(tokens, w_qkv, gain, bias, cosine, sine, normed_ref, kv_ref):
    inputs = tokens[...].astype(f32)
    normed = (inputs * rms_scale(inputs) * gain[...]).astype(bf16)
    normed_ref[...] = normed
    rows = dot(normed, w_qkv[...]) + bias[:, D:]
    for j in range(KVH):
        part = rows[:, head(j)]
        kv_ref[:, head(j)] = (part * cosine[...] + swap_halves(part) * sine[...]).astype(bf16)
    kv_ref[:, KVW:] = rows[:, KVW:].astype(bf16)


def project_q_kernel(normed, w_qkv, bias, cosine, sine, query_ref):
    rows = dot(normed[...], w_qkv[...]) + bias[:, :D]
    for j in range(HEADS):
        part = rows[:, head(j)]
        query_ref[:, head(j)] = (part * cosine[...] + swap_halves(part) * sine[...]).astype(bf16)


def project_kv(tokens, w_qkv, gain, bias, cosine, sine):
    rows = tokens.shape[0]
    return kernel_call(
        project_kv_kernel,
        "project_kv",
        (shape_of((rows, D), bf16), shape_of((rows, 2 * KVW), bf16)),
        (tokens, w_qkv, gain, bias, cosine, sine),
        megabytes=58,
        grid=(1,),
        in_specs=[vmem, pl.BlockSpec((D, 2 * KVW), lambda i: (0, D // (2 * KVW)))] + [vmem] * 4,
        out_specs=(vmem, vmem),
    )


def project_q(normed, w_qkv, bias, cosine, sine):
    return kernel_call(
        project_q_kernel,
        "project_q",
        shape_of(normed.shape, bf16),
        (normed, w_qkv, bias, cosine, sine),
        megabytes=58,
        grid=(1,),
        in_specs=[vmem, pl.BlockSpec((D, D), lambda i: (0, 0))] + [vmem] * 3,
        out_specs=vmem,
    )


def mask_keys(values, query_bases, key_bases, first_run, fill):
    later = lax.broadcasted_iota(jnp.int32, (PIECE, PIECE), 0) - lax.broadcasted_iota(
        jnp.int32, (PIECE, PIECE), 1
    )
    keys, queries = values.shape
    rows = []
    for r in range(keys // PIECE):
        down = slice(r * PIECE, (r + 1) * PIECE)
        row = []
        for q in range(queries // PIECE):
            gap = query_bases[q] - key_bases[first_run + r]
            row.append(jnp.where(later <= gap, values[down, q * PIECE : (q + 1) * PIECE], fill))
        rows.append(jnp.concatenate(row, axis=1))
    return jnp.concatenate(rows, axis=0)


def attend_kernel(query_bases, key_bases, q_ref, *refs):
    pieces, (out_ref, lse_ref, kv_ref) = refs[:-3], refs[-3:]
    rows = q_ref.shape[0]
    for i, piece in enumerate(pieces):
        kv_ref[i * rows : (i + 1) * rows, :] = piece[...]
    groups = HEADS // KVH
    scale = HD**-0.5 * log2_e
    for kv in range(KVH):
        values = kv_ref[:, head(KVH + kv)].T
        for h in range(kv * groups, (kv + 1) * groups):
            queries = q_ref[:, head(h)]
            scores = []
            for run in range(key_bases.shape[0]):
                keys = kv_ref[run * PIECE : (run + 1) * PIECE, head(kv)]
                part = dot_transposed(keys, queries)
                scores.append(mask_keys(part, query_bases, key_bases, run, masked_score))
            scores = jnp.concatenate(scores, axis=0)
            top = jnp.max(scores, axis=0, keepdims=True)
            weights = jnp.exp2((scores - top) * scale)
            total = jnp.sum(weights, axis=0, keepdims=True)
            mixed = dot(values, weights.astype(bf16))
            out_ref[:, head(h)] = (mixed / total).T
            lse_ref[h : h + 1, :] = top * scale + jnp.log2(total)


def attend(queries, pieces, query_bases, key_bases):
    rows, total = queries.shape[0], key_bases.shape[0] * PIECE
    return kernel_call(
        attend_kernel,
        "attend",
        (
            shape_of((rows, D), f32),
            shape_of((HEADS, rows), f32),
            shape_of((total, 2 * KVW), bf16),
        ),
        (query_bases, key_bases, queries, *pieces),
        in_specs=[smem] * 2 + [vmem] * (1 + len(pieces)),
    )


def out_kernel(tokens, attended, w_out, gain, residual_ref, normed_ref, low_ref):
    low = attended[...].astype(bf16)
    low_ref[...] = low
    residual = tokens[...].astype(f32) + dot(low, w_out[...])
    residual_ref[...] = residual
    normed_ref[...] = (residual * rms_scale(residual) * gain[...]).astype(bf16)


def out_project(tokens, attended, w_out, gain):
    dims = tokens.shape
    return kernel_call(
        out_kernel,
        "out_project",
        (shape_of(dims, f32), shape_of(dims, bf16), shape_of(dims, bf16)),
        (tokens, attended, w_out, gain),
    )


def ffn_kernel(
    normed_own, normed_other, grad_own, grad_other, w_gate_up, w_down, *refs, earlier
):
    refs = refs[earlier:]
    out_refs, grad_refs = refs[:2], refs[2:4]
    normed_ref, ffn_grad_ref, hidden_ref, gate_ref, up_ref = refs[4:]
    rows = normed_own.shape[0]
    for i, (normed_in, grad_in) in enumerate(((normed_own, grad_own), (normed_other, grad_other))):
        to = slice(i * rows, (i + 1) * rows)
        normed, ffn_grad = normed_in[...], grad_in[...]
        normed_ref[0, to, :] = normed
        ffn_grad_ref[0, to, :] = ffn_grad
        gate = dot(normed, w_gate_up[0])
        up = dot(normed, w_gate_up[1])
        sigmoid = 1.0 / (1.0 + jnp.exp(-gate))
        silu = gate * sigmoid
        hidden = (silu * up).astype(bf16)
        hidden_ref[0, to, :] = hidden
        out_refs[i][...] = dot(hidden, w_down[...]).astype(bf16)
        hidden_grad = dot_transposed(ffn_grad, w_down[...])
        gate_grad = (hidden_grad * up * sigmoid * (1.0 + gate * (1.0 - sigmoid))).astype(bf16)
        up_grad = (hidden_grad * silu).astype(bf16)
        gate_ref[0, to, :] = gate_grad
        up_ref[0, to, :] = up_grad
        grad_refs[i][...] = (
            dot_transposed(gate_grad, w_gate_up[0]) + dot_transposed(up_grad, w_gate_up[1])
        ).astype(bf16)


def feed_forward(normed, grads, w_gate_up, w_down, slot, slots, kept):
    rows, width = normed[0].shape
    ff_own = w_down.shape[0]
    token = shape_of((rows, width), bf16)
    widths = (width, width, ff_own, ff_own, ff_own)
    operands = (*normed, *grads, w_gate_up, w_down)
    return kernel_call(
        functools.partial(ffn_kernel, earlier=len(kept)),
        "feed_forward",
        (token,) * 4 + tuple(shape_of((slots, 2 * rows, w), bf16) for w in widths),
        (*operands, *kept),
        grid=(1,),
        in_specs=[vmem] * len(operands) + [anywhere] * len(kept),
        out_specs=(vmem,) * 4
        + tuple(pl.BlockSpec((1, 2 * rows, w), lambda i: (slot, 0, 0)) for w in widths),
        input_output_aliases={len(operands) + i: 4 + i for i in range(len(kept))},
    )


def norm_back_kernel(
    got, own, other, residual_ref, cotangent, gain, w_out, grad_ref, low_ref, back_ref, gain_ref
):
    normed_grad = got[...].astype(f32) + own[...].astype(f32) + other[...].astype(f32)
    residual = residual_ref[...]
    scale = rms_scale(residual)
    unit = residual * scale
    gain_ref[...] = jnp.sum(normed_grad * unit, axis=0, keepdims=True)
    weighted = normed_grad * gain[...]
    grad = cotangent[...].astype(f32) + scale * (
        weighted - unit * jnp.mean(weighted * unit, axis=-1, keepdims=True)
    )
    grad_ref[...] = grad
    low = grad.astype(bf16)
    low_ref[...] = low
    back_ref[...] = dot_transposed(low, w_out[...]).astype(bf16)


def norm_back(got, own, other, residual, cotangent, gain, w_out):
    dims = residual.shape
    return kernel_call(
        norm_back_kernel,
        "norm_back",
        (shape_of(dims, f32), shape_of(dims, bf16), shape_of(dims, bf16), shape_of((1, D), f32)),
        (got, own, other, residual, cotangent, gain, w_out),
    )


def attend_back_kernel(
    query_bases,
    key_bases,
    q_ref,
    kv_ref,
    grad_ref,
    out_ref,
    lse_ref,
    cosine,
    sine,
    q_grad_ref,
    kv_own_ref,
    kv_other_ref,
    q_rows,
    grad_rows,
    deltas,
    q_sums,
):
    rows = q_ref.shape[0]
    groups = HEADS // KVH
    scale = HD**-0.5
    for kv in range(KVH):
        for j in range(groups):
            part = slice(j * rows, (j + 1) * rows)
            columns = head(kv * groups + j)
            q_rows[part, :] = q_ref[:, columns]
            grads = grad_ref[:, columns]
            grad_rows[part, :] = grads
            product = grads.astype(f32) * out_ref[:, columns]
            deltas[:, part] = jnp.sum(product.T, axis=0, keepdims=True)
        q_sums[...] = jnp.zeros_like(q_sums)

        @pl.loop(0, kv_ref.shape[0] // (2 * rows), unroll=2)
        def _(step):
            at = pl.ds(pl.multiple_of(step * (2 * rows), 2 * rows), 2 * rows)
            runs = 2 * rows // PIECE
            keys = kv_ref[at, head(kv)]
            values = kv_ref[at, head(KVH + kv)]
            key_sum = value_sum = None
            for j in range(groups):
                part = slice(j * rows, (j + 1) * rows)
                h = kv * groups + j
                queries, grads = q_rows[part, :], grad_rows[part, :]
                scores = dot_transposed(keys, queries)
                weights = jnp.exp2(scores * (scale * log2_e) - lse_ref[h : h + 1, :])
                weights = mask_keys(weights, query_bases, key_bases, step * runs, 0.0)
                weight_grads = dot_transposed(values, grads)
                score_grads = (weights * (weight_grads - deltas[:, part])).astype(bf16)
                value_part = dot(weights.astype(bf16), grads)
                key_part = dot(score_grads, queries)
                key_sum = key_part if key_sum is None else key_sum + key_part
                value_sum = value_part if value_sum is None else value_sum + value_part
                q_sums[part, :] += lax.dot_general(
                    score_grads, keys, (((0,), (0,)), ((), ())), preferred_element_type=f32
                )
            key_sum = (key_sum * scale).astype(bf16)
            value_sum = value_sum.astype(bf16)
            to = pl.ds(pl.multiple_of(step * rows, rows), rows)
            for ref, mine in ((kv_own_ref, slice(0, rows)), (kv_other_ref, slice(rows, 2 * rows))):
                ref[to, head(kv)] = key_sum[mine, :]
                ref[to, head(KVH + kv)] = value_sum[mine, :]

        for j in range(groups):
            part = q_sums[j * rows : (j + 1) * rows, :] * scale
            q_grad_ref[:, head(kv * groups + j)] = (
                part * cosine[...] - swap_halves(part) * sine[...]
            ).astype(bf16)


def attend_back(queries, key_value, grads, attended, lse, query_bases, key_bases, cosine, sine):
    rows, total = queries.shape[0], key_value.shape[0]
    groups = HEADS // KVH
    return kernel_call(
        attend_back_kernel,
        "attend_back",
        (
            shape_of((rows, D), bf16),
            shape_of((total // 2, 2 * KVW), bf16),
            shape_of((total // 2, 2 * KVW), bf16),
        ),
        (query_bases, key_bases, queries, key_value, grads, attended, lse, cosine, sine),
        in_specs=[smem] * 2 + [vmem] * 7,
        scratch_shapes=[
            pltpu.VMEM((groups * rows, HD), bf16),
            pltpu.VMEM((groups * rows, HD), bf16),
            pltpu.VMEM((1, groups * rows), f32),
            pltpu.VMEM((groups * rows, HD), f32),
        ],
    )


def input_kernel(
    tokens, gain, w_qkv, query_grad, cosine, sine, residual_grad, own, *refs
):
    got, (kv_ref, input_ref, gain_ref, bias_ref) = refs[:-4], refs[-4:]
    rows = own[...].astype(f32)
    for piece in got:
        rows = rows + piece[...].astype(f32)
    for j in range(KVH):
        part = rows[:, head(j)]
        kv_ref[:, head(j)] = (part * cosine[...] - swap_halves(part) * sine[...]).astype(bf16)
    kv_ref[:, KVW:] = rows[:, KVW:].astype(bf16)
    kv_grad = kv_ref[...]
    q_grad = query_grad[...]
    bias_ref[:, :D] = jnp.sum(q_grad.astype(f32), axis=0, keepdims=True)
    bias_ref[:, D:] = jnp.sum(kv_grad.astype(f32), axis=0, keepdims=True)
    normed_grad = dot_transposed(q_grad, w_qkv[:, :D]) + dot_transposed(kv_grad, w_qkv[:, D:])
    inputs = tokens[...].astype(f32)
    scale = rms_scale(inputs)
    unit = inputs * scale
    gain_ref[...] = jnp.sum(normed_grad * unit, axis=0, keepdims=True)
    weighted = normed_grad * gain[...]
    input_ref[...] = residual_grad[...] + scale * (
        weighted - unit * jnp.mean(weighted * unit, axis=-1, keepdims=True)
    )


def input_back(tokens, gain, w_qkv, query_grad, cosine, sine, residual_grad, own, got):
    rows = tokens.shape[0]
    return kernel_call(
        input_kernel,
        "input_back",
        (
            shape_of((rows, 2 * KVW), bf16),
            shape_of((rows, D), f32),
            shape_of((1, D), f32),
            shape_of((1, D + 2 * KVW), f32),
        ),
        (tokens, gain, w_qkv, query_grad, cosine, sine, residual_grad, own, *got),
        megabytes=58,
    )


def split_kernel(sides, values, *outs, cuts, bits):
    blocks = values.shape[0]
    for i, ((lo, hi), bit) in enumerate(zip(cuts, bits)):
        for out, side in ((outs[2 * i], sides[i]), (outs[2 * i + 1], 1 - sides[i])):
            for o in range(blocks // (2 * bit)):
                for j in range(bit):
                    out[o * bit + j] = values[(2 * o + side) * bit + j, :, lo:hi]


def split_columns(values, sides, cuts, bits):
    blocks, rows, _ = values.shape
    outs = kernel_call(
        functools.partial(split_kernel, cuts=cuts, bits=bits),
        "split_columns",
        tuple(shape_of((blocks // 2, rows, hi - lo), bf16) for lo, hi in cuts for _ in range(2)),
        (sides, values),
        in_specs=[smem, vmem],
    )
    return [(outs[2 * i], outs[2 * i + 1]) for i in range(len(cuts))]


def weight_grad_kernel(sides, left, *refs, count, inners, based):
    rights, refs = refs[:count], refs[count:]
    bases, outs = refs[: count * based], refs[count * based :]
    turned = left[...].reshape(-1, left.shape[-1]).T
    for i, right in enumerate(rights):
        result = dot(turned, right[...].reshape(-1, right.shape[-1]))
        if based:
            result = result + bases[i][...]
        if not inners:
            outs[i][...] = result.astype(outs[i].dtype)
            continue
        stays, goes = outs[2 * i], outs[2 * i + 1]
        rows = stays.shape[2]
        result = result.astype(bf16)
        for side, refs_of in ((0, (stays, goes)), (1, (goes, stays))):

            @pl.when(sides[i] == side)
            def _():
                for o in range(stays.shape[0]):
                    for bit in range(2):
                        for j in range(inners[i]):
                            block = (o * 2 + bit) * inners[i] + j
                            refs_of[bit][o, j] = result[block * rows : (block + 1) * rows]


def weight_grad(
    left, rights, slots=(0, 1), bases=(), split=None, rows=0, part=(0, 1), kind=bf16
):
    n_slots, tokens, m = left.shape
    n_slots = n_slots // slots[1]
    m = m // part[1]
    block = 3 * HD if m % (3 * HD) == 0 else HD
    steps = m // block
    first = part[0] * steps
    whole = pl.Buffered(buffer_count=1)
    sides, inners = split if split else (jnp.zeros((1,), jnp.int32), ())
    out_shape, out_specs = [], []
    for i, right in enumerate(rights):
        n = right.shape[-1]
        if not inners:
            out_shape.append(shape_of((m, n), kind))
            out_specs.append(pl.BlockSpec((block, n), lambda i: (i, 0)))
            continue
        outer = block // (2 * inners[i] * rows)
        for _ in range(2):
            out_shape.append(shape_of((steps * outer, inners[i], rows, n), bf16))
            out_specs.append(pl.BlockSpec((outer, inners[i], rows, n), lambda i: (i, 0, 0, 0)))
    outs = kernel_call(
        functools.partial(
            weight_grad_kernel, count=len(rights), inners=inners, based=int(bool(bases))
        ),
        "weight_grad",
        tuple(out_shape),
        (sides, left, *rights, *bases),
        megabytes=44,
        grid=(steps,),
        in_specs=[
            smem,
            pl.BlockSpec((n_slots, tokens, block), lambda i: (slots[0], 0, i + first)),
        ]
        + [
            pl.BlockSpec(
                (n_slots, tokens, right.shape[-1]),
                lambda i: (slots[0], 0, 0),
                pipeline_mode=whole,
            )
            for right in rights
        ]
        + [pl.BlockSpec((block, base.shape[1]), lambda i: (i + first, 0)) for base in bases],
        out_specs=tuple(out_specs),
    )
    if not inners:
        return outs
    outs = [out.reshape((-1,) + out.shape[2:]) for out in outs]
    return [(outs[2 * i], outs[2 * i + 1]) for i in range(len(rights))]


def stack_kernel(*refs, cuts):
    pieces, outs = refs[: -len(cuts)], refs[-len(cuts) :]
    for i, piece in enumerate(pieces):
        for out, (lo, hi) in zip(outs, cuts):
            out[i] = piece[:, lo:hi]


def stack_columns(pieces, cuts):
    return kernel_call(
        functools.partial(stack_kernel, cuts=cuts),
        "stack_columns",
        tuple(shape_of((len(pieces), pieces[0].shape[0], hi - lo), bf16) for lo, hi in cuts),
        tuple(pieces),
    )


def cut_kernel(core, values, kept_ref, sent_ref, *, n_dp, own, padded):
    kept_ref[...] = jnp.zeros_like(kept_ref)
    sent_ref[...] = jnp.zeros_like(sent_ref)
    for side, refs in ((0, (kept_ref, sent_ref)), (1, (sent_ref, kept_ref))):

        @pl.when(core[0] == side)
        def _():
            for s in range(2 * kept_ref.shape[0]):
                for d in range(n_dp):
                    start = (s * n_dp + d) * own
                    refs[s % 2][s // 2, 0, :, d * padded : d * padded + own] = values[
                        0, :, start : start + own
                    ].astype(bf16)


def cut_hidden(values, core, n_chips, n_dp, padded):
    two, rows, ff = values.shape
    own = ff // (2 * n_chips * n_dp)
    dims = (n_chips, two, rows, n_dp * padded)
    return kernel_call(
        functools.partial(cut_kernel, n_dp=n_dp, own=own, padded=padded),
        "cut_hidden",
        (shape_of(dims, bf16),) * 2,
        (core, values),
        grid=(two,),
        in_specs=[smem, pl.BlockSpec((1, rows, ff), lambda g: (g, 0, 0))],
        out_specs=(pl.BlockSpec((n_chips, 1, rows, n_dp * padded), lambda g: (0, g, 0, 0)),) * 2,
    )


def turn_kernel(chip, *refs, n_chips):
    ins, outs = refs[: len(refs) - n_chips], refs[len(refs) - n_chips :]
    per_side = len(ins) // 2
    for t, out in enumerate(outs):
        at = lax.rem(chip[0] + t, n_chips)
        for side in range(2):
            if per_side == 1:
                out[side] = ins[side][at]
            else:
                for g in range(2):
                    out[side, g] = ins[2 * side + g][at]


def turn_pairs(kept, got, chip, n_chips):
    rows, width = kept[0].shape[-2:]
    return kernel_call(
        functools.partial(turn_kernel, n_chips=n_chips),
        "turn_pairs",
        (shape_of((2, 2, rows, width), bf16),) * n_chips,
        (chip, *kept, *got),
        in_specs=[smem] + [vmem] * (len(kept) + len(got)),
    )


def add_kernel(*refs):
    *ins, out = refs
    total = ins[0][...].astype(f32)
    for ref in ins[1:]:
        total = total + ref[...].astype(f32)
    out[...] = total.astype(bf16)


def add(*arrays):
    return kernel_call(add_kernel, "add", shape_of(arrays[0].shape, bf16), arrays)


def add_turn_kernel(chip, kept, got, *outs):
    n = kept.shape[0]
    for t, out in enumerate(outs):
        at = lax.rem(chip[0] + t, n)
        out[...] = (kept[at].astype(f32) + got[at].astype(f32)).astype(bf16)


def add_turn(kept, got, chip):
    n = kept.shape[0]
    return kernel_call(
        add_turn_kernel,
        "add_turn",
        (shape_of(kept.shape[1:], bf16),) * n,
        (chip, kept, got),
        in_specs=[smem, vmem, vmem],
    )


def add_halve_kernel(mine, *refs):
    parts, (stays, goes) = refs[:-2], refs[-2:]
    count = len(parts) // 2
    at = 0
    for kept, got in zip(parts[:count], parts[count:]):
        for o in range(kept.shape[0]):
            for out, side in ((stays, mine[0]), (goes, 1 - mine[0])):
                out[at] = (kept[o, side].astype(f32) + got[o, side].astype(f32)).astype(bf16)
            at += 1


def add_halve(kept, got, mine, outer):
    rows, width = kept[0].shape[1:]
    blocks = sum(part.shape[0] for part in kept)
    inner = blocks // (2 * outer)
    half = shape_of((outer, inner, rows, width), bf16)
    stays, goes = kernel_call(
        add_halve_kernel,
        "add_halve",
        (half, half),
        (mine, *[part.reshape(-1, 2, inner, rows, width) for part in (*kept, *got)]),
        in_specs=[smem] + [vmem] * (len(kept) + len(got)),
        megabytes=40,
    )
    return stays.reshape(-1, rows, width), goes.reshape(-1, rows, width)


def adamw_update(master, moment_one, moment_two, gradient, step_rate, decay_weight):
    first_new = beta_one * moment_one + (1.0 - beta_one) * gradient
    second_new = beta_two * moment_two + (1.0 - beta_two) * gradient * gradient
    first_hat = first_new / (1.0 - beta_one**STEP)
    second_hat = second_new / (1.0 - beta_two**STEP)
    master_new = master - step_rate * (
        first_hat / (jnp.sqrt(second_hat) + adam_eps) + decay_weight * master
    )
    return (first_new, second_new, master_new)


def adamw_kernel(where, master, first, second, *refs, n_dp, own, padded, rate, decay):
    pieces, (first_ref, second_ref, master_ref, slots, joined) = refs[:-5], refs[-5:]
    for t, piece in enumerate(pieces):
        for o in range(2):
            slots[where[2 * t + o]] = piece[o, 0]
    for s in range(slots.shape[0]):
        for d in range(n_dp):
            start = (s * n_dp + d) * own
            joined[:, start : start + own] = slots[
                s, :, d * padded : d * padded + own
            ].astype(f32)
    first_ref[0], second_ref[0], master_ref[0] = adamw_update(
        master[0], first[0], second[0], joined[...], rate, decay
    )


def adamw_hidden(master, first, second, pieces, where, n_dp, padded, rate, decay):
    two, rows, ff = master.shape
    n_seq = 2 * len(pieces)
    own = ff // (n_seq * n_dp)
    block = pl.BlockSpec((1, rows, ff), lambda g: (g, 0, 0))
    part = pl.BlockSpec((2, 1, rows, n_dp * padded), lambda g: (0, g, 0, 0))
    return kernel_call(
        functools.partial(
            adamw_kernel, n_dp=n_dp, own=own, padded=padded, rate=rate, decay=decay
        ),
        "adamw_hidden",
        (shape_of(master.shape, f32),) * 3,
        (where, master, first, second, *pieces),
        megabytes=44,
        grid=(two,),
        in_specs=[smem] + [block] * 3 + [part] * len(pieces),
        out_specs=(block,) * 3,
        scratch_shapes=[
            pltpu.VMEM((n_seq, rows, n_dp * padded), bf16),
            pltpu.VMEM((rows, ff), f32),
        ],
    )


def assemble_kernel(where, *refs, splits, counts):
    ins, outs, sems = refs[: len(counts)], refs[len(counts) : -1], refs[-1]
    copies = []
    entry = 0
    for ref, (column, count) in zip(ins, counts):
        for i in range(count):
            for out, start, width in splits[column]:
                copies.append(
                    pltpu.make_async_copy(
                        ref.at[i, :, pl.ds(start, width)],
                        outs[out[0]].at[where[entry], :, pl.ds(out[1], width)],
                        sems.at[len(copies)],
                    )
                )
            entry += 1
    for copy in copies:
        copy.start()
    for copy in copies:
        copy.wait()


def assemble(pieces, where, splits, out_widths):
    counts = [(column, array.shape[0]) for array, column in pieces]
    rows = pieces[0][0].shape[1]
    blocks = sum(count for column, count in counts if column == 0)
    n_copies = sum(count * len(splits[column]) for column, count in counts)
    return kernel_call(
        functools.partial(assemble_kernel, splits=splits, counts=counts),
        "assemble",
        tuple(shape_of((blocks, rows, w), bf16) for w in out_widths),
        (where.astype(jnp.int32), *[array for array, _ in pieces]),
        in_specs=[smem] + [anywhere] * len(pieces),
        out_specs=(vmem,) * len(out_widths),
        scratch_shapes=[pltpu.SemaphoreType.DMA((n_copies,))],
    )


def seq_perm(values, chips, flip):
    count = lax.axis_size("seq")
    return lax.ppermute(
        values, "seq", [(i, ((i + 2 * chips) % count) ^ flip) for i in range(count)]
    )


def dp_perm(values, bit):
    return lax.ppermute(values, "dp", [(i, i ^ bit) for i in range(lax.axis_size("dp"))])


def dp_bits():
    return [1 << i for i in range(lax.axis_size("dp").bit_length() - 1)]


def pick(values, index, axis):
    return lax.dynamic_index_in_dim(values, index, axis, keepdims=False)


def places_of():
    n_chips = lax.axis_size("seq") // 2
    seq_at = lax.axis_index("seq")
    return n_chips, seq_at // 2, seq_at % 2, lax.axis_size("dp"), lax.axis_index("dp")


def swap(values):
    return seq_perm(values, 0, 1)


def sent_pieces(values):
    return [values] + [seq_perm(values, t, 0) for t in range(1, lax.axis_size("seq") // 2)]


def shards(
    tokens,
    cotangent,
    positions,
    qkv_master,
    qkv_first,
    qkv_second,
    out_master,
    out_first,
    out_second,
    gate_up_master,
    gate_up_first,
    gate_up_second,
    down_master,
    down_first,
    down_second,
    small_master,
    small_first,
    small_second,
):
    n_chips, chip_at, core_at, n_dp, dp_at = places_of()
    n_seq = 2 * n_chips
    n_all = n_seq * n_dp
    bits = dp_bits()
    rows_own, qkv_width = qkv_master.shape
    half = qkv_width // 2
    small_own = small_master.shape[0]
    ff_dev = down_master.shape[0]
    ff_pad = -(-ff_dev // 16) * 16
    ff_own = n_dp * ff_pad
    inputs = tokens[0]
    upstream = cotangent[0]
    tok_rows = inputs.shape[0]
    seq_length = positions.shape[1]
    shifts = list(range(1, n_chips))

    ring_chips = [(chip_at - t) % n_chips for t in range(n_chips)]
    ring_order = jnp.stack(
        [chip * 2 + (core_at ^ flip) for chip in ring_chips for flip in range(2)]
    ).astype(jnp.int32)
    bases = positions[0, ::PIECE].reshape(n_seq, tok_rows // PIECE)
    key_bases = jnp.take(bases, ring_order, axis=0)
    query_bases = key_bases[0]
    key_bases = key_bases.reshape(-1)
    own_places = lax.dynamic_slice_in_dim(
        positions[0], (chip_at * 2 + core_at) * tok_rows, tok_rows, 0
    )
    cosine, sine = rotary_tables(own_places)

    small_block = jnp.pad(
        small_master.astype(bf16), (0, rows_own * HD - small_own)
    ).reshape(rows_own, HD)
    packed = jnp.concatenate([small_block, qkv_master.astype(bf16)], axis=1)
    qkv_ring = sent_pieces(packed)
    core_side = core_at.reshape(1).astype(jnp.int32)
    chip_side = chip_at.reshape(1).astype(jnp.int32)
    bit_sides = {bit: ((dp_at // bit) % 2).reshape(1).astype(jnp.int32) for bit in bits}
    cut_kept, cut_sent = cut_hidden(gate_up_master, core_side, n_chips, n_dp, ff_pad)
    to_send = turn_pairs([cut_kept], [swap(cut_sent)], chip_side, n_chips)
    qkv_ring, to_send, cosine, sine = fence(qkv_ring, to_send, cosine, sine)

    def exchange(shift):
        return seq_perm(to_send[shift], shift, 0)

    w_out = lax.all_gather(
        after(out_master.astype(bf16), *to_send), ("seq", "dp"), axis=0, tiled=True
    )

    columns = ((0, HD + half), (HD + half, HD + qkv_width))
    orders = (bits, bits[::-1])
    held = list(stack_columns(qkv_ring, columns))
    flips = [[0], [0]]
    gate_up_pieces = {0: to_send[0]}
    groups = [shifts[:1], shifts[-1:], shifts[1:-1]] if n_chips > 2 else [shifts, [], []]
    for stage in range(len(bits)):
        got = [dp_perm(h, order[stage]) for h, order in zip(held, orders)]
        if stage == len(bits) - 1:
            swapped = [swap(h) for h in held]
        for shift in groups[min(stage, 1)] if stage < 2 else []:
            gate_up_pieces[shift] = exchange(shift)
        got, held, gate_up_pieces = fence(got, held, gate_up_pieces)
        flips = [f + [k ^ order[stage] for k in f] for f, order in zip(flips, orders)]
        if stage < len(bits) - 1:
            held = [jnp.concatenate([h, g], axis=0) for h, g in zip(held, got)]
    (swapped,) = fence(swapped)
    for shift in groups[2]:
        gate_up_pieces[shift] = exchange(shift)
    down_cuts = ((0, D // 2), (D // 2, D))
    down_share = after(jnp.pad(down_master.astype(bf16), ((0, ff_pad - ff_dev), (0, 0))), *got)
    down_pieces, down_where = [], []
    for column, ((lo, hi), order) in enumerate(zip(down_cuts, orders)):
        parts, ks = [down_share[:, lo:hi]], [0]
        for bit in order:
            parts += [dp_perm(part, bit) for part in parts]
            ks += [k ^ bit for k in ks]
        down_pieces += [(part[None], column) for part in parts]
        down_where += [dp_at ^ k for k in ks]
    got_swapped = [swap(g) for g in got]
    pieces, where = [], []
    for column in range(2):
        for flip, part, ks in (
            (0, held[column], flips[column][: n_dp // 2]),
            (0, got[column], flips[column][n_dp // 2 :]),
            (1, swapped[column], flips[column][: n_dp // 2]),
            (1, got_swapped[column], flips[column][n_dp // 2 :]),
        ):
            pieces.append((part, column))
            where += [
                (chip * 2 + (core_at ^ flip)) * n_dp + (dp_at ^ k) for k in ks for chip in ring_chips
            ]
    w_qkv, small_blocks = assemble(
        pieces,
        jnp.stack(where),
        ((((1, 0), 0, HD), ((0, 0), HD, half)), (((0, half), 0, half),)),
        (qkv_width, HD),
    )
    w_qkv = w_qkv.reshape(D, qkv_width)
    small_params = small_blocks.reshape(n_all, rows_own * HD)[:, :small_own].reshape(1, -1)
    small_params = small_params.astype(f32)
    gain_one = small_params[:, :D]
    gain_two = small_params[:, D : 2 * D]
    qkv_bias = small_params[:, 2 * D :]
    normed_one, key_value = project_kv(inputs, w_qkv, gain_one, qkv_bias, cosine, sine)
    gate_up_held = [
        jnp.concatenate([gate_up_pieces[t] for t in ts], axis=0)
        for ts in (range(n_chips // 2), range(n_chips // 2, n_chips))
    ]
    (w_down,) = assemble(
        down_pieces,
        jnp.stack(down_where),
        tuple((((0, lo), 0, hi - lo),) for lo, hi in down_cuts),
        (D,),
    )
    w_down = w_down.reshape(ff_own, D)
    normed_one, key_value, gate_up_held, w_down = fence(normed_one, key_value, gate_up_held, w_down)

    kv_ring = sent_pieces(key_value)
    gate_up_parts = [
        [held, dp_perm(held, order[0])] for held, order in zip(gate_up_held, orders)
    ]
    gate_up_flips = [[0, order[0]] for order in orders]
    queries = project_q(normed_one, w_qkv, qkv_bias, cosine, sine)
    kv_swapped = [swap(kv_ring[0])] + [swap(after(piece, queries)) for piece in kv_ring[1:]]
    kv_ring, kv_swapped, gate_up_parts, queries, upstream = fence(
        kv_ring, kv_swapped, gate_up_parts, queries, upstream
    )

    def cross(start, stop, stage):
        for parts, flips_of, order in zip(gate_up_parts, gate_up_flips, orders):
            parts += [dp_perm(piece, order[stage]) for piece in parts[start:stop]]
            flips_of += [k ^ order[stage] for k in flips_of[start:stop]]

    upstream_ring = [upstream, seq_perm(upstream, 1, 0)]
    cross(0, 1 if len(bits) == 2 else 2, 1)
    attended, logsum, key_value_all = attend(
        queries, [piece for pair in zip(kv_ring, kv_swapped) for piece in pair], query_bases, key_bases
    )
    gate_up_parts, upstream_ring, attended, logsum, key_value_all = fence(
        gate_up_parts, upstream_ring, attended, logsum, key_value_all
    )

    def ring_step(pieces):
        return pieces + [seq_perm(pieces[-1], 1, 0)] if len(pieces) < n_chips else pieces

    upstream_ring = ring_step(upstream_ring)
    if len(bits) == 2:
        cross(1, 2, 1)
    else:
        cross(0, 4, 2)
    upstream_swapped = [swap(piece) for piece in upstream_ring[:2]]
    residual, normed_two, attended_low = out_project(inputs, attended, w_out, gain_two)
    normed_ring, normed_swapped = [normed_two], [swap(normed_two)]
    gate_up_parts, upstream_ring, upstream_swapped, normed_ring, normed_swapped, residual = fence(
        gate_up_parts, upstream_ring, upstream_swapped, normed_ring, normed_swapped, residual
    )

    pieces, where = [], []
    for column, (parts, flips_of) in enumerate(zip(gate_up_parts, gate_up_flips)):
        slots = ring_order[:n_chips] if column == 0 else ring_order[n_chips:]
        for part, k in zip(parts, flips_of):
            pieces.append((part.reshape(-1, rows_own, ff_own), 0))
            block = slots * n_dp + (dp_at ^ k)
            where.append(jnp.stack([block, n_all + block], axis=1).reshape(-1))
    (w_gate_up,) = assemble(
        pieces, jnp.concatenate(where), ((((0, 0), 0, ff_own),),), (ff_own,)
    )
    w_gate_up = w_gate_up.reshape(2, D, ff_own)
    out_parts, kept = [], ()
    running = None
    for slot in range(n_chips):
        sent = None if running is None else seq_perm(running, 1, 0)
        normed_ring = ring_step(normed_ring)
        upstream_ring = ring_step(upstream_ring)
        out_own, out_other, grad_own, grad_other, *kept = feed_forward(
            (normed_ring[slot], normed_swapped[slot]),
            (upstream_ring[slot], upstream_swapped[slot]),
            w_gate_up,
            w_down,
            slot,
            n_chips,
            kept,
        )
        out_parts.append((out_own, out_other))
        grad_swapped = swap(grad_other)
        if slot + 1 < n_chips:
            normed_swapped = normed_swapped + [swap(after(normed_ring[slot + 1], grad_own))]
        if slot + 2 < n_chips and len(upstream_swapped) < slot + 3:
            upstream_swapped = upstream_swapped + [swap(after(upstream_ring[slot + 2], grad_own))]
        if slot == 0:
            grad_first = (grad_own, grad_swapped)
        elif sent is None:
            running = add(grad_own, grad_swapped)
        else:
            running = add(grad_own, grad_swapped, after(sent, grad_own))
        running, normed_ring, normed_swapped, upstream_ring, upstream_swapped, out_parts, kept = fence(
            running, normed_ring, normed_swapped, upstream_ring, upstream_swapped, out_parts, kept
        )
        if slot == 1:
            out_pair = (out_parts[1][0], swap(out_parts[1][1]))
            ring_first = add(*out_pair)

    grad_ring = jnp.zeros_like(grad_first[0]) if running is None else seq_perm(running, 1, 0)
    normed_all, ffn_all, hidden_all, gate_grads_all, up_grads_all = kept
    first_split = (
        jnp.concatenate([bit_sides[order[0]] for order in orders]),
        tuple(order[0] for order in orders),
    )
    halves = [
        weight_grad(
            normed_all,
            (gate_grads_all, up_grads_all),
            split=first_split,
            rows=rows_own,
            part=(part, 2),
        )
        for part in range(2)
    ]
    out_running = seq_perm(ring_first, 1, 0) if n_chips > 1 else None
    out_pairs = [
        (own, swap(after(other, *halves[0][0]))) for t, (own, other) in enumerate(out_parts) if t != 1
    ]
    out_total = [ring_first] + [add(own, other) for own, other in out_pairs[1:]]
    if n_chips > 2:
        out_running = add(after(out_running, *halves[0][0]), out_total[1])
    grad_ring, halves, out_pairs, out_total, out_running = fence(
        grad_ring, halves, out_pairs, out_total, out_running
    )

    got_one = [dp_perm(goes, order[0]) for (_, goes), order in zip(halves[0], orders)]
    if n_chips > 2:
        out_running = seq_perm(out_running, 1, 0)
    residual_grads, branch_grads, attended_grads, gain_two_grad = norm_back(
        grad_ring, *grad_first, residual, upstream, gain_two, w_out
    )
    query_pre, kv_grad_own, kv_grad_other = attend_back(
        queries,
        key_value_all,
        attended_grads,
        attended,
        logsum,
        query_bases,
        key_bases,
        cosine,
        sine,
    )
    got_one, kv_grad_own, kv_grad_other, query_pre, branch_grads, out_running = fence(
        got_one, kv_grad_own, kv_grad_other, query_pre, branch_grads, out_running
    )
    own_parts = kv_grad_own.reshape(n_chips, tok_rows, 2 * KVW)
    other_parts = swap(kv_grad_other).reshape(n_chips, tok_rows, 2 * KVW)
    kv_sum = add_turn(own_parts, other_parts, jnp.zeros_like(chip_side))
    kv_sum, halves, query_pre, branch_grads, kept = fence(
        kv_sum, halves, query_pre, branch_grads, kept
    )

    def next_split(kept_parts, got, done_bits, left_bits):
        rest = [bit for bit in bits[::-1] if bit not in done_bits]
        bit = left_bits[0]
        lead = sum(part.shape[0] for part in kept_parts) // 2 ** len(rest)
        return add_halve(kept_parts, got, bit_sides[bit], lead * 2 ** rest.index(bit))

    kv_got = [seq_perm(kv_sum[t], n_chips - t, 0) for t in range(1, n_chips)]
    got_two = [dp_perm(goes, order[0]) for (_, goes), order in zip(halves[1], orders)]
    by_core = (core_side, (n_dp,))
    (query_split,) = weight_grad(normed_one[None], (query_pre[None],), split=by_core, rows=rows_own)
    (out_split,) = weight_grad(
        attended_low[None], (branch_grads[None],), split=by_core, rows=rows_own
    )
    (down_grad,) = weight_grad(kept[2], (kept[1],))
    if n_chips > 3:
        out_running = add(out_running, out_total[2])
    kv_got, got_two, query_split, out_split, down_grad, out_running = fence(
        kv_got, got_two, query_split, out_split, down_grad, out_running
    )

    if n_chips > 3:
        out_running = seq_perm(out_running, 1, 0)
    gate_up_split = [
        next_split([one[0], two[0]], [got, other], order[:1], order[1:])
        for one, two, got, other, order in zip(*halves, got_one, got_two, orders)
    ]
    gate_up_sums = [dp_perm(goes, order[1]) for (_, goes), order in zip(gate_up_split, orders)]
    both = [(split[0], swap(split[1])) for split in (query_split, out_split)]
    key_value_pre, input_grads, gain_one_grad, bias_grad = input_back(
        inputs,
        gain_one,
        w_qkv,
        query_pre,
        cosine,
        sine,
        residual_grads,
        kv_sum[0],
        kv_got,
    )
    ((kv_stays, kv_goes),) = weight_grad(
        normed_one[None], (key_value_pre[None],), split=by_core, rows=rows_own
    )
    gate_up_split, gate_up_sums, both, input_grads, kv_stays, kv_goes, out_running, small_parts = fence(
        gate_up_split,
        gate_up_sums,
        both,
        input_grads,
        kv_stays,
        kv_goes,
        out_running,
        (gain_one_grad, gain_two_grad, bias_grad),
    )

    ready = []
    for split, got, order in zip(gate_up_split, gate_up_sums, orders):
        kept_part = split[0]
        for i in range(2, len(order)):
            kept_part, goes = next_split([kept_part], [got], order[:i], order[i:])
            got = dp_perm(goes, order[i])
        ready.append(add_halve([kept_part], [got], core_side, n_chips))
    both = [
        next_split([kept_part], [got], [], order) for (kept_part, got), order in zip(both, orders)
    ]
    to_send = turn_pairs(
        [kept_part for kept_part, _ in ready],
        [swap(sent) for _, sent in ready],
        chip_side,
        n_chips,
    )
    small_grad = jnp.concatenate(small_parts, axis=1).astype(bf16)
    small_grad = jnp.pad(
        small_grad.reshape(n_all, small_own), ((0, 0), (0, rows_own * HD - small_own))
    ).reshape(n_chips, 2, n_dp, rows_own, HD)
    kv_stays = jnp.concatenate(
        [pick(small_grad, core_at, 1).reshape(-1, rows_own, HD), kv_stays], axis=2
    )
    kv_goes = jnp.concatenate(
        [pick(small_grad, 1 - core_at, 1).reshape(-1, rows_own, HD), kv_goes], axis=2
    )
    kv_side = (kv_stays, swap(kv_goes))
    to_send, both, kv_side, out_running = fence(to_send, both, kv_side, out_running)

    gate_up_owned = {0: to_send[0]}
    both_got = [dp_perm(goes, order[0]) for (_, goes), order in zip(both, orders)]
    for shift in groups[0] + groups[1]:
        gate_up_owned[shift] = exchange(shift)
    kv_split = next_split([kv_side[0]], [kv_side[1]], [], orders[0])
    kv_sums = dp_perm(kv_split[1], orders[0][0])
    down_split = split_columns(
        down_grad.reshape(n_dp, ff_pad, D),
        first_split[0],
        down_cuts,
        tuple(order[0] for order in orders),
    )
    gate_up_owned, both_got, kv_split, kv_sums, down_split = fence(
        gate_up_owned, both_got, kv_split, kv_sums, down_split
    )

    for shift in groups[2]:
        gate_up_owned[shift] = exchange(shift)
    three = [(both[0], both_got[0], orders[0]), (both[1], both_got[1], orders[1])]
    three.append((kv_split, kv_sums, orders[0]))
    rest_send = []
    for (kept_part, _), got, order in three:
        for i in range(1, len(order)):
            kept_part, goes = next_split([kept_part], [got], order[:i], order[i:])
            got = dp_perm(goes, order[i])
        rest_send.append(add_turn(kept_part, got, chip_side))
    down_got = [dp_perm(goes, order[0]) for (_, goes), order in zip(down_split, orders)]
    gate_up_owned, rest_send, down_got = fence(gate_up_owned, rest_send, down_got)
    down_owned = []
    for (kept_part, _), got, order in zip(down_split, down_got, orders):
        for i in range(1, len(order)):
            kept_part, goes = next_split([kept_part], [got], order[:i], order[i:])
            got = dp_perm(goes, order[i])
        down_owned.append(kept_part[0, :ff_dev].astype(f32) + got[0, :ff_dev].astype(f32))
    down_owned = jnp.concatenate(down_owned, axis=1)

    rest_send = [
        jnp.concatenate([parts[t] for parts in rest_send], axis=1) for t in range(n_chips)
    ]
    total = rest_send[0].astype(f32)
    for shift in shifts:
        total = total + seq_perm(rest_send[shift], shift, 0).astype(f32)
    for t in range(4, n_chips):
        out_running = seq_perm(add(out_running, out_total[t - 1]), 1, 0)
    outputs = residual + out_pairs[0][0].astype(f32) + out_pairs[0][1].astype(f32)
    if n_chips > 1:
        outputs = outputs + out_running.astype(f32)
    outputs = outputs.astype(bf16)
    gate_up_new = adamw_hidden(
        gate_up_master,
        gate_up_first,
        gate_up_second,
        [gate_up_owned[t] for t in range(n_chips)],
        ring_order,
        n_dp,
        ff_pad,
        0.064,
        0.1,
    )
    query_owned, out_owned, small_owned, kv_owned = jnp.split(
        total, (D, 2 * D, 2 * D + HD), axis=1
    )
    qkv_owned = jnp.concatenate([query_owned, kv_owned], axis=1)
    small_owned = small_owned.reshape(-1)[:small_own]

    qkv_new = adamw_update(qkv_master, qkv_first, qkv_second, qkv_owned, 0.09, 0.1)
    out_new = adamw_update(out_master, out_first, out_second, out_owned, 0.18, 0.1)
    down_new = adamw_update(down_master, down_first, down_second, down_owned, 0.026, 0.1)
    small_new = adamw_update(small_master, small_first, small_second, small_owned, 0.6, 0.0)
    return (
        outputs[None],
        input_grads[None],
        *qkv_new,
        *out_new,
        *gate_up_new,
        *down_new,
        *small_new,
    )


def solution(mesh):
    in_specs = (
        P("dp", "seq", None),
        P("dp", "seq", None),
        P("dp", None),
        P(("seq", "dp"), None),
        P(("seq", "dp"), None),
        P(("seq", "dp"), None),
        P(("seq", "dp"), None),
        P(("seq", "dp"), None),
        P(("seq", "dp"), None),
        P(None, ("seq", "dp"), None),
        P(None, ("seq", "dp"), None),
        P(None, ("seq", "dp"), None),
        P(("seq", "dp"), None),
        P(("seq", "dp"), None),
        P(("seq", "dp"), None),
        P(("seq", "dp")),
        P(("seq", "dp")),
        P(("seq", "dp")),
    )
    out_specs = (
        P("dp", "seq", None),
        P("dp", "seq", None),
        P(("seq", "dp"), None),
        P(("seq", "dp"), None),
        P(("seq", "dp"), None),
        P(("seq", "dp"), None),
        P(("seq", "dp"), None),
        P(("seq", "dp"), None),
        P(None, ("seq", "dp"), None),
        P(None, ("seq", "dp"), None),
        P(None, ("seq", "dp"), None),
        P(("seq", "dp"), None),
        P(("seq", "dp"), None),
        P(("seq", "dp"), None),
        P(("seq", "dp")),
        P(("seq", "dp")),
        P(("seq", "dp")),
    )
    return jax.shard_map(shards, mesh=mesh, in_specs=in_specs, out_specs=out_specs, check_vma=False)
```

```python
import functools

import jax
import jax.numpy as jnp
from jax import lax
from jax.experimental import pallas as pl
from jax.experimental.pallas import tpu as pltpu
from jax.sharding import PartitionSpec as P

D = 1536
HEADS = 12
KVH = 2
HD = 128
STEP = 10
KVW = KVH * HD
PIECE = 128


norm_eps = 1e-06
rope_base = 1000000.0
beta_one = 0.9
beta_two = 0.95
adam_eps = 1e-08
masked_score = -1e30
log2_e = 1.4426950408889634
bf16 = jnp.bfloat16
f32 = jnp.float32
vmem = pl.BlockSpec(memory_space=pltpu.VMEM)
smem = pl.BlockSpec(memory_space=pltpu.SMEM)
anywhere = pl.BlockSpec(memory_space=pl.ANY)


def shape_of(dims, kind):
    return jax.ShapeDtypeStruct(dims, kind)


def kernel_call(kernel, name, out_shape, operands, megabytes=32, **options):
    return pl.pallas_call(
        kernel,
        name=name,
        out_shape=out_shape,
        compiler_params=pltpu.CompilerParams(vmem_limit_bytes=megabytes << 20),
        cost_estimate=pl.CostEstimate(flops=10**6, bytes_accessed=10**6, transcendentals=0),
        **options,
    )(*operands)


def after(values, *others):
    return lax.optimization_barrier((values,) + others)[0]


def fence(*groups):
    flat, tree = jax.tree.flatten(groups)
    return jax.tree.unflatten(tree, lax.optimization_barrier(tuple(flat)))


def dot(left, right):
    return jnp.dot(left, right, preferred_element_type=f32)


def dot_transposed(left, right):
    return lax.dot_general(left, right, (((1,), (1,)), ((), ())), preferred_element_type=f32)


def rotary_tables(places):
    half_size = HD // 2
    freqs = rope_base ** (-(jnp.arange(half_size).astype(f32) * (2.0 / HD)))
    angles = places.astype(f32)[:, None] * freqs[None, :]
    cosine, sine = jnp.cos(angles), jnp.sin(angles)
    return jnp.concatenate([cosine, cosine], axis=1), jnp.concatenate([-sine, sine], axis=1)


def rms_scale(values):
    return lax.rsqrt(jnp.mean(values * values, axis=-1, keepdims=True) + norm_eps)


def swap_halves(values):
    return pltpu.roll(values, HD // 2, 1)


def head(index):
    return slice(index * HD, (index + 1) * HD)


def project_kv_kernel(tokens, w_qkv, gain, bias, cosine, sine, normed_ref, kv_ref):
    inputs = tokens[...].astype(f32)
    normed = (inputs * rms_scale(inputs) * gain[...]).astype(bf16)
    normed_ref[...] = normed
    rows = dot(normed, w_qkv[...]) + bias[:, D:]
    for j in range(KVH):
        part = rows[:, head(j)]
        kv_ref[:, head(j)] = (part * cosine[...] + swap_halves(part) * sine[...]).astype(bf16)
    kv_ref[:, KVW:] = rows[:, KVW:].astype(bf16)


def project_q_kernel(normed, w_qkv, bias, cosine, sine, query_ref):
    rows = dot(normed[...], w_qkv[...]) + bias[:, :D]
    for j in range(HEADS):
        part = rows[:, head(j)]
        query_ref[:, head(j)] = (part * cosine[...] + swap_halves(part) * sine[...]).astype(bf16)


def project_kv(tokens, w_qkv, gain, bias, cosine, sine):
    rows = tokens.shape[0]
    return kernel_call(
        project_kv_kernel,
        "project_kv",
        (shape_of((rows, D), bf16), shape_of((rows, 2 * KVW), bf16)),
        (tokens, w_qkv, gain, bias, cosine, sine),
        megabytes=58,
        grid=(1,),
        in_specs=[vmem, pl.BlockSpec((D, 2 * KVW), lambda i: (0, D // (2 * KVW)))] + [vmem] * 4,
        out_specs=(vmem, vmem),
    )


def project_q(normed, w_qkv, bias, cosine, sine):
    return kernel_call(
        project_q_kernel,
        "project_q",
        shape_of(normed.shape, bf16),
        (normed, w_qkv, bias, cosine, sine),
        megabytes=58,
        grid=(1,),
        in_specs=[vmem, pl.BlockSpec((D, D), lambda i: (0, 0))] + [vmem] * 3,
        out_specs=vmem,
    )


def mask_keys(values, query_bases, key_bases, first_run, fill):
    later = lax.broadcasted_iota(jnp.int32, (PIECE, PIECE), 0) - lax.broadcasted_iota(
        jnp.int32, (PIECE, PIECE), 1
    )
    keys, queries = values.shape
    rows = []
    for r in range(keys // PIECE):
        down = slice(r * PIECE, (r + 1) * PIECE)
        row = []
        for q in range(queries // PIECE):
            gap = query_bases[q] - key_bases[first_run + r]
            row.append(jnp.where(later <= gap, values[down, q * PIECE : (q + 1) * PIECE], fill))
        rows.append(jnp.concatenate(row, axis=1))
    return jnp.concatenate(rows, axis=0)


def attend_kernel(query_bases, key_bases, q_ref, *refs):
    pieces, (out_ref, lse_ref, kv_ref) = refs[:-3], refs[-3:]
    rows = q_ref.shape[0]
    for i, piece in enumerate(pieces):
        kv_ref[i * rows : (i + 1) * rows, :] = piece[...]
    groups = HEADS // KVH
    scale = HD**-0.5 * log2_e
    for kv in range(KVH):
        values = kv_ref[:, head(KVH + kv)].T
        for h in range(kv * groups, (kv + 1) * groups):
            queries = q_ref[:, head(h)]
            scores = []
            for run in range(key_bases.shape[0]):
                keys = kv_ref[run * PIECE : (run + 1) * PIECE, head(kv)]
                part = dot_transposed(keys, queries)
                scores.append(mask_keys(part, query_bases, key_bases, run, masked_score))
            scores = jnp.concatenate(scores, axis=0)
            top = jnp.max(scores, axis=0, keepdims=True)
            weights = jnp.exp2((scores - top) * scale)
            total = jnp.sum(weights, axis=0, keepdims=True)
            mixed = dot(values, weights.astype(bf16))
            out_ref[:, head(h)] = (mixed / total).T
            lse_ref[h : h + 1, :] = top * scale + jnp.log2(total)


def attend(queries, pieces, query_bases, key_bases):
    rows, total = queries.shape[0], key_bases.shape[0] * PIECE
    return kernel_call(
        attend_kernel,
        "attend",
        (
            shape_of((rows, D), f32),
            shape_of((HEADS, rows), f32),
            shape_of((total, 2 * KVW), bf16),
        ),
        (query_bases, key_bases, queries, *pieces),
        in_specs=[smem] * 2 + [vmem] * (1 + len(pieces)),
    )


def out_kernel(tokens, attended, w_out, gain, residual_ref, normed_ref, low_ref):
    low = attended[...].astype(bf16)
    low_ref[...] = low
    residual = tokens[...].astype(f32) + dot(low, w_out[...])
    residual_ref[...] = residual
    normed_ref[...] = (residual * rms_scale(residual) * gain[...]).astype(bf16)


def out_project(tokens, attended, w_out, gain):
    dims = tokens.shape
    return kernel_call(
        out_kernel,
        "out_project",
        (shape_of(dims, f32), shape_of(dims, bf16), shape_of(dims, bf16)),
        (tokens, attended, w_out, gain),
    )


def ffn_kernel(
    normed_own, normed_other, grad_own, grad_other, w_gate_up, w_down, *refs, earlier
):
    refs = refs[earlier:]
    out_refs, grad_refs = refs[:2], refs[2:4]
    normed_ref, ffn_grad_ref, hidden_ref, gate_ref, up_ref = refs[4:]
    rows = normed_own.shape[0]
    for i, (normed_in, grad_in) in enumerate(((normed_own, grad_own), (normed_other, grad_other))):
        to = slice(i * rows, (i + 1) * rows)
        normed, ffn_grad = normed_in[...], grad_in[...]
        normed_ref[0, to, :] = normed
        ffn_grad_ref[0, to, :] = ffn_grad
        gate = dot(normed, w_gate_up[0])
        up = dot(normed, w_gate_up[1])
        sigmoid = 1.0 / (1.0 + jnp.exp(-gate))
        silu = gate * sigmoid
        hidden = (silu * up).astype(bf16)
        hidden_ref[0, to, :] = hidden
        out_refs[i][...] = dot(hidden, w_down[...]).astype(bf16)
        hidden_grad = dot_transposed(ffn_grad, w_down[...])
        gate_grad = (hidden_grad * up * sigmoid * (1.0 + gate * (1.0 - sigmoid))).astype(bf16)
        up_grad = (hidden_grad * silu).astype(bf16)
        gate_ref[0, to, :] = gate_grad
        up_ref[0, to, :] = up_grad
        grad_refs[i][...] = (
            dot_transposed(gate_grad, w_gate_up[0]) + dot_transposed(up_grad, w_gate_up[1])
        ).astype(bf16)


def feed_forward(normed, grads, w_gate_up, w_down, slot, slots, kept):
    rows, width = normed[0].shape
    ff_own = w_down.shape[0]
    token = shape_of((rows, width), bf16)
    widths = (width, width, ff_own, ff_own, ff_own)
    operands = (*normed, *grads, w_gate_up, w_down)
    return kernel_call(
        functools.partial(ffn_kernel, earlier=len(kept)),
        "feed_forward",
        (token,) * 4 + tuple(shape_of((slots, 2 * rows, w), bf16) for w in widths),
        (*operands, *kept),
        grid=(1,),
        in_specs=[vmem] * len(operands) + [anywhere] * len(kept),
        out_specs=(vmem,) * 4
        + tuple(pl.BlockSpec((1, 2 * rows, w), lambda i: (slot, 0, 0)) for w in widths),
        input_output_aliases={len(operands) + i: 4 + i for i in range(len(kept))},
    )


def norm_back_kernel(
    got, own, other, residual_ref, cotangent, gain, w_out, grad_ref, low_ref, back_ref, gain_ref
):
    normed_grad = got[...].astype(f32) + own[...].astype(f32) + other[...].astype(f32)
    residual = residual_ref[...]
    scale = rms_scale(residual)
    unit = residual * scale
    gain_ref[...] = jnp.sum(normed_grad * unit, axis=0, keepdims=True)
    weighted = normed_grad * gain[...]
    grad = cotangent[...].astype(f32) + scale * (
        weighted - unit * jnp.mean(weighted * unit, axis=-1, keepdims=True)
    )
    grad_ref[...] = grad
    low = grad.astype(bf16)
    low_ref[...] = low
    back_ref[...] = dot_transposed(low, w_out[...]).astype(bf16)


def norm_back(got, own, other, residual, cotangent, gain, w_out):
    dims = residual.shape
    return kernel_call(
        norm_back_kernel,
        "norm_back",
        (shape_of(dims, f32), shape_of(dims, bf16), shape_of(dims, bf16), shape_of((1, D), f32)),
        (got, own, other, residual, cotangent, gain, w_out),
    )


def attend_back_kernel(
    query_bases,
    key_bases,
    q_ref,
    kv_ref,
    grad_ref,
    out_ref,
    lse_ref,
    cosine,
    sine,
    q_grad_ref,
    kv_own_ref,
    kv_other_ref,
    q_rows,
    grad_rows,
    deltas,
    q_sums,
):
    rows = q_ref.shape[0]
    groups = HEADS // KVH
    scale = HD**-0.5
    for kv in range(KVH):
        for j in range(groups):
            part = slice(j * rows, (j + 1) * rows)
            columns = head(kv * groups + j)
            q_rows[part, :] = q_ref[:, columns]
            grads = grad_ref[:, columns]
            grad_rows[part, :] = grads
            product = grads.astype(f32) * out_ref[:, columns]
            deltas[:, part] = jnp.sum(product.T, axis=0, keepdims=True)
        q_sums[...] = jnp.zeros_like(q_sums)

        @pl.loop(0, kv_ref.shape[0] // (2 * rows), unroll=2)
        def _(step):
            at = pl.ds(pl.multiple_of(step * (2 * rows), 2 * rows), 2 * rows)
            runs = 2 * rows // PIECE
            keys = kv_ref[at, head(kv)]
            values = kv_ref[at, head(KVH + kv)]
            key_sum = value_sum = None
            for j in range(groups):
                part = slice(j * rows, (j + 1) * rows)
                h = kv * groups + j
                queries, grads = q_rows[part, :], grad_rows[part, :]
                scores = dot_transposed(keys, queries)
                weights = jnp.exp2(scores * (scale * log2_e) - lse_ref[h : h + 1, :])
                weights = mask_keys(weights, query_bases, key_bases, step * runs, 0.0)
                weight_grads = dot_transposed(values, grads)
                score_grads = (weights * (weight_grads - deltas[:, part])).astype(bf16)
                value_part = dot(weights.astype(bf16), grads)
                key_part = dot(score_grads, queries)
                key_sum = key_part if key_sum is None else key_sum + key_part
                value_sum = value_part if value_sum is None else value_sum + value_part
                q_sums[part, :] += lax.dot_general(
                    score_grads, keys, (((0,), (0,)), ((), ())), preferred_element_type=f32
                )
            key_sum = (key_sum * scale).astype(bf16)
            value_sum = value_sum.astype(bf16)
            to = pl.ds(pl.multiple_of(step * rows, rows), rows)
            for ref, mine in ((kv_own_ref, slice(0, rows)), (kv_other_ref, slice(rows, 2 * rows))):
                ref[to, head(kv)] = key_sum[mine, :]
                ref[to, head(KVH + kv)] = value_sum[mine, :]

        for j in range(groups):
            part = q_sums[j * rows : (j + 1) * rows, :] * scale
            q_grad_ref[:, head(kv * groups + j)] = (
                part * cosine[...] - swap_halves(part) * sine[...]
            ).astype(bf16)


def attend_back(queries, key_value, grads, attended, lse, query_bases, key_bases, cosine, sine):
    rows, total = queries.shape[0], key_value.shape[0]
    groups = HEADS // KVH
    return kernel_call(
        attend_back_kernel,
        "attend_back",
        (
            shape_of((rows, D), bf16),
            shape_of((total // 2, 2 * KVW), bf16),
            shape_of((total // 2, 2 * KVW), bf16),
        ),
        (query_bases, key_bases, queries, key_value, grads, attended, lse, cosine, sine),
        in_specs=[smem] * 2 + [vmem] * 7,
        scratch_shapes=[
            pltpu.VMEM((groups * rows, HD), bf16),
            pltpu.VMEM((groups * rows, HD), bf16),
            pltpu.VMEM((1, groups * rows), f32),
            pltpu.VMEM((groups * rows, HD), f32),
        ],
    )


def input_kernel(
    tokens, gain, w_qkv, query_grad, cosine, sine, residual_grad, own, *refs
):
    got, (kv_ref, input_ref, gain_ref, bias_ref) = refs[:-4], refs[-4:]
    rows = own[...].astype(f32)
    for piece in got:
        rows = rows + piece[...].astype(f32)
    for j in range(KVH):
        part = rows[:, head(j)]
        kv_ref[:, head(j)] = (part * cosine[...] - swap_halves(part) * sine[...]).astype(bf16)
    kv_ref[:, KVW:] = rows[:, KVW:].astype(bf16)
    kv_grad = kv_ref[...]
    q_grad = query_grad[...]
    bias_ref[:, :D] = jnp.sum(q_grad.astype(f32), axis=0, keepdims=True)
    bias_ref[:, D:] = jnp.sum(kv_grad.astype(f32), axis=0, keepdims=True)
    normed_grad = dot_transposed(q_grad, w_qkv[:, :D]) + dot_transposed(kv_grad, w_qkv[:, D:])
    inputs = tokens[...].astype(f32)
    scale = rms_scale(inputs)
    unit = inputs * scale
    gain_ref[...] = jnp.sum(normed_grad * unit, axis=0, keepdims=True)
    weighted = normed_grad * gain[...]
    input_ref[...] = residual_grad[...] + scale * (
        weighted - unit * jnp.mean(weighted * unit, axis=-1, keepdims=True)
    )


def input_back(tokens, gain, w_qkv, query_grad, cosine, sine, residual_grad, own, got):
    rows = tokens.shape[0]
    return kernel_call(
        input_kernel,
        "input_back",
        (
            shape_of((rows, 2 * KVW), bf16),
            shape_of((rows, D), f32),
            shape_of((1, D), f32),
            shape_of((1, D + 2 * KVW), f32),
        ),
        (tokens, gain, w_qkv, query_grad, cosine, sine, residual_grad, own, *got),
        megabytes=58,
    )


def weight_grad_kernel(sides, left, *refs, count, inners, based):
    rights, refs = refs[:count], refs[count:]
    bases, outs = refs[: count * based], refs[count * based :]
    turned = left[...].reshape(-1, left.shape[-1]).T
    for i, right in enumerate(rights):
        result = dot(turned, right[...].reshape(-1, right.shape[-1]))
        if based:
            result = result + bases[i][...]
        if not inners:
            outs[i][...] = result.astype(outs[i].dtype)
            continue
        stays, goes = outs[2 * i], outs[2 * i + 1]
        rows = stays.shape[2]
        result = result.astype(bf16)
        for side, refs_of in ((0, (stays, goes)), (1, (goes, stays))):

            @pl.when(sides[i] == side)
            def _():
                for o in range(stays.shape[0]):
                    for bit in range(2):
                        for j in range(inners[i]):
                            block = (o * 2 + bit) * inners[i] + j
                            refs_of[bit][o, j] = result[block * rows : (block + 1) * rows]


def weight_grad(
    left, rights, slots=(0, 1), bases=(), split=None, rows=0, part=(0, 1), kind=bf16
):
    n_slots, tokens, m = left.shape
    n_slots = n_slots // slots[1]
    m = m // part[1]
    block = 3 * HD if m % (3 * HD) == 0 else HD
    steps = m // block
    first = part[0] * steps
    whole = pl.Buffered(buffer_count=1)
    sides, inners = split if split else (jnp.zeros((1,), jnp.int32), ())
    out_shape, out_specs = [], []
    for i, right in enumerate(rights):
        n = right.shape[-1]
        if not inners:
            out_shape.append(shape_of((m, n), kind))
            out_specs.append(pl.BlockSpec((block, n), lambda i: (i, 0)))
            continue
        outer = block // (2 * inners[i] * rows)
        for _ in range(2):
            out_shape.append(shape_of((steps * outer, inners[i], rows, n), bf16))
            out_specs.append(pl.BlockSpec((outer, inners[i], rows, n), lambda i: (i, 0, 0, 0)))
    outs = kernel_call(
        functools.partial(
            weight_grad_kernel, count=len(rights), inners=inners, based=int(bool(bases))
        ),
        "weight_grad",
        tuple(out_shape),
        (sides, left, *rights, *bases),
        megabytes=44,
        grid=(steps,),
        in_specs=[
            smem,
            pl.BlockSpec((n_slots, tokens, block), lambda i: (slots[0], 0, i + first)),
        ]
        + [
            pl.BlockSpec(
                (n_slots, tokens, right.shape[-1]),
                lambda i: (slots[0], 0, 0),
                pipeline_mode=whole,
            )
            for right in rights
        ]
        + [pl.BlockSpec((block, base.shape[1]), lambda i: (i + first, 0)) for base in bases],
        out_specs=tuple(out_specs),
    )
    if not inners:
        return outs
    outs = [out.reshape((-1,) + out.shape[2:]) for out in outs]
    return [(outs[2 * i], outs[2 * i + 1]) for i in range(len(rights))]


def stack_kernel(*refs, cuts):
    pieces, outs = refs[: -len(cuts)], refs[-len(cuts) :]
    for i, piece in enumerate(pieces):
        for out, (lo, hi) in zip(outs, cuts):
            out[i] = piece[:, lo:hi]


def stack_columns(pieces, cuts):
    return kernel_call(
        functools.partial(stack_kernel, cuts=cuts),
        "stack_columns",
        tuple(shape_of((len(pieces), pieces[0].shape[0], hi - lo), bf16) for lo, hi in cuts),
        tuple(pieces),
    )


def cut_kernel(core, values, kept_ref, sent_ref, *, n_dp, own, padded):
    kept_ref[...] = jnp.zeros_like(kept_ref)
    sent_ref[...] = jnp.zeros_like(sent_ref)
    for side, refs in ((0, (kept_ref, sent_ref)), (1, (sent_ref, kept_ref))):

        @pl.when(core[0] == side)
        def _():
            for s in range(2 * kept_ref.shape[0]):
                for d in range(n_dp):
                    start = (s * n_dp + d) * own
                    refs[s % 2][s // 2, 0, :, d * padded : d * padded + own] = values[
                        0, :, start : start + own
                    ].astype(bf16)


def cut_hidden(values, core, n_chips, n_dp, padded):
    two, rows, ff = values.shape
    own = ff // (2 * n_chips * n_dp)
    dims = (n_chips, two, rows, n_dp * padded)
    return kernel_call(
        functools.partial(cut_kernel, n_dp=n_dp, own=own, padded=padded),
        "cut_hidden",
        (shape_of(dims, bf16),) * 2,
        (core, values),
        grid=(two,),
        in_specs=[smem, pl.BlockSpec((1, rows, ff), lambda g: (g, 0, 0))],
        out_specs=(pl.BlockSpec((n_chips, 1, rows, n_dp * padded), lambda g: (0, g, 0, 0)),) * 2,
    )


def turn_kernel(chip, *refs, n_chips):
    ins, outs = refs[: len(refs) - n_chips], refs[len(refs) - n_chips :]
    per_side = len(ins) // 2
    for t, out in enumerate(outs):
        at = lax.rem(chip[0] + t, n_chips)
        for side in range(2):
            if per_side == 1:
                out[side] = ins[side][at]
            else:
                for g in range(2):
                    out[side, g] = ins[2 * side + g][at]


def turn_pairs(kept, got, chip, n_chips):
    rows, width = kept[0].shape[-2:]
    return kernel_call(
        functools.partial(turn_kernel, n_chips=n_chips),
        "turn_pairs",
        (shape_of((2, 2, rows, width), bf16),) * n_chips,
        (chip, *kept, *got),
        in_specs=[smem] + [vmem] * (len(kept) + len(got)),
    )


def add_kernel(*refs):
    *ins, out = refs
    total = ins[0][...].astype(f32)
    for ref in ins[1:]:
        total = total + ref[...].astype(f32)
    out[...] = total.astype(bf16)


def add(*arrays):
    return kernel_call(add_kernel, "add", shape_of(arrays[0].shape, bf16), arrays)


def add_turn_kernel(chip, kept, got, *outs):
    n = kept.shape[0]
    for t, out in enumerate(outs):
        at = lax.rem(chip[0] + t, n)
        out[...] = (kept[at].astype(f32) + got[at].astype(f32)).astype(bf16)


def add_turn(kept, got, chip):
    n = kept.shape[0]
    return kernel_call(
        add_turn_kernel,
        "add_turn",
        (shape_of(kept.shape[1:], bf16),) * n,
        (chip, kept, got),
        in_specs=[smem, vmem, vmem],
    )


def add_halve_kernel(mine, *refs):
    parts, (stays, goes) = refs[:-2], refs[-2:]
    count = len(parts) // 2
    at = 0
    for kept, got in zip(parts[:count], parts[count:]):
        for o in range(kept.shape[0]):
            for out, side in ((stays, mine[0]), (goes, 1 - mine[0])):
                out[at] = (kept[o, side].astype(f32) + got[o, side].astype(f32)).astype(bf16)
            at += 1


def add_halve(kept, got, mine, outer):
    rows, width = kept[0].shape[1:]
    blocks = sum(part.shape[0] for part in kept)
    inner = blocks // (2 * outer)
    half = shape_of((outer, inner, rows, width), bf16)
    stays, goes = kernel_call(
        add_halve_kernel,
        "add_halve",
        (half, half),
        (mine, *[part.reshape(-1, 2, inner, rows, width) for part in (*kept, *got)]),
        in_specs=[smem] + [vmem] * (len(kept) + len(got)),
        megabytes=40,
    )
    return stays.reshape(-1, rows, width), goes.reshape(-1, rows, width)


def add_halve_columns_kernel(mine, *refs, cuts):
    parts, (stays, goes) = refs[:-2], refs[-2:]
    count = len(parts) // 2
    lo = 0
    for kept, got, (first, last) in zip(parts[:count], parts[count:], cuts):
        hi = lo + last - first
        for o in range(kept.shape[0]):
            for out, side in ((stays, mine[0]), (goes, 1 - mine[0])):
                total = kept[o, side, :, :, first:last].astype(f32) + got[
                    o, side, :, :, first:last
                ].astype(f32)
                out[o, :, :, lo:hi] = total.astype(bf16)
        lo = hi


def add_halve_columns(kept, got, cuts, mine, outer):
    blocks, rows, _ = kept[0].shape
    inner = blocks // (2 * outer)
    width = sum(last - first for first, last in cuts)
    half = shape_of((outer, inner, rows, width), bf16)
    stays, goes = kernel_call(
        functools.partial(add_halve_columns_kernel, cuts=cuts),
        "add_halve",
        (half, half),
        (mine, *[part.reshape(outer, 2, inner, rows, -1) for part in (*kept, *got)]),
        in_specs=[smem] + [vmem] * (len(kept) + len(got)),
        megabytes=44,
    )
    return stays.reshape(-1, rows, width), goes.reshape(-1, rows, width)


def adamw_update(master, moment_one, moment_two, gradient, step_rate, decay_weight):
    first_new = beta_one * moment_one + (1.0 - beta_one) * gradient
    second_new = beta_two * moment_two + (1.0 - beta_two) * gradient * gradient
    first_hat = first_new / (1.0 - beta_one**STEP)
    second_hat = second_new / (1.0 - beta_two**STEP)
    master_new = master - step_rate * (
        first_hat / (jnp.sqrt(second_hat) + adam_eps) + decay_weight * master
    )
    return (first_new, second_new, master_new)


def adamw_kernel(where, master, first, second, *refs, n_dp, own, padded, rate, decay):
    pieces, (first_ref, second_ref, master_ref, slots, joined) = refs[:-5], refs[-5:]
    for t, piece in enumerate(pieces):
        for o in range(2):
            slots[where[2 * t + o]] = piece[o, 0]
    for s in range(slots.shape[0]):
        for d in range(n_dp):
            start = (s * n_dp + d) * own
            joined[:, start : start + own] = slots[
                s, :, d * padded : d * padded + own
            ].astype(f32)
    first_ref[0], second_ref[0], master_ref[0] = adamw_update(
        master[0], first[0], second[0], joined[...], rate, decay
    )


def adamw_hidden(master, first, second, pieces, where, n_dp, padded, rate, decay):
    two, rows, ff = master.shape
    n_seq = 2 * len(pieces)
    own = ff // (n_seq * n_dp)
    block = pl.BlockSpec((1, rows, ff), lambda g: (g, 0, 0))
    part = pl.BlockSpec((2, 1, rows, n_dp * padded), lambda g: (0, g, 0, 0))
    return kernel_call(
        functools.partial(
            adamw_kernel, n_dp=n_dp, own=own, padded=padded, rate=rate, decay=decay
        ),
        "adamw_hidden",
        (shape_of(master.shape, f32),) * 3,
        (where, master, first, second, *pieces),
        megabytes=44,
        grid=(two,),
        in_specs=[smem] + [block] * 3 + [part] * len(pieces),
        out_specs=(block,) * 3,
        scratch_shapes=[
            pltpu.VMEM((n_seq, rows, n_dp * padded), bf16),
            pltpu.VMEM((rows, ff), f32),
        ],
    )


def assemble_kernel(where, *refs, splits, counts):
    ins, outs, sems = refs[: len(counts)], refs[len(counts) : -1], refs[-1]
    copies = []
    entry = 0
    for ref, (column, count) in zip(ins, counts):
        for i in range(count):
            for out, start, width in splits[column]:
                copies.append(
                    pltpu.make_async_copy(
                        ref.at[i, :, pl.ds(start, width)],
                        outs[out[0]].at[where[entry], :, pl.ds(out[1], width)],
                        sems.at[len(copies)],
                    )
                )
            entry += 1
    for copy in copies:
        copy.start()
    for copy in copies:
        copy.wait()


def assemble(pieces, where, splits, out_widths):
    counts = [(column, array.shape[0]) for array, column in pieces]
    rows = pieces[0][0].shape[1]
    blocks = sum(count for column, count in counts if column == 0)
    n_copies = sum(count * len(splits[column]) for column, count in counts)
    return kernel_call(
        functools.partial(assemble_kernel, splits=splits, counts=counts),
        "assemble",
        tuple(shape_of((blocks, rows, w), bf16) for w in out_widths),
        (where.astype(jnp.int32), *[array for array, _ in pieces]),
        in_specs=[smem] + [anywhere] * len(pieces),
        out_specs=(vmem,) * len(out_widths),
        scratch_shapes=[pltpu.SemaphoreType.DMA((n_copies,))],
    )


def seq_perm(values, chips, flip):
    count = lax.axis_size("seq")
    return lax.ppermute(
        values, "seq", [(i, ((i + 2 * chips) % count) ^ flip) for i in range(count)]
    )


def dp_perm(values, bit):
    return lax.ppermute(values, "dp", [(i, i ^ bit) for i in range(lax.axis_size("dp"))])


def dp_bits():
    return [1 << i for i in range(lax.axis_size("dp").bit_length() - 1)]


def pick(values, index, axis):
    return lax.dynamic_index_in_dim(values, index, axis, keepdims=False)


def places_of():
    n_chips = lax.axis_size("seq") // 2
    seq_at = lax.axis_index("seq")
    return n_chips, seq_at // 2, seq_at % 2, lax.axis_size("dp"), lax.axis_index("dp")


def swap(values):
    return seq_perm(values, 0, 1)


def sent_pieces(values):
    return [values] + [seq_perm(values, t, 0) for t in range(1, lax.axis_size("seq") // 2)]


def shards(
    tokens,
    cotangent,
    positions,
    qkv_master,
    qkv_first,
    qkv_second,
    out_master,
    out_first,
    out_second,
    gate_up_master,
    gate_up_first,
    gate_up_second,
    down_master,
    down_first,
    down_second,
    small_master,
    small_first,
    small_second,
):
    n_chips, chip_at, core_at, n_dp, dp_at = places_of()
    n_seq = 2 * n_chips
    n_all = n_seq * n_dp
    bits = dp_bits()
    rows_own, qkv_width = qkv_master.shape
    half = qkv_width // 2
    small_own = small_master.shape[0]
    ff_dev = down_master.shape[0]
    ff_pad = -(-ff_dev // 16) * 16
    ff_own = n_dp * ff_pad
    inputs = tokens[0]
    upstream = cotangent[0]
    tok_rows = inputs.shape[0]
    seq_length = positions.shape[1]
    shifts = list(range(1, n_chips))

    ring_chips = [(chip_at - t) % n_chips for t in range(n_chips)]
    ring_order = jnp.stack(
        [chip * 2 + (core_at ^ flip) for chip in ring_chips for flip in range(2)]
    ).astype(jnp.int32)
    bases = positions[0, ::PIECE].reshape(n_seq, tok_rows // PIECE)
    key_bases = jnp.take(bases, ring_order, axis=0)
    query_bases = key_bases[0]
    key_bases = key_bases.reshape(-1)
    own_places = lax.dynamic_slice_in_dim(
        positions[0], (chip_at * 2 + core_at) * tok_rows, tok_rows, 0
    )
    cosine, sine = rotary_tables(own_places)

    small_block = jnp.pad(
        small_master.astype(bf16), (0, rows_own * HD - small_own)
    ).reshape(rows_own, HD)
    packed = jnp.concatenate([small_block, qkv_master.astype(bf16)], axis=1)
    qkv_ring = sent_pieces(packed)
    core_side = core_at.reshape(1).astype(jnp.int32)
    chip_side = chip_at.reshape(1).astype(jnp.int32)
    bit_sides = {bit: ((dp_at // bit) % 2).reshape(1).astype(jnp.int32) for bit in bits}
    cut_kept, cut_sent = cut_hidden(gate_up_master, core_side, n_chips, n_dp, ff_pad)
    to_send = turn_pairs([cut_kept], [swap(cut_sent)], chip_side, n_chips)
    qkv_ring, to_send, cosine, sine = fence(qkv_ring, to_send, cosine, sine)

    def exchange(shift):
        return seq_perm(to_send[shift], shift, 0)

    w_out = lax.all_gather(
        after(out_master.astype(bf16), *to_send), ("seq", "dp"), axis=0, tiled=True
    )

    columns = ((0, HD + half), (HD + half, HD + qkv_width))
    orders = (bits, bits[::-1])
    held = list(stack_columns(qkv_ring, columns))
    flips = [[0], [0]]
    gate_up_pieces = {0: to_send[0]}
    groups = [shifts[:1], shifts[-1:], shifts[1:-1]] if n_chips > 2 else [shifts, [], []]
    for stage in range(len(bits)):
        got = [dp_perm(h, order[stage]) for h, order in zip(held, orders)]
        if stage == len(bits) - 1:
            swapped = [swap(h) for h in held]
        for shift in groups[min(stage, 1)] if stage < 2 else []:
            gate_up_pieces[shift] = exchange(shift)
        got, held, gate_up_pieces = fence(got, held, gate_up_pieces)
        flips = [f + [k ^ order[stage] for k in f] for f, order in zip(flips, orders)]
        if stage < len(bits) - 1:
            held = [jnp.concatenate([h, g], axis=0) for h, g in zip(held, got)]
    (swapped,) = fence(swapped)
    for shift in groups[2]:
        gate_up_pieces[shift] = exchange(shift)
    down_share = jnp.pad(down_master.astype(bf16), ((0, ff_pad - ff_dev), (0, 0)))
    w_down = lax.all_gather(after(down_share, *got), "dp", axis=0, tiled=True)
    got_swapped = [swap(g) for g in got]
    pieces, where = [], []
    for column in range(2):
        for flip, part, ks in (
            (0, held[column], flips[column][: n_dp // 2]),
            (0, got[column], flips[column][n_dp // 2 :]),
            (1, swapped[column], flips[column][: n_dp // 2]),
            (1, got_swapped[column], flips[column][n_dp // 2 :]),
        ):
            pieces.append((part, column))
            where += [
                (chip * 2 + (core_at ^ flip)) * n_dp + (dp_at ^ k) for k in ks for chip in ring_chips
            ]
    w_qkv, small_blocks = assemble(
        pieces,
        jnp.stack(where),
        ((((1, 0), 0, HD), ((0, 0), HD, half)), (((0, half), 0, half),)),
        (qkv_width, HD),
    )
    w_qkv = w_qkv.reshape(D, qkv_width)
    small_params = small_blocks.reshape(n_all, rows_own * HD)[:, :small_own].reshape(1, -1)
    small_params = small_params.astype(f32)
    gain_one = small_params[:, :D]
    gain_two = small_params[:, D : 2 * D]
    qkv_bias = small_params[:, 2 * D :]
    normed_one, key_value = project_kv(inputs, w_qkv, gain_one, qkv_bias, cosine, sine)
    gate_up_held = [
        jnp.concatenate([gate_up_pieces[t] for t in ts], axis=0)
        for ts in (range(n_chips // 2), range(n_chips // 2, n_chips))
    ]
    normed_one, key_value, gate_up_held = fence(normed_one, key_value, gate_up_held)

    kv_ring = sent_pieces(key_value)
    gate_up_parts = [
        [held, dp_perm(held, order[0])] for held, order in zip(gate_up_held, orders)
    ]
    gate_up_flips = [[0, order[0]] for order in orders]
    queries = project_q(normed_one, w_qkv, qkv_bias, cosine, sine)
    kv_swapped = [swap(kv_ring[0])] + [swap(after(piece, queries)) for piece in kv_ring[1:]]
    kv_ring, kv_swapped, gate_up_parts, queries, upstream = fence(
        kv_ring, kv_swapped, gate_up_parts, queries, upstream
    )

    def cross(start, stop, stage):
        for parts, flips_of, order in zip(gate_up_parts, gate_up_flips, orders):
            parts += [dp_perm(piece, order[stage]) for piece in parts[start:stop]]
            flips_of += [k ^ order[stage] for k in flips_of[start:stop]]

    upstream_ring = [upstream, seq_perm(upstream, 1, 0)]
    cross(0, 1 if len(bits) == 2 else 2, 1)
    attended, logsum, key_value_all = attend(
        queries, [piece for pair in zip(kv_ring, kv_swapped) for piece in pair], query_bases, key_bases
    )
    gate_up_parts, upstream_ring, attended, logsum, key_value_all = fence(
        gate_up_parts, upstream_ring, attended, logsum, key_value_all
    )

    def ring_step(pieces):
        return pieces + [seq_perm(pieces[-1], 1, 0)] if len(pieces) < n_chips else pieces

    upstream_ring = ring_step(upstream_ring)
    if len(bits) == 2:
        cross(1, 2, 1)
    else:
        cross(0, 4, 2)
    upstream_swapped = [swap(piece) for piece in upstream_ring[:2]]
    residual, normed_two, attended_low = out_project(inputs, attended, w_out, gain_two)
    normed_ring, normed_swapped = [normed_two], [swap(normed_two)]
    gate_up_parts, upstream_ring, upstream_swapped, normed_ring, normed_swapped, residual = fence(
        gate_up_parts, upstream_ring, upstream_swapped, normed_ring, normed_swapped, residual
    )

    pieces, where = [], []
    for column, (parts, flips_of) in enumerate(zip(gate_up_parts, gate_up_flips)):
        slots = ring_order[:n_chips] if column == 0 else ring_order[n_chips:]
        for part, k in zip(parts, flips_of):
            pieces.append((part.reshape(-1, rows_own, ff_own), 0))
            block = slots * n_dp + (dp_at ^ k)
            where.append(jnp.stack([block, n_all + block], axis=1).reshape(-1))
    (w_gate_up,) = assemble(
        pieces, jnp.concatenate(where), ((((0, 0), 0, ff_own),),), (ff_own,)
    )
    w_gate_up = w_gate_up.reshape(2, D, ff_own)
    out_parts, kept = [], ()
    running = None
    for slot in range(n_chips):
        sent = None if running is None else seq_perm(running, 1, 0)
        normed_ring = ring_step(normed_ring)
        upstream_ring = ring_step(upstream_ring)
        out_own, out_other, grad_own, grad_other, *kept = feed_forward(
            (normed_ring[slot], normed_swapped[slot]),
            (upstream_ring[slot], upstream_swapped[slot]),
            w_gate_up,
            w_down,
            slot,
            n_chips,
            kept,
        )
        out_parts.append((out_own, out_other))
        grad_swapped = swap(grad_other)
        if slot + 1 < n_chips:
            normed_swapped = normed_swapped + [swap(after(normed_ring[slot + 1], grad_own))]
        if slot + 2 < n_chips and len(upstream_swapped) < slot + 3:
            upstream_swapped = upstream_swapped + [swap(after(upstream_ring[slot + 2], grad_own))]
        if slot == 0:
            grad_first = (grad_own, grad_swapped)
        elif sent is None:
            running = add(grad_own, grad_swapped)
        else:
            running = add(grad_own, grad_swapped, after(sent, grad_own))
        running, normed_ring, normed_swapped, upstream_ring, upstream_swapped, out_parts, kept = fence(
            running, normed_ring, normed_swapped, upstream_ring, upstream_swapped, out_parts, kept
        )
        if slot == 1:
            out_pair = (out_parts[1][0], swap(out_parts[1][1]))
            ring_first = add(*out_pair)

    grad_ring = jnp.zeros_like(grad_first[0]) if running is None else seq_perm(running, 1, 0)
    normed_all, ffn_all, hidden_all, gate_grads_all, up_grads_all = kept
    first_split = (
        jnp.concatenate([bit_sides[order[0]] for order in orders]),
        tuple(order[0] for order in orders),
    )
    halves = [
        weight_grad(
            normed_all,
            (gate_grads_all, up_grads_all),
            split=first_split,
            rows=rows_own,
            part=(part, 2),
        )
        for part in range(2)
    ]
    out_running = seq_perm(ring_first, 1, 0) if n_chips > 1 else None
    out_pairs = [
        (own, swap(after(other, *halves[0][0]))) for t, (own, other) in enumerate(out_parts) if t != 1
    ]
    out_total = [ring_first] + [add(own, other) for own, other in out_pairs[1:]]
    if n_chips > 2:
        out_running = add(after(out_running, *halves[0][0]), out_total[1])
    grad_ring, halves, out_pairs, out_total, out_running = fence(
        grad_ring, halves, out_pairs, out_total, out_running
    )

    got_one = [dp_perm(goes, order[0]) for (_, goes), order in zip(halves[0], orders)]
    if n_chips > 2:
        out_running = seq_perm(out_running, 1, 0)
    residual_grads, branch_grads, attended_grads, gain_two_grad = norm_back(
        grad_ring, *grad_first, residual, upstream, gain_two, w_out
    )
    query_pre, kv_grad_own, kv_grad_other = attend_back(
        queries,
        key_value_all,
        attended_grads,
        attended,
        logsum,
        query_bases,
        key_bases,
        cosine,
        sine,
    )
    got_one, kv_grad_own, kv_grad_other, query_pre, branch_grads, out_running = fence(
        got_one, kv_grad_own, kv_grad_other, query_pre, branch_grads, out_running
    )
    own_parts = kv_grad_own.reshape(n_chips, tok_rows, 2 * KVW)
    other_parts = swap(kv_grad_other).reshape(n_chips, tok_rows, 2 * KVW)
    kv_sum = add_turn(own_parts, other_parts, jnp.zeros_like(chip_side))
    kv_sum, halves, query_pre, branch_grads, kept = fence(
        kv_sum, halves, query_pre, branch_grads, kept
    )

    def next_split(kept_parts, got, done_bits, left_bits):
        rest = [bit for bit in bits[::-1] if bit not in done_bits]
        bit = left_bits[0]
        lead = sum(part.shape[0] for part in kept_parts) // 2 ** len(rest)
        return add_halve(kept_parts, got, bit_sides[bit], lead * 2 ** rest.index(bit))

    kv_got = [seq_perm(kv_sum[t], n_chips - t, 0) for t in range(1, n_chips)]
    got_two = [dp_perm(goes, order[0]) for (_, goes), order in zip(halves[1], orders)]
    by_core = (core_side, (n_dp,))
    (query_split,) = weight_grad(normed_one[None], (query_pre[None],), split=by_core, rows=rows_own)
    (out_split,) = weight_grad(
        attended_low[None], (branch_grads[None],), split=by_core, rows=rows_own
    )
    (down_grad,) = weight_grad(kept[2], (kept[1],))
    if n_chips > 3:
        out_running = add(out_running, out_total[2])
    kv_got, got_two, query_split, out_split, down_grad, out_running = fence(
        kv_got, got_two, query_split, out_split, down_grad, out_running
    )
    down_owned = lax.psum_scatter(down_grad, "dp", scatter_dimension=0, tiled=True)
    down_owned = down_owned[:ff_dev].astype(f32)

    if n_chips > 3:
        out_running = seq_perm(out_running, 1, 0)
    gate_up_split = [
        next_split([one[0], two[0]], [got, other], order[:1], order[1:])
        for one, two, got, other, order in zip(*halves, got_one, got_two, orders)
    ]
    gate_up_sums = [dp_perm(goes, order[1]) for (_, goes), order in zip(gate_up_split, orders)]
    both = [(split[0], swap(split[1])) for split in (query_split, out_split)]
    key_value_pre, input_grads, gain_one_grad, bias_grad = input_back(
        inputs,
        gain_one,
        w_qkv,
        query_pre,
        cosine,
        sine,
        residual_grads,
        kv_sum[0],
        kv_got,
    )
    ((kv_stays, kv_goes),) = weight_grad(
        normed_one[None], (key_value_pre[None],), split=by_core, rows=rows_own
    )
    gate_up_split, gate_up_sums, both, input_grads, kv_stays, kv_goes, out_running, small_parts = fence(
        gate_up_split,
        gate_up_sums,
        both,
        input_grads,
        kv_stays,
        kv_goes,
        out_running,
        (gain_one_grad, gain_two_grad, bias_grad),
    )

    ready = []
    for split, got, order in zip(gate_up_split, gate_up_sums, orders):
        kept_part = split[0]
        for i in range(2, len(order)):
            kept_part, goes = next_split([kept_part], [got], order[:i], order[i:])
            got = dp_perm(goes, order[i])
        ready.append(add_halve([kept_part], [got], core_side, n_chips))
    to_send = turn_pairs(
        [kept_part for kept_part, _ in ready],
        [swap(sent) for _, sent in ready],
        chip_side,
        n_chips,
    )
    small_grad = jnp.concatenate(small_parts, axis=1).astype(bf16)
    small_grad = jnp.pad(
        small_grad.reshape(n_all, small_own), ((0, 0), (0, rows_own * HD - small_own))
    ).reshape(n_chips, 2, n_dp, rows_own, HD)
    kv_stays = jnp.concatenate(
        [pick(small_grad, core_at, 1).reshape(-1, rows_own, HD), kv_stays], axis=2
    )
    kv_goes = jnp.concatenate(
        [pick(small_grad, 1 - core_at, 1).reshape(-1, rows_own, HD), kv_goes], axis=2
    )
    kv_got = swap(kv_goes)
    rest_cuts = (((0, D), (0, 3 * HD)), ((0, D), (3 * HD, HD + 2 * KVW)))
    rest = [
        add_halve_columns(
            [kept_part, kv_stays],
            [got, kv_got],
            cuts,
            bit_sides[order[0]],
            n_chips * n_dp // (2 * order[0]),
        )
        for (kept_part, got), cuts, order in zip(both, rest_cuts, orders)
    ]
    to_send, rest, out_running = fence(to_send, rest, out_running)

    gate_up_owned = {0: to_send[0]}
    rest_got = [dp_perm(goes, order[0]) for (_, goes), order in zip(rest, orders)]
    for shift in groups[0] + groups[2]:
        gate_up_owned[shift] = exchange(shift)
    gate_up_owned, rest_got, down_owned = fence(gate_up_owned, rest_got, down_owned)

    for shift in groups[1]:
        gate_up_owned[shift] = exchange(shift)
    rest_send = []
    for (kept_part, _), got, order in zip(rest, rest_got, orders):
        for i in range(1, len(order)):
            kept_part, goes = next_split([kept_part], [got], order[:i], order[i:])
            got = dp_perm(goes, order[i])
        rest_send.append(add_turn(kept_part, got, chip_side))
    gate_up_owned, rest_send = fence(gate_up_owned, rest_send)

    rest_send = [
        jnp.concatenate([parts[t] for parts in rest_send], axis=1) for t in range(n_chips)
    ]
    total = rest_send[0].astype(f32)
    for shift in shifts:
        total = total + seq_perm(rest_send[shift], shift, 0).astype(f32)
    for t in range(4, n_chips):
        out_running = seq_perm(add(out_running, out_total[t - 1]), 1, 0)
    outputs = residual + out_pairs[0][0].astype(f32) + out_pairs[0][1].astype(f32)
    if n_chips > 1:
        outputs = outputs + out_running.astype(f32)
    outputs = outputs.astype(bf16)
    gate_up_new = adamw_hidden(
        gate_up_master,
        gate_up_first,
        gate_up_second,
        [gate_up_owned[t] for t in range(n_chips)],
        ring_order,
        n_dp,
        ff_pad,
        0.064,
        0.1,
    )
    wide = D + 3 * HD
    query_owned, out_owned = total[:, :D], total[:, wide : wide + D]
    small_owned = total[:, D : D + HD]
    qkv_owned = jnp.concatenate(
        [query_owned, total[:, D + HD : wide], total[:, wide + D :]], axis=1
    )
    small_owned = small_owned.reshape(-1)[:small_own]

    qkv_new = adamw_update(qkv_master, qkv_first, qkv_second, qkv_owned, 0.09, 0.1)
    out_new = adamw_update(out_master, out_first, out_second, out_owned, 0.18, 0.1)
    down_new = adamw_update(down_master, down_first, down_second, down_owned, 0.026, 0.1)
    small_new = adamw_update(small_master, small_first, small_second, small_owned, 0.6, 0.0)
    return (
        outputs[None],
        input_grads[None],
        *qkv_new,
        *out_new,
        *gate_up_new,
        *down_new,
        *small_new,
    )


def solution(mesh):
    in_specs = (
        P("dp", "seq", None),
        P("dp", "seq", None),
        P("dp", None),
        P(("seq", "dp"), None),
        P(("seq", "dp"), None),
        P(("seq", "dp"), None),
        P(("seq", "dp"), None),
        P(("seq", "dp"), None),
        P(("seq", "dp"), None),
        P(None, ("seq", "dp"), None),
        P(None, ("seq", "dp"), None),
        P(None, ("seq", "dp"), None),
        P(("seq", "dp"), None),
        P(("seq", "dp"), None),
        P(("seq", "dp"), None),
        P(("seq", "dp")),
        P(("seq", "dp")),
        P(("seq", "dp")),
    )
    out_specs = (
        P("dp", "seq", None),
        P("dp", "seq", None),
        P(("seq", "dp"), None),
        P(("seq", "dp"), None),
        P(("seq", "dp"), None),
        P(("seq", "dp"), None),
        P(("seq", "dp"), None),
        P(("seq", "dp"), None),
        P(None, ("seq", "dp"), None),
        P(None, ("seq", "dp"), None),
        P(None, ("seq", "dp"), None),
        P(("seq", "dp"), None),
        P(("seq", "dp"), None),
        P(("seq", "dp"), None),
        P(("seq", "dp")),
        P(("seq", "dp")),
        P(("seq", "dp")),
    )
    return jax.shard_map(shards, mesh=mesh, in_specs=in_specs, out_specs=out_specs, check_vma=False)
```

```python
import functools

import jax
import jax.numpy as jnp
from jax import lax
from jax.experimental import pallas as pl
from jax.experimental.pallas import tpu as pltpu
from jax.sharding import PartitionSpec as P

D = 1536
HEADS = 12
KVH = 2
HD = 128
STEP = 10
KVW = KVH * HD
PIECE = 128


norm_eps = 1e-06
rope_base = 1000000.0
beta_one = 0.9
beta_two = 0.95
adam_eps = 1e-08
masked_score = -1e30
log2_e = 1.4426950408889634
bf16 = jnp.bfloat16
f32 = jnp.float32
vmem = pl.BlockSpec(memory_space=pltpu.VMEM)
smem = pl.BlockSpec(memory_space=pltpu.SMEM)
anywhere = pl.BlockSpec(memory_space=pl.ANY)


def shape_of(dims, kind):
    return jax.ShapeDtypeStruct(dims, kind)


def kernel_call(kernel, name, out_shape, operands, megabytes=32, **options):
    return pl.pallas_call(
        kernel,
        name=name,
        out_shape=out_shape,
        compiler_params=pltpu.CompilerParams(vmem_limit_bytes=megabytes << 20),
        cost_estimate=pl.CostEstimate(flops=10**6, bytes_accessed=10**6, transcendentals=0),
        **options,
    )(*operands)


def after(values, *others):
    return lax.optimization_barrier((values,) + others)[0]


def fence(*groups):
    flat, tree = jax.tree.flatten(groups)
    return jax.tree.unflatten(tree, lax.optimization_barrier(tuple(flat)))


def dot(left, right):
    return jnp.dot(left, right, preferred_element_type=f32)


def dot_transposed(left, right):
    return lax.dot_general(left, right, (((1,), (1,)), ((), ())), preferred_element_type=f32)


def rotary_tables(places):
    half_size = HD // 2
    freqs = rope_base ** (-(jnp.arange(half_size).astype(f32) * (2.0 / HD)))
    angles = places.astype(f32)[:, None] * freqs[None, :]
    cosine, sine = jnp.cos(angles), jnp.sin(angles)
    return jnp.concatenate([cosine, cosine], axis=1), jnp.concatenate([-sine, sine], axis=1)


def rms_scale(values):
    return lax.rsqrt(jnp.mean(values * values, axis=-1, keepdims=True) + norm_eps)


def swap_halves(values):
    return pltpu.roll(values, HD // 2, 1)


def head(index):
    return slice(index * HD, (index + 1) * HD)


def project_kv_kernel(tokens, w_qkv, gain, bias, cosine, sine, normed_ref, kv_ref):
    inputs = tokens[...].astype(f32)
    normed = (inputs * rms_scale(inputs) * gain[...]).astype(bf16)
    normed_ref[...] = normed
    rows = dot(normed, w_qkv[...]) + bias[:, D:]
    for j in range(KVH):
        part = rows[:, head(j)]
        kv_ref[:, head(j)] = (part * cosine[...] + swap_halves(part) * sine[...]).astype(bf16)
    kv_ref[:, KVW:] = rows[:, KVW:].astype(bf16)


def project_q_kernel(normed, w_qkv, bias, cosine, sine, query_ref):
    rows = dot(normed[...], w_qkv[...]) + bias[:, :D]
    for j in range(HEADS):
        part = rows[:, head(j)]
        query_ref[:, head(j)] = (part * cosine[...] + swap_halves(part) * sine[...]).astype(bf16)


def project_kv(tokens, w_qkv, gain, bias, cosine, sine):
    rows = tokens.shape[0]
    return kernel_call(
        project_kv_kernel,
        "project_kv",
        (shape_of((rows, D), bf16), shape_of((rows, 2 * KVW), bf16)),
        (tokens, w_qkv, gain, bias, cosine, sine),
        megabytes=58,
        grid=(1,),
        in_specs=[vmem, pl.BlockSpec((D, 2 * KVW), lambda i: (0, D // (2 * KVW)))] + [vmem] * 4,
        out_specs=(vmem, vmem),
    )


def project_q(normed, w_qkv, bias, cosine, sine):
    return kernel_call(
        project_q_kernel,
        "project_q",
        shape_of(normed.shape, bf16),
        (normed, w_qkv, bias, cosine, sine),
        megabytes=58,
        grid=(1,),
        in_specs=[vmem, pl.BlockSpec((D, D), lambda i: (0, 0))] + [vmem] * 3,
        out_specs=vmem,
    )


def mask_keys(values, query_bases, key_bases, first_run, fill):
    later = lax.broadcasted_iota(jnp.int32, (PIECE, PIECE), 0) - lax.broadcasted_iota(
        jnp.int32, (PIECE, PIECE), 1
    )
    keys, queries = values.shape
    rows = []
    for r in range(keys // PIECE):
        down = slice(r * PIECE, (r + 1) * PIECE)
        row = []
        for q in range(queries // PIECE):
            gap = query_bases[q] - key_bases[first_run + r]
            row.append(jnp.where(later <= gap, values[down, q * PIECE : (q + 1) * PIECE], fill))
        rows.append(jnp.concatenate(row, axis=1))
    return jnp.concatenate(rows, axis=0)


def attend_kernel(query_bases, key_bases, q_ref, *refs):
    pieces, (out_ref, lse_ref, kv_ref) = refs[:-3], refs[-3:]
    rows = q_ref.shape[0]
    for i, piece in enumerate(pieces):
        kv_ref[i * rows : (i + 1) * rows, :] = piece[...]
    groups = HEADS // KVH
    scale = HD**-0.5 * log2_e
    for kv in range(KVH):
        values = kv_ref[:, head(KVH + kv)].T
        for h in range(kv * groups, (kv + 1) * groups):
            queries = q_ref[:, head(h)]
            scores = []
            for run in range(key_bases.shape[0]):
                keys = kv_ref[run * PIECE : (run + 1) * PIECE, head(kv)]
                part = dot_transposed(keys, queries)
                scores.append(mask_keys(part, query_bases, key_bases, run, masked_score))
            scores = jnp.concatenate(scores, axis=0)
            top = jnp.max(scores, axis=0, keepdims=True)
            weights = jnp.exp2((scores - top) * scale)
            total = jnp.sum(weights, axis=0, keepdims=True)
            mixed = dot(values, weights.astype(bf16))
            out_ref[:, head(h)] = (mixed / total).T
            lse_ref[h : h + 1, :] = top * scale + jnp.log2(total)


def attend(queries, pieces, query_bases, key_bases):
    rows, total = queries.shape[0], key_bases.shape[0] * PIECE
    return kernel_call(
        attend_kernel,
        "attend",
        (
            shape_of((rows, D), f32),
            shape_of((HEADS, rows), f32),
            shape_of((total, 2 * KVW), bf16),
        ),
        (query_bases, key_bases, queries, *pieces),
        in_specs=[smem] * 2 + [vmem] * (1 + len(pieces)),
    )


def out_kernel(tokens, attended, w_out, gain, residual_ref, normed_ref, low_ref):
    low = attended[...].astype(bf16)
    low_ref[...] = low
    residual = tokens[...].astype(f32) + dot(low, w_out[...])
    residual_ref[...] = residual
    normed_ref[...] = (residual * rms_scale(residual) * gain[...]).astype(bf16)


def out_project(tokens, attended, w_out, gain):
    dims = tokens.shape
    return kernel_call(
        out_kernel,
        "out_project",
        (shape_of(dims, f32), shape_of(dims, bf16), shape_of(dims, bf16)),
        (tokens, attended, w_out, gain),
    )


def ffn_kernel(
    normed_own, normed_other, grad_own, grad_other, w_gate_up, w_down, *refs, earlier
):
    refs = refs[earlier:]
    out_refs, grad_refs = refs[:2], refs[2:4]
    normed_ref, ffn_grad_ref, hidden_ref, gate_ref, up_ref = refs[4:]
    rows = normed_own.shape[0]
    for i, (normed_in, grad_in) in enumerate(((normed_own, grad_own), (normed_other, grad_other))):
        to = slice(i * rows, (i + 1) * rows)
        normed, ffn_grad = normed_in[...], grad_in[...]
        normed_ref[0, to, :] = normed
        ffn_grad_ref[0, to, :] = ffn_grad
        gate = dot(normed, w_gate_up[0])
        up = dot(normed, w_gate_up[1])
        sigmoid = 1.0 / (1.0 + jnp.exp(-gate))
        silu = gate * sigmoid
        hidden = (silu * up).astype(bf16)
        hidden_ref[0, to, :] = hidden
        out_refs[i][...] = dot(hidden, w_down[...]).astype(bf16)
        hidden_grad = dot_transposed(ffn_grad, w_down[...])
        gate_grad = (hidden_grad * up * sigmoid * (1.0 + gate * (1.0 - sigmoid))).astype(bf16)
        up_grad = (hidden_grad * silu).astype(bf16)
        gate_ref[0, to, :] = gate_grad
        up_ref[0, to, :] = up_grad
        grad_refs[i][...] = (
            dot_transposed(gate_grad, w_gate_up[0]) + dot_transposed(up_grad, w_gate_up[1])
        ).astype(bf16)


def feed_forward(normed, grads, w_gate_up, w_down, slot, slots, kept):
    rows, width = normed[0].shape
    ff_own = w_down.shape[0]
    token = shape_of((rows, width), bf16)
    widths = (width, width, ff_own, ff_own, ff_own)
    operands = (*normed, *grads, w_gate_up, w_down)
    return kernel_call(
        functools.partial(ffn_kernel, earlier=len(kept)),
        "feed_forward",
        (token,) * 4 + tuple(shape_of((slots, 2 * rows, w), bf16) for w in widths),
        (*operands, *kept),
        grid=(1,),
        in_specs=[vmem] * len(operands) + [anywhere] * len(kept),
        out_specs=(vmem,) * 4
        + tuple(pl.BlockSpec((1, 2 * rows, w), lambda i: (slot, 0, 0)) for w in widths),
        input_output_aliases={len(operands) + i: 4 + i for i in range(len(kept))},
    )


def norm_back_kernel(
    got, own, other, residual_ref, cotangent, gain, w_out, grad_ref, low_ref, back_ref, gain_ref
):
    normed_grad = got[...].astype(f32) + own[...].astype(f32) + other[...].astype(f32)
    residual = residual_ref[...]
    scale = rms_scale(residual)
    unit = residual * scale
    gain_ref[...] = jnp.sum(normed_grad * unit, axis=0, keepdims=True)
    weighted = normed_grad * gain[...]
    grad = cotangent[...].astype(f32) + scale * (
        weighted - unit * jnp.mean(weighted * unit, axis=-1, keepdims=True)
    )
    grad_ref[...] = grad
    low = grad.astype(bf16)
    low_ref[...] = low
    back_ref[...] = dot_transposed(low, w_out[...]).astype(bf16)


def norm_back(got, own, other, residual, cotangent, gain, w_out):
    dims = residual.shape
    return kernel_call(
        norm_back_kernel,
        "norm_back",
        (shape_of(dims, f32), shape_of(dims, bf16), shape_of(dims, bf16), shape_of((1, D), f32)),
        (got, own, other, residual, cotangent, gain, w_out),
    )


def attend_back_kernel(
    query_bases,
    key_bases,
    q_ref,
    kv_ref,
    grad_ref,
    out_ref,
    lse_ref,
    cosine,
    sine,
    q_grad_ref,
    kv_own_ref,
    kv_other_ref,
    q_rows,
    grad_rows,
    deltas,
    q_sums,
):
    rows = q_ref.shape[0]
    groups = HEADS // KVH
    scale = HD**-0.5
    for kv in range(KVH):
        for j in range(groups):
            part = slice(j * rows, (j + 1) * rows)
            columns = head(kv * groups + j)
            q_rows[part, :] = q_ref[:, columns]
            grads = grad_ref[:, columns]
            grad_rows[part, :] = grads
            product = grads.astype(f32) * out_ref[:, columns]
            deltas[:, part] = jnp.sum(product.T, axis=0, keepdims=True)
        q_sums[...] = jnp.zeros_like(q_sums)

        @pl.loop(0, kv_ref.shape[0] // (2 * rows), unroll=2)
        def _(step):
            at = pl.ds(pl.multiple_of(step * (2 * rows), 2 * rows), 2 * rows)
            runs = 2 * rows // PIECE
            keys = kv_ref[at, head(kv)]
            values = kv_ref[at, head(KVH + kv)]
            key_sum = value_sum = None
            for j in range(groups):
                part = slice(j * rows, (j + 1) * rows)
                h = kv * groups + j
                queries, grads = q_rows[part, :], grad_rows[part, :]
                scores = dot_transposed(keys, queries)
                weights = jnp.exp2(scores * (scale * log2_e) - lse_ref[h : h + 1, :])
                weights = mask_keys(weights, query_bases, key_bases, step * runs, 0.0)
                weight_grads = dot_transposed(values, grads)
                score_grads = (weights * (weight_grads - deltas[:, part])).astype(bf16)
                value_part = dot(weights.astype(bf16), grads)
                key_part = dot(score_grads, queries)
                key_sum = key_part if key_sum is None else key_sum + key_part
                value_sum = value_part if value_sum is None else value_sum + value_part
                q_sums[part, :] += lax.dot_general(
                    score_grads, keys, (((0,), (0,)), ((), ())), preferred_element_type=f32
                )
            key_sum = (key_sum * scale).astype(bf16)
            value_sum = value_sum.astype(bf16)
            to = pl.ds(pl.multiple_of(step * rows, rows), rows)
            for ref, mine in ((kv_own_ref, slice(0, rows)), (kv_other_ref, slice(rows, 2 * rows))):
                ref[to, head(kv)] = key_sum[mine, :]
                ref[to, head(KVH + kv)] = value_sum[mine, :]

        for j in range(groups):
            part = q_sums[j * rows : (j + 1) * rows, :] * scale
            q_grad_ref[:, head(kv * groups + j)] = (
                part * cosine[...] - swap_halves(part) * sine[...]
            ).astype(bf16)


def attend_back(queries, key_value, grads, attended, lse, query_bases, key_bases, cosine, sine):
    rows, total = queries.shape[0], key_value.shape[0]
    groups = HEADS // KVH
    return kernel_call(
        attend_back_kernel,
        "attend_back",
        (
            shape_of((rows, D), bf16),
            shape_of((total // 2, 2 * KVW), bf16),
            shape_of((total // 2, 2 * KVW), bf16),
        ),
        (query_bases, key_bases, queries, key_value, grads, attended, lse, cosine, sine),
        in_specs=[smem] * 2 + [vmem] * 7,
        scratch_shapes=[
            pltpu.VMEM((groups * rows, HD), bf16),
            pltpu.VMEM((groups * rows, HD), bf16),
            pltpu.VMEM((1, groups * rows), f32),
            pltpu.VMEM((groups * rows, HD), f32),
        ],
    )


def input_kernel(
    tokens, gain, w_qkv, query_grad, cosine, sine, residual_grad, own, *refs
):
    got, (kv_ref, input_ref, gain_ref, bias_ref) = refs[:-4], refs[-4:]
    rows = own[...].astype(f32)
    for piece in got:
        rows = rows + piece[...].astype(f32)
    for j in range(KVH):
        part = rows[:, head(j)]
        kv_ref[:, head(j)] = (part * cosine[...] - swap_halves(part) * sine[...]).astype(bf16)
    kv_ref[:, KVW:] = rows[:, KVW:].astype(bf16)
    kv_grad = kv_ref[...]
    q_grad = query_grad[...]
    bias_ref[:, :D] = jnp.sum(q_grad.astype(f32), axis=0, keepdims=True)
    bias_ref[:, D:] = jnp.sum(kv_grad.astype(f32), axis=0, keepdims=True)
    normed_grad = dot_transposed(q_grad, w_qkv[:, :D]) + dot_transposed(kv_grad, w_qkv[:, D:])
    inputs = tokens[...].astype(f32)
    scale = rms_scale(inputs)
    unit = inputs * scale
    gain_ref[...] = jnp.sum(normed_grad * unit, axis=0, keepdims=True)
    weighted = normed_grad * gain[...]
    input_ref[...] = residual_grad[...] + scale * (
        weighted - unit * jnp.mean(weighted * unit, axis=-1, keepdims=True)
    )


def input_back(tokens, gain, w_qkv, query_grad, cosine, sine, residual_grad, own, got):
    rows = tokens.shape[0]
    return kernel_call(
        input_kernel,
        "input_back",
        (
            shape_of((rows, 2 * KVW), bf16),
            shape_of((rows, D), f32),
            shape_of((1, D), f32),
            shape_of((1, D + 2 * KVW), f32),
        ),
        (tokens, gain, w_qkv, query_grad, cosine, sine, residual_grad, own, *got),
        megabytes=58,
    )


def split_kernel(sides, values, *outs, cuts, bits):
    blocks = values.shape[0]
    for i, ((lo, hi), bit) in enumerate(zip(cuts, bits)):
        for out, side in ((outs[2 * i], sides[i]), (outs[2 * i + 1], 1 - sides[i])):
            for o in range(blocks // (2 * bit)):
                for j in range(bit):
                    out[o * bit + j] = values[(2 * o + side) * bit + j, :, lo:hi]


def split_columns(values, sides, cuts, bits):
    blocks, rows, _ = values.shape
    outs = kernel_call(
        functools.partial(split_kernel, cuts=cuts, bits=bits),
        "split_columns",
        tuple(shape_of((blocks // 2, rows, hi - lo), bf16) for lo, hi in cuts for _ in range(2)),
        (sides, values),
        in_specs=[smem, vmem],
    )
    return [(outs[2 * i], outs[2 * i + 1]) for i in range(len(cuts))]


def weight_grad_kernel(sides, left, *refs, count, inners, based):
    rights, refs = refs[:count], refs[count:]
    bases, outs = refs[: count * based], refs[count * based :]
    turned = left[...].reshape(-1, left.shape[-1]).T
    for i, right in enumerate(rights):
        result = dot(turned, right[...].reshape(-1, right.shape[-1]))
        if based:
            result = result + bases[i][...]
        if not inners:
            outs[i][...] = result.astype(outs[i].dtype)
            continue
        stays, goes = outs[2 * i], outs[2 * i + 1]
        rows = stays.shape[2]
        result = result.astype(bf16)
        for side, refs_of in ((0, (stays, goes)), (1, (goes, stays))):

            @pl.when(sides[i] == side)
            def _():
                for o in range(stays.shape[0]):
                    for bit in range(2):
                        for j in range(inners[i]):
                            block = (o * 2 + bit) * inners[i] + j
                            refs_of[bit][o, j] = result[block * rows : (block + 1) * rows]


def weight_grad(
    left, rights, slots=(0, 1), bases=(), split=None, rows=0, part=(0, 1), kind=bf16
):
    n_slots, tokens, m = left.shape
    n_slots = n_slots // slots[1]
    m = m // part[1]
    block = 3 * HD if m % (3 * HD) == 0 else HD
    steps = m // block
    first = part[0] * steps
    whole = pl.Buffered(buffer_count=1)
    sides, inners = split if split else (jnp.zeros((1,), jnp.int32), ())
    out_shape, out_specs = [], []
    for i, right in enumerate(rights):
        n = right.shape[-1]
        if not inners:
            out_shape.append(shape_of((m, n), kind))
            out_specs.append(pl.BlockSpec((block, n), lambda i: (i, 0)))
            continue
        outer = block // (2 * inners[i] * rows)
        for _ in range(2):
            out_shape.append(shape_of((steps * outer, inners[i], rows, n), bf16))
            out_specs.append(pl.BlockSpec((outer, inners[i], rows, n), lambda i: (i, 0, 0, 0)))
    outs = kernel_call(
        functools.partial(
            weight_grad_kernel, count=len(rights), inners=inners, based=int(bool(bases))
        ),
        "weight_grad",
        tuple(out_shape),
        (sides, left, *rights, *bases),
        megabytes=44,
        grid=(steps,),
        in_specs=[
            smem,
            pl.BlockSpec((n_slots, tokens, block), lambda i: (slots[0], 0, i + first)),
        ]
        + [
            pl.BlockSpec(
                (n_slots, tokens, right.shape[-1]),
                lambda i: (slots[0], 0, 0),
                pipeline_mode=whole,
            )
            for right in rights
        ]
        + [pl.BlockSpec((block, base.shape[1]), lambda i: (i + first, 0)) for base in bases],
        out_specs=tuple(out_specs),
    )
    if not inners:
        return outs
    outs = [out.reshape((-1,) + out.shape[2:]) for out in outs]
    return [(outs[2 * i], outs[2 * i + 1]) for i in range(len(rights))]


def stack_kernel(*refs, cuts):
    pieces, outs = refs[: -len(cuts)], refs[-len(cuts) :]
    for i, piece in enumerate(pieces):
        for out, (lo, hi) in zip(outs, cuts):
            out[i] = piece[:, lo:hi]


def stack_columns(pieces, cuts):
    return kernel_call(
        functools.partial(stack_kernel, cuts=cuts),
        "stack_columns",
        tuple(shape_of((len(pieces), pieces[0].shape[0], hi - lo), bf16) for lo, hi in cuts),
        tuple(pieces),
    )


def cut_kernel(core, values, kept_ref, sent_ref, *, n_dp, own, padded):
    kept_ref[...] = jnp.zeros_like(kept_ref)
    sent_ref[...] = jnp.zeros_like(sent_ref)
    for side, refs in ((0, (kept_ref, sent_ref)), (1, (sent_ref, kept_ref))):

        @pl.when(core[0] == side)
        def _():
            for s in range(2 * kept_ref.shape[0]):
                for d in range(n_dp):
                    start = (s * n_dp + d) * own
                    refs[s % 2][s // 2, 0, :, d * padded : d * padded + own] = values[
                        0, :, start : start + own
                    ].astype(bf16)


def cut_hidden(values, core, n_chips, n_dp, padded):
    two, rows, ff = values.shape
    own = ff // (2 * n_chips * n_dp)
    dims = (n_chips, two, rows, n_dp * padded)
    return kernel_call(
        functools.partial(cut_kernel, n_dp=n_dp, own=own, padded=padded),
        "cut_hidden",
        (shape_of(dims, bf16),) * 2,
        (core, values),
        grid=(two,),
        in_specs=[smem, pl.BlockSpec((1, rows, ff), lambda g: (g, 0, 0))],
        out_specs=(pl.BlockSpec((n_chips, 1, rows, n_dp * padded), lambda g: (0, g, 0, 0)),) * 2,
    )


def turn_kernel(chip, *refs, n_chips):
    ins, outs = refs[: len(refs) - n_chips], refs[len(refs) - n_chips :]
    per_side = len(ins) // 2
    for t, out in enumerate(outs):
        at = lax.rem(chip[0] + t, n_chips)
        for side in range(2):
            if per_side == 1:
                out[side] = ins[side][at]
            else:
                for g in range(2):
                    out[side, g] = ins[2 * side + g][at]


def turn_pairs(kept, got, chip, n_chips):
    rows, width = kept[0].shape[-2:]
    return kernel_call(
        functools.partial(turn_kernel, n_chips=n_chips),
        "turn_pairs",
        (shape_of((2, 2, rows, width), bf16),) * n_chips,
        (chip, *kept, *got),
        in_specs=[smem] + [vmem] * (len(kept) + len(got)),
    )


def add_kernel(*refs):
    *ins, out = refs
    total = ins[0][...].astype(f32)
    for ref in ins[1:]:
        total = total + ref[...].astype(f32)
    out[...] = total.astype(bf16)


def add(*arrays):
    return kernel_call(add_kernel, "add", shape_of(arrays[0].shape, bf16), arrays)


def add_turn_kernel(chip, kept, got, *outs):
    n = kept.shape[0]
    for t, out in enumerate(outs):
        at = lax.rem(chip[0] + t, n)
        out[...] = (kept[at].astype(f32) + got[at].astype(f32)).astype(bf16)


def add_turn(kept, got, chip):
    n = kept.shape[0]
    return kernel_call(
        add_turn_kernel,
        "add_turn",
        (shape_of(kept.shape[1:], bf16),) * n,
        (chip, kept, got),
        in_specs=[smem, vmem, vmem],
    )


def add_halve_kernel(mine, *refs):
    parts, (stays, goes) = refs[:-2], refs[-2:]
    count = len(parts) // 2
    at = 0
    for kept, got in zip(parts[:count], parts[count:]):
        for o in range(kept.shape[0]):
            for out, side in ((stays, mine[0]), (goes, 1 - mine[0])):
                out[at] = (kept[o, side].astype(f32) + got[o, side].astype(f32)).astype(bf16)
            at += 1


def add_halve(kept, got, mine, outer):
    rows, width = kept[0].shape[1:]
    blocks = sum(part.shape[0] for part in kept)
    inner = blocks // (2 * outer)
    half = shape_of((outer, inner, rows, width), bf16)
    stays, goes = kernel_call(
        add_halve_kernel,
        "add_halve",
        (half, half),
        (mine, *[part.reshape(-1, 2, inner, rows, width) for part in (*kept, *got)]),
        in_specs=[smem] + [vmem] * (len(kept) + len(got)),
        megabytes=40,
    )
    return stays.reshape(-1, rows, width), goes.reshape(-1, rows, width)


def add_halve_columns_kernel(mine, *refs, cuts):
    parts, (stays, goes) = refs[:-2], refs[-2:]
    count = len(parts) // 2
    lo = 0
    for kept, got, (first, last) in zip(parts[:count], parts[count:], cuts):
        hi = lo + last - first
        for o in range(kept.shape[0]):
            for out, side in ((stays, mine[0]), (goes, 1 - mine[0])):
                total = kept[o, side, :, :, first:last].astype(f32) + got[
                    o, side, :, :, first:last
                ].astype(f32)
                out[o, :, :, lo:hi] = total.astype(bf16)
        lo = hi


def add_halve_columns(kept, got, cuts, mine, outer):
    blocks, rows, _ = kept[0].shape
    inner = blocks // (2 * outer)
    width = sum(last - first for first, last in cuts)
    half = shape_of((outer, inner, rows, width), bf16)
    stays, goes = kernel_call(
        functools.partial(add_halve_columns_kernel, cuts=cuts),
        "add_halve",
        (half, half),
        (mine, *[part.reshape(outer, 2, inner, rows, -1) for part in (*kept, *got)]),
        in_specs=[smem] + [vmem] * (len(kept) + len(got)),
        megabytes=44,
    )
    return stays.reshape(-1, rows, width), goes.reshape(-1, rows, width)


def adamw_update(master, moment_one, moment_two, gradient, step_rate, decay_weight):
    first_new = beta_one * moment_one + (1.0 - beta_one) * gradient
    second_new = beta_two * moment_two + (1.0 - beta_two) * gradient * gradient
    first_hat = first_new / (1.0 - beta_one**STEP)
    second_hat = second_new / (1.0 - beta_two**STEP)
    master_new = master - step_rate * (
        first_hat / (jnp.sqrt(second_hat) + adam_eps) + decay_weight * master
    )
    return (first_new, second_new, master_new)


def adamw_kernel(where, master, first, second, *refs, n_dp, own, padded, rate, decay):
    pieces, (first_ref, second_ref, master_ref, slots, joined) = refs[:-5], refs[-5:]
    for t, piece in enumerate(pieces):
        for o in range(2):
            slots[where[2 * t + o]] = piece[o, 0]
    for s in range(slots.shape[0]):
        for d in range(n_dp):
            start = (s * n_dp + d) * own
            joined[:, start : start + own] = slots[
                s, :, d * padded : d * padded + own
            ].astype(f32)
    first_ref[0], second_ref[0], master_ref[0] = adamw_update(
        master[0], first[0], second[0], joined[...], rate, decay
    )


def adamw_hidden(master, first, second, pieces, where, n_dp, padded, rate, decay):
    two, rows, ff = master.shape
    n_seq = 2 * len(pieces)
    own = ff // (n_seq * n_dp)
    block = pl.BlockSpec((1, rows, ff), lambda g: (g, 0, 0))
    part = pl.BlockSpec((2, 1, rows, n_dp * padded), lambda g: (0, g, 0, 0))
    return kernel_call(
        functools.partial(
            adamw_kernel, n_dp=n_dp, own=own, padded=padded, rate=rate, decay=decay
        ),
        "adamw_hidden",
        (shape_of(master.shape, f32),) * 3,
        (where, master, first, second, *pieces),
        megabytes=44,
        grid=(two,),
        in_specs=[smem] + [block] * 3 + [part] * len(pieces),
        out_specs=(block,) * 3,
        scratch_shapes=[
            pltpu.VMEM((n_seq, rows, n_dp * padded), bf16),
            pltpu.VMEM((rows, ff), f32),
        ],
    )


def assemble_kernel(where, *refs, splits, counts):
    ins, outs, sems = refs[: len(counts)], refs[len(counts) : -1], refs[-1]
    copies = []
    entry = 0
    for ref, (column, count) in zip(ins, counts):
        for i in range(count):
            for out, start, width in splits[column]:
                copies.append(
                    pltpu.make_async_copy(
                        ref.at[i, :, pl.ds(start, width)],
                        outs[out[0]].at[where[entry], :, pl.ds(out[1], width)],
                        sems.at[len(copies)],
                    )
                )
            entry += 1
    for copy in copies:
        copy.start()
    for copy in copies:
        copy.wait()


def assemble(pieces, where, splits, out_widths):
    counts = [(column, array.shape[0]) for array, column in pieces]
    rows = pieces[0][0].shape[1]
    blocks = sum(count for column, count in counts if column == 0)
    n_copies = sum(count * len(splits[column]) for column, count in counts)
    return kernel_call(
        functools.partial(assemble_kernel, splits=splits, counts=counts),
        "assemble",
        tuple(shape_of((blocks, rows, w), bf16) for w in out_widths),
        (where.astype(jnp.int32), *[array for array, _ in pieces]),
        in_specs=[smem] + [anywhere] * len(pieces),
        out_specs=(vmem,) * len(out_widths),
        scratch_shapes=[pltpu.SemaphoreType.DMA((n_copies,))],
    )


def seq_perm(values, chips, flip):
    count = lax.axis_size("seq")
    return lax.ppermute(
        values, "seq", [(i, ((i + 2 * chips) % count) ^ flip) for i in range(count)]
    )


def dp_perm(values, bit):
    return lax.ppermute(values, "dp", [(i, i ^ bit) for i in range(lax.axis_size("dp"))])


def dp_bits():
    return [1 << i for i in range(lax.axis_size("dp").bit_length() - 1)]


def pick(values, index, axis):
    return lax.dynamic_index_in_dim(values, index, axis, keepdims=False)


def places_of():
    n_chips = lax.axis_size("seq") // 2
    seq_at = lax.axis_index("seq")
    return n_chips, seq_at // 2, seq_at % 2, lax.axis_size("dp"), lax.axis_index("dp")


def swap(values):
    return seq_perm(values, 0, 1)


def sent_pieces(values):
    return [values] + [seq_perm(values, t, 0) for t in range(1, lax.axis_size("seq") // 2)]


def shards(
    tokens,
    cotangent,
    positions,
    qkv_master,
    qkv_first,
    qkv_second,
    out_master,
    out_first,
    out_second,
    gate_up_master,
    gate_up_first,
    gate_up_second,
    down_master,
    down_first,
    down_second,
    small_master,
    small_first,
    small_second,
):
    n_chips, chip_at, core_at, n_dp, dp_at = places_of()
    n_seq = 2 * n_chips
    n_all = n_seq * n_dp
    bits = dp_bits()
    rows_own, qkv_width = qkv_master.shape
    half = qkv_width // 2
    small_own = small_master.shape[0]
    ff_dev = down_master.shape[0]
    ff_pad = -(-ff_dev // 16) * 16
    ff_own = n_dp * ff_pad
    inputs = tokens[0]
    upstream = cotangent[0]
    tok_rows = inputs.shape[0]
    seq_length = positions.shape[1]
    shifts = list(range(1, n_chips))

    ring_chips = [(chip_at - t) % n_chips for t in range(n_chips)]
    ring_order = jnp.stack(
        [chip * 2 + (core_at ^ flip) for chip in ring_chips for flip in range(2)]
    ).astype(jnp.int32)
    bases = positions[0, ::PIECE].reshape(n_seq, tok_rows // PIECE)
    key_bases = jnp.take(bases, ring_order, axis=0)
    query_bases = key_bases[0]
    key_bases = key_bases.reshape(-1)
    own_places = lax.dynamic_slice_in_dim(
        positions[0], (chip_at * 2 + core_at) * tok_rows, tok_rows, 0
    )
    cosine, sine = rotary_tables(own_places)

    small_block = jnp.pad(
        small_master.astype(bf16), (0, rows_own * HD - small_own)
    ).reshape(rows_own, HD)
    packed = jnp.concatenate([small_block, qkv_master.astype(bf16)], axis=1)
    qkv_ring = sent_pieces(packed)
    core_side = core_at.reshape(1).astype(jnp.int32)
    chip_side = chip_at.reshape(1).astype(jnp.int32)
    bit_sides = {bit: ((dp_at // bit) % 2).reshape(1).astype(jnp.int32) for bit in bits}
    cut_kept, cut_sent = cut_hidden(gate_up_master, core_side, n_chips, n_dp, ff_pad)
    to_send = turn_pairs([cut_kept], [swap(cut_sent)], chip_side, n_chips)
    qkv_ring, to_send, cosine, sine = fence(qkv_ring, to_send, cosine, sine)

    def exchange(shift):
        return seq_perm(to_send[shift], shift, 0)

    w_out = lax.all_gather(out_master.astype(bf16), ("seq", "dp"), axis=0, tiled=True)

    columns = ((0, HD + half), (HD + half, HD + qkv_width))
    orders = (bits, bits[::-1])
    held = list(stack_columns(qkv_ring, columns))
    flips = [[0], [0]]
    gate_up_pieces = {0: to_send[0]}
    groups = [shifts[:1], shifts[-1:], shifts[1:-1]] if n_chips > 2 else [shifts, [], []]
    for stage in range(len(bits)):
        got = [dp_perm(h, order[stage]) for h, order in zip(held, orders)]
        if stage == len(bits) - 1:
            swapped = [swap(h) for h in held]
        for shift in groups[min(stage, 1)] if stage < 2 else []:
            gate_up_pieces[shift] = exchange(shift)
        got, held, gate_up_pieces = fence(got, held, gate_up_pieces)
        flips = [f + [k ^ order[stage] for k in f] for f, order in zip(flips, orders)]
        if stage < len(bits) - 1:
            held = [jnp.concatenate([h, g], axis=0) for h, g in zip(held, got)]
    (swapped,) = fence(swapped)
    for shift in groups[2]:
        gate_up_pieces[shift] = exchange(shift)
    down_share = jnp.pad(down_master.astype(bf16), ((0, ff_pad - ff_dev), (0, 0)))
    w_down = lax.all_gather(after(down_share, *got), "dp", axis=0, tiled=True)
    got_swapped = [swap(g) for g in got]
    pieces, where = [], []
    for column in range(2):
        for flip, part, ks in (
            (0, held[column], flips[column][: n_dp // 2]),
            (0, got[column], flips[column][n_dp // 2 :]),
            (1, swapped[column], flips[column][: n_dp // 2]),
            (1, got_swapped[column], flips[column][n_dp // 2 :]),
        ):
            pieces.append((part, column))
            where += [
                (chip * 2 + (core_at ^ flip)) * n_dp + (dp_at ^ k) for k in ks for chip in ring_chips
            ]
    w_qkv, small_blocks = assemble(
        pieces,
        jnp.stack(where),
        ((((1, 0), 0, HD), ((0, 0), HD, half)), (((0, half), 0, half),)),
        (qkv_width, HD),
    )
    w_qkv = w_qkv.reshape(D, qkv_width)
    small_params = small_blocks.reshape(n_all, rows_own * HD)[:, :small_own].reshape(1, -1)
    small_params = small_params.astype(f32)
    gain_one = small_params[:, :D]
    gain_two = small_params[:, D : 2 * D]
    qkv_bias = small_params[:, 2 * D :]
    normed_one, key_value = project_kv(inputs, w_qkv, gain_one, qkv_bias, cosine, sine)
    gate_up_held = [
        jnp.concatenate([gate_up_pieces[t] for t in ts], axis=0)
        for ts in (range(n_chips // 2), range(n_chips // 2, n_chips))
    ]
    normed_one, key_value, gate_up_held = fence(normed_one, key_value, gate_up_held)

    kv_ring = sent_pieces(key_value)
    gate_up_parts = [
        [held, dp_perm(held, order[0])] for held, order in zip(gate_up_held, orders)
    ]
    gate_up_flips = [[0, order[0]] for order in orders]
    queries = project_q(normed_one, w_qkv, qkv_bias, cosine, sine)
    kv_swapped = [swap(kv_ring[0])] + [swap(after(piece, queries)) for piece in kv_ring[1:]]
    kv_ring, kv_swapped, gate_up_parts, queries, upstream = fence(
        kv_ring, kv_swapped, gate_up_parts, queries, upstream
    )

    def cross(start, stop, stage):
        for parts, flips_of, order in zip(gate_up_parts, gate_up_flips, orders):
            parts += [dp_perm(piece, order[stage]) for piece in parts[start:stop]]
            flips_of += [k ^ order[stage] for k in flips_of[start:stop]]

    upstream_ring = [upstream, seq_perm(upstream, 1, 0)]
    cross(0, 1 if len(bits) == 2 else 2, 1)
    attended, logsum, key_value_all = attend(
        queries, [piece for pair in zip(kv_ring, kv_swapped) for piece in pair], query_bases, key_bases
    )
    gate_up_parts, upstream_ring, attended, logsum, key_value_all = fence(
        gate_up_parts, upstream_ring, attended, logsum, key_value_all
    )

    def ring_step(pieces):
        return pieces + [seq_perm(pieces[-1], 1, 0)] if len(pieces) < n_chips else pieces

    upstream_ring = ring_step(upstream_ring)
    if len(bits) == 2:
        cross(1, 2, 1)
    else:
        cross(0, 4, 2)
    upstream_swapped = [swap(piece) for piece in upstream_ring[:2]]
    residual, normed_two, attended_low = out_project(inputs, attended, w_out, gain_two)
    normed_ring, normed_swapped = [normed_two], [swap(normed_two)]
    gate_up_parts, upstream_ring, upstream_swapped, normed_ring, normed_swapped, residual = fence(
        gate_up_parts, upstream_ring, upstream_swapped, normed_ring, normed_swapped, residual
    )

    pieces, where = [], []
    for column, (parts, flips_of) in enumerate(zip(gate_up_parts, gate_up_flips)):
        slots = ring_order[:n_chips] if column == 0 else ring_order[n_chips:]
        for part, k in zip(parts, flips_of):
            pieces.append((part.reshape(-1, rows_own, ff_own), 0))
            block = slots * n_dp + (dp_at ^ k)
            where.append(jnp.stack([block, n_all + block], axis=1).reshape(-1))
    (w_gate_up,) = assemble(
        pieces, jnp.concatenate(where), ((((0, 0), 0, ff_own),),), (ff_own,)
    )
    w_gate_up = w_gate_up.reshape(2, D, ff_own)
    out_pairs, kept = [], ()
    running = None
    for slot in range(n_chips):
        sent = None if running is None else seq_perm(running, 1, 0)
        normed_ring = ring_step(normed_ring)
        upstream_ring = ring_step(upstream_ring)
        out_own, out_other, grad_own, grad_other, *kept = feed_forward(
            (normed_ring[slot], normed_swapped[slot]),
            (upstream_ring[slot], upstream_swapped[slot]),
            w_gate_up,
            w_down,
            slot,
            n_chips,
            kept,
        )
        grad_swapped = swap(grad_other)
        if slot + 1 < n_chips:
            normed_swapped = normed_swapped + [swap(after(normed_ring[slot + 1], grad_own))]
        if slot + 2 < n_chips and len(upstream_swapped) < slot + 3:
            upstream_swapped = upstream_swapped + [swap(after(upstream_ring[slot + 2], grad_own))]
        if slot == 0:
            grad_first = (grad_own, grad_swapped)
        elif sent is None:
            running = add(grad_own, grad_swapped)
        else:
            running = add(grad_own, grad_swapped, after(sent, grad_own))
        running, normed_ring, normed_swapped, upstream_ring, upstream_swapped, kept = fence(
            running, normed_ring, normed_swapped, upstream_ring, upstream_swapped, kept
        )
        out_pairs = out_pairs + [(out_own, out_other)]
        if 1 < slot:
            out_pairs[slot - 1] = (out_pairs[slot - 1][0], swap(out_pairs[slot - 1][1]))
        if slot == 2:
            ring_first = add(*out_pairs[1])

    grad_ring = jnp.zeros_like(grad_first[0]) if running is None else seq_perm(running, 1, 0)
    normed_all, ffn_all, hidden_all, gate_grads_all, up_grads_all = kept
    first_split = (
        jnp.concatenate([bit_sides[order[0]] for order in orders]),
        tuple(order[0] for order in orders),
    )
    halves = [
        weight_grad(
            normed_all,
            (gate_grads_all, up_grads_all),
            split=first_split,
            rows=rows_own,
            part=(part, 2),
        )
        for part in range(2)
    ]
    out_running = seq_perm(ring_first, 1, 0)
    out_running = add(after(out_running, *halves[0][0]), *out_pairs[2])
    grad_ring, halves, out_pairs, out_running = fence(grad_ring, halves, out_pairs, out_running)

    got_one = [dp_perm(goes, order[0]) for (_, goes), order in zip(halves[0], orders)]
    out_running = seq_perm(out_running, 1, 0)
    out_pairs[-1] = (out_pairs[-1][0], swap(out_pairs[-1][1]))
    residual_grads, branch_grads, attended_grads, gain_two_grad = norm_back(
        grad_ring, *grad_first, residual, upstream, gain_two, w_out
    )
    query_pre, kv_grad_own, kv_grad_other = attend_back(
        queries,
        key_value_all,
        attended_grads,
        attended,
        logsum,
        query_bases,
        key_bases,
        cosine,
        sine,
    )
    got_one, kv_grad_own, kv_grad_other, query_pre, branch_grads, out_running, out_pairs = fence(
        got_one, kv_grad_own, kv_grad_other, query_pre, branch_grads, out_running, out_pairs
    )
    own_parts = kv_grad_own.reshape(n_chips, tok_rows, 2 * KVW)
    other_parts = swap(kv_grad_other).reshape(n_chips, tok_rows, 2 * KVW)
    kv_sum = add_turn(own_parts, other_parts, jnp.zeros_like(chip_side))
    kv_sum, halves, query_pre, branch_grads, kept = fence(
        kv_sum, halves, query_pre, branch_grads, kept
    )

    def next_split(kept_parts, got, done_bits, left_bits):
        rest = [bit for bit in bits[::-1] if bit not in done_bits]
        bit = left_bits[0]
        lead = sum(part.shape[0] for part in kept_parts) // 2 ** len(rest)
        return add_halve(kept_parts, got, bit_sides[bit], lead * 2 ** rest.index(bit))

    kv_got = [seq_perm(kv_sum[t], n_chips - t, 0) for t in range(1, n_chips)]
    got_two = [dp_perm(goes, order[0]) for (_, goes), order in zip(halves[1], orders)]
    by_core = (core_side, (n_dp,))
    (query_split,) = weight_grad(normed_one[None], (query_pre[None],), split=by_core, rows=rows_own)
    (out_split,) = weight_grad(
        attended_low[None], (branch_grads[None],), split=by_core, rows=rows_own
    )
    (down_grad,) = weight_grad(kept[2], (kept[1],))
    out_running = add(out_running, *out_pairs[3])
    kv_got, got_two, query_split, out_split, down_grad, out_running = fence(
        kv_got, got_two, query_split, out_split, down_grad, out_running
    )

    out_running = seq_perm(out_running, 1, 0)
    gate_up_split = [
        next_split([one[0], two[0]], [got, other], order[:1], order[1:])
        for one, two, got, other, order in zip(*halves, got_one, got_two, orders)
    ]
    gate_up_sums = [dp_perm(goes, order[1]) for (_, goes), order in zip(gate_up_split, orders)]
    both = [(split[0], swap(split[1])) for split in (query_split, out_split)]
    key_value_pre, input_grads, gain_one_grad, bias_grad = input_back(
        inputs,
        gain_one,
        w_qkv,
        query_pre,
        cosine,
        sine,
        residual_grads,
        kv_sum[0],
        kv_got,
    )
    down_split = split_columns(
        down_grad.reshape(n_dp, ff_pad, D),
        first_split[0],
        ((0, D // 2), (D // 2, D)),
        tuple(order[0] for order in orders),
    )
    ((kv_stays, kv_goes),) = weight_grad(
        normed_one[None], (key_value_pre[None],), split=by_core, rows=rows_own
    )
    (
        gate_up_split,
        gate_up_sums,
        down_split,
        both,
        input_grads,
        kv_stays,
        kv_goes,
        out_running,
        small_parts,
    ) = fence(
        gate_up_split,
        gate_up_sums,
        down_split,
        both,
        input_grads,
        kv_stays,
        kv_goes,
        out_running,
        (gain_one_grad, gain_two_grad, bias_grad),
    )

    down_got = [dp_perm(goes, order[0]) for (_, goes), order in zip(down_split, orders)]
    ready = []
    for split, got, order in zip(gate_up_split, gate_up_sums, orders):
        kept_part = split[0]
        for i in range(2, len(order)):
            kept_part, goes = next_split([kept_part], [got], order[:i], order[i:])
            got = dp_perm(goes, order[i])
        ready.append(add_halve([kept_part], [got], core_side, n_chips))
    to_send = turn_pairs(
        [kept_part for kept_part, _ in ready],
        [swap(sent) for _, sent in ready],
        chip_side,
        n_chips,
    )
    small_grad = jnp.concatenate(small_parts, axis=1).astype(bf16)
    small_grad = jnp.pad(
        small_grad.reshape(n_all, small_own), ((0, 0), (0, rows_own * HD - small_own))
    ).reshape(n_chips, 2, n_dp, rows_own, HD)
    kv_stays = jnp.concatenate(
        [pick(small_grad, core_at, 1).reshape(-1, rows_own, HD), kv_stays], axis=2
    )
    kv_goes = jnp.concatenate(
        [pick(small_grad, 1 - core_at, 1).reshape(-1, rows_own, HD), kv_goes], axis=2
    )
    kv_got = swap(kv_goes)
    rest_cuts = (((0, D), (0, 3 * HD)), ((0, D), (3 * HD, HD + 2 * KVW)))
    rest = [
        add_halve_columns(
            [kept_part, kv_stays],
            [got, kv_got],
            cuts,
            bit_sides[order[0]],
            n_chips * n_dp // (2 * order[0]),
        )
        for (kept_part, got), cuts, order in zip(both, rest_cuts, orders)
    ]
    to_send, rest, out_running, down_got = fence(to_send, rest, out_running, down_got)

    gate_up_owned = {0: to_send[0]}
    rest_got = [dp_perm(goes, order[0]) for (_, goes), order in zip(rest, orders)]
    for shift in groups[0] + groups[2]:
        gate_up_owned[shift] = exchange(shift)
    if len(bits) > 1:
        down_split = [
            next_split([kept_part], [got], order[:1], order[1:])
            for (kept_part, _), got, order in zip(down_split, down_got, orders)
        ]
    out_pairs[0] = (out_pairs[0][0], swap(out_pairs[0][1]))
    gate_up_owned, rest_got, down_split, out_pairs = fence(
        gate_up_owned, rest_got, down_split, out_pairs
    )

    for shift in groups[1]:
        gate_up_owned[shift] = exchange(shift)
    rest_send = []
    for (kept_part, _), got, order in zip(rest, rest_got, orders):
        for i in range(1, len(order)):
            kept_part, goes = next_split([kept_part], [got], order[:i], order[i:])
            got = dp_perm(goes, order[i])
        rest_send.append(add_turn(kept_part, got, chip_side))
    gate_up_owned, rest_send, down_split = fence(gate_up_owned, rest_send, down_split)

    rest_send = [
        jnp.concatenate([parts[t] for parts in rest_send], axis=1) for t in range(n_chips)
    ]
    rest_ring = [rest_send[0]] + [seq_perm(rest_send[shift], shift, 0) for shift in shifts]
    down_owned = []
    for (kept_part, goes), got, order in zip(down_split, down_got, orders):
        for i in range(1, len(order)):
            if i > 1:
                kept_part, goes = next_split([kept_part], [got], order[:i], order[i:])
            got = dp_perm(goes, order[i])
        down_owned.append(kept_part[0, :ff_dev].astype(f32) + got[0, :ff_dev].astype(f32))
    down_owned = jnp.concatenate(down_owned, axis=1)
    down_new = adamw_update(down_master, down_first, down_second, down_owned, 0.026, 0.1)
    rest_ring, down_new = fence(rest_ring, down_new)
    total = sum(piece.astype(f32) for piece in rest_ring)
    for t in range(4, n_chips):
        out_running = seq_perm(add(out_running, *out_pairs[t]), 1, 0)
    outputs = residual + out_pairs[0][0].astype(f32) + out_pairs[0][1].astype(f32)
    outputs = outputs + out_running.astype(f32)
    outputs = outputs.astype(bf16)
    gate_up_new = adamw_hidden(
        gate_up_master,
        gate_up_first,
        gate_up_second,
        [gate_up_owned[t] for t in range(n_chips)],
        ring_order,
        n_dp,
        ff_pad,
        0.064,
        0.1,
    )
    wide = D + 3 * HD
    query_owned, out_owned = total[:, :D], total[:, wide : wide + D]
    small_owned = total[:, D : D + HD]
    qkv_owned = jnp.concatenate(
        [query_owned, total[:, D + HD : wide], total[:, wide + D :]], axis=1
    )
    small_owned = small_owned.reshape(-1)[:small_own]

    qkv_new = adamw_update(qkv_master, qkv_first, qkv_second, qkv_owned, 0.09, 0.1)
    out_new = adamw_update(out_master, out_first, out_second, out_owned, 0.18, 0.1)
    small_new = adamw_update(small_master, small_first, small_second, small_owned, 0.6, 0.0)
    return (
        outputs[None],
        input_grads[None],
        *qkv_new,
        *out_new,
        *gate_up_new,
        *down_new,
        *small_new,
    )


def solution(mesh):
    in_specs = (
        P("dp", "seq", None),
        P("dp", "seq", None),
        P("dp", None),
        P(("seq", "dp"), None),
        P(("seq", "dp"), None),
        P(("seq", "dp"), None),
        P(("seq", "dp"), None),
        P(("seq", "dp"), None),
        P(("seq", "dp"), None),
        P(None, ("seq", "dp"), None),
        P(None, ("seq", "dp"), None),
        P(None, ("seq", "dp"), None),
        P(("seq", "dp"), None),
        P(("seq", "dp"), None),
        P(("seq", "dp"), None),
        P(("seq", "dp")),
        P(("seq", "dp")),
        P(("seq", "dp")),
    )
    out_specs = (
        P("dp", "seq", None),
        P("dp", "seq", None),
        P(("seq", "dp"), None),
        P(("seq", "dp"), None),
        P(("seq", "dp"), None),
        P(("seq", "dp"), None),
        P(("seq", "dp"), None),
        P(("seq", "dp"), None),
        P(None, ("seq", "dp"), None),
        P(None, ("seq", "dp"), None),
        P(None, ("seq", "dp"), None),
        P(("seq", "dp"), None),
        P(("seq", "dp"), None),
        P(("seq", "dp"), None),
        P(("seq", "dp")),
        P(("seq", "dp")),
        P(("seq", "dp")),
    )
    return jax.shard_map(shards, mesh=mesh, in_specs=in_specs, out_specs=out_specs, check_vma=False)
```

```python
import functools

import jax
import jax.numpy as jnp
from jax import lax
from jax.experimental import pallas as pl
from jax.experimental.pallas import tpu as pltpu
from jax.sharding import PartitionSpec as P

D = 1536
HEADS = 12
KVH = 2
HD = 128
STEP = 10
KVW = KVH * HD
PIECE = 128


norm_eps = 1e-06
rope_base = 1000000.0
beta_one = 0.9
beta_two = 0.95
adam_eps = 1e-08
masked_score = -1e30
log2_e = 1.4426950408889634
bf16 = jnp.bfloat16
f32 = jnp.float32
vmem = pl.BlockSpec(memory_space=pltpu.VMEM)
smem = pl.BlockSpec(memory_space=pltpu.SMEM)
anywhere = pl.BlockSpec(memory_space=pl.ANY)


def shape_of(dims, kind):
    return jax.ShapeDtypeStruct(dims, kind)


def kernel_call(kernel, name, out_shape, operands, megabytes=32, **options):
    return pl.pallas_call(
        kernel,
        name=name,
        out_shape=out_shape,
        compiler_params=pltpu.CompilerParams(vmem_limit_bytes=megabytes << 20),
        cost_estimate=pl.CostEstimate(flops=10**6, bytes_accessed=10**6, transcendentals=0),
        **options,
    )(*operands)


def after(values, *others):
    return lax.optimization_barrier((values,) + others)[0]


def fence(*groups):
    flat, tree = jax.tree.flatten(groups)
    return jax.tree.unflatten(tree, lax.optimization_barrier(tuple(flat)))


def dot(left, right):
    return jnp.dot(left, right, preferred_element_type=f32)


def dot_transposed(left, right):
    return lax.dot_general(left, right, (((1,), (1,)), ((), ())), preferred_element_type=f32)


def rotary_tables(places):
    half_size = HD // 2
    freqs = rope_base ** (-(jnp.arange(half_size).astype(f32) * (2.0 / HD)))
    angles = places.astype(f32)[:, None] * freqs[None, :]
    cosine, sine = jnp.cos(angles), jnp.sin(angles)
    return jnp.concatenate([cosine, cosine], axis=1), jnp.concatenate([-sine, sine], axis=1)


def rms_scale(values):
    return lax.rsqrt(jnp.mean(values * values, axis=-1, keepdims=True) + norm_eps)


def swap_halves(values):
    return pltpu.roll(values, HD // 2, 1)


def head(index):
    return slice(index * HD, (index + 1) * HD)


def project_kv_kernel(tokens, w_qkv, gain, bias, cosine, sine, normed_ref, kv_ref):
    inputs = tokens[...].astype(f32)
    normed = (inputs * rms_scale(inputs) * gain[...]).astype(bf16)
    normed_ref[...] = normed
    rows = dot(normed, w_qkv[...]) + bias[:, D:]
    for j in range(KVH):
        part = rows[:, head(j)]
        kv_ref[:, head(j)] = (part * cosine[...] + swap_halves(part) * sine[...]).astype(bf16)
    kv_ref[:, KVW:] = rows[:, KVW:].astype(bf16)


def project_q_kernel(normed, w_qkv, bias, cosine, sine, query_ref):
    rows = dot(normed[...], w_qkv[...]) + bias[:, :D]
    for j in range(HEADS):
        part = rows[:, head(j)]
        query_ref[:, head(j)] = (part * cosine[...] + swap_halves(part) * sine[...]).astype(bf16)


def project_kv(tokens, w_qkv, gain, bias, cosine, sine):
    rows = tokens.shape[0]
    return kernel_call(
        project_kv_kernel,
        "project_kv",
        (shape_of((rows, D), bf16), shape_of((rows, 2 * KVW), bf16)),
        (tokens, w_qkv, gain, bias, cosine, sine),
        megabytes=58,
        grid=(1,),
        in_specs=[vmem, pl.BlockSpec((D, 2 * KVW), lambda i: (0, D // (2 * KVW)))] + [vmem] * 4,
        out_specs=(vmem, vmem),
    )


def project_q(normed, w_qkv, bias, cosine, sine):
    return kernel_call(
        project_q_kernel,
        "project_q",
        shape_of(normed.shape, bf16),
        (normed, w_qkv, bias, cosine, sine),
        megabytes=58,
        grid=(1,),
        in_specs=[vmem, pl.BlockSpec((D, D), lambda i: (0, 0))] + [vmem] * 3,
        out_specs=vmem,
    )


def mask_keys(values, query_bases, key_bases, first_run, fill):
    later = lax.broadcasted_iota(jnp.int32, (PIECE, PIECE), 0) - lax.broadcasted_iota(
        jnp.int32, (PIECE, PIECE), 1
    )
    keys, queries = values.shape
    rows = []
    for r in range(keys // PIECE):
        down = slice(r * PIECE, (r + 1) * PIECE)
        row = []
        for q in range(queries // PIECE):
            gap = query_bases[q] - key_bases[first_run + r]
            row.append(jnp.where(later <= gap, values[down, q * PIECE : (q + 1) * PIECE], fill))
        rows.append(jnp.concatenate(row, axis=1))
    return jnp.concatenate(rows, axis=0)


def attend_kernel(query_bases, key_bases, q_ref, *refs):
    pieces, (out_ref, lse_ref, kv_ref) = refs[:-3], refs[-3:]
    rows = q_ref.shape[0]
    for i, piece in enumerate(pieces):
        kv_ref[i * rows : (i + 1) * rows, :] = piece[...]
    groups = HEADS // KVH
    scale = HD**-0.5 * log2_e
    for kv in range(KVH):
        values = kv_ref[:, head(KVH + kv)].T
        for h in range(kv * groups, (kv + 1) * groups):
            queries = q_ref[:, head(h)]
            scores = []
            for run in range(key_bases.shape[0]):
                keys = kv_ref[run * PIECE : (run + 1) * PIECE, head(kv)]
                part = dot_transposed(keys, queries)
                scores.append(mask_keys(part, query_bases, key_bases, run, masked_score))
            scores = jnp.concatenate(scores, axis=0)
            top = jnp.max(scores, axis=0, keepdims=True)
            weights = jnp.exp2((scores - top) * scale)
            total = jnp.sum(weights, axis=0, keepdims=True)
            mixed = dot(values, weights.astype(bf16))
            out_ref[:, head(h)] = (mixed / total).T
            lse_ref[h : h + 1, :] = top * scale + jnp.log2(total)


def attend(queries, pieces, query_bases, key_bases):
    rows, total = queries.shape[0], key_bases.shape[0] * PIECE
    return kernel_call(
        attend_kernel,
        "attend",
        (
            shape_of((rows, D), f32),
            shape_of((HEADS, rows), f32),
            shape_of((total, 2 * KVW), bf16),
        ),
        (query_bases, key_bases, queries, *pieces),
        in_specs=[smem] * 2 + [vmem] * (1 + len(pieces)),
    )


def out_kernel(tokens, attended, w_out, gain, residual_ref, normed_ref, low_ref):
    low = attended[...].astype(bf16)
    low_ref[...] = low
    residual = tokens[...].astype(f32) + dot(low, w_out[...])
    residual_ref[...] = residual
    normed_ref[...] = (residual * rms_scale(residual) * gain[...]).astype(bf16)


def out_project(tokens, attended, w_out, gain):
    dims = tokens.shape
    return kernel_call(
        out_kernel,
        "out_project",
        (shape_of(dims, f32), shape_of(dims, bf16), shape_of(dims, bf16)),
        (tokens, attended, w_out, gain),
    )


def ffn_kernel(
    normed_own, normed_other, grad_own, grad_other, w_gate_up, w_down, *refs, earlier
):
    refs = refs[earlier:]
    out_refs, grad_refs = refs[:2], refs[2:4]
    normed_ref, ffn_grad_ref, hidden_ref, gate_ref, up_ref = refs[4:]
    rows = normed_own.shape[0]
    for i, (normed_in, grad_in) in enumerate(((normed_own, grad_own), (normed_other, grad_other))):
        to = slice(i * rows, (i + 1) * rows)
        normed, ffn_grad = normed_in[...], grad_in[...]
        normed_ref[0, to, :] = normed
        ffn_grad_ref[0, to, :] = ffn_grad
        gate = dot(normed, w_gate_up[0])
        up = dot(normed, w_gate_up[1])
        sigmoid = 1.0 / (1.0 + jnp.exp(-gate))
        silu = gate * sigmoid
        hidden = (silu * up).astype(bf16)
        hidden_ref[0, to, :] = hidden
        out_refs[i][...] = dot(hidden, w_down[...]).astype(bf16)
        hidden_grad = dot_transposed(ffn_grad, w_down[...])
        gate_grad = (hidden_grad * up * sigmoid * (1.0 + gate * (1.0 - sigmoid))).astype(bf16)
        up_grad = (hidden_grad * silu).astype(bf16)
        gate_ref[0, to, :] = gate_grad
        up_ref[0, to, :] = up_grad
        grad_refs[i][...] = (
            dot_transposed(gate_grad, w_gate_up[0]) + dot_transposed(up_grad, w_gate_up[1])
        ).astype(bf16)


def feed_forward(normed, grads, w_gate_up, w_down, slot, slots, kept):
    rows, width = normed[0].shape
    ff_own = w_down.shape[0]
    token = shape_of((rows, width), bf16)
    widths = (width, width, ff_own, ff_own, ff_own)
    operands = (*normed, *grads, w_gate_up, w_down)
    return kernel_call(
        functools.partial(ffn_kernel, earlier=len(kept)),
        "feed_forward",
        (token,) * 4 + tuple(shape_of((slots, 2 * rows, w), bf16) for w in widths),
        (*operands, *kept),
        grid=(1,),
        in_specs=[vmem] * len(operands) + [anywhere] * len(kept),
        out_specs=(vmem,) * 4
        + tuple(pl.BlockSpec((1, 2 * rows, w), lambda i: (slot, 0, 0)) for w in widths),
        input_output_aliases={len(operands) + i: 4 + i for i in range(len(kept))},
    )


def norm_back_kernel(
    got, own, other, residual_ref, cotangent, gain, w_out, grad_ref, low_ref, back_ref, gain_ref
):
    normed_grad = got[...].astype(f32) + own[...].astype(f32) + other[...].astype(f32)
    residual = residual_ref[...]
    scale = rms_scale(residual)
    unit = residual * scale
    gain_ref[...] = jnp.sum(normed_grad * unit, axis=0, keepdims=True)
    weighted = normed_grad * gain[...]
    grad = cotangent[...].astype(f32) + scale * (
        weighted - unit * jnp.mean(weighted * unit, axis=-1, keepdims=True)
    )
    grad_ref[...] = grad
    low = grad.astype(bf16)
    low_ref[...] = low
    back_ref[...] = dot_transposed(low, w_out[...]).astype(bf16)


def norm_back(got, own, other, residual, cotangent, gain, w_out):
    dims = residual.shape
    return kernel_call(
        norm_back_kernel,
        "norm_back",
        (shape_of(dims, f32), shape_of(dims, bf16), shape_of(dims, bf16), shape_of((1, D), f32)),
        (got, own, other, residual, cotangent, gain, w_out),
    )


def attend_back_kernel(
    query_bases,
    key_bases,
    q_ref,
    kv_ref,
    grad_ref,
    out_ref,
    lse_ref,
    cosine,
    sine,
    q_grad_ref,
    kv_own_ref,
    kv_other_ref,
    q_rows,
    grad_rows,
    deltas,
    q_sums,
):
    rows = q_ref.shape[0]
    groups = HEADS // KVH
    scale = HD**-0.5
    for kv in range(KVH):
        for j in range(groups):
            part = slice(j * rows, (j + 1) * rows)
            columns = head(kv * groups + j)
            q_rows[part, :] = q_ref[:, columns]
            grads = grad_ref[:, columns]
            grad_rows[part, :] = grads
            product = grads.astype(f32) * out_ref[:, columns]
            deltas[:, part] = jnp.sum(product.T, axis=0, keepdims=True)
        q_sums[...] = jnp.zeros_like(q_sums)

        @pl.loop(0, kv_ref.shape[0] // (2 * rows), unroll=2)
        def _(step):
            at = pl.ds(pl.multiple_of(step * (2 * rows), 2 * rows), 2 * rows)
            runs = 2 * rows // PIECE
            keys = kv_ref[at, head(kv)]
            values = kv_ref[at, head(KVH + kv)]
            key_sum = value_sum = None
            for j in range(groups):
                part = slice(j * rows, (j + 1) * rows)
                h = kv * groups + j
                queries, grads = q_rows[part, :], grad_rows[part, :]
                scores = dot_transposed(keys, queries)
                weights = jnp.exp2(scores * (scale * log2_e) - lse_ref[h : h + 1, :])
                weights = mask_keys(weights, query_bases, key_bases, step * runs, 0.0)
                weight_grads = dot_transposed(values, grads)
                score_grads = (weights * (weight_grads - deltas[:, part])).astype(bf16)
                value_part = dot(weights.astype(bf16), grads)
                key_part = dot(score_grads, queries)
                key_sum = key_part if key_sum is None else key_sum + key_part
                value_sum = value_part if value_sum is None else value_sum + value_part
                q_sums[part, :] += lax.dot_general(
                    score_grads, keys, (((0,), (0,)), ((), ())), preferred_element_type=f32
                )
            key_sum = (key_sum * scale).astype(bf16)
            value_sum = value_sum.astype(bf16)
            to = pl.ds(pl.multiple_of(step * rows, rows), rows)
            for ref, mine in ((kv_own_ref, slice(0, rows)), (kv_other_ref, slice(rows, 2 * rows))):
                ref[to, head(kv)] = key_sum[mine, :]
                ref[to, head(KVH + kv)] = value_sum[mine, :]

        for j in range(groups):
            part = q_sums[j * rows : (j + 1) * rows, :] * scale
            q_grad_ref[:, head(kv * groups + j)] = (
                part * cosine[...] - swap_halves(part) * sine[...]
            ).astype(bf16)


def attend_back(queries, key_value, grads, attended, lse, query_bases, key_bases, cosine, sine):
    rows, total = queries.shape[0], key_value.shape[0]
    groups = HEADS // KVH
    return kernel_call(
        attend_back_kernel,
        "attend_back",
        (
            shape_of((rows, D), bf16),
            shape_of((total // 2, 2 * KVW), bf16),
            shape_of((total // 2, 2 * KVW), bf16),
        ),
        (query_bases, key_bases, queries, key_value, grads, attended, lse, cosine, sine),
        in_specs=[smem] * 2 + [vmem] * 7,
        scratch_shapes=[
            pltpu.VMEM((groups * rows, HD), bf16),
            pltpu.VMEM((groups * rows, HD), bf16),
            pltpu.VMEM((1, groups * rows), f32),
            pltpu.VMEM((groups * rows, HD), f32),
        ],
    )


def input_kernel(
    tokens, gain, w_qkv, query_grad, cosine, sine, residual_grad, own, *refs
):
    got, (kv_ref, input_ref, gain_ref, bias_ref) = refs[:-4], refs[-4:]
    rows = own[...].astype(f32)
    for piece in got:
        rows = rows + piece[...].astype(f32)
    for j in range(KVH):
        part = rows[:, head(j)]
        kv_ref[:, head(j)] = (part * cosine[...] - swap_halves(part) * sine[...]).astype(bf16)
    kv_ref[:, KVW:] = rows[:, KVW:].astype(bf16)
    kv_grad = kv_ref[...]
    q_grad = query_grad[...]
    bias_ref[:, :D] = jnp.sum(q_grad.astype(f32), axis=0, keepdims=True)
    bias_ref[:, D:] = jnp.sum(kv_grad.astype(f32), axis=0, keepdims=True)
    normed_grad = dot_transposed(q_grad, w_qkv[:, :D]) + dot_transposed(kv_grad, w_qkv[:, D:])
    inputs = tokens[...].astype(f32)
    scale = rms_scale(inputs)
    unit = inputs * scale
    gain_ref[...] = jnp.sum(normed_grad * unit, axis=0, keepdims=True)
    weighted = normed_grad * gain[...]
    input_ref[...] = residual_grad[...] + scale * (
        weighted - unit * jnp.mean(weighted * unit, axis=-1, keepdims=True)
    )


def input_back(tokens, gain, w_qkv, query_grad, cosine, sine, residual_grad, own, got):
    rows = tokens.shape[0]
    return kernel_call(
        input_kernel,
        "input_back",
        (
            shape_of((rows, 2 * KVW), bf16),
            shape_of((rows, D), f32),
            shape_of((1, D), f32),
            shape_of((1, D + 2 * KVW), f32),
        ),
        (tokens, gain, w_qkv, query_grad, cosine, sine, residual_grad, own, *got),
        megabytes=58,
    )


def split_kernel(sides, values, *outs, cuts, bits):
    blocks = values.shape[0]
    for i, ((lo, hi), bit) in enumerate(zip(cuts, bits)):
        for out, side in ((outs[2 * i], sides[i]), (outs[2 * i + 1], 1 - sides[i])):
            for o in range(blocks // (2 * bit)):
                for j in range(bit):
                    out[o * bit + j] = values[(2 * o + side) * bit + j, :, lo:hi]


def split_columns(values, sides, cuts, bits):
    blocks, rows, _ = values.shape
    outs = kernel_call(
        functools.partial(split_kernel, cuts=cuts, bits=bits),
        "split_columns",
        tuple(shape_of((blocks // 2, rows, hi - lo), bf16) for lo, hi in cuts for _ in range(2)),
        (sides, values),
        in_specs=[smem, vmem],
    )
    return [(outs[2 * i], outs[2 * i + 1]) for i in range(len(cuts))]


def weight_grad_kernel(sides, left, *refs, count, inners, based):
    rights, refs = refs[:count], refs[count:]
    bases, outs = refs[: count * based], refs[count * based :]
    turned = left[...].reshape(-1, left.shape[-1]).T
    for i, right in enumerate(rights):
        result = dot(turned, right[...].reshape(-1, right.shape[-1]))
        if based:
            result = result + bases[i][...]
        if not inners:
            outs[i][...] = result.astype(outs[i].dtype)
            continue
        stays, goes = outs[2 * i], outs[2 * i + 1]
        rows = stays.shape[2]
        result = result.astype(bf16)
        for side, refs_of in ((0, (stays, goes)), (1, (goes, stays))):

            @pl.when(sides[i] == side)
            def _():
                for o in range(stays.shape[0]):
                    for bit in range(2):
                        for j in range(inners[i]):
                            block = (o * 2 + bit) * inners[i] + j
                            refs_of[bit][o, j] = result[block * rows : (block + 1) * rows]


def weight_grad(
    left, rights, slots=(0, 1), bases=(), split=None, rows=0, part=(0, 1), kind=bf16
):
    n_slots, tokens, m = left.shape
    n_slots = n_slots // slots[1]
    m = m // part[1]
    block = 3 * HD if m % (3 * HD) == 0 else HD
    steps = m // block
    first = part[0] * steps
    whole = pl.Buffered(buffer_count=1)
    sides, inners = split if split else (jnp.zeros((1,), jnp.int32), ())
    out_shape, out_specs = [], []
    for i, right in enumerate(rights):
        n = right.shape[-1]
        if not inners:
            out_shape.append(shape_of((m, n), kind))
            out_specs.append(pl.BlockSpec((block, n), lambda i: (i, 0)))
            continue
        outer = block // (2 * inners[i] * rows)
        for _ in range(2):
            out_shape.append(shape_of((steps * outer, inners[i], rows, n), bf16))
            out_specs.append(pl.BlockSpec((outer, inners[i], rows, n), lambda i: (i, 0, 0, 0)))
    outs = kernel_call(
        functools.partial(
            weight_grad_kernel, count=len(rights), inners=inners, based=int(bool(bases))
        ),
        "weight_grad",
        tuple(out_shape),
        (sides, left, *rights, *bases),
        megabytes=32,
        grid=(steps,),
        in_specs=[
            smem,
            pl.BlockSpec((n_slots, tokens, block), lambda i: (slots[0], 0, i + first)),
        ]
        + [
            vmem
            if slots == (0, 1)
            else pl.BlockSpec(
                (n_slots, tokens, right.shape[-1]),
                lambda i: (slots[0], 0, 0),
                pipeline_mode=whole,
            )
            for right in rights
        ]
        + [pl.BlockSpec((block, base.shape[1]), lambda i: (i + first, 0)) for base in bases],
        out_specs=tuple(out_specs),
    )
    if not inners:
        return outs
    outs = [out.reshape((-1,) + out.shape[2:]) for out in outs]
    return [(outs[2 * i], outs[2 * i + 1]) for i in range(len(rights))]


def stack_kernel(*refs, cuts):
    pieces, outs = refs[: -len(cuts)], refs[-len(cuts) :]
    for i, piece in enumerate(pieces):
        for out, (lo, hi) in zip(outs, cuts):
            out[i] = piece[:, lo:hi]


def stack_columns(pieces, cuts):
    return kernel_call(
        functools.partial(stack_kernel, cuts=cuts),
        "stack_columns",
        tuple(shape_of((len(pieces), pieces[0].shape[0], hi - lo), bf16) for lo, hi in cuts),
        tuple(pieces),
    )


def cut_kernel(core, values, kept_ref, sent_ref, *, n_dp, own, padded):
    kept_ref[...] = jnp.zeros_like(kept_ref)
    sent_ref[...] = jnp.zeros_like(sent_ref)
    for side, refs in ((0, (kept_ref, sent_ref)), (1, (sent_ref, kept_ref))):

        @pl.when(core[0] == side)
        def _():
            for s in range(2 * kept_ref.shape[0]):
                for d in range(n_dp):
                    start = (s * n_dp + d) * own
                    refs[s % 2][s // 2, 0, :, d * padded : d * padded + own] = values[
                        0, :, start : start + own
                    ].astype(bf16)


def cut_hidden(values, core, n_chips, n_dp, padded):
    two, rows, ff = values.shape
    own = ff // (2 * n_chips * n_dp)
    dims = (n_chips, two, rows, n_dp * padded)
    return kernel_call(
        functools.partial(cut_kernel, n_dp=n_dp, own=own, padded=padded),
        "cut_hidden",
        (shape_of(dims, bf16),) * 2,
        (core, values),
        grid=(two,),
        in_specs=[smem, pl.BlockSpec((1, rows, ff), lambda g: (g, 0, 0))],
        out_specs=(pl.BlockSpec((n_chips, 1, rows, n_dp * padded), lambda g: (0, g, 0, 0)),) * 2,
    )


def turn_kernel(chip, *refs, n_chips):
    ins, outs = refs[: len(refs) - n_chips], refs[len(refs) - n_chips :]
    per_side = len(ins) // 2
    for t, out in enumerate(outs):
        at = lax.rem(chip[0] + t, n_chips)
        for side in range(2):
            if per_side == 1:
                out[side] = ins[side][at]
            else:
                for g in range(2):
                    out[side, g] = ins[2 * side + g][at]


def turn_pairs(kept, got, chip, n_chips):
    rows, width = kept[0].shape[-2:]
    return kernel_call(
        functools.partial(turn_kernel, n_chips=n_chips),
        "turn_pairs",
        (shape_of((2, 2, rows, width), bf16),) * n_chips,
        (chip, *kept, *got),
        in_specs=[smem] + [vmem] * (len(kept) + len(got)),
    )


def add_kernel(*refs):
    *ins, out = refs
    total = ins[0][...].astype(f32)
    for ref in ins[1:]:
        total = total + ref[...].astype(f32)
    out[...] = total.astype(bf16)


def add(*arrays):
    return kernel_call(add_kernel, "add", shape_of(arrays[0].shape, bf16), arrays)


def add_turn_kernel(chip, kept, got, *outs):
    n = kept.shape[0]
    for t, out in enumerate(outs):
        at = lax.rem(chip[0] + t, n)
        out[...] = (kept[at].astype(f32) + got[at].astype(f32)).astype(bf16)


def add_turn(kept, got, chip):
    n = kept.shape[0]
    return kernel_call(
        add_turn_kernel,
        "add_turn",
        (shape_of(kept.shape[1:], bf16),) * n,
        (chip, kept, got),
        in_specs=[smem, vmem, vmem],
    )


def add_halve_kernel(mine, *refs):
    parts, (stays, goes) = refs[:-2], refs[-2:]
    count = len(parts) // 2
    at = 0
    for kept, got in zip(parts[:count], parts[count:]):
        for o in range(kept.shape[0]):
            for out, side in ((stays, mine[0]), (goes, 1 - mine[0])):
                out[at] = (kept[o, side].astype(f32) + got[o, side].astype(f32)).astype(bf16)
            at += 1


def add_halve(kept, got, mine, outer):
    rows, width = kept[0].shape[1:]
    blocks = sum(part.shape[0] for part in kept)
    inner = blocks // (2 * outer)
    half = shape_of((outer, inner, rows, width), bf16)
    stays, goes = kernel_call(
        add_halve_kernel,
        "add_halve",
        (half, half),
        (mine, *[part.reshape(-1, 2, inner, rows, width) for part in (*kept, *got)]),
        in_specs=[smem] + [vmem] * (len(kept) + len(got)),
        megabytes=40,
    )
    return stays.reshape(-1, rows, width), goes.reshape(-1, rows, width)


def add_halve_columns_kernel(mine, *refs, cuts):
    parts, (stays, goes) = refs[:-2], refs[-2:]
    count = len(parts) // 2
    lo = 0
    for kept, got, (first, last) in zip(parts[:count], parts[count:], cuts):
        hi = lo + last - first
        for o in range(kept.shape[0]):
            for out, side in ((stays, mine[0]), (goes, 1 - mine[0])):
                total = kept[o, side, :, :, first:last].astype(f32) + got[
                    o, side, :, :, first:last
                ].astype(f32)
                out[o, :, :, lo:hi] = total.astype(bf16)
        lo = hi


def add_halve_columns(kept, got, cuts, mine, outer):
    blocks, rows, _ = kept[0].shape
    inner = blocks // (2 * outer)
    width = sum(last - first for first, last in cuts)
    half = shape_of((outer, inner, rows, width), bf16)
    stays, goes = kernel_call(
        functools.partial(add_halve_columns_kernel, cuts=cuts),
        "add_halve",
        (half, half),
        (mine, *[part.reshape(outer, 2, inner, rows, -1) for part in (*kept, *got)]),
        in_specs=[smem] + [vmem] * (len(kept) + len(got)),
        megabytes=44,
    )
    return stays.reshape(-1, rows, width), goes.reshape(-1, rows, width)


def adamw_update(master, moment_one, moment_two, gradient, step_rate, decay_weight):
    first_new = beta_one * moment_one + (1.0 - beta_one) * gradient
    second_new = beta_two * moment_two + (1.0 - beta_two) * gradient * gradient
    first_hat = first_new / (1.0 - beta_one**STEP)
    second_hat = second_new / (1.0 - beta_two**STEP)
    master_new = master - step_rate * (
        first_hat / (jnp.sqrt(second_hat) + adam_eps) + decay_weight * master
    )
    return (first_new, second_new, master_new)


def adamw_kernel(where, master, first, second, *refs, n_dp, own, padded, rate, decay):
    pieces, (first_ref, second_ref, master_ref, slots, joined) = refs[:-5], refs[-5:]
    for t, piece in enumerate(pieces):
        for o in range(2):
            slots[where[2 * t + o]] = piece[o, 0]
    for s in range(slots.shape[0]):
        for d in range(n_dp):
            start = (s * n_dp + d) * own
            joined[:, start : start + own] = slots[
                s, :, d * padded : d * padded + own
            ].astype(f32)
    first_ref[0], second_ref[0], master_ref[0] = adamw_update(
        master[0], first[0], second[0], joined[...], rate, decay
    )


def adamw_hidden(master, first, second, pieces, where, n_dp, padded, rate, decay):
    two, rows, ff = master.shape
    n_seq = 2 * len(pieces)
    own = ff // (n_seq * n_dp)
    block = pl.BlockSpec((1, rows, ff), lambda g: (g, 0, 0))
    part = pl.BlockSpec((2, 1, rows, n_dp * padded), lambda g: (0, g, 0, 0))
    return kernel_call(
        functools.partial(
            adamw_kernel, n_dp=n_dp, own=own, padded=padded, rate=rate, decay=decay
        ),
        "adamw_hidden",
        (shape_of(master.shape, f32),) * 3,
        (where, master, first, second, *pieces),
        megabytes=44,
        grid=(two,),
        in_specs=[smem] + [block] * 3 + [part] * len(pieces),
        out_specs=(block,) * 3,
        scratch_shapes=[
            pltpu.VMEM((n_seq, rows, n_dp * padded), bf16),
            pltpu.VMEM((rows, ff), f32),
        ],
    )


def assemble_kernel(where, *refs, splits, counts):
    ins, outs, sems = refs[: len(counts)], refs[len(counts) : -1], refs[-1]
    copies = []
    entry = 0
    for ref, (column, count) in zip(ins, counts):
        for i in range(count):
            for out, start, width in splits[column]:
                copies.append(
                    pltpu.make_async_copy(
                        ref.at[i, :, pl.ds(start, width)],
                        outs[out[0]].at[where[entry], :, pl.ds(out[1], width)],
                        sems.at[len(copies)],
                    )
                )
            entry += 1
    for copy in copies:
        copy.start()
    for copy in copies:
        copy.wait()


def assemble(pieces, where, splits, out_widths):
    counts = [(column, array.shape[0]) for array, column in pieces]
    rows = pieces[0][0].shape[1]
    blocks = sum(count for column, count in counts if column == 0)
    n_copies = sum(count * len(splits[column]) for column, count in counts)
    return kernel_call(
        functools.partial(assemble_kernel, splits=splits, counts=counts),
        "assemble",
        tuple(shape_of((blocks, rows, w), bf16) for w in out_widths),
        (where.astype(jnp.int32), *[array for array, _ in pieces]),
        in_specs=[smem] + [anywhere] * len(pieces),
        out_specs=(vmem,) * len(out_widths),
        scratch_shapes=[pltpu.SemaphoreType.DMA((n_copies,))],
    )


def seq_perm(values, chips, flip):
    count = lax.axis_size("seq")
    return lax.ppermute(
        values, "seq", [(i, ((i + 2 * chips) % count) ^ flip) for i in range(count)]
    )


def dp_perm(values, bit):
    return lax.ppermute(values, "dp", [(i, i ^ bit) for i in range(lax.axis_size("dp"))])


def dp_bits():
    return [1 << i for i in range(lax.axis_size("dp").bit_length() - 1)]


def pick(values, index, axis):
    return lax.dynamic_index_in_dim(values, index, axis, keepdims=False)


def places_of():
    n_chips = lax.axis_size("seq") // 2
    seq_at = lax.axis_index("seq")
    return n_chips, seq_at // 2, seq_at % 2, lax.axis_size("dp"), lax.axis_index("dp")


def swap(values):
    return seq_perm(values, 0, 1)


def sent_pieces(values):
    return [values] + [seq_perm(values, t, 0) for t in range(1, lax.axis_size("seq") // 2)]


def shards(
    tokens,
    cotangent,
    positions,
    qkv_master,
    qkv_first,
    qkv_second,
    out_master,
    out_first,
    out_second,
    gate_up_master,
    gate_up_first,
    gate_up_second,
    down_master,
    down_first,
    down_second,
    small_master,
    small_first,
    small_second,
):
    n_chips, chip_at, core_at, n_dp, dp_at = places_of()
    n_seq = 2 * n_chips
    n_all = n_seq * n_dp
    bits = dp_bits()
    rows_own, qkv_width = qkv_master.shape
    half = qkv_width // 2
    small_own = small_master.shape[0]
    ff_dev = down_master.shape[0]
    ff_pad = -(-ff_dev // 16) * 16
    ff_own = n_dp * ff_pad
    inputs = tokens[0]
    upstream = cotangent[0]
    tok_rows = inputs.shape[0]
    seq_length = positions.shape[1]
    shifts = list(range(1, n_chips))

    ring_chips = [(chip_at - t) % n_chips for t in range(n_chips)]
    ring_order = jnp.stack(
        [chip * 2 + (core_at ^ flip) for chip in ring_chips for flip in range(2)]
    ).astype(jnp.int32)
    bases = positions[0, ::PIECE].reshape(n_seq, tok_rows // PIECE)
    key_bases = jnp.take(bases, ring_order, axis=0)
    query_bases = key_bases[0]
    key_bases = key_bases.reshape(-1)
    own_places = lax.dynamic_slice_in_dim(
        positions[0], (chip_at * 2 + core_at) * tok_rows, tok_rows, 0
    )
    cosine, sine = rotary_tables(own_places)

    small_block = jnp.pad(
        small_master.astype(bf16), (0, rows_own * HD - small_own)
    ).reshape(rows_own, HD)
    packed = jnp.concatenate([small_block, qkv_master.astype(bf16)], axis=1)
    qkv_ring = sent_pieces(packed)
    core_side = core_at.reshape(1).astype(jnp.int32)
    chip_side = chip_at.reshape(1).astype(jnp.int32)
    bit_sides = {bit: ((dp_at // bit) % 2).reshape(1).astype(jnp.int32) for bit in bits}
    cut_kept, cut_sent = cut_hidden(gate_up_master, core_side, n_chips, n_dp, ff_pad)
    to_send = turn_pairs([cut_kept], [swap(cut_sent)], chip_side, n_chips)
    qkv_ring, to_send, cosine, sine = fence(qkv_ring, to_send, cosine, sine)

    def exchange(shift):
        return seq_perm(to_send[shift], shift, 0)

    w_out = lax.all_gather(
        after(out_master.astype(bf16), *to_send), ("seq", "dp"), axis=0, tiled=True
    )

    columns = ((0, HD + half), (HD + half, HD + qkv_width))
    orders = (bits, bits[::-1])
    held = list(stack_columns(qkv_ring, columns))
    flips = [[0], [0]]
    gate_up_pieces = {0: to_send[0]}
    groups = [shifts[:1], shifts[-1:], shifts[1:-1]] if n_chips > 2 else [shifts, [], []]
    for stage in range(len(bits)):
        got = [dp_perm(h, order[stage]) for h, order in zip(held, orders)]
        if stage == len(bits) - 1:
            swapped = [swap(h) for h in held]
        for shift in groups[min(stage, 1)] if stage < 2 else []:
            gate_up_pieces[shift] = exchange(shift)
        got, held, gate_up_pieces = fence(got, held, gate_up_pieces)
        flips = [f + [k ^ order[stage] for k in f] for f, order in zip(flips, orders)]
        if stage < len(bits) - 1:
            held = [jnp.concatenate([h, g], axis=0) for h, g in zip(held, got)]
    (swapped,) = fence(swapped)
    for shift in groups[2]:
        gate_up_pieces[shift] = exchange(shift)
    down_share = jnp.pad(down_master.astype(bf16), ((0, ff_pad - ff_dev), (0, 0)))
    w_down = lax.all_gather(after(down_share, *got), "dp", axis=0, tiled=True)
    got_swapped = [swap(g) for g in got]
    pieces, where = [], []
    for column in range(2):
        for flip, part, ks in (
            (0, held[column], flips[column][: n_dp // 2]),
            (0, got[column], flips[column][n_dp // 2 :]),
            (1, swapped[column], flips[column][: n_dp // 2]),
            (1, got_swapped[column], flips[column][n_dp // 2 :]),
        ):
            pieces.append((part, column))
            where += [
                (chip * 2 + (core_at ^ flip)) * n_dp + (dp_at ^ k) for k in ks for chip in ring_chips
            ]
    w_qkv, small_blocks = assemble(
        pieces,
        jnp.stack(where),
        ((((1, 0), 0, HD), ((0, 0), HD, half)), (((0, half), 0, half),)),
        (qkv_width, HD),
    )
    w_qkv = w_qkv.reshape(D, qkv_width)
    small_params = small_blocks.reshape(n_all, rows_own * HD)[:, :small_own].reshape(1, -1)
    small_params = small_params.astype(f32)
    gain_one = small_params[:, :D]
    gain_two = small_params[:, D : 2 * D]
    qkv_bias = small_params[:, 2 * D :]
    normed_one, key_value = project_kv(inputs, w_qkv, gain_one, qkv_bias, cosine, sine)
    gate_up_held = [
        jnp.concatenate([gate_up_pieces[t] for t in ts], axis=0)
        for ts in (range(n_chips // 2), range(n_chips // 2, n_chips))
    ]
    normed_one, key_value, gate_up_held = fence(normed_one, key_value, gate_up_held)

    kv_ring = sent_pieces(key_value)
    gate_up_parts = [
        [held, dp_perm(held, order[0])] for held, order in zip(gate_up_held, orders)
    ]
    gate_up_flips = [[0, order[0]] for order in orders]
    queries = project_q(normed_one, w_qkv, qkv_bias, cosine, sine)
    kv_swapped = [swap(kv_ring[0])] + [swap(after(piece, queries)) for piece in kv_ring[1:]]
    kv_ring, kv_swapped, gate_up_parts, queries, upstream = fence(
        kv_ring, kv_swapped, gate_up_parts, queries, upstream
    )

    def cross(start, stop, stage):
        for parts, flips_of, order in zip(gate_up_parts, gate_up_flips, orders):
            parts += [dp_perm(piece, order[stage]) for piece in parts[start:stop]]
            flips_of += [k ^ order[stage] for k in flips_of[start:stop]]

    upstream_ring = [upstream, seq_perm(upstream, 1, 0)]
    cross(0, 1 if len(bits) == 2 else 2, 1)
    attended, logsum, key_value_all = attend(
        queries, [piece for pair in zip(kv_ring, kv_swapped) for piece in pair], query_bases, key_bases
    )
    gate_up_parts, upstream_ring, attended, logsum, key_value_all = fence(
        gate_up_parts, upstream_ring, attended, logsum, key_value_all
    )

    def ring_step(pieces):
        return pieces + [seq_perm(pieces[-1], 1, 0)] if len(pieces) < n_chips else pieces

    upstream_ring = ring_step(upstream_ring)
    if len(bits) == 2:
        cross(1, 2, 1)
    else:
        cross(0, 4, 2)
    upstream_swapped = [swap(piece) for piece in upstream_ring[:2]]
    residual, normed_two, attended_low = out_project(inputs, attended, w_out, gain_two)
    normed_ring, normed_swapped = [normed_two], [swap(normed_two)]
    gate_up_parts, upstream_ring, upstream_swapped, normed_ring, normed_swapped, residual = fence(
        gate_up_parts, upstream_ring, upstream_swapped, normed_ring, normed_swapped, residual
    )

    pieces, where = [], []
    for column, (parts, flips_of) in enumerate(zip(gate_up_parts, gate_up_flips)):
        slots = ring_order[:n_chips] if column == 0 else ring_order[n_chips:]
        for part, k in zip(parts, flips_of):
            pieces.append((part.reshape(-1, rows_own, ff_own), 0))
            block = slots * n_dp + (dp_at ^ k)
            where.append(jnp.stack([block, n_all + block], axis=1).reshape(-1))
    (w_gate_up,) = assemble(
        pieces, jnp.concatenate(where), ((((0, 0), 0, ff_own),),), (ff_own,)
    )
    w_gate_up = w_gate_up.reshape(2, D, ff_own)
    out_pairs, kept = [], ()
    running = None
    for slot in range(n_chips):
        sent = None if running is None else seq_perm(running, 1, 0)
        normed_ring = ring_step(normed_ring)
        upstream_ring = ring_step(upstream_ring)
        out_own, out_other, grad_own, grad_other, *kept = feed_forward(
            (normed_ring[slot], normed_swapped[slot]),
            (upstream_ring[slot], upstream_swapped[slot]),
            w_gate_up,
            w_down,
            slot,
            n_chips,
            kept,
        )
        grad_swapped = swap(grad_other)
        if slot + 1 < n_chips:
            normed_swapped = normed_swapped + [swap(after(normed_ring[slot + 1], grad_own))]
        if slot + 2 < n_chips and len(upstream_swapped) < slot + 3:
            upstream_swapped = upstream_swapped + [swap(after(upstream_ring[slot + 2], grad_own))]
        if slot == 0:
            grad_first = (grad_own, grad_swapped)
        elif sent is None:
            running = add(grad_own, grad_swapped)
        else:
            running = add(grad_own, grad_swapped, after(sent, grad_own))
        running, normed_ring, normed_swapped, upstream_ring, upstream_swapped, kept = fence(
            running, normed_ring, normed_swapped, upstream_ring, upstream_swapped, kept
        )
        out_pairs = out_pairs + [(out_own, out_other)]
        if 1 < slot:
            out_pairs[slot - 1] = (out_pairs[slot - 1][0], swap(out_pairs[slot - 1][1]))
        if slot == 2:
            ring_first = add(*out_pairs[1])

    grad_ring = jnp.zeros_like(grad_first[0]) if running is None else seq_perm(running, 1, 0)
    normed_all, ffn_all, hidden_all, gate_grads_all, up_grads_all = kept
    first_split = (
        jnp.concatenate([bit_sides[order[0]] for order in orders]),
        tuple(order[0] for order in orders),
    )
    halves = [
        weight_grad(
            normed_all,
            (gate_grads_all, up_grads_all),
            split=first_split,
            rows=rows_own,
            part=(part, 2),
        )
        for part in range(2)
    ]
    out_running = seq_perm(ring_first, 1, 0)
    out_running = add(after(out_running, *halves[0][0]), *out_pairs[2])
    grad_ring, halves, out_pairs, out_running = fence(grad_ring, halves, out_pairs, out_running)

    got_one = [dp_perm(goes, order[0]) for (_, goes), order in zip(halves[0], orders)]
    out_running = seq_perm(out_running, 1, 0)
    out_pairs[-1] = (out_pairs[-1][0], swap(out_pairs[-1][1]))
    residual_grads, branch_grads, attended_grads, gain_two_grad = norm_back(
        grad_ring, *grad_first, residual, upstream, gain_two, w_out
    )
    query_pre, kv_grad_own, kv_grad_other = attend_back(
        queries,
        key_value_all,
        attended_grads,
        attended,
        logsum,
        query_bases,
        key_bases,
        cosine,
        sine,
    )
    got_one, kv_grad_own, kv_grad_other, query_pre, branch_grads, out_running, out_pairs = fence(
        got_one, kv_grad_own, kv_grad_other, query_pre, branch_grads, out_running, out_pairs
    )
    own_parts = kv_grad_own.reshape(n_chips, tok_rows, 2 * KVW)
    other_parts = swap(kv_grad_other).reshape(n_chips, tok_rows, 2 * KVW)
    kv_sum = add_turn(own_parts, other_parts, jnp.zeros_like(chip_side))
    kv_sum, halves, query_pre, branch_grads, kept = fence(
        kv_sum, halves, query_pre, branch_grads, kept
    )

    def next_split(kept_parts, got, done_bits, left_bits):
        rest = [bit for bit in bits[::-1] if bit not in done_bits]
        bit = left_bits[0]
        lead = sum(part.shape[0] for part in kept_parts) // 2 ** len(rest)
        return add_halve(kept_parts, got, bit_sides[bit], lead * 2 ** rest.index(bit))

    kv_got = [seq_perm(kv_sum[t], n_chips - t, 0) for t in range(1, n_chips)]
    got_two = [dp_perm(goes, order[0]) for (_, goes), order in zip(halves[1], orders)]
    by_core = (core_side, (n_dp,))
    (query_split,) = weight_grad(normed_one[None], (query_pre[None],), split=by_core, rows=rows_own)
    (out_split,) = weight_grad(
        attended_low[None], (branch_grads[None],), split=by_core, rows=rows_own
    )
    (down_grad,) = weight_grad(kept[2], (kept[1],))
    out_running = add(out_running, *out_pairs[3])
    kv_got, got_two, query_split, out_split, down_grad, out_running = fence(
        kv_got, got_two, query_split, out_split, down_grad, out_running
    )

    out_running = seq_perm(out_running, 1, 0)
    gate_up_split = [
        next_split([one[0], two[0]], [got, other], order[:1], order[1:])
        for one, two, got, other, order in zip(*halves, got_one, got_two, orders)
    ]
    gate_up_sums = [dp_perm(goes, order[1]) for (_, goes), order in zip(gate_up_split, orders)]
    both = [(split[0], swap(split[1])) for split in (query_split, out_split)]
    key_value_pre, input_grads, gain_one_grad, bias_grad = input_back(
        inputs,
        gain_one,
        w_qkv,
        query_pre,
        cosine,
        sine,
        residual_grads,
        kv_sum[0],
        kv_got,
    )
    down_split = split_columns(
        down_grad.reshape(n_dp, ff_pad, D),
        first_split[0],
        ((0, D // 2), (D // 2, D)),
        tuple(order[0] for order in orders),
    )
    ((kv_stays, kv_goes),) = weight_grad(
        normed_one[None], (key_value_pre[None],), split=by_core, rows=rows_own
    )
    (
        gate_up_split,
        gate_up_sums,
        down_split,
        both,
        input_grads,
        kv_stays,
        kv_goes,
        out_running,
        small_parts,
    ) = fence(
        gate_up_split,
        gate_up_sums,
        down_split,
        both,
        input_grads,
        kv_stays,
        kv_goes,
        out_running,
        (gain_one_grad, gain_two_grad, bias_grad),
    )

    down_got = [dp_perm(goes, order[0]) for (_, goes), order in zip(down_split, orders)]
    ready = []
    for split, got, order in zip(gate_up_split, gate_up_sums, orders):
        kept_part = split[0]
        for i in range(2, len(order)):
            kept_part, goes = next_split([kept_part], [got], order[:i], order[i:])
            got = dp_perm(goes, order[i])
        ready.append(add_halve([kept_part], [got], core_side, n_chips))
    to_send = turn_pairs(
        [kept_part for kept_part, _ in ready],
        [swap(sent) for _, sent in ready],
        chip_side,
        n_chips,
    )
    small_grad = jnp.concatenate(small_parts, axis=1).astype(bf16)
    small_grad = jnp.pad(
        small_grad.reshape(n_all, small_own), ((0, 0), (0, rows_own * HD - small_own))
    ).reshape(n_chips, 2, n_dp, rows_own, HD)
    kv_stays = jnp.concatenate(
        [pick(small_grad, core_at, 1).reshape(-1, rows_own, HD), kv_stays], axis=2
    )
    kv_goes = jnp.concatenate(
        [pick(small_grad, 1 - core_at, 1).reshape(-1, rows_own, HD), kv_goes], axis=2
    )
    kv_got = swap(kv_goes)
    rest_cuts = (((0, D), (0, 3 * HD)), ((0, D), (3 * HD, HD + 2 * KVW)))
    rest = [
        add_halve_columns(
            [kept_part, kv_stays],
            [got, kv_got],
            cuts,
            bit_sides[order[0]],
            n_chips * n_dp // (2 * order[0]),
        )
        for (kept_part, got), cuts, order in zip(both, rest_cuts, orders)
    ]
    to_send, rest, out_running, down_got = fence(to_send, rest, out_running, down_got)

    gate_up_owned = {0: to_send[0]}
    rest_got = [dp_perm(goes, order[0]) for (_, goes), order in zip(rest, orders)]
    for shift in groups[0] + groups[2]:
        gate_up_owned[shift] = exchange(shift)
    if len(bits) > 1:
        down_split = [
            next_split([kept_part], [got], order[:1], order[1:])
            for (kept_part, _), got, order in zip(down_split, down_got, orders)
        ]
    out_pairs[0] = (out_pairs[0][0], swap(out_pairs[0][1]))
    gate_up_owned, rest_got, down_split, out_pairs = fence(
        gate_up_owned, rest_got, down_split, out_pairs
    )

    for shift in groups[1]:
        gate_up_owned[shift] = exchange(shift)
    rest_send = []
    for (kept_part, _), got, order in zip(rest, rest_got, orders):
        for i in range(1, len(order)):
            kept_part, goes = next_split([kept_part], [got], order[:i], order[i:])
            got = dp_perm(goes, order[i])
        rest_send.append(add_turn(kept_part, got, chip_side))
    gate_up_owned, rest_send, down_split = fence(gate_up_owned, rest_send, down_split)

    rest_send = [
        jnp.concatenate([parts[t] for parts in rest_send], axis=1) for t in range(n_chips)
    ]
    rest_ring = [rest_send[0]] + [seq_perm(rest_send[shift], shift, 0) for shift in shifts]
    down_owned = []
    for (kept_part, goes), got, order in zip(down_split, down_got, orders):
        for i in range(1, len(order)):
            if i > 1:
                kept_part, goes = next_split([kept_part], [got], order[:i], order[i:])
            got = dp_perm(goes, order[i])
        down_owned.append(kept_part[0, :ff_dev].astype(f32) + got[0, :ff_dev].astype(f32))
    down_owned = jnp.concatenate(down_owned, axis=1)
    down_new = adamw_update(down_master, down_first, down_second, down_owned, 0.026, 0.1)
    rest_ring, down_new = fence(rest_ring, down_new)
    total = sum(piece.astype(f32) for piece in rest_ring)
    for t in range(4, n_chips):
        out_running = seq_perm(add(out_running, *out_pairs[t]), 1, 0)
    outputs = residual + out_pairs[0][0].astype(f32) + out_pairs[0][1].astype(f32)
    outputs = outputs + out_running.astype(f32)
    outputs = outputs.astype(bf16)
    gate_up_new = adamw_hidden(
        gate_up_master,
        gate_up_first,
        gate_up_second,
        [gate_up_owned[t] for t in range(n_chips)],
        ring_order,
        n_dp,
        ff_pad,
        0.064,
        0.1,
    )
    wide = D + 3 * HD
    query_owned, out_owned = total[:, :D], total[:, wide : wide + D]
    small_owned = total[:, D : D + HD]
    qkv_owned = jnp.concatenate(
        [query_owned, total[:, D + HD : wide], total[:, wide + D :]], axis=1
    )
    small_owned = small_owned.reshape(-1)[:small_own]

    qkv_new = adamw_update(qkv_master, qkv_first, qkv_second, qkv_owned, 0.09, 0.1)
    out_new = adamw_update(out_master, out_first, out_second, out_owned, 0.18, 0.1)
    small_new = adamw_update(small_master, small_first, small_second, small_owned, 0.6, 0.0)
    return (
        outputs[None],
        input_grads[None],
        *qkv_new,
        *out_new,
        *gate_up_new,
        *down_new,
        *small_new,
    )


def solution(mesh):
    in_specs = (
        P("dp", "seq", None),
        P("dp", "seq", None),
        P("dp", None),
        P(("seq", "dp"), None),
        P(("seq", "dp"), None),
        P(("seq", "dp"), None),
        P(("seq", "dp"), None),
        P(("seq", "dp"), None),
        P(("seq", "dp"), None),
        P(None, ("seq", "dp"), None),
        P(None, ("seq", "dp"), None),
        P(None, ("seq", "dp"), None),
        P(("seq", "dp"), None),
        P(("seq", "dp"), None),
        P(("seq", "dp"), None),
        P(("seq", "dp")),
        P(("seq", "dp")),
        P(("seq", "dp")),
    )
    out_specs = (
        P("dp", "seq", None),
        P("dp", "seq", None),
        P(("seq", "dp"), None),
        P(("seq", "dp"), None),
        P(("seq", "dp"), None),
        P(("seq", "dp"), None),
        P(("seq", "dp"), None),
        P(("seq", "dp"), None),
        P(None, ("seq", "dp"), None),
        P(None, ("seq", "dp"), None),
        P(None, ("seq", "dp"), None),
        P(("seq", "dp"), None),
        P(("seq", "dp"), None),
        P(("seq", "dp"), None),
        P(("seq", "dp")),
        P(("seq", "dp")),
        P(("seq", "dp")),
    )
    return jax.shard_map(shards, mesh=mesh, in_specs=in_specs, out_specs=out_specs, check_vma=False)
```

```python
import functools

import jax
import jax.numpy as jnp
from jax import lax
from jax.experimental import pallas as pl
from jax.experimental.pallas import tpu as pltpu
from jax.sharding import PartitionSpec as P

D = 1536
HEADS = 12
KVH = 2
HD = 128
STEP = 10
KVW = KVH * HD
PIECE = 128


norm_eps = 1e-06
rope_base = 1000000.0
beta_one = 0.9
beta_two = 0.95
adam_eps = 1e-08
masked_score = -1e30
log2_e = 1.4426950408889634
bf16 = jnp.bfloat16
f32 = jnp.float32
vmem = pl.BlockSpec(memory_space=pltpu.VMEM)
smem = pl.BlockSpec(memory_space=pltpu.SMEM)
anywhere = pl.BlockSpec(memory_space=pl.ANY)


def shape_of(dims, kind):
    return jax.ShapeDtypeStruct(dims, kind)


def kernel_call(kernel, name, out_shape, operands, megabytes=32, **options):
    return pl.pallas_call(
        kernel,
        name=name,
        out_shape=out_shape,
        compiler_params=pltpu.CompilerParams(vmem_limit_bytes=megabytes << 20),
        cost_estimate=pl.CostEstimate(flops=10**6, bytes_accessed=10**6, transcendentals=0),
        **options,
    )(*operands)


def after(values, *others):
    return lax.optimization_barrier((values,) + others)[0]


def fence(*groups):
    flat, tree = jax.tree.flatten(groups)
    return jax.tree.unflatten(tree, lax.optimization_barrier(tuple(flat)))


def dot(left, right):
    return jnp.dot(left, right, preferred_element_type=f32)


def dot_transposed(left, right):
    return lax.dot_general(left, right, (((1,), (1,)), ((), ())), preferred_element_type=f32)


def rotary_tables(places):
    half_size = HD // 2
    freqs = rope_base ** (-(jnp.arange(half_size).astype(f32) * (2.0 / HD)))
    angles = places.astype(f32)[:, None] * freqs[None, :]
    cosine, sine = jnp.cos(angles), jnp.sin(angles)
    return jnp.concatenate([cosine, cosine], axis=1), jnp.concatenate([-sine, sine], axis=1)


def rms_scale(values):
    return lax.rsqrt(jnp.mean(values * values, axis=-1, keepdims=True) + norm_eps)


def swap_halves(values):
    return pltpu.roll(values, HD // 2, 1)


def head(index):
    return slice(index * HD, (index + 1) * HD)


def project_kv_kernel(tokens, w_qkv, gain, bias, cosine, sine, normed_ref, kv_ref):
    inputs = tokens[...].astype(f32)
    normed = (inputs * rms_scale(inputs) * gain[...]).astype(bf16)
    normed_ref[...] = normed
    rows = dot(normed, w_qkv[...]) + bias[:, D:]
    for j in range(KVH):
        part = rows[:, head(j)]
        kv_ref[:, head(j)] = (part * cosine[...] + swap_halves(part) * sine[...]).astype(bf16)
    kv_ref[:, KVW:] = rows[:, KVW:].astype(bf16)


def project_q_kernel(normed, w_qkv, bias, cosine, sine, query_ref):
    rows = dot(normed[...], w_qkv[...]) + bias[:, :D]
    for j in range(HEADS):
        part = rows[:, head(j)]
        query_ref[:, head(j)] = (part * cosine[...] + swap_halves(part) * sine[...]).astype(bf16)


def project_kv(tokens, w_qkv, gain, bias, cosine, sine):
    rows = tokens.shape[0]
    return kernel_call(
        project_kv_kernel,
        "project_kv",
        (shape_of((rows, D), bf16), shape_of((rows, 2 * KVW), bf16)),
        (tokens, w_qkv, gain, bias, cosine, sine),
        megabytes=58,
        grid=(1,),
        in_specs=[vmem, pl.BlockSpec((D, 2 * KVW), lambda i: (0, D // (2 * KVW)))] + [vmem] * 4,
        out_specs=(vmem, vmem),
    )


def project_q(normed, w_qkv, bias, cosine, sine):
    return kernel_call(
        project_q_kernel,
        "project_q",
        shape_of(normed.shape, bf16),
        (normed, w_qkv, bias, cosine, sine),
        megabytes=58,
        grid=(1,),
        in_specs=[vmem, pl.BlockSpec((D, D), lambda i: (0, 0))] + [vmem] * 3,
        out_specs=vmem,
    )


def mask_keys(values, query_bases, key_bases, first_run, fill):
    later = lax.broadcasted_iota(jnp.int32, (PIECE, PIECE), 0) - lax.broadcasted_iota(
        jnp.int32, (PIECE, PIECE), 1
    )
    keys, queries = values.shape
    rows = []
    for r in range(keys // PIECE):
        down = slice(r * PIECE, (r + 1) * PIECE)
        row = []
        for q in range(queries // PIECE):
            gap = query_bases[q] - key_bases[first_run + r]
            row.append(jnp.where(later <= gap, values[down, q * PIECE : (q + 1) * PIECE], fill))
        rows.append(jnp.concatenate(row, axis=1))
    return jnp.concatenate(rows, axis=0)


def attend_kernel(query_bases, key_bases, q_ref, *refs):
    pieces, (out_ref, lse_ref, kv_ref) = refs[:-3], refs[-3:]
    rows = q_ref.shape[0]
    for i, piece in enumerate(pieces):
        kv_ref[i * rows : (i + 1) * rows, :] = piece[...]
    groups = HEADS // KVH
    scale = HD**-0.5 * log2_e
    for kv in range(KVH):
        values = kv_ref[:, head(KVH + kv)].T
        for h in range(kv * groups, (kv + 1) * groups):
            queries = q_ref[:, head(h)]
            scores = []
            for run in range(key_bases.shape[0]):
                keys = kv_ref[run * PIECE : (run + 1) * PIECE, head(kv)]
                part = dot_transposed(keys, queries)
                scores.append(mask_keys(part, query_bases, key_bases, run, masked_score))
            scores = jnp.concatenate(scores, axis=0)
            top = jnp.max(scores, axis=0, keepdims=True)
            weights = jnp.exp2((scores - top) * scale)
            total = jnp.sum(weights, axis=0, keepdims=True)
            mixed = dot(values, weights.astype(bf16))
            out_ref[:, head(h)] = (mixed / total).T
            lse_ref[h : h + 1, :] = top * scale + jnp.log2(total)


def attend(queries, pieces, query_bases, key_bases):
    rows, total = queries.shape[0], key_bases.shape[0] * PIECE
    return kernel_call(
        attend_kernel,
        "attend",
        (
            shape_of((rows, D), f32),
            shape_of((HEADS, rows), f32),
            shape_of((total, 2 * KVW), bf16),
        ),
        (query_bases, key_bases, queries, *pieces),
        in_specs=[smem] * 2 + [vmem] * (1 + len(pieces)),
    )


def out_kernel(tokens, attended, w_out, gain, residual_ref, normed_ref, low_ref):
    low = attended[...].astype(bf16)
    low_ref[...] = low
    residual = tokens[...].astype(f32) + dot(low, w_out[...])
    residual_ref[...] = residual
    normed_ref[...] = (residual * rms_scale(residual) * gain[...]).astype(bf16)


def out_project(tokens, attended, w_out, gain):
    dims = tokens.shape
    return kernel_call(
        out_kernel,
        "out_project",
        (shape_of(dims, f32), shape_of(dims, bf16), shape_of(dims, bf16)),
        (tokens, attended, w_out, gain),
    )


def ffn_kernel(
    normed_own, normed_other, grad_own, grad_other, w_gate_up, w_down, *refs, earlier
):
    refs = refs[earlier:]
    out_refs, grad_refs = refs[:2], refs[2:4]
    normed_ref, ffn_grad_ref, hidden_ref, gate_ref, up_ref = refs[4:]
    rows = normed_own.shape[0]
    for i, (normed_in, grad_in) in enumerate(((normed_own, grad_own), (normed_other, grad_other))):
        to = slice(i * rows, (i + 1) * rows)
        normed, ffn_grad = normed_in[...], grad_in[...]
        normed_ref[0, to, :] = normed
        ffn_grad_ref[0, to, :] = ffn_grad
        gate = dot(normed, w_gate_up[0])
        up = dot(normed, w_gate_up[1])
        sigmoid = 1.0 / (1.0 + jnp.exp(-gate))
        silu = gate * sigmoid
        hidden = (silu * up).astype(bf16)
        hidden_ref[0, to, :] = hidden
        out_refs[i][...] = dot(hidden, w_down[...]).astype(bf16)
        hidden_grad = dot_transposed(ffn_grad, w_down[...])
        gate_grad = (hidden_grad * up * sigmoid * (1.0 + gate * (1.0 - sigmoid))).astype(bf16)
        up_grad = (hidden_grad * silu).astype(bf16)
        gate_ref[0, to, :] = gate_grad
        up_ref[0, to, :] = up_grad
        grad_refs[i][...] = (
            dot_transposed(gate_grad, w_gate_up[0]) + dot_transposed(up_grad, w_gate_up[1])
        ).astype(bf16)


def feed_forward(normed, grads, w_gate_up, w_down, slot, slots, kept):
    rows, width = normed[0].shape
    ff_own = w_down.shape[0]
    token = shape_of((rows, width), bf16)
    widths = (width, width, ff_own, ff_own, ff_own)
    operands = (*normed, *grads, w_gate_up, w_down)
    return kernel_call(
        functools.partial(ffn_kernel, earlier=len(kept)),
        "feed_forward",
        (token,) * 4 + tuple(shape_of((slots, 2 * rows, w), bf16) for w in widths),
        (*operands, *kept),
        grid=(1,),
        in_specs=[vmem] * len(operands) + [anywhere] * len(kept),
        out_specs=(vmem,) * 4
        + tuple(pl.BlockSpec((1, 2 * rows, w), lambda i: (slot, 0, 0)) for w in widths),
        input_output_aliases={len(operands) + i: 4 + i for i in range(len(kept))},
    )


def norm_back_kernel(
    got, own, other, residual_ref, cotangent, gain, w_out, grad_ref, low_ref, back_ref, gain_ref
):
    normed_grad = got[...].astype(f32) + own[...].astype(f32) + other[...].astype(f32)
    residual = residual_ref[...]
    scale = rms_scale(residual)
    unit = residual * scale
    gain_ref[...] = jnp.sum(normed_grad * unit, axis=0, keepdims=True)
    weighted = normed_grad * gain[...]
    grad = cotangent[...].astype(f32) + scale * (
        weighted - unit * jnp.mean(weighted * unit, axis=-1, keepdims=True)
    )
    grad_ref[...] = grad
    low = grad.astype(bf16)
    low_ref[...] = low
    back_ref[...] = dot_transposed(low, w_out[...]).astype(bf16)


def norm_back(got, own, other, residual, cotangent, gain, w_out):
    dims = residual.shape
    return kernel_call(
        norm_back_kernel,
        "norm_back",
        (shape_of(dims, f32), shape_of(dims, bf16), shape_of(dims, bf16), shape_of((1, D), f32)),
        (got, own, other, residual, cotangent, gain, w_out),
    )


def attend_back_kernel(
    query_bases,
    key_bases,
    q_ref,
    kv_ref,
    grad_ref,
    out_ref,
    lse_ref,
    cosine,
    sine,
    q_grad_ref,
    kv_own_ref,
    kv_other_ref,
    q_rows,
    grad_rows,
    deltas,
    q_sums,
):
    rows = q_ref.shape[0]
    groups = HEADS // KVH
    scale = HD**-0.5
    for kv in range(KVH):
        for j in range(groups):
            part = slice(j * rows, (j + 1) * rows)
            columns = head(kv * groups + j)
            q_rows[part, :] = q_ref[:, columns]
            grads = grad_ref[:, columns]
            grad_rows[part, :] = grads
            product = grads.astype(f32) * out_ref[:, columns]
            deltas[:, part] = jnp.sum(product.T, axis=0, keepdims=True)
        q_sums[...] = jnp.zeros_like(q_sums)

        @pl.loop(0, kv_ref.shape[0] // (2 * rows), unroll=2)
        def _(step):
            at = pl.ds(pl.multiple_of(step * (2 * rows), 2 * rows), 2 * rows)
            runs = 2 * rows // PIECE
            keys = kv_ref[at, head(kv)]
            values = kv_ref[at, head(KVH + kv)]
            key_sum = value_sum = None
            for j in range(groups):
                part = slice(j * rows, (j + 1) * rows)
                h = kv * groups + j
                queries, grads = q_rows[part, :], grad_rows[part, :]
                scores = dot_transposed(keys, queries)
                weights = jnp.exp2(scores * (scale * log2_e) - lse_ref[h : h + 1, :])
                weights = mask_keys(weights, query_bases, key_bases, step * runs, 0.0)
                weight_grads = dot_transposed(values, grads)
                score_grads = (weights * (weight_grads - deltas[:, part])).astype(bf16)
                value_part = dot(weights.astype(bf16), grads)
                key_part = dot(score_grads, queries)
                key_sum = key_part if key_sum is None else key_sum + key_part
                value_sum = value_part if value_sum is None else value_sum + value_part
                q_sums[part, :] += lax.dot_general(
                    score_grads, keys, (((0,), (0,)), ((), ())), preferred_element_type=f32
                )
            key_sum = (key_sum * scale).astype(bf16)
            value_sum = value_sum.astype(bf16)
            to = pl.ds(pl.multiple_of(step * rows, rows), rows)
            for ref, mine in ((kv_own_ref, slice(0, rows)), (kv_other_ref, slice(rows, 2 * rows))):
                ref[to, head(kv)] = key_sum[mine, :]
                ref[to, head(KVH + kv)] = value_sum[mine, :]

        for j in range(groups):
            part = q_sums[j * rows : (j + 1) * rows, :] * scale
            q_grad_ref[:, head(kv * groups + j)] = (
                part * cosine[...] - swap_halves(part) * sine[...]
            ).astype(bf16)


def attend_back(queries, key_value, grads, attended, lse, query_bases, key_bases, cosine, sine):
    rows, total = queries.shape[0], key_value.shape[0]
    groups = HEADS // KVH
    return kernel_call(
        attend_back_kernel,
        "attend_back",
        (
            shape_of((rows, D), bf16),
            shape_of((total // 2, 2 * KVW), bf16),
            shape_of((total // 2, 2 * KVW), bf16),
        ),
        (query_bases, key_bases, queries, key_value, grads, attended, lse, cosine, sine),
        in_specs=[smem] * 2 + [vmem] * 7,
        scratch_shapes=[
            pltpu.VMEM((groups * rows, HD), bf16),
            pltpu.VMEM((groups * rows, HD), bf16),
            pltpu.VMEM((1, groups * rows), f32),
            pltpu.VMEM((groups * rows, HD), f32),
        ],
    )


def input_kernel(
    tokens, gain, w_qkv, query_grad, cosine, sine, residual_grad, own, *refs
):
    got, (kv_ref, input_ref, gain_ref, bias_ref) = refs[:-4], refs[-4:]
    rows = own[...].astype(f32)
    for piece in got:
        rows = rows + piece[...].astype(f32)
    for j in range(KVH):
        part = rows[:, head(j)]
        kv_ref[:, head(j)] = (part * cosine[...] - swap_halves(part) * sine[...]).astype(bf16)
    kv_ref[:, KVW:] = rows[:, KVW:].astype(bf16)
    kv_grad = kv_ref[...]
    q_grad = query_grad[...]
    bias_ref[:, :D] = jnp.sum(q_grad.astype(f32), axis=0, keepdims=True)
    bias_ref[:, D:] = jnp.sum(kv_grad.astype(f32), axis=0, keepdims=True)
    normed_grad = dot_transposed(q_grad, w_qkv[:, :D]) + dot_transposed(kv_grad, w_qkv[:, D:])
    inputs = tokens[...].astype(f32)
    scale = rms_scale(inputs)
    unit = inputs * scale
    gain_ref[...] = jnp.sum(normed_grad * unit, axis=0, keepdims=True)
    weighted = normed_grad * gain[...]
    input_ref[...] = residual_grad[...] + scale * (
        weighted - unit * jnp.mean(weighted * unit, axis=-1, keepdims=True)
    )


def input_back(tokens, gain, w_qkv, query_grad, cosine, sine, residual_grad, own, got):
    rows = tokens.shape[0]
    return kernel_call(
        input_kernel,
        "input_back",
        (
            shape_of((rows, 2 * KVW), bf16),
            shape_of((rows, D), f32),
            shape_of((1, D), f32),
            shape_of((1, D + 2 * KVW), f32),
        ),
        (tokens, gain, w_qkv, query_grad, cosine, sine, residual_grad, own, *got),
        megabytes=58,
    )


def split_kernel(sides, values, *outs, cuts, bits):
    blocks = values.shape[0]
    for i, ((lo, hi), bit) in enumerate(zip(cuts, bits)):
        for out, side in ((outs[2 * i], sides[i]), (outs[2 * i + 1], 1 - sides[i])):
            for o in range(blocks // (2 * bit)):
                for j in range(bit):
                    out[o * bit + j] = values[(2 * o + side) * bit + j, :, lo:hi]


def split_columns(values, sides, cuts, bits):
    blocks, rows, _ = values.shape
    outs = kernel_call(
        functools.partial(split_kernel, cuts=cuts, bits=bits),
        "split_columns",
        tuple(shape_of((blocks // 2, rows, hi - lo), bf16) for lo, hi in cuts for _ in range(2)),
        (sides, values),
        in_specs=[smem, vmem],
    )
    return [(outs[2 * i], outs[2 * i + 1]) for i in range(len(cuts))]


def weight_grad_kernel(sides, left, *refs, count, inners, based):
    rights, refs = refs[:count], refs[count:]
    bases, outs = refs[: count * based], refs[count * based :]
    turned = left[...].reshape(-1, left.shape[-1]).T
    for i, right in enumerate(rights):
        result = dot(turned, right[...].reshape(-1, right.shape[-1]))
        if based:
            result = result + bases[i][...]
        if not inners:
            outs[i][...] = result.astype(outs[i].dtype)
            continue
        stays, goes = outs[2 * i], outs[2 * i + 1]
        rows = stays.shape[2]
        result = result.astype(bf16)
        for side, refs_of in ((0, (stays, goes)), (1, (goes, stays))):

            @pl.when(sides[i] == side)
            def _():
                for o in range(stays.shape[0]):
                    for bit in range(2):
                        for j in range(inners[i]):
                            block = (o * 2 + bit) * inners[i] + j
                            refs_of[bit][o, j] = result[block * rows : (block + 1) * rows]


def weight_grad(
    left, rights, slots=(0, 1), bases=(), split=None, rows=0, part=(0, 1), kind=bf16
):
    n_slots, tokens, m = left.shape
    n_slots = n_slots // slots[1]
    m = m // part[1]
    block = 3 * HD if m % (3 * HD) == 0 else HD
    steps = m // block
    first = part[0] * steps
    whole = pl.Buffered(buffer_count=1)
    sides, inners = split if split else (jnp.zeros((1,), jnp.int32), ())
    out_shape, out_specs = [], []
    for i, right in enumerate(rights):
        n = right.shape[-1]
        if not inners:
            out_shape.append(shape_of((m, n), kind))
            out_specs.append(pl.BlockSpec((block, n), lambda i: (i, 0)))
            continue
        outer = block // (2 * inners[i] * rows)
        for _ in range(2):
            out_shape.append(shape_of((steps * outer, inners[i], rows, n), bf16))
            out_specs.append(pl.BlockSpec((outer, inners[i], rows, n), lambda i: (i, 0, 0, 0)))
    outs = kernel_call(
        functools.partial(
            weight_grad_kernel, count=len(rights), inners=inners, based=int(bool(bases))
        ),
        "weight_grad",
        tuple(out_shape),
        (sides, left, *rights, *bases),
        megabytes=32,
        grid=(steps,),
        in_specs=[
            smem,
            pl.BlockSpec((n_slots, tokens, block), lambda i: (slots[0], 0, i + first)),
        ]
        + [
            vmem
            if slots == (0, 1)
            else pl.BlockSpec(
                (n_slots, tokens, right.shape[-1]),
                lambda i: (slots[0], 0, 0),
                pipeline_mode=whole,
            )
            for right in rights
        ]
        + [pl.BlockSpec((block, base.shape[1]), lambda i: (i + first, 0)) for base in bases],
        out_specs=tuple(out_specs),
    )
    if not inners:
        return outs
    outs = [out.reshape((-1,) + out.shape[2:]) for out in outs]
    return [(outs[2 * i], outs[2 * i + 1]) for i in range(len(rights))]


def stack_kernel(*refs, cuts):
    pieces, outs = refs[: -len(cuts)], refs[-len(cuts) :]
    for i, piece in enumerate(pieces):
        for out, (lo, hi) in zip(outs, cuts):
            out[i] = piece[:, lo:hi]


def stack_columns(pieces, cuts):
    return kernel_call(
        functools.partial(stack_kernel, cuts=cuts),
        "stack_columns",
        tuple(shape_of((len(pieces), pieces[0].shape[0], hi - lo), bf16) for lo, hi in cuts),
        tuple(pieces),
    )


def cut_kernel(core, values, kept_ref, sent_ref, *, n_dp, own, padded):
    kept_ref[...] = jnp.zeros_like(kept_ref)
    sent_ref[...] = jnp.zeros_like(sent_ref)
    for side, refs in ((0, (kept_ref, sent_ref)), (1, (sent_ref, kept_ref))):

        @pl.when(core[0] == side)
        def _():
            for s in range(2 * kept_ref.shape[0]):
                for d in range(n_dp):
                    start = (s * n_dp + d) * own
                    refs[s % 2][s // 2, 0, :, d * padded : d * padded + own] = values[
                        0, :, start : start + own
                    ].astype(bf16)


def cut_hidden(values, core, n_chips, n_dp, padded):
    two, rows, ff = values.shape
    own = ff // (2 * n_chips * n_dp)
    dims = (n_chips, two, rows, n_dp * padded)
    return kernel_call(
        functools.partial(cut_kernel, n_dp=n_dp, own=own, padded=padded),
        "cut_hidden",
        (shape_of(dims, bf16),) * 2,
        (core, values),
        grid=(two,),
        in_specs=[smem, pl.BlockSpec((1, rows, ff), lambda g: (g, 0, 0))],
        out_specs=(pl.BlockSpec((n_chips, 1, rows, n_dp * padded), lambda g: (0, g, 0, 0)),) * 2,
    )


def turn_kernel(chip, *refs, n_chips):
    ins, outs = refs[: len(refs) - n_chips], refs[len(refs) - n_chips :]
    per_side = len(ins) // 2
    for t, out in enumerate(outs):
        at = lax.rem(chip[0] + t, n_chips)
        for side in range(2):
            if per_side == 1:
                out[side] = ins[side][at]
            else:
                for g in range(2):
                    out[side, g] = ins[2 * side + g][at]


def turn_pairs(kept, got, chip, n_chips):
    rows, width = kept[0].shape[-2:]
    return kernel_call(
        functools.partial(turn_kernel, n_chips=n_chips),
        "turn_pairs",
        (shape_of((2, 2, rows, width), bf16),) * n_chips,
        (chip, *kept, *got),
        in_specs=[smem] + [vmem] * (len(kept) + len(got)),
    )


def add_kernel(*refs):
    *ins, out = refs
    total = ins[0][...].astype(f32)
    for ref in ins[1:]:
        total = total + ref[...].astype(f32)
    out[...] = total.astype(bf16)


def add(*arrays):
    return kernel_call(add_kernel, "add", shape_of(arrays[0].shape, bf16), arrays)


def add_turn_kernel(chip, kept, got, *outs):
    n = kept.shape[0]
    for t, out in enumerate(outs):
        at = lax.rem(chip[0] + t, n)
        out[...] = (kept[at].astype(f32) + got[at].astype(f32)).astype(bf16)


def add_turn(kept, got, chip):
    n = kept.shape[0]
    return kernel_call(
        add_turn_kernel,
        "add_turn",
        (shape_of(kept.shape[1:], bf16),) * n,
        (chip, kept, got),
        in_specs=[smem, vmem, vmem],
    )


def add_halve_kernel(mine, *refs):
    parts, (stays, goes) = refs[:-2], refs[-2:]
    count = len(parts) // 2
    at = 0
    for kept, got in zip(parts[:count], parts[count:]):
        for o in range(kept.shape[0]):
            for out, side in ((stays, mine[0]), (goes, 1 - mine[0])):
                out[at] = (kept[o, side].astype(f32) + got[o, side].astype(f32)).astype(bf16)
            at += 1


def add_halve(kept, got, mine, outer):
    rows, width = kept[0].shape[1:]
    blocks = sum(part.shape[0] for part in kept)
    inner = blocks // (2 * outer)
    half = shape_of((outer, inner, rows, width), bf16)
    stays, goes = kernel_call(
        add_halve_kernel,
        "add_halve",
        (half, half),
        (mine, *[part.reshape(-1, 2, inner, rows, width) for part in (*kept, *got)]),
        in_specs=[smem] + [vmem] * (len(kept) + len(got)),
        megabytes=40,
    )
    return stays.reshape(-1, rows, width), goes.reshape(-1, rows, width)


def add_halve_columns_kernel(mine, *refs, cuts):
    parts, (stays, goes) = refs[:-2], refs[-2:]
    count = len(parts) // 2
    lo = 0
    for kept, got, (first, last) in zip(parts[:count], parts[count:], cuts):
        hi = lo + last - first
        for o in range(kept.shape[0]):
            for out, side in ((stays, mine[0]), (goes, 1 - mine[0])):
                total = kept[o, side, :, :, first:last].astype(f32) + got[
                    o, side, :, :, first:last
                ].astype(f32)
                out[o, :, :, lo:hi] = total.astype(bf16)
        lo = hi


def add_halve_columns(kept, got, cuts, mine, outer):
    blocks, rows, _ = kept[0].shape
    inner = blocks // (2 * outer)
    width = sum(last - first for first, last in cuts)
    half = shape_of((outer, inner, rows, width), bf16)
    stays, goes = kernel_call(
        functools.partial(add_halve_columns_kernel, cuts=cuts),
        "add_halve",
        (half, half),
        (mine, *[part.reshape(outer, 2, inner, rows, -1) for part in (*kept, *got)]),
        in_specs=[smem] + [vmem] * (len(kept) + len(got)),
        megabytes=44,
    )
    return stays.reshape(-1, rows, width), goes.reshape(-1, rows, width)


def adamw_update(master, moment_one, moment_two, gradient, step_rate, decay_weight):
    first_new = beta_one * moment_one + (1.0 - beta_one) * gradient
    second_new = beta_two * moment_two + (1.0 - beta_two) * gradient * gradient
    first_hat = first_new / (1.0 - beta_one**STEP)
    second_hat = second_new / (1.0 - beta_two**STEP)
    master_new = master - step_rate * (
        first_hat / (jnp.sqrt(second_hat) + adam_eps) + decay_weight * master
    )
    return (first_new, second_new, master_new)


def adamw_kernel(where, master, first, second, *refs, n_dp, own, padded, rate, decay):
    pieces, (first_ref, second_ref, master_ref, slots, joined) = refs[:-5], refs[-5:]
    for t, piece in enumerate(pieces):
        for o in range(2):
            slots[where[2 * t + o]] = piece[o, 0]
    for s in range(slots.shape[0]):
        for d in range(n_dp):
            start = (s * n_dp + d) * own
            joined[:, start : start + own] = slots[
                s, :, d * padded : d * padded + own
            ].astype(f32)
    first_ref[0], second_ref[0], master_ref[0] = adamw_update(
        master[0], first[0], second[0], joined[...], rate, decay
    )


def adamw_hidden(master, first, second, pieces, where, n_dp, padded, rate, decay):
    two, rows, ff = master.shape
    n_seq = 2 * len(pieces)
    own = ff // (n_seq * n_dp)
    block = pl.BlockSpec((1, rows, ff), lambda g: (g, 0, 0))
    part = pl.BlockSpec((2, 1, rows, n_dp * padded), lambda g: (0, g, 0, 0))
    return kernel_call(
        functools.partial(
            adamw_kernel, n_dp=n_dp, own=own, padded=padded, rate=rate, decay=decay
        ),
        "adamw_hidden",
        (shape_of(master.shape, f32),) * 3,
        (where, master, first, second, *pieces),
        megabytes=44,
        grid=(two,),
        in_specs=[smem] + [block] * 3 + [part] * len(pieces),
        out_specs=(block,) * 3,
        scratch_shapes=[
            pltpu.VMEM((n_seq, rows, n_dp * padded), bf16),
            pltpu.VMEM((rows, ff), f32),
        ],
    )


def assemble_kernel(where, *refs, splits, counts):
    ins, outs, sems = refs[: len(counts)], refs[len(counts) : -1], refs[-1]
    copies = []
    entry = 0
    for ref, (column, count) in zip(ins, counts):
        for i in range(count):
            for out, start, width in splits[column]:
                copies.append(
                    pltpu.make_async_copy(
                        ref.at[i, :, pl.ds(start, width)],
                        outs[out[0]].at[where[entry], :, pl.ds(out[1], width)],
                        sems.at[len(copies)],
                    )
                )
            entry += 1
    for copy in copies:
        copy.start()
    for copy in copies:
        copy.wait()


def assemble(pieces, where, splits, out_widths):
    counts = [(column, array.shape[0]) for array, column in pieces]
    rows = pieces[0][0].shape[1]
    blocks = sum(count for column, count in counts if column == 0)
    n_copies = sum(count * len(splits[column]) for column, count in counts)
    return kernel_call(
        functools.partial(assemble_kernel, splits=splits, counts=counts),
        "assemble",
        tuple(shape_of((blocks, rows, w), bf16) for w in out_widths),
        (where.astype(jnp.int32), *[array for array, _ in pieces]),
        in_specs=[smem] + [anywhere] * len(pieces),
        out_specs=(vmem,) * len(out_widths),
        scratch_shapes=[pltpu.SemaphoreType.DMA((n_copies,))],
    )


def seq_perm(values, chips, flip):
    count = lax.axis_size("seq")
    return lax.ppermute(
        values, "seq", [(i, ((i + 2 * chips) % count) ^ flip) for i in range(count)]
    )


def dp_perm(values, bit):
    return lax.ppermute(values, "dp", [(i, i ^ bit) for i in range(lax.axis_size("dp"))])


def dp_bits():
    return [1 << i for i in range(lax.axis_size("dp").bit_length() - 1)]


def pick(values, index, axis):
    return lax.dynamic_index_in_dim(values, index, axis, keepdims=False)


def places_of():
    n_chips = lax.axis_size("seq") // 2
    seq_at = lax.axis_index("seq")
    return n_chips, seq_at // 2, seq_at % 2, lax.axis_size("dp"), lax.axis_index("dp")


def swap(values):
    return seq_perm(values, 0, 1)


def sent_pieces(values):
    return [values] + [seq_perm(values, t, 0) for t in range(1, lax.axis_size("seq") // 2)]


def shards(
    tokens,
    cotangent,
    positions,
    qkv_master,
    qkv_first,
    qkv_second,
    out_master,
    out_first,
    out_second,
    gate_up_master,
    gate_up_first,
    gate_up_second,
    down_master,
    down_first,
    down_second,
    small_master,
    small_first,
    small_second,
):
    n_chips, chip_at, core_at, n_dp, dp_at = places_of()
    n_seq = 2 * n_chips
    n_all = n_seq * n_dp
    bits = dp_bits()
    rows_own, qkv_width = qkv_master.shape
    half = qkv_width // 2
    small_own = small_master.shape[0]
    ff_dev = down_master.shape[0]
    ff_pad = -(-ff_dev // 16) * 16
    ff_own = n_dp * ff_pad
    inputs = tokens[0]
    upstream = cotangent[0]
    tok_rows = inputs.shape[0]
    seq_length = positions.shape[1]
    shifts = list(range(1, n_chips))

    ring_chips = [(chip_at - t) % n_chips for t in range(n_chips)]
    ring_order = jnp.stack(
        [chip * 2 + (core_at ^ flip) for chip in ring_chips for flip in range(2)]
    ).astype(jnp.int32)
    bases = positions[0, ::PIECE].reshape(n_seq, tok_rows // PIECE)
    key_bases = jnp.take(bases, ring_order, axis=0)
    query_bases = key_bases[0]
    key_bases = key_bases.reshape(-1)
    own_places = lax.dynamic_slice_in_dim(
        positions[0], (chip_at * 2 + core_at) * tok_rows, tok_rows, 0
    )
    cosine, sine = rotary_tables(own_places)

    small_block = jnp.pad(
        small_master.astype(bf16), (0, rows_own * HD - small_own)
    ).reshape(rows_own, HD)
    packed = jnp.concatenate([small_block, qkv_master.astype(bf16)], axis=1)
    qkv_ring = sent_pieces(packed)
    core_side = core_at.reshape(1).astype(jnp.int32)
    chip_side = chip_at.reshape(1).astype(jnp.int32)
    bit_sides = {bit: ((dp_at // bit) % 2).reshape(1).astype(jnp.int32) for bit in bits}
    cut_kept, cut_sent = cut_hidden(gate_up_master, core_side, n_chips, n_dp, ff_pad)
    to_send = turn_pairs([cut_kept], [swap(cut_sent)], chip_side, n_chips)
    qkv_ring, to_send, cosine, sine = fence(qkv_ring, to_send, cosine, sine)

    def exchange(shift):
        return seq_perm(to_send[shift], shift, 0)

    w_out = lax.all_gather(
        after(out_master.astype(bf16), *to_send), ("seq", "dp"), axis=0, tiled=True
    )

    columns = ((0, HD + half), (HD + half, HD + qkv_width))
    orders = (bits, bits[::-1])
    held = list(stack_columns(qkv_ring, columns))
    flips = [[0], [0]]
    gate_up_pieces = {0: to_send[0]}
    groups = [shifts[:1], shifts[-1:], shifts[1:-1]] if n_chips > 2 else [shifts, [], []]
    for stage in range(len(bits)):
        got = [dp_perm(h, order[stage]) for h, order in zip(held, orders)]
        if stage == len(bits) - 1:
            swapped = [swap(h) for h in held]
        for shift in groups[min(stage, 1)] if stage < 2 else []:
            gate_up_pieces[shift] = exchange(shift)
        got, held, gate_up_pieces = fence(got, held, gate_up_pieces)
        flips = [f + [k ^ order[stage] for k in f] for f, order in zip(flips, orders)]
        if stage < len(bits) - 1:
            held = [jnp.concatenate([h, g], axis=0) for h, g in zip(held, got)]
    (swapped,) = fence(swapped)
    for shift in groups[2]:
        gate_up_pieces[shift] = exchange(shift)
    down_share = jnp.pad(down_master.astype(bf16), ((0, ff_pad - ff_dev), (0, 0)))
    w_down = lax.all_gather(after(down_share, *got), "dp", axis=0, tiled=True)
    got_swapped = [swap(g) for g in got]
    pieces, where = [], []
    for column in range(2):
        for flip, part, ks in (
            (0, held[column], flips[column][: n_dp // 2]),
            (0, got[column], flips[column][n_dp // 2 :]),
            (1, swapped[column], flips[column][: n_dp // 2]),
            (1, got_swapped[column], flips[column][n_dp // 2 :]),
        ):
            pieces.append((part, column))
            where += [
                (chip * 2 + (core_at ^ flip)) * n_dp + (dp_at ^ k) for k in ks for chip in ring_chips
            ]
    w_qkv, small_blocks = assemble(
        pieces,
        jnp.stack(where),
        ((((1, 0), 0, HD), ((0, 0), HD, half)), (((0, half), 0, half),)),
        (qkv_width, HD),
    )
    w_qkv = w_qkv.reshape(D, qkv_width)
    small_params = small_blocks.reshape(n_all, rows_own * HD)[:, :small_own].reshape(1, -1)
    small_params = small_params.astype(f32)
    gain_one = small_params[:, :D]
    gain_two = small_params[:, D : 2 * D]
    qkv_bias = small_params[:, 2 * D :]
    normed_one, key_value = project_kv(inputs, w_qkv, gain_one, qkv_bias, cosine, sine)
    for shift in groups[2]:
        gate_up_pieces[shift] = after(gate_up_pieces[shift], key_value)
    gate_up_held = [
        jnp.concatenate([gate_up_pieces[t] for t in ts], axis=0)
        for ts in (range(n_chips // 2), range(n_chips // 2, n_chips))
    ]
    normed_one, key_value, gate_up_held = fence(normed_one, key_value, gate_up_held)

    kv_ring = sent_pieces(key_value)
    gate_up_parts = [
        [held, dp_perm(held, order[0])] for held, order in zip(gate_up_held, orders)
    ]
    gate_up_flips = [[0, order[0]] for order in orders]
    queries = project_q(normed_one, w_qkv, qkv_bias, cosine, sine)
    kv_swapped = [swap(kv_ring[0])] + [swap(after(piece, queries)) for piece in kv_ring[1:]]
    kv_ring, kv_swapped, gate_up_parts, queries, upstream = fence(
        kv_ring, kv_swapped, gate_up_parts, queries, upstream
    )

    def cross(start, stop, stage):
        for parts, flips_of, order in zip(gate_up_parts, gate_up_flips, orders):
            parts += [dp_perm(piece, order[stage]) for piece in parts[start:stop]]
            flips_of += [k ^ order[stage] for k in flips_of[start:stop]]

    upstream_ring = [upstream, seq_perm(upstream, 1, 0)]
    cross(0, 1 if len(bits) == 2 else 2, 1)
    attended, logsum, key_value_all = attend(
        queries, [piece for pair in zip(kv_ring, kv_swapped) for piece in pair], query_bases, key_bases
    )
    gate_up_parts, upstream_ring, attended, logsum, key_value_all = fence(
        gate_up_parts, upstream_ring, attended, logsum, key_value_all
    )

    def ring_step(pieces):
        return pieces + [seq_perm(pieces[-1], 1, 0)] if len(pieces) < n_chips else pieces

    upstream_ring = ring_step(upstream_ring)
    if len(bits) == 2:
        cross(1, 2, 1)
    else:
        cross(0, 4, 2)
    upstream_swapped = [swap(piece) for piece in upstream_ring[:2]]
    residual, normed_two, attended_low = out_project(inputs, attended, w_out, gain_two)
    normed_ring, normed_swapped = [normed_two], [swap(normed_two)]
    (
        gate_up_parts,
        upstream_ring,
        upstream_swapped,
        normed_ring,
        normed_swapped,
        residual,
        w_down,
    ) = fence(
        gate_up_parts,
        upstream_ring,
        upstream_swapped,
        normed_ring,
        normed_swapped,
        residual,
        w_down,
    )

    pieces, where = [], []
    for column, (parts, flips_of) in enumerate(zip(gate_up_parts, gate_up_flips)):
        slots = ring_order[:n_chips] if column == 0 else ring_order[n_chips:]
        for part, k in zip(parts, flips_of):
            pieces.append((part.reshape(-1, rows_own, ff_own), 0))
            block = slots * n_dp + (dp_at ^ k)
            where.append(jnp.stack([block, n_all + block], axis=1).reshape(-1))
    (w_gate_up,) = assemble(
        pieces, jnp.concatenate(where), ((((0, 0), 0, ff_own),),), (ff_own,)
    )
    w_gate_up = w_gate_up.reshape(2, D, ff_own)
    out_pairs, kept = [], ()
    running = None
    for slot in range(n_chips):
        sent = None if running is None else seq_perm(running, 1, 0)
        normed_ring = ring_step(normed_ring)
        upstream_ring = ring_step(upstream_ring)
        out_own, out_other, grad_own, grad_other, *kept = feed_forward(
            (normed_ring[slot], normed_swapped[slot]),
            (upstream_ring[slot], upstream_swapped[slot]),
            w_gate_up,
            w_down,
            slot,
            n_chips,
            kept,
        )
        grad_swapped = swap(grad_other)
        if slot + 1 < n_chips:
            normed_swapped = normed_swapped + [swap(after(normed_ring[slot + 1], grad_own))]
        if slot + 2 < n_chips and len(upstream_swapped) < slot + 3:
            upstream_swapped = upstream_swapped + [swap(after(upstream_ring[slot + 2], grad_own))]
        if slot == 0:
            grad_first = (grad_own, grad_swapped)
        elif sent is None:
            running = add(grad_own, grad_swapped)
        else:
            running = add(grad_own, grad_swapped, after(sent, grad_own))
        running, normed_ring, normed_swapped, upstream_ring, upstream_swapped, kept = fence(
            running, normed_ring, normed_swapped, upstream_ring, upstream_swapped, kept
        )
        out_pairs = out_pairs + [(out_own, out_other)]
        if 1 < slot:
            out_pairs[slot - 1] = (out_pairs[slot - 1][0], swap(out_pairs[slot - 1][1]))
        if slot == 2:
            ring_first = add(*out_pairs[1])

    grad_ring = jnp.zeros_like(grad_first[0]) if running is None else seq_perm(running, 1, 0)
    normed_all, ffn_all, hidden_all, gate_grads_all, up_grads_all = kept
    first_split = (
        jnp.concatenate([bit_sides[order[0]] for order in orders]),
        tuple(order[0] for order in orders),
    )
    halves = [
        weight_grad(
            normed_all,
            (gate_grads_all, up_grads_all),
            split=first_split,
            rows=rows_own,
            part=(part, 2),
        )
        for part in range(2)
    ]
    out_running = seq_perm(ring_first, 1, 0)
    out_running = add(after(out_running, *halves[0][0]), *out_pairs[2])
    grad_ring, halves, out_pairs, out_running = fence(grad_ring, halves, out_pairs, out_running)

    got_one = [dp_perm(goes, order[0]) for (_, goes), order in zip(halves[0], orders)]
    out_running = seq_perm(out_running, 1, 0)
    out_pairs[-1] = (out_pairs[-1][0], swap(out_pairs[-1][1]))
    residual_grads, branch_grads, attended_grads, gain_two_grad = norm_back(
        grad_ring, *grad_first, residual, upstream, gain_two, w_out
    )
    query_pre, kv_grad_own, kv_grad_other = attend_back(
        queries,
        key_value_all,
        attended_grads,
        attended,
        logsum,
        query_bases,
        key_bases,
        cosine,
        sine,
    )
    got_one, kv_grad_own, kv_grad_other, query_pre, branch_grads, out_running, out_pairs = fence(
        got_one, kv_grad_own, kv_grad_other, query_pre, branch_grads, out_running, out_pairs
    )
    own_parts = kv_grad_own.reshape(n_chips, tok_rows, 2 * KVW)
    other_parts = swap(kv_grad_other).reshape(n_chips, tok_rows, 2 * KVW)
    kv_sum = add_turn(own_parts, other_parts, jnp.zeros_like(chip_side))
    kv_sum, halves, query_pre, branch_grads, kept = fence(
        kv_sum, halves, query_pre, branch_grads, kept
    )

    def next_split(kept_parts, got, done_bits, left_bits):
        rest = [bit for bit in bits[::-1] if bit not in done_bits]
        bit = left_bits[0]
        lead = sum(part.shape[0] for part in kept_parts) // 2 ** len(rest)
        return add_halve(kept_parts, got, bit_sides[bit], lead * 2 ** rest.index(bit))

    kv_got = [seq_perm(kv_sum[t], n_chips - t, 0) for t in range(1, n_chips)]
    got_two = [dp_perm(goes, order[0]) for (_, goes), order in zip(halves[1], orders)]
    by_core = (core_side, (n_dp,))
    (query_split,) = weight_grad(normed_one[None], (query_pre[None],), split=by_core, rows=rows_own)
    (out_split,) = weight_grad(
        attended_low[None], (branch_grads[None],), split=by_core, rows=rows_own
    )
    (down_grad,) = weight_grad(kept[2], (kept[1],))
    out_running = add(out_running, *out_pairs[3])
    kv_got, got_two, query_split, out_split, down_grad, out_running = fence(
        kv_got, got_two, query_split, out_split, down_grad, out_running
    )

    out_running = seq_perm(out_running, 1, 0)
    gate_up_split = [
        next_split([one[0], two[0]], [got, other], order[:1], order[1:])
        for one, two, got, other, order in zip(*halves, got_one, got_two, orders)
    ]
    gate_up_sums = [dp_perm(goes, order[1]) for (_, goes), order in zip(gate_up_split, orders)]
    both = [(split[0], swap(split[1])) for split in (query_split, out_split)]
    key_value_pre, input_grads, gain_one_grad, bias_grad = input_back(
        inputs,
        gain_one,
        w_qkv,
        query_pre,
        cosine,
        sine,
        residual_grads,
        kv_sum[0],
        kv_got,
    )
    down_split = split_columns(
        down_grad.reshape(n_dp, ff_pad, D),
        first_split[0],
        ((0, D // 2), (D // 2, D)),
        tuple(order[0] for order in orders),
    )
    ((kv_stays, kv_goes),) = weight_grad(
        normed_one[None], (key_value_pre[None],), split=by_core, rows=rows_own
    )
    (
        gate_up_split,
        gate_up_sums,
        down_split,
        both,
        input_grads,
        kv_stays,
        kv_goes,
        out_running,
        small_parts,
    ) = fence(
        gate_up_split,
        gate_up_sums,
        down_split,
        both,
        input_grads,
        kv_stays,
        kv_goes,
        out_running,
        (gain_one_grad, gain_two_grad, bias_grad),
    )

    down_got = [dp_perm(goes, order[0]) for (_, goes), order in zip(down_split, orders)]
    ready = []
    for split, got, order in zip(gate_up_split, gate_up_sums, orders):
        kept_part = split[0]
        for i in range(2, len(order)):
            kept_part, goes = next_split([kept_part], [got], order[:i], order[i:])
            got = dp_perm(goes, order[i])
        ready.append(add_halve([kept_part], [got], core_side, n_chips))
    to_send = turn_pairs(
        [kept_part for kept_part, _ in ready],
        [swap(sent) for _, sent in ready],
        chip_side,
        n_chips,
    )
    small_grad = jnp.concatenate(small_parts, axis=1).astype(bf16)
    small_grad = jnp.pad(
        small_grad.reshape(n_all, small_own), ((0, 0), (0, rows_own * HD - small_own))
    ).reshape(n_chips, 2, n_dp, rows_own, HD)
    kv_stays = jnp.concatenate(
        [pick(small_grad, core_at, 1).reshape(-1, rows_own, HD), kv_stays], axis=2
    )
    kv_goes = jnp.concatenate(
        [pick(small_grad, 1 - core_at, 1).reshape(-1, rows_own, HD), kv_goes], axis=2
    )
    kv_got = swap(kv_goes)
    rest_cuts = (((0, D), (0, 3 * HD)), ((0, D), (3 * HD, HD + 2 * KVW)))
    rest = [
        add_halve_columns(
            [kept_part, kv_stays],
            [got, kv_got],
            cuts,
            bit_sides[order[0]],
            n_chips * n_dp // (2 * order[0]),
        )
        for (kept_part, got), cuts, order in zip(both, rest_cuts, orders)
    ]
    to_send, rest, out_running, down_got = fence(to_send, rest, out_running, down_got)

    gate_up_owned = {0: to_send[0]}
    rest_got = [dp_perm(goes, order[0]) for (_, goes), order in zip(rest, orders)]
    for shift in groups[0] + groups[2]:
        gate_up_owned[shift] = exchange(shift)
    if len(bits) > 1:
        down_split = [
            next_split([kept_part], [got], order[:1], order[1:])
            for (kept_part, _), got, order in zip(down_split, down_got, orders)
        ]
    out_pairs[0] = (out_pairs[0][0], swap(out_pairs[0][1]))
    gate_up_owned, rest_got, down_split, out_pairs = fence(
        gate_up_owned, rest_got, down_split, out_pairs
    )

    for shift in groups[1]:
        gate_up_owned[shift] = exchange(shift)
    rest_send = []
    for (kept_part, _), got, order in zip(rest, rest_got, orders):
        for i in range(1, len(order)):
            kept_part, goes = next_split([kept_part], [got], order[:i], order[i:])
            got = dp_perm(goes, order[i])
        rest_send.append(add_turn(kept_part, got, chip_side))
    gate_up_owned, rest_send, down_split = fence(gate_up_owned, rest_send, down_split)

    rest_send = [
        jnp.concatenate([parts[t] for parts in rest_send], axis=1) for t in range(n_chips)
    ]
    rest_ring = [rest_send[0]] + [seq_perm(rest_send[shift], shift, 0) for shift in shifts]
    down_owned = []
    for (kept_part, goes), got, order in zip(down_split, down_got, orders):
        for i in range(1, len(order)):
            if i > 1:
                kept_part, goes = next_split([kept_part], [got], order[:i], order[i:])
            got = dp_perm(goes, order[i])
        down_owned.append(kept_part[0, :ff_dev].astype(f32) + got[0, :ff_dev].astype(f32))
    down_owned = jnp.concatenate(down_owned, axis=1)
    down_new = adamw_update(down_master, down_first, down_second, down_owned, 0.026, 0.1)
    rest_ring, down_new = fence(rest_ring, down_new)
    total = sum(piece.astype(f32) for piece in rest_ring)
    for t in range(4, n_chips):
        out_running = seq_perm(add(out_running, *out_pairs[t]), 1, 0)
    outputs = residual + out_pairs[0][0].astype(f32) + out_pairs[0][1].astype(f32)
    outputs = outputs + out_running.astype(f32)
    outputs = outputs.astype(bf16)
    gate_up_new = adamw_hidden(
        gate_up_master,
        gate_up_first,
        gate_up_second,
        [gate_up_owned[t] for t in range(n_chips)],
        ring_order,
        n_dp,
        ff_pad,
        0.064,
        0.1,
    )
    wide = D + 3 * HD
    query_owned, out_owned = total[:, :D], total[:, wide : wide + D]
    small_owned = total[:, D : D + HD]
    qkv_owned = jnp.concatenate(
        [query_owned, total[:, D + HD : wide], total[:, wide + D :]], axis=1
    )
    small_owned = small_owned.reshape(-1)[:small_own]

    qkv_new = adamw_update(qkv_master, qkv_first, qkv_second, qkv_owned, 0.09, 0.1)
    out_new = adamw_update(out_master, out_first, out_second, out_owned, 0.18, 0.1)
    small_new = adamw_update(small_master, small_first, small_second, small_owned, 0.6, 0.0)
    return (
        outputs[None],
        input_grads[None],
        *qkv_new,
        *out_new,
        *gate_up_new,
        *down_new,
        *small_new,
    )


def solution(mesh):
    in_specs = (
        P("dp", "seq", None),
        P("dp", "seq", None),
        P("dp", None),
        P(("seq", "dp"), None),
        P(("seq", "dp"), None),
        P(("seq", "dp"), None),
        P(("seq", "dp"), None),
        P(("seq", "dp"), None),
        P(("seq", "dp"), None),
        P(None, ("seq", "dp"), None),
        P(None, ("seq", "dp"), None),
        P(None, ("seq", "dp"), None),
        P(("seq", "dp"), None),
        P(("seq", "dp"), None),
        P(("seq", "dp"), None),
        P(("seq", "dp")),
        P(("seq", "dp")),
        P(("seq", "dp")),
    )
    out_specs = (
        P("dp", "seq", None),
        P("dp", "seq", None),
        P(("seq", "dp"), None),
        P(("seq", "dp"), None),
        P(("seq", "dp"), None),
        P(("seq", "dp"), None),
        P(("seq", "dp"), None),
        P(("seq", "dp"), None),
        P(None, ("seq", "dp"), None),
        P(None, ("seq", "dp"), None),
        P(None, ("seq", "dp"), None),
        P(("seq", "dp"), None),
        P(("seq", "dp"), None),
        P(("seq", "dp"), None),
        P(("seq", "dp")),
        P(("seq", "dp")),
        P(("seq", "dp")),
    )
    return jax.shard_map(shards, mesh=mesh, in_specs=in_specs, out_specs=out_specs, check_vma=False)
```

```python
import functools

import jax
import jax.numpy as jnp
from jax import lax
from jax.experimental import pallas as pl
from jax.experimental.pallas import tpu as pltpu
from jax.sharding import PartitionSpec as P

D = 1536
HEADS = 12
KVH = 2
HD = 128
STEP = 10
KVW = KVH * HD
PIECE = 128


norm_eps = 1e-06
rope_base = 1000000.0
beta_one = 0.9
beta_two = 0.95
adam_eps = 1e-08
masked_score = -1e30
log2_e = 1.4426950408889634
bf16 = jnp.bfloat16
f32 = jnp.float32
vmem = pl.BlockSpec(memory_space=pltpu.VMEM)
smem = pl.BlockSpec(memory_space=pltpu.SMEM)
anywhere = pl.BlockSpec(memory_space=pl.ANY)


def shape_of(dims, kind):
    return jax.ShapeDtypeStruct(dims, kind)


def kernel_call(kernel, name, out_shape, operands, megabytes=32, **options):
    return pl.pallas_call(
        kernel,
        name=name,
        out_shape=out_shape,
        compiler_params=pltpu.CompilerParams(vmem_limit_bytes=megabytes << 20),
        cost_estimate=pl.CostEstimate(flops=10**6, bytes_accessed=10**6, transcendentals=0),
        **options,
    )(*operands)


def after(values, *others):
    return lax.optimization_barrier((values,) + others)[0]


def fence(*groups):
    flat, tree = jax.tree.flatten(groups)
    return jax.tree.unflatten(tree, lax.optimization_barrier(tuple(flat)))


def dot(left, right):
    return jnp.dot(left, right, preferred_element_type=f32)


def dot_transposed(left, right):
    return lax.dot_general(left, right, (((1,), (1,)), ((), ())), preferred_element_type=f32)


def rotary_tables(places):
    half_size = HD // 2
    freqs = rope_base ** (-(jnp.arange(half_size).astype(f32) * (2.0 / HD)))
    angles = places.astype(f32)[:, None] * freqs[None, :]
    cosine, sine = jnp.cos(angles), jnp.sin(angles)
    return jnp.concatenate([cosine, cosine], axis=1), jnp.concatenate([-sine, sine], axis=1)


def rms_scale(values):
    return lax.rsqrt(jnp.mean(values * values, axis=-1, keepdims=True) + norm_eps)


def swap_halves(values):
    return pltpu.roll(values, HD // 2, 1)


def head(index):
    return slice(index * HD, (index + 1) * HD)


def project_kv_kernel(tokens, w_qkv, gain, bias, cosine, sine, normed_ref, kv_ref):
    inputs = tokens[...].astype(f32)
    normed = (inputs * rms_scale(inputs) * gain[...]).astype(bf16)
    normed_ref[...] = normed
    rows = dot(normed, w_qkv[...]) + bias[:, D:]
    for j in range(KVH):
        part = rows[:, head(j)]
        kv_ref[:, head(j)] = (part * cosine[...] + swap_halves(part) * sine[...]).astype(bf16)
    kv_ref[:, KVW:] = rows[:, KVW:].astype(bf16)


def project_q_kernel(normed, w_qkv, bias, cosine, sine, query_ref):
    rows = dot(normed[...], w_qkv[...]) + bias[:, :D]
    for j in range(HEADS):
        part = rows[:, head(j)]
        query_ref[:, head(j)] = (part * cosine[...] + swap_halves(part) * sine[...]).astype(bf16)


def project_kv(tokens, w_qkv, gain, bias, cosine, sine):
    rows = tokens.shape[0]
    return kernel_call(
        project_kv_kernel,
        "project_kv",
        (shape_of((rows, D), bf16), shape_of((rows, 2 * KVW), bf16)),
        (tokens, w_qkv, gain, bias, cosine, sine),
        megabytes=58,
        grid=(1,),
        in_specs=[vmem, pl.BlockSpec((D, 2 * KVW), lambda i: (0, D // (2 * KVW)))] + [vmem] * 4,
        out_specs=(vmem, vmem),
    )


def project_q(normed, w_qkv, bias, cosine, sine):
    return kernel_call(
        project_q_kernel,
        "project_q",
        shape_of(normed.shape, bf16),
        (normed, w_qkv, bias, cosine, sine),
        megabytes=58,
        grid=(1,),
        in_specs=[vmem, pl.BlockSpec((D, D), lambda i: (0, 0))] + [vmem] * 3,
        out_specs=vmem,
    )


def mask_keys(values, query_bases, key_bases, first_run, fill):
    later = lax.broadcasted_iota(jnp.int32, (PIECE, PIECE), 0) - lax.broadcasted_iota(
        jnp.int32, (PIECE, PIECE), 1
    )
    keys, queries = values.shape
    rows = []
    for r in range(keys // PIECE):
        down = slice(r * PIECE, (r + 1) * PIECE)
        row = []
        for q in range(queries // PIECE):
            gap = query_bases[q] - key_bases[first_run + r]
            row.append(jnp.where(later <= gap, values[down, q * PIECE : (q + 1) * PIECE], fill))
        rows.append(jnp.concatenate(row, axis=1))
    return jnp.concatenate(rows, axis=0)


def attend_kernel(query_bases, key_bases, q_ref, *refs):
    pieces, (out_ref, lse_ref, kv_ref) = refs[:-3], refs[-3:]
    rows = q_ref.shape[0]
    for i, piece in enumerate(pieces):
        kv_ref[i * rows : (i + 1) * rows, :] = piece[...]
    groups = HEADS // KVH
    scale = HD**-0.5 * log2_e
    for kv in range(KVH):
        values = kv_ref[:, head(KVH + kv)].T
        for h in range(kv * groups, (kv + 1) * groups):
            queries = q_ref[:, head(h)]
            scores = []
            for run in range(key_bases.shape[0]):
                keys = kv_ref[run * PIECE : (run + 1) * PIECE, head(kv)]
                part = dot_transposed(keys, queries)
                scores.append(mask_keys(part, query_bases, key_bases, run, masked_score))
            scores = jnp.concatenate(scores, axis=0)
            top = jnp.max(scores, axis=0, keepdims=True)
            weights = jnp.exp2((scores - top) * scale)
            total = jnp.sum(weights, axis=0, keepdims=True)
            mixed = dot(values, weights.astype(bf16))
            out_ref[:, head(h)] = (mixed / total).T
            lse_ref[h : h + 1, :] = top * scale + jnp.log2(total)


def attend(queries, pieces, query_bases, key_bases):
    rows, total = queries.shape[0], key_bases.shape[0] * PIECE
    return kernel_call(
        attend_kernel,
        "attend",
        (
            shape_of((rows, D), f32),
            shape_of((HEADS, rows), f32),
            shape_of((total, 2 * KVW), bf16),
        ),
        (query_bases, key_bases, queries, *pieces),
        in_specs=[smem] * 2 + [vmem] * (1 + len(pieces)),
    )


def out_kernel(tokens, attended, w_out, gain, residual_ref, normed_ref, low_ref):
    low = attended[...].astype(bf16)
    low_ref[...] = low
    residual = tokens[...].astype(f32) + dot(low, w_out[...])
    residual_ref[...] = residual
    normed_ref[...] = (residual * rms_scale(residual) * gain[...]).astype(bf16)


def out_project(tokens, attended, w_out, gain):
    dims = tokens.shape
    return kernel_call(
        out_kernel,
        "out_project",
        (shape_of(dims, f32), shape_of(dims, bf16), shape_of(dims, bf16)),
        (tokens, attended, w_out, gain),
    )


def ffn_kernel(
    normed_own, normed_other, grad_own, grad_other, w_gate_up, w_down, *refs, earlier
):
    refs = refs[earlier:]
    out_refs, grad_refs = refs[:2], refs[2:4]
    normed_ref, ffn_grad_ref, hidden_ref, gate_ref, up_ref = refs[4:]
    rows = normed_own.shape[0]
    for i, (normed_in, grad_in) in enumerate(((normed_own, grad_own), (normed_other, grad_other))):
        to = slice(i * rows, (i + 1) * rows)
        normed, ffn_grad = normed_in[...], grad_in[...]
        normed_ref[0, to, :] = normed
        ffn_grad_ref[0, to, :] = ffn_grad
        gate = dot(normed, w_gate_up[0])
        up = dot(normed, w_gate_up[1])
        sigmoid = 1.0 / (1.0 + jnp.exp(-gate))
        silu = gate * sigmoid
        hidden = (silu * up).astype(bf16)
        hidden_ref[0, to, :] = hidden
        out_refs[i][...] = dot(hidden, w_down[...]).astype(bf16)
        hidden_grad = dot_transposed(ffn_grad, w_down[...])
        gate_grad = (hidden_grad * up * sigmoid * (1.0 + gate * (1.0 - sigmoid))).astype(bf16)
        up_grad = (hidden_grad * silu).astype(bf16)
        gate_ref[0, to, :] = gate_grad
        up_ref[0, to, :] = up_grad
        grad_refs[i][...] = (
            dot_transposed(gate_grad, w_gate_up[0]) + dot_transposed(up_grad, w_gate_up[1])
        ).astype(bf16)


def feed_forward(normed, grads, w_gate_up, w_down, slot, slots, kept):
    rows, width = normed[0].shape
    ff_own = w_down.shape[0]
    token = shape_of((rows, width), bf16)
    widths = (width, width, ff_own, ff_own, ff_own)
    operands = (*normed, *grads, w_gate_up, w_down)
    return kernel_call(
        functools.partial(ffn_kernel, earlier=len(kept)),
        "feed_forward",
        (token,) * 4 + tuple(shape_of((slots, 2 * rows, w), bf16) for w in widths),
        (*operands, *kept),
        grid=(1,),
        in_specs=[vmem] * len(operands) + [anywhere] * len(kept),
        out_specs=(vmem,) * 4
        + tuple(pl.BlockSpec((1, 2 * rows, w), lambda i: (slot, 0, 0)) for w in widths),
        input_output_aliases={len(operands) + i: 4 + i for i in range(len(kept))},
    )


def norm_back_kernel(
    got, own, other, residual_ref, cotangent, gain, w_out, grad_ref, low_ref, back_ref, gain_ref
):
    normed_grad = got[...].astype(f32) + own[...].astype(f32) + other[...].astype(f32)
    residual = residual_ref[...]
    scale = rms_scale(residual)
    unit = residual * scale
    gain_ref[...] = jnp.sum(normed_grad * unit, axis=0, keepdims=True)
    weighted = normed_grad * gain[...]
    grad = cotangent[...].astype(f32) + scale * (
        weighted - unit * jnp.mean(weighted * unit, axis=-1, keepdims=True)
    )
    grad_ref[...] = grad
    low = grad.astype(bf16)
    low_ref[...] = low
    back_ref[...] = dot_transposed(low, w_out[...]).astype(bf16)


def norm_back(got, own, other, residual, cotangent, gain, w_out):
    dims = residual.shape
    return kernel_call(
        norm_back_kernel,
        "norm_back",
        (shape_of(dims, f32), shape_of(dims, bf16), shape_of(dims, bf16), shape_of((1, D), f32)),
        (got, own, other, residual, cotangent, gain, w_out),
    )


def attend_back_kernel(
    query_bases,
    key_bases,
    q_ref,
    kv_ref,
    grad_ref,
    out_ref,
    lse_ref,
    cosine,
    sine,
    q_grad_ref,
    kv_own_ref,
    kv_other_ref,
    q_rows,
    grad_rows,
    deltas,
    q_sums,
):
    rows = q_ref.shape[0]
    groups = HEADS // KVH
    scale = HD**-0.5
    for kv in range(KVH):
        for j in range(groups):
            part = slice(j * rows, (j + 1) * rows)
            columns = head(kv * groups + j)
            q_rows[part, :] = q_ref[:, columns]
            grads = grad_ref[:, columns]
            grad_rows[part, :] = grads
            product = grads.astype(f32) * out_ref[:, columns]
            deltas[:, part] = jnp.sum(product.T, axis=0, keepdims=True)
        q_sums[...] = jnp.zeros_like(q_sums)

        @pl.loop(0, kv_ref.shape[0] // (2 * rows), unroll=2)
        def _(step):
            at = pl.ds(pl.multiple_of(step * (2 * rows), 2 * rows), 2 * rows)
            runs = 2 * rows // PIECE
            keys = kv_ref[at, head(kv)]
            values = kv_ref[at, head(KVH + kv)]
            key_sum = value_sum = None
            for j in range(groups):
                part = slice(j * rows, (j + 1) * rows)
                h = kv * groups + j
                queries, grads = q_rows[part, :], grad_rows[part, :]
                scores = dot_transposed(keys, queries)
                weights = jnp.exp2(scores * (scale * log2_e) - lse_ref[h : h + 1, :])
                weights = mask_keys(weights, query_bases, key_bases, step * runs, 0.0)
                weight_grads = dot_transposed(values, grads)
                score_grads = (weights * (weight_grads - deltas[:, part])).astype(bf16)
                value_part = dot(weights.astype(bf16), grads)
                key_part = dot(score_grads, queries)
                key_sum = key_part if key_sum is None else key_sum + key_part
                value_sum = value_part if value_sum is None else value_sum + value_part
                q_sums[part, :] += lax.dot_general(
                    score_grads, keys, (((0,), (0,)), ((), ())), preferred_element_type=f32
                )
            key_sum = (key_sum * scale).astype(bf16)
            value_sum = value_sum.astype(bf16)
            to = pl.ds(pl.multiple_of(step * rows, rows), rows)
            for ref, mine in ((kv_own_ref, slice(0, rows)), (kv_other_ref, slice(rows, 2 * rows))):
                ref[to, head(kv)] = key_sum[mine, :]
                ref[to, head(KVH + kv)] = value_sum[mine, :]

        for j in range(groups):
            part = q_sums[j * rows : (j + 1) * rows, :] * scale
            q_grad_ref[:, head(kv * groups + j)] = (
                part * cosine[...] - swap_halves(part) * sine[...]
            ).astype(bf16)


def attend_back(queries, key_value, grads, attended, lse, query_bases, key_bases, cosine, sine):
    rows, total = queries.shape[0], key_value.shape[0]
    groups = HEADS // KVH
    return kernel_call(
        attend_back_kernel,
        "attend_back",
        (
            shape_of((rows, D), bf16),
            shape_of((total // 2, 2 * KVW), bf16),
            shape_of((total // 2, 2 * KVW), bf16),
        ),
        (query_bases, key_bases, queries, key_value, grads, attended, lse, cosine, sine),
        in_specs=[smem] * 2 + [vmem] * 7,
        scratch_shapes=[
            pltpu.VMEM((groups * rows, HD), bf16),
            pltpu.VMEM((groups * rows, HD), bf16),
            pltpu.VMEM((1, groups * rows), f32),
            pltpu.VMEM((groups * rows, HD), f32),
        ],
    )


def input_kernel(
    tokens, gain, w_qkv, query_grad, cosine, sine, residual_grad, own, *refs
):
    got, (kv_ref, input_ref, gain_ref, bias_ref) = refs[:-4], refs[-4:]
    rows = own[...].astype(f32)
    for piece in got:
        rows = rows + piece[...].astype(f32)
    for j in range(KVH):
        part = rows[:, head(j)]
        kv_ref[:, head(j)] = (part * cosine[...] - swap_halves(part) * sine[...]).astype(bf16)
    kv_ref[:, KVW:] = rows[:, KVW:].astype(bf16)
    kv_grad = kv_ref[...]
    q_grad = query_grad[...]
    bias_ref[:, :D] = jnp.sum(q_grad.astype(f32), axis=0, keepdims=True)
    bias_ref[:, D:] = jnp.sum(kv_grad.astype(f32), axis=0, keepdims=True)
    normed_grad = dot_transposed(q_grad, w_qkv[:, :D]) + dot_transposed(kv_grad, w_qkv[:, D:])
    inputs = tokens[...].astype(f32)
    scale = rms_scale(inputs)
    unit = inputs * scale
    gain_ref[...] = jnp.sum(normed_grad * unit, axis=0, keepdims=True)
    weighted = normed_grad * gain[...]
    input_ref[...] = residual_grad[...] + scale * (
        weighted - unit * jnp.mean(weighted * unit, axis=-1, keepdims=True)
    )


def input_back(tokens, gain, w_qkv, query_grad, cosine, sine, residual_grad, own, got):
    rows = tokens.shape[0]
    return kernel_call(
        input_kernel,
        "input_back",
        (
            shape_of((rows, 2 * KVW), bf16),
            shape_of((rows, D), f32),
            shape_of((1, D), f32),
            shape_of((1, D + 2 * KVW), f32),
        ),
        (tokens, gain, w_qkv, query_grad, cosine, sine, residual_grad, own, *got),
        megabytes=58,
    )


def split_kernel(sides, values, *outs, cuts, bits):
    blocks = values.shape[0]
    for i, ((lo, hi), bit) in enumerate(zip(cuts, bits)):
        for out, side in ((outs[2 * i], sides[i]), (outs[2 * i + 1], 1 - sides[i])):
            for o in range(blocks // (2 * bit)):
                for j in range(bit):
                    out[o * bit + j] = values[(2 * o + side) * bit + j, :, lo:hi]


def split_columns(values, sides, cuts, bits):
    blocks, rows, _ = values.shape
    outs = kernel_call(
        functools.partial(split_kernel, cuts=cuts, bits=bits),
        "split_columns",
        tuple(shape_of((blocks // 2, rows, hi - lo), bf16) for lo, hi in cuts for _ in range(2)),
        (sides, values),
        in_specs=[smem, vmem],
    )
    return [(outs[2 * i], outs[2 * i + 1]) for i in range(len(cuts))]


def weight_grad_kernel(sides, left, *refs, count, inners, based):
    rights, refs = refs[:count], refs[count:]
    bases, outs = refs[: count * based], refs[count * based :]
    turned = left[...].reshape(-1, left.shape[-1]).T
    for i, right in enumerate(rights):
        result = dot(turned, right[...].reshape(-1, right.shape[-1]))
        if based:
            result = result + bases[i][...]
        if not inners:
            outs[i][...] = result.astype(outs[i].dtype)
            continue
        stays, goes = outs[2 * i], outs[2 * i + 1]
        rows = stays.shape[2]
        result = result.astype(bf16)
        for side, refs_of in ((0, (stays, goes)), (1, (goes, stays))):

            @pl.when(sides[i] == side)
            def _():
                for o in range(stays.shape[0]):
                    for bit in range(2):
                        for j in range(inners[i]):
                            block = (o * 2 + bit) * inners[i] + j
                            refs_of[bit][o, j] = result[block * rows : (block + 1) * rows]


def weight_grad(
    left, rights, slots=(0, 1), bases=(), split=None, rows=0, part=(0, 1), kind=bf16
):
    n_slots, tokens, m = left.shape
    n_slots = n_slots // slots[1]
    m = m // part[1]
    block = 3 * HD if m % (3 * HD) == 0 else HD
    steps = m // block
    first = part[0] * steps
    whole = pl.Buffered(buffer_count=1)
    sides, inners = split if split else (jnp.zeros((1,), jnp.int32), ())
    out_shape, out_specs = [], []
    for i, right in enumerate(rights):
        n = right.shape[-1]
        if not inners:
            out_shape.append(shape_of((m, n), kind))
            out_specs.append(pl.BlockSpec((block, n), lambda i: (i, 0)))
            continue
        outer = block // (2 * inners[i] * rows)
        for _ in range(2):
            out_shape.append(shape_of((steps * outer, inners[i], rows, n), bf16))
            out_specs.append(pl.BlockSpec((outer, inners[i], rows, n), lambda i: (i, 0, 0, 0)))
    outs = kernel_call(
        functools.partial(
            weight_grad_kernel, count=len(rights), inners=inners, based=int(bool(bases))
        ),
        "weight_grad",
        tuple(out_shape),
        (sides, left, *rights, *bases),
        megabytes=32,
        grid=(steps,),
        in_specs=[
            smem,
            pl.BlockSpec((n_slots, tokens, block), lambda i: (slots[0], 0, i + first)),
        ]
        + [
            vmem
            if slots == (0, 1)
            else pl.BlockSpec(
                (n_slots, tokens, right.shape[-1]),
                lambda i: (slots[0], 0, 0),
                pipeline_mode=whole,
            )
            for right in rights
        ]
        + [pl.BlockSpec((block, base.shape[1]), lambda i: (i + first, 0)) for base in bases],
        out_specs=tuple(out_specs),
    )
    if not inners:
        return outs
    outs = [out.reshape((-1,) + out.shape[2:]) for out in outs]
    return [(outs[2 * i], outs[2 * i + 1]) for i in range(len(rights))]


def stack_kernel(*refs, cuts):
    pieces, outs = refs[: -len(cuts)], refs[-len(cuts) :]
    for i, piece in enumerate(pieces):
        for out, (lo, hi) in zip(outs, cuts):
            out[i] = piece[:, lo:hi]


def stack_columns(pieces, cuts):
    return kernel_call(
        functools.partial(stack_kernel, cuts=cuts),
        "stack_columns",
        tuple(shape_of((len(pieces), pieces[0].shape[0], hi - lo), bf16) for lo, hi in cuts),
        tuple(pieces),
    )


def cut_kernel(core, values, kept_ref, sent_ref, *, n_dp, own, padded):
    kept_ref[...] = jnp.zeros_like(kept_ref)
    sent_ref[...] = jnp.zeros_like(sent_ref)
    for side, refs in ((0, (kept_ref, sent_ref)), (1, (sent_ref, kept_ref))):

        @pl.when(core[0] == side)
        def _():
            for s in range(2 * kept_ref.shape[0]):
                for d in range(n_dp):
                    start = (s * n_dp + d) * own
                    refs[s % 2][s // 2, 0, :, d * padded : d * padded + own] = values[
                        0, :, start : start + own
                    ].astype(bf16)


def cut_hidden(values, core, n_chips, n_dp, padded):
    two, rows, ff = values.shape
    own = ff // (2 * n_chips * n_dp)
    dims = (n_chips, two, rows, n_dp * padded)
    return kernel_call(
        functools.partial(cut_kernel, n_dp=n_dp, own=own, padded=padded),
        "cut_hidden",
        (shape_of(dims, bf16),) * 2,
        (core, values),
        grid=(two,),
        in_specs=[smem, pl.BlockSpec((1, rows, ff), lambda g: (g, 0, 0))],
        out_specs=(pl.BlockSpec((n_chips, 1, rows, n_dp * padded), lambda g: (0, g, 0, 0)),) * 2,
    )


def turn_kernel(chip, *refs, n_chips):
    ins, outs = refs[: len(refs) - n_chips], refs[len(refs) - n_chips :]
    per_side = len(ins) // 2
    for t, out in enumerate(outs):
        at = lax.rem(chip[0] + t, n_chips)
        for side in range(2):
            if per_side == 1:
                out[side] = ins[side][at]
            else:
                for g in range(2):
                    out[side, g] = ins[2 * side + g][at]


def turn_pairs(kept, got, chip, n_chips):
    rows, width = kept[0].shape[-2:]
    return kernel_call(
        functools.partial(turn_kernel, n_chips=n_chips),
        "turn_pairs",
        (shape_of((2, 2, rows, width), bf16),) * n_chips,
        (chip, *kept, *got),
        in_specs=[smem] + [vmem] * (len(kept) + len(got)),
    )


def add_kernel(*refs):
    *ins, out = refs
    total = ins[0][...].astype(f32)
    for ref in ins[1:]:
        total = total + ref[...].astype(f32)
    out[...] = total.astype(bf16)


def add(*arrays):
    return kernel_call(add_kernel, "add", shape_of(arrays[0].shape, bf16), arrays)


def add_turn_kernel(chip, kept, got, *outs):
    n = kept.shape[0]
    for t, out in enumerate(outs):
        at = lax.rem(chip[0] + t, n)
        out[...] = (kept[at].astype(f32) + got[at].astype(f32)).astype(bf16)


def add_turn(kept, got, chip):
    n = kept.shape[0]
    return kernel_call(
        add_turn_kernel,
        "add_turn",
        (shape_of(kept.shape[1:], bf16),) * n,
        (chip, kept, got),
        in_specs=[smem, vmem, vmem],
    )


def add_halve_kernel(mine, *refs):
    parts, (stays, goes) = refs[:-2], refs[-2:]
    count = len(parts) // 2
    at = 0
    for kept, got in zip(parts[:count], parts[count:]):
        for o in range(kept.shape[0]):
            for out, side in ((stays, mine[0]), (goes, 1 - mine[0])):
                out[at] = (kept[o, side].astype(f32) + got[o, side].astype(f32)).astype(bf16)
            at += 1


def add_halve(kept, got, mine, outer):
    rows, width = kept[0].shape[1:]
    blocks = sum(part.shape[0] for part in kept)
    inner = blocks // (2 * outer)
    half = shape_of((outer, inner, rows, width), bf16)
    stays, goes = kernel_call(
        add_halve_kernel,
        "add_halve",
        (half, half),
        (mine, *[part.reshape(-1, 2, inner, rows, width) for part in (*kept, *got)]),
        in_specs=[smem] + [vmem] * (len(kept) + len(got)),
        megabytes=40,
    )
    return stays.reshape(-1, rows, width), goes.reshape(-1, rows, width)


def add_halve_columns_kernel(mine, *refs, cuts):
    parts, (stays, goes) = refs[:-2], refs[-2:]
    count = len(parts) // 2
    lo = 0
    for kept, got, (first, last) in zip(parts[:count], parts[count:], cuts):
        hi = lo + last - first
        for o in range(kept.shape[0]):
            for out, side in ((stays, mine[0]), (goes, 1 - mine[0])):
                total = kept[o, side, :, :, first:last].astype(f32) + got[
                    o, side, :, :, first:last
                ].astype(f32)
                out[o, :, :, lo:hi] = total.astype(bf16)
        lo = hi


def add_halve_columns(kept, got, cuts, mine, outer):
    blocks, rows, _ = kept[0].shape
    inner = blocks // (2 * outer)
    width = sum(last - first for first, last in cuts)
    half = shape_of((outer, inner, rows, width), bf16)
    stays, goes = kernel_call(
        functools.partial(add_halve_columns_kernel, cuts=cuts),
        "add_halve",
        (half, half),
        (mine, *[part.reshape(outer, 2, inner, rows, -1) for part in (*kept, *got)]),
        in_specs=[smem] + [vmem] * (len(kept) + len(got)),
        megabytes=44,
    )
    return stays.reshape(-1, rows, width), goes.reshape(-1, rows, width)


def adamw_update(master, moment_one, moment_two, gradient, step_rate, decay_weight):
    first_new = beta_one * moment_one + (1.0 - beta_one) * gradient
    second_new = beta_two * moment_two + (1.0 - beta_two) * gradient * gradient
    first_hat = first_new / (1.0 - beta_one**STEP)
    second_hat = second_new / (1.0 - beta_two**STEP)
    master_new = master - step_rate * (
        first_hat / (jnp.sqrt(second_hat) + adam_eps) + decay_weight * master
    )
    return (first_new, second_new, master_new)


def adamw_kernel(where, master, first, second, *refs, n_dp, own, padded, rate, decay):
    pieces, (first_ref, second_ref, master_ref, slots, joined) = refs[:-5], refs[-5:]
    for t, piece in enumerate(pieces):
        for o in range(2):
            slots[where[2 * t + o]] = piece[o, 0]
    for s in range(slots.shape[0]):
        for d in range(n_dp):
            start = (s * n_dp + d) * own
            joined[:, start : start + own] = slots[
                s, :, d * padded : d * padded + own
            ].astype(f32)
    first_ref[0], second_ref[0], master_ref[0] = adamw_update(
        master[0], first[0], second[0], joined[...], rate, decay
    )


def adamw_hidden(master, first, second, pieces, where, n_dp, padded, rate, decay):
    two, rows, ff = master.shape
    n_seq = 2 * len(pieces)
    own = ff // (n_seq * n_dp)
    block = pl.BlockSpec((1, rows, ff), lambda g: (g, 0, 0))
    part = pl.BlockSpec((2, 1, rows, n_dp * padded), lambda g: (0, g, 0, 0))
    return kernel_call(
        functools.partial(
            adamw_kernel, n_dp=n_dp, own=own, padded=padded, rate=rate, decay=decay
        ),
        "adamw_hidden",
        (shape_of(master.shape, f32),) * 3,
        (where, master, first, second, *pieces),
        megabytes=44,
        grid=(two,),
        in_specs=[smem] + [block] * 3 + [part] * len(pieces),
        out_specs=(block,) * 3,
        scratch_shapes=[
            pltpu.VMEM((n_seq, rows, n_dp * padded), bf16),
            pltpu.VMEM((rows, ff), f32),
        ],
    )


def assemble_kernel(where, *refs, splits, counts):
    ins, outs, sems = refs[: len(counts)], refs[len(counts) : -1], refs[-1]
    copies = []
    entry = 0
    for ref, (column, count) in zip(ins, counts):
        for i in range(count):
            for out, start, width in splits[column]:
                copies.append(
                    pltpu.make_async_copy(
                        ref.at[i, :, pl.ds(start, width)],
                        outs[out[0]].at[where[entry], :, pl.ds(out[1], width)],
                        sems.at[len(copies)],
                    )
                )
            entry += 1
    for copy in copies:
        copy.start()
    for copy in copies:
        copy.wait()


def assemble(pieces, where, splits, out_widths):
    counts = [(column, array.shape[0]) for array, column in pieces]
    rows = pieces[0][0].shape[1]
    blocks = sum(count for column, count in counts if column == 0)
    n_copies = sum(count * len(splits[column]) for column, count in counts)
    return kernel_call(
        functools.partial(assemble_kernel, splits=splits, counts=counts),
        "assemble",
        tuple(shape_of((blocks, rows, w), bf16) for w in out_widths),
        (where.astype(jnp.int32), *[array for array, _ in pieces]),
        in_specs=[smem] + [anywhere] * len(pieces),
        out_specs=(vmem,) * len(out_widths),
        scratch_shapes=[pltpu.SemaphoreType.DMA((n_copies,))],
    )


def seq_perm(values, chips, flip):
    count = lax.axis_size("seq")
    return lax.ppermute(
        values, "seq", [(i, ((i + 2 * chips) % count) ^ flip) for i in range(count)]
    )


def dp_perm(values, bit):
    return lax.ppermute(values, "dp", [(i, i ^ bit) for i in range(lax.axis_size("dp"))])


def dp_bits():
    return [1 << i for i in range(lax.axis_size("dp").bit_length() - 1)]


def pick(values, index, axis):
    return lax.dynamic_index_in_dim(values, index, axis, keepdims=False)


def places_of():
    n_chips = lax.axis_size("seq") // 2
    seq_at = lax.axis_index("seq")
    return n_chips, seq_at // 2, seq_at % 2, lax.axis_size("dp"), lax.axis_index("dp")


def swap(values):
    return seq_perm(values, 0, 1)


def sent_pieces(values):
    return [values] + [seq_perm(values, t, 0) for t in range(1, lax.axis_size("seq") // 2)]


def shards(
    tokens,
    cotangent,
    positions,
    qkv_master,
    qkv_first,
    qkv_second,
    out_master,
    out_first,
    out_second,
    gate_up_master,
    gate_up_first,
    gate_up_second,
    down_master,
    down_first,
    down_second,
    small_master,
    small_first,
    small_second,
):
    n_chips, chip_at, core_at, n_dp, dp_at = places_of()
    n_seq = 2 * n_chips
    n_all = n_seq * n_dp
    bits = dp_bits()
    rows_own, qkv_width = qkv_master.shape
    half = qkv_width // 2
    small_own = small_master.shape[0]
    ff_dev = down_master.shape[0]
    ff_pad = -(-ff_dev // 16) * 16
    ff_own = n_dp * ff_pad
    inputs = tokens[0]
    upstream = cotangent[0]
    tok_rows = inputs.shape[0]
    seq_length = positions.shape[1]
    shifts = list(range(1, n_chips))

    ring_chips = [(chip_at - t) % n_chips for t in range(n_chips)]
    ring_order = jnp.stack(
        [chip * 2 + (core_at ^ flip) for chip in ring_chips for flip in range(2)]
    ).astype(jnp.int32)
    bases = positions[0, ::PIECE].reshape(n_seq, tok_rows // PIECE)
    key_bases = jnp.take(bases, ring_order, axis=0)
    query_bases = key_bases[0]
    key_bases = key_bases.reshape(-1)
    own_places = lax.dynamic_slice_in_dim(
        positions[0], (chip_at * 2 + core_at) * tok_rows, tok_rows, 0
    )
    cosine, sine = rotary_tables(own_places)

    small_block = jnp.pad(
        small_master.astype(bf16), (0, rows_own * HD - small_own)
    ).reshape(rows_own, HD)
    packed = jnp.concatenate([small_block, qkv_master.astype(bf16)], axis=1)
    qkv_ring = sent_pieces(packed)
    core_side = core_at.reshape(1).astype(jnp.int32)
    chip_side = chip_at.reshape(1).astype(jnp.int32)
    bit_sides = {bit: ((dp_at // bit) % 2).reshape(1).astype(jnp.int32) for bit in bits}
    cut_kept, cut_sent = cut_hidden(
        after(gate_up_master, qkv_ring[1]), core_side, n_chips, n_dp, ff_pad
    )
    to_send = turn_pairs([cut_kept], [swap(cut_sent)], chip_side, n_chips)
    qkv_ring, to_send, cosine, sine = fence(qkv_ring, to_send, cosine, sine)

    def exchange(shift):
        return seq_perm(to_send[shift], shift, 0)

    w_out = lax.all_gather(
        after(out_master.astype(bf16), *to_send), ("seq", "dp"), axis=0, tiled=True
    )

    columns = ((0, HD + half), (HD + half, HD + qkv_width))
    orders = (bits, bits[::-1])
    held = list(stack_columns(qkv_ring, columns))
    flips = [[0], [0]]
    gate_up_pieces = {0: to_send[0]}
    groups = [shifts[:1], shifts[-1:], shifts[1:-1]] if n_chips > 2 else [shifts, [], []]
    for stage in range(len(bits)):
        got = [dp_perm(h, order[stage]) for h, order in zip(held, orders)]
        if stage == len(bits) - 1:
            swapped = [swap(h) for h in held]
        for shift in groups[min(stage, 1)] if stage < 2 else []:
            gate_up_pieces[shift] = exchange(shift)
        got, held, gate_up_pieces = fence(got, held, gate_up_pieces)
        flips = [f + [k ^ order[stage] for k in f] for f, order in zip(flips, orders)]
        if stage < len(bits) - 1:
            held = [jnp.concatenate([h, g], axis=0) for h, g in zip(held, got)]
    (swapped,) = fence(swapped)
    for shift in groups[2]:
        gate_up_pieces[shift] = exchange(shift)
    down_share = jnp.pad(down_master.astype(bf16), ((0, ff_pad - ff_dev), (0, 0)))
    w_down = lax.all_gather(after(down_share, *got), "dp", axis=0, tiled=True)
    got_swapped = [swap(g) for g in got]
    pieces, where = [], []
    for column in range(2):
        for flip, part, ks in (
            (0, held[column], flips[column][: n_dp // 2]),
            (0, got[column], flips[column][n_dp // 2 :]),
            (1, swapped[column], flips[column][: n_dp // 2]),
            (1, got_swapped[column], flips[column][n_dp // 2 :]),
        ):
            pieces.append((part, column))
            where += [
                (chip * 2 + (core_at ^ flip)) * n_dp + (dp_at ^ k) for k in ks for chip in ring_chips
            ]
    w_qkv, small_blocks = assemble(
        pieces,
        jnp.stack(where),
        ((((1, 0), 0, HD), ((0, 0), HD, half)), (((0, half), 0, half),)),
        (qkv_width, HD),
    )
    w_qkv = w_qkv.reshape(D, qkv_width)
    small_params = small_blocks.reshape(n_all, rows_own * HD)[:, :small_own].reshape(1, -1)
    small_params = small_params.astype(f32)
    gain_one = small_params[:, :D]
    gain_two = small_params[:, D : 2 * D]
    qkv_bias = small_params[:, 2 * D :]
    normed_one, key_value = project_kv(inputs, w_qkv, gain_one, qkv_bias, cosine, sine)
    gate_up_held = [
        jnp.concatenate([gate_up_pieces[t] for t in ts], axis=0)
        for ts in (range(n_chips // 2), range(n_chips // 2, n_chips))
    ]
    normed_one, key_value, gate_up_held = fence(normed_one, key_value, gate_up_held)

    kv_ring = sent_pieces(key_value)
    gate_up_parts = [
        [held, dp_perm(held, order[0])] for held, order in zip(gate_up_held, orders)
    ]
    gate_up_flips = [[0, order[0]] for order in orders]
    queries = project_q(normed_one, w_qkv, qkv_bias, cosine, sine)
    kv_swapped = [swap(kv_ring[0])] + [swap(after(piece, queries)) for piece in kv_ring[1:]]
    kv_ring, kv_swapped, gate_up_parts, queries, upstream = fence(
        kv_ring, kv_swapped, gate_up_parts, queries, upstream
    )

    def cross(start, stop, stage):
        for parts, flips_of, order in zip(gate_up_parts, gate_up_flips, orders):
            parts += [dp_perm(piece, order[stage]) for piece in parts[start:stop]]
            flips_of += [k ^ order[stage] for k in flips_of[start:stop]]

    upstream_ring = [upstream, seq_perm(upstream, 1, 0)]
    cross(0, 1 if len(bits) == 2 else 2, 1)
    attended, logsum, key_value_all = attend(
        queries, [piece for pair in zip(kv_ring, kv_swapped) for piece in pair], query_bases, key_bases
    )
    gate_up_parts, upstream_ring, attended, logsum, key_value_all = fence(
        gate_up_parts, upstream_ring, attended, logsum, key_value_all
    )

    def ring_step(pieces):
        return pieces + [seq_perm(pieces[-1], 1, 0)] if len(pieces) < n_chips else pieces

    upstream_ring = ring_step(upstream_ring)
    if len(bits) == 2:
        cross(1, 2, 1)
    else:
        cross(0, 4, 2)
    upstream_swapped = [swap(piece) for piece in upstream_ring[:2]]
    residual, normed_two, attended_low = out_project(inputs, attended, w_out, gain_two)
    normed_ring, normed_swapped = [normed_two], [swap(normed_two)]
    gate_up_parts, upstream_ring, upstream_swapped, normed_ring, normed_swapped, residual = fence(
        gate_up_parts, upstream_ring, upstream_swapped, normed_ring, normed_swapped, residual
    )

    pieces, where = [], []
    for column, (parts, flips_of) in enumerate(zip(gate_up_parts, gate_up_flips)):
        slots = ring_order[:n_chips] if column == 0 else ring_order[n_chips:]
        for part, k in zip(parts, flips_of):
            pieces.append((part.reshape(-1, rows_own, ff_own), 0))
            block = slots * n_dp + (dp_at ^ k)
            where.append(jnp.stack([block, n_all + block], axis=1).reshape(-1))
    (w_gate_up,) = assemble(
        pieces, jnp.concatenate(where), ((((0, 0), 0, ff_own),),), (ff_own,)
    )
    w_gate_up = w_gate_up.reshape(2, D, ff_own)
    out_pairs, kept = [], ()
    running = None
    for slot in range(n_chips):
        sent = None if running is None else seq_perm(running, 1, 0)
        normed_ring = ring_step(normed_ring)
        upstream_ring = ring_step(upstream_ring)
        out_own, out_other, grad_own, grad_other, *kept = feed_forward(
            (normed_ring[slot], normed_swapped[slot]),
            (upstream_ring[slot], upstream_swapped[slot]),
            w_gate_up,
            w_down,
            slot,
            n_chips,
            kept,
        )
        grad_swapped = swap(grad_other)
        if slot + 1 < n_chips:
            normed_swapped = normed_swapped + [swap(after(normed_ring[slot + 1], grad_own))]
        if slot + 2 < n_chips and len(upstream_swapped) < slot + 3:
            upstream_swapped = upstream_swapped + [swap(after(upstream_ring[slot + 2], grad_own))]
        if slot == 0:
            grad_first = (grad_own, grad_swapped)
        elif sent is None:
            running = add(grad_own, grad_swapped)
        else:
            running = add(grad_own, grad_swapped, after(sent, grad_own))
        running, normed_ring, normed_swapped, upstream_ring, upstream_swapped, kept = fence(
            running, normed_ring, normed_swapped, upstream_ring, upstream_swapped, kept
        )
        out_pairs = out_pairs + [(out_own, out_other)]
        if 1 < slot:
            out_pairs[slot - 1] = (out_pairs[slot - 1][0], swap(out_pairs[slot - 1][1]))
        if slot == 2:
            ring_first = add(*out_pairs[1])

    grad_ring = jnp.zeros_like(grad_first[0]) if running is None else seq_perm(running, 1, 0)
    normed_all, ffn_all, hidden_all, gate_grads_all, up_grads_all = kept
    first_split = (
        jnp.concatenate([bit_sides[order[0]] for order in orders]),
        tuple(order[0] for order in orders),
    )
    halves = [
        weight_grad(
            normed_all,
            (gate_grads_all, up_grads_all),
            split=first_split,
            rows=rows_own,
            part=(part, 2),
        )
        for part in range(2)
    ]
    out_running = seq_perm(ring_first, 1, 0)
    out_running = add(after(out_running, *halves[0][0]), *out_pairs[2])
    grad_ring, halves, out_pairs, out_running = fence(grad_ring, halves, out_pairs, out_running)

    got_one = [dp_perm(goes, order[0]) for (_, goes), order in zip(halves[0], orders)]
    out_running = seq_perm(out_running, 1, 0)
    out_pairs[-1] = (out_pairs[-1][0], swap(out_pairs[-1][1]))
    residual_grads, branch_grads, attended_grads, gain_two_grad = norm_back(
        grad_ring, *grad_first, residual, upstream, gain_two, w_out
    )
    query_pre, kv_grad_own, kv_grad_other = attend_back(
        queries,
        key_value_all,
        attended_grads,
        attended,
        logsum,
        query_bases,
        key_bases,
        cosine,
        sine,
    )
    got_one, kv_grad_own, kv_grad_other, query_pre, branch_grads, out_running, out_pairs = fence(
        got_one, kv_grad_own, kv_grad_other, query_pre, branch_grads, out_running, out_pairs
    )
    own_parts = kv_grad_own.reshape(n_chips, tok_rows, 2 * KVW)
    other_parts = swap(kv_grad_other).reshape(n_chips, tok_rows, 2 * KVW)
    kv_sum = add_turn(own_parts, other_parts, jnp.zeros_like(chip_side))
    kv_sum, halves, query_pre, branch_grads, kept = fence(
        kv_sum, halves, query_pre, branch_grads, kept
    )

    def next_split(kept_parts, got, done_bits, left_bits):
        rest = [bit for bit in bits[::-1] if bit not in done_bits]
        bit = left_bits[0]
        lead = sum(part.shape[0] for part in kept_parts) // 2 ** len(rest)
        return add_halve(kept_parts, got, bit_sides[bit], lead * 2 ** rest.index(bit))

    kv_got = [seq_perm(kv_sum[t], n_chips - t, 0) for t in range(1, n_chips)]
    got_two = [dp_perm(goes, order[0]) for (_, goes), order in zip(halves[1], orders)]
    by_core = (core_side, (n_dp,))
    (query_split,) = weight_grad(normed_one[None], (query_pre[None],), split=by_core, rows=rows_own)
    (out_split,) = weight_grad(
        attended_low[None], (branch_grads[None],), split=by_core, rows=rows_own
    )
    (down_grad,) = weight_grad(kept[2], (kept[1],))
    out_running = add(out_running, *out_pairs[3])
    kv_got, got_two, query_split, out_split, down_grad, out_running = fence(
        kv_got, got_two, query_split, out_split, down_grad, out_running
    )

    out_running = seq_perm(out_running, 1, 0)
    gate_up_split = [
        next_split([one[0], two[0]], [got, other], order[:1], order[1:])
        for one, two, got, other, order in zip(*halves, got_one, got_two, orders)
    ]
    gate_up_sums = [dp_perm(goes, order[1]) for (_, goes), order in zip(gate_up_split, orders)]
    both = [(split[0], swap(split[1])) for split in (query_split, out_split)]
    key_value_pre, input_grads, gain_one_grad, bias_grad = input_back(
        inputs,
        gain_one,
        w_qkv,
        query_pre,
        cosine,
        sine,
        residual_grads,
        kv_sum[0],
        kv_got,
    )
    down_split = split_columns(
        down_grad.reshape(n_dp, ff_pad, D),
        first_split[0],
        ((0, D // 2), (D // 2, D)),
        tuple(order[0] for order in orders),
    )
    ((kv_stays, kv_goes),) = weight_grad(
        normed_one[None], (key_value_pre[None],), split=by_core, rows=rows_own
    )
    (
        gate_up_split,
        gate_up_sums,
        down_split,
        both,
        input_grads,
        kv_stays,
        kv_goes,
        out_running,
        small_parts,
    ) = fence(
        gate_up_split,
        gate_up_sums,
        down_split,
        both,
        input_grads,
        kv_stays,
        kv_goes,
        out_running,
        (gain_one_grad, gain_two_grad, bias_grad),
    )

    down_got = [dp_perm(goes, order[0]) for (_, goes), order in zip(down_split, orders)]
    ready = []
    for split, got, order in zip(gate_up_split, gate_up_sums, orders):
        kept_part = split[0]
        for i in range(2, len(order)):
            kept_part, goes = next_split([kept_part], [got], order[:i], order[i:])
            got = dp_perm(goes, order[i])
        ready.append(add_halve([kept_part], [got], core_side, n_chips))
    to_send = turn_pairs(
        [kept_part for kept_part, _ in ready],
        [swap(sent) for _, sent in ready],
        chip_side,
        n_chips,
    )
    small_grad = jnp.concatenate(small_parts, axis=1).astype(bf16)
    small_grad = jnp.pad(
        small_grad.reshape(n_all, small_own), ((0, 0), (0, rows_own * HD - small_own))
    ).reshape(n_chips, 2, n_dp, rows_own, HD)
    kv_stays = jnp.concatenate(
        [pick(small_grad, core_at, 1).reshape(-1, rows_own, HD), kv_stays], axis=2
    )
    kv_goes = jnp.concatenate(
        [pick(small_grad, 1 - core_at, 1).reshape(-1, rows_own, HD), kv_goes], axis=2
    )
    kv_got = swap(kv_goes)
    rest_cuts = (((0, D), (0, 3 * HD)), ((0, D), (3 * HD, HD + 2 * KVW)))
    rest = [
        add_halve_columns(
            [kept_part, kv_stays],
            [got, kv_got],
            cuts,
            bit_sides[order[0]],
            n_chips * n_dp // (2 * order[0]),
        )
        for (kept_part, got), cuts, order in zip(both, rest_cuts, orders)
    ]
    to_send, rest, out_running, down_got = fence(to_send, rest, out_running, down_got)

    gate_up_owned = {0: to_send[0]}
    rest_got = [dp_perm(goes, order[0]) for (_, goes), order in zip(rest, orders)]
    for shift in groups[0] + groups[2]:
        gate_up_owned[shift] = exchange(shift)
    if len(bits) > 1:
        down_split = [
            next_split([kept_part], [got], order[:1], order[1:])
            for (kept_part, _), got, order in zip(down_split, down_got, orders)
        ]
    out_pairs[0] = (out_pairs[0][0], swap(out_pairs[0][1]))
    gate_up_owned, rest_got, down_split, out_pairs = fence(
        gate_up_owned, rest_got, down_split, out_pairs
    )

    for shift in groups[1]:
        gate_up_owned[shift] = exchange(shift)
    rest_send = []
    for (kept_part, _), got, order in zip(rest, rest_got, orders):
        for i in range(1, len(order)):
            kept_part, goes = next_split([kept_part], [got], order[:i], order[i:])
            got = dp_perm(goes, order[i])
        rest_send.append(add_turn(kept_part, got, chip_side))
    gate_up_owned, rest_send, down_split = fence(gate_up_owned, rest_send, down_split)

    rest_send = [
        jnp.concatenate([parts[t] for parts in rest_send], axis=1) for t in range(n_chips)
    ]
    rest_ring = [rest_send[0]] + [seq_perm(rest_send[shift], shift, 0) for shift in shifts]
    down_owned = []
    for (kept_part, goes), got, order in zip(down_split, down_got, orders):
        for i in range(1, len(order)):
            if i > 1:
                kept_part, goes = next_split([kept_part], [got], order[:i], order[i:])
            got = dp_perm(goes, order[i])
        down_owned.append(kept_part[0, :ff_dev].astype(f32) + got[0, :ff_dev].astype(f32))
    down_owned = jnp.concatenate(down_owned, axis=1)
    down_new = adamw_update(down_master, down_first, down_second, down_owned, 0.026, 0.1)
    rest_ring, down_new = fence(rest_ring, down_new)
    total = sum(piece.astype(f32) for piece in rest_ring)
    for t in range(4, n_chips):
        out_running = seq_perm(add(out_running, *out_pairs[t]), 1, 0)
    outputs = residual + out_pairs[0][0].astype(f32) + out_pairs[0][1].astype(f32)
    outputs = outputs + out_running.astype(f32)
    outputs = outputs.astype(bf16)
    gate_up_new = adamw_hidden(
        gate_up_master,
        gate_up_first,
        gate_up_second,
        [gate_up_owned[t] for t in range(n_chips)],
        ring_order,
        n_dp,
        ff_pad,
        0.064,
        0.1,
    )
    wide = D + 3 * HD
    query_owned, out_owned = total[:, :D], total[:, wide : wide + D]
    small_owned = total[:, D : D + HD]
    qkv_owned = jnp.concatenate(
        [query_owned, total[:, D + HD : wide], total[:, wide + D :]], axis=1
    )
    small_owned = small_owned.reshape(-1)[:small_own]

    qkv_new = adamw_update(qkv_master, qkv_first, qkv_second, qkv_owned, 0.09, 0.1)
    out_new = adamw_update(out_master, out_first, out_second, out_owned, 0.18, 0.1)
    small_new = adamw_update(small_master, small_first, small_second, small_owned, 0.6, 0.0)
    return (
        outputs[None],
        input_grads[None],
        *qkv_new,
        *out_new,
        *gate_up_new,
        *down_new,
        *small_new,
    )


def solution(mesh):
    in_specs = (
        P("dp", "seq", None),
        P("dp", "seq", None),
        P("dp", None),
        P(("seq", "dp"), None),
        P(("seq", "dp"), None),
        P(("seq", "dp"), None),
        P(("seq", "dp"), None),
        P(("seq", "dp"), None),
        P(("seq", "dp"), None),
        P(None, ("seq", "dp"), None),
        P(None, ("seq", "dp"), None),
        P(None, ("seq", "dp"), None),
        P(("seq", "dp"), None),
        P(("seq", "dp"), None),
        P(("seq", "dp"), None),
        P(("seq", "dp")),
        P(("seq", "dp")),
        P(("seq", "dp")),
    )
    out_specs = (
        P("dp", "seq", None),
        P("dp", "seq", None),
        P(("seq", "dp"), None),
        P(("seq", "dp"), None),
        P(("seq", "dp"), None),
        P(("seq", "dp"), None),
        P(("seq", "dp"), None),
        P(("seq", "dp"), None),
        P(None, ("seq", "dp"), None),
        P(None, ("seq", "dp"), None),
        P(None, ("seq", "dp"), None),
        P(("seq", "dp"), None),
        P(("seq", "dp"), None),
        P(("seq", "dp"), None),
        P(("seq", "dp")),
        P(("seq", "dp")),
        P(("seq", "dp")),
    )
    return jax.shard_map(shards, mesh=mesh, in_specs=in_specs, out_specs=out_specs, check_vma=False)
```

```python
import functools

import jax
import jax.numpy as jnp
from jax import lax
from jax.experimental import pallas as pl
from jax.experimental.pallas import tpu as pltpu
from jax.sharding import PartitionSpec as P

D = 1536
HEADS = 12
KVH = 2
HD = 128
STEP = 10
KVW = KVH * HD
PIECE = 128


norm_eps = 1e-06
rope_base = 1000000.0
beta_one = 0.9
beta_two = 0.95
adam_eps = 1e-08
masked_score = -1e30
log2_e = 1.4426950408889634
bf16 = jnp.bfloat16
f32 = jnp.float32
vmem = pl.BlockSpec(memory_space=pltpu.VMEM)
smem = pl.BlockSpec(memory_space=pltpu.SMEM)
anywhere = pl.BlockSpec(memory_space=pl.ANY)


def shape_of(dims, kind):
    return jax.ShapeDtypeStruct(dims, kind)


def kernel_call(kernel, name, out_shape, operands, megabytes=32, **options):
    return pl.pallas_call(
        kernel,
        name=name,
        out_shape=out_shape,
        compiler_params=pltpu.CompilerParams(vmem_limit_bytes=megabytes << 20),
        cost_estimate=pl.CostEstimate(flops=10**6, bytes_accessed=10**6, transcendentals=0),
        **options,
    )(*operands)


def after(values, *others):
    return lax.optimization_barrier((values,) + others)[0]


def fence(*groups):
    flat, tree = jax.tree.flatten(groups)
    return jax.tree.unflatten(tree, lax.optimization_barrier(tuple(flat)))


def dot(left, right):
    return jnp.dot(left, right, preferred_element_type=f32)


def dot_transposed(left, right):
    return lax.dot_general(left, right, (((1,), (1,)), ((), ())), preferred_element_type=f32)


def rotary_tables(places):
    half_size = HD // 2
    freqs = rope_base ** (-(jnp.arange(half_size).astype(f32) * (2.0 / HD)))
    angles = places.astype(f32)[:, None] * freqs[None, :]
    cosine, sine = jnp.cos(angles), jnp.sin(angles)
    return jnp.concatenate([cosine, cosine], axis=1), jnp.concatenate([-sine, sine], axis=1)


def rms_scale(values):
    return lax.rsqrt(jnp.mean(values * values, axis=-1, keepdims=True) + norm_eps)


def swap_halves(values):
    return pltpu.roll(values, HD // 2, 1)


def head(index):
    return slice(index * HD, (index + 1) * HD)


def project_kv_kernel(tokens, w_qkv, gain, bias, cosine, sine, normed_ref, kv_ref):
    inputs = tokens[...].astype(f32)
    normed = (inputs * rms_scale(inputs) * gain[...]).astype(bf16)
    normed_ref[...] = normed
    rows = dot(normed, w_qkv[...]) + bias[:, D:]
    for j in range(KVH):
        part = rows[:, head(j)]
        kv_ref[:, head(j)] = (part * cosine[...] + swap_halves(part) * sine[...]).astype(bf16)
    kv_ref[:, KVW:] = rows[:, KVW:].astype(bf16)


def project_q_kernel(normed, w_qkv, bias, cosine, sine, query_ref):
    rows = dot(normed[...], w_qkv[...]) + bias[:, :D]
    for j in range(HEADS):
        part = rows[:, head(j)]
        query_ref[:, head(j)] = (part * cosine[...] + swap_halves(part) * sine[...]).astype(bf16)


def project_kv(tokens, w_qkv, gain, bias, cosine, sine):
    rows = tokens.shape[0]
    return kernel_call(
        project_kv_kernel,
        "project_kv",
        (shape_of((rows, D), bf16), shape_of((rows, 2 * KVW), bf16)),
        (tokens, w_qkv, gain, bias, cosine, sine),
        megabytes=58,
        grid=(1,),
        in_specs=[vmem, pl.BlockSpec((D, 2 * KVW), lambda i: (0, D // (2 * KVW)))] + [vmem] * 4,
        out_specs=(vmem, vmem),
    )


def project_q(normed, w_qkv, bias, cosine, sine):
    return kernel_call(
        project_q_kernel,
        "project_q",
        shape_of(normed.shape, bf16),
        (normed, w_qkv, bias, cosine, sine),
        megabytes=58,
        grid=(1,),
        in_specs=[vmem, pl.BlockSpec((D, D), lambda i: (0, 0))] + [vmem] * 3,
        out_specs=vmem,
    )


def mask_keys(values, query_bases, key_bases, first_run, fill):
    later = lax.broadcasted_iota(jnp.int32, (PIECE, PIECE), 0) - lax.broadcasted_iota(
        jnp.int32, (PIECE, PIECE), 1
    )
    keys, queries = values.shape
    rows = []
    for r in range(keys // PIECE):
        down = slice(r * PIECE, (r + 1) * PIECE)
        row = []
        for q in range(queries // PIECE):
            gap = query_bases[q] - key_bases[first_run + r]
            row.append(jnp.where(later <= gap, values[down, q * PIECE : (q + 1) * PIECE], fill))
        rows.append(jnp.concatenate(row, axis=1))
    return jnp.concatenate(rows, axis=0)


def attend_kernel(query_bases, key_bases, q_ref, *refs):
    pieces, (out_ref, lse_ref, kv_ref) = refs[:-3], refs[-3:]
    rows = q_ref.shape[0]
    for i, piece in enumerate(pieces):
        kv_ref[i * rows : (i + 1) * rows, :] = piece[...]
    groups = HEADS // KVH
    scale = HD**-0.5 * log2_e
    for kv in range(KVH):
        values = kv_ref[:, head(KVH + kv)].T
        for h in range(kv * groups, (kv + 1) * groups):
            queries = q_ref[:, head(h)]
            scores = []
            for run in range(key_bases.shape[0]):
                keys = kv_ref[run * PIECE : (run + 1) * PIECE, head(kv)]
                part = dot_transposed(keys, queries)
                scores.append(mask_keys(part, query_bases, key_bases, run, masked_score))
            scores = jnp.concatenate(scores, axis=0)
            top = jnp.max(scores, axis=0, keepdims=True)
            weights = jnp.exp2((scores - top) * scale)
            total = jnp.sum(weights, axis=0, keepdims=True)
            mixed = dot(values, weights.astype(bf16))
            out_ref[:, head(h)] = (mixed / total).T
            lse_ref[h : h + 1, :] = top * scale + jnp.log2(total)


def attend(queries, pieces, query_bases, key_bases):
    rows, total = queries.shape[0], key_bases.shape[0] * PIECE
    return kernel_call(
        attend_kernel,
        "attend",
        (
            shape_of((rows, D), f32),
            shape_of((HEADS, rows), f32),
            shape_of((total, 2 * KVW), bf16),
        ),
        (query_bases, key_bases, queries, *pieces),
        in_specs=[smem] * 2 + [vmem] * (1 + len(pieces)),
    )


def out_kernel(tokens, attended, w_out, gain, residual_ref, normed_ref, low_ref):
    low = attended[...].astype(bf16)
    low_ref[...] = low
    residual = tokens[...].astype(f32) + dot(low, w_out[...])
    residual_ref[...] = residual
    normed_ref[...] = (residual * rms_scale(residual) * gain[...]).astype(bf16)


def out_project(tokens, attended, w_out, gain):
    dims = tokens.shape
    return kernel_call(
        out_kernel,
        "out_project",
        (shape_of(dims, f32), shape_of(dims, bf16), shape_of(dims, bf16)),
        (tokens, attended, w_out, gain),
    )


def ffn_kernel(
    normed_own, normed_other, grad_own, grad_other, w_gate_up, w_down, *refs, earlier
):
    refs = refs[earlier:]
    out_refs, grad_refs = refs[:2], refs[2:4]
    normed_ref, ffn_grad_ref, hidden_ref, gate_ref, up_ref = refs[4:]
    rows = normed_own.shape[0]
    for i, (normed_in, grad_in) in enumerate(((normed_own, grad_own), (normed_other, grad_other))):
        to = slice(i * rows, (i + 1) * rows)
        normed, ffn_grad = normed_in[...], grad_in[...]
        normed_ref[0, to, :] = normed
        ffn_grad_ref[0, to, :] = ffn_grad
        gate = dot(normed, w_gate_up[0])
        up = dot(normed, w_gate_up[1])
        sigmoid = 1.0 / (1.0 + jnp.exp(-gate))
        silu = gate * sigmoid
        hidden = (silu * up).astype(bf16)
        hidden_ref[0, to, :] = hidden
        out_refs[i][...] = dot(hidden, w_down[...]).astype(bf16)
        hidden_grad = dot_transposed(ffn_grad, w_down[...])
        gate_grad = (hidden_grad * up * sigmoid * (1.0 + gate * (1.0 - sigmoid))).astype(bf16)
        up_grad = (hidden_grad * silu).astype(bf16)
        gate_ref[0, to, :] = gate_grad
        up_ref[0, to, :] = up_grad
        grad_refs[i][...] = (
            dot_transposed(gate_grad, w_gate_up[0]) + dot_transposed(up_grad, w_gate_up[1])
        ).astype(bf16)


def feed_forward(normed, grads, w_gate_up, w_down, slot, slots, kept):
    rows, width = normed[0].shape
    ff_own = w_down.shape[0]
    token = shape_of((rows, width), bf16)
    widths = (width, width, ff_own, ff_own, ff_own)
    operands = (*normed, *grads, w_gate_up, w_down)
    return kernel_call(
        functools.partial(ffn_kernel, earlier=len(kept)),
        "feed_forward",
        (token,) * 4 + tuple(shape_of((slots, 2 * rows, w), bf16) for w in widths),
        (*operands, *kept),
        grid=(1,),
        in_specs=[vmem] * len(operands) + [anywhere] * len(kept),
        out_specs=(vmem,) * 4
        + tuple(pl.BlockSpec((1, 2 * rows, w), lambda i: (slot, 0, 0)) for w in widths),
        input_output_aliases={len(operands) + i: 4 + i for i in range(len(kept))},
    )


def norm_back_kernel(
    got, own, other, residual_ref, cotangent, gain, w_out, grad_ref, low_ref, back_ref, gain_ref
):
    normed_grad = got[...].astype(f32) + own[...].astype(f32) + other[...].astype(f32)
    residual = residual_ref[...]
    scale = rms_scale(residual)
    unit = residual * scale
    gain_ref[...] = jnp.sum(normed_grad * unit, axis=0, keepdims=True)
    weighted = normed_grad * gain[...]
    grad = cotangent[...].astype(f32) + scale * (
        weighted - unit * jnp.mean(weighted * unit, axis=-1, keepdims=True)
    )
    grad_ref[...] = grad
    low = grad.astype(bf16)
    low_ref[...] = low
    back_ref[...] = dot_transposed(low, w_out[...]).astype(bf16)


def norm_back(got, own, other, residual, cotangent, gain, w_out):
    dims = residual.shape
    return kernel_call(
        norm_back_kernel,
        "norm_back",
        (shape_of(dims, f32), shape_of(dims, bf16), shape_of(dims, bf16), shape_of((1, D), f32)),
        (got, own, other, residual, cotangent, gain, w_out),
    )


def attend_back_kernel(
    query_bases,
    key_bases,
    q_ref,
    kv_ref,
    grad_ref,
    out_ref,
    lse_ref,
    cosine,
    sine,
    q_grad_ref,
    kv_own_ref,
    kv_other_ref,
    q_rows,
    grad_rows,
    deltas,
    q_sums,
):
    rows = q_ref.shape[0]
    groups = HEADS // KVH
    scale = HD**-0.5
    for kv in range(KVH):
        for j in range(groups):
            part = slice(j * rows, (j + 1) * rows)
            columns = head(kv * groups + j)
            q_rows[part, :] = q_ref[:, columns]
            grads = grad_ref[:, columns]
            grad_rows[part, :] = grads
            product = grads.astype(f32) * out_ref[:, columns]
            deltas[:, part] = jnp.sum(product.T, axis=0, keepdims=True)
        q_sums[...] = jnp.zeros_like(q_sums)

        @pl.loop(0, kv_ref.shape[0] // (2 * rows), unroll=2)
        def _(step):
            at = pl.ds(pl.multiple_of(step * (2 * rows), 2 * rows), 2 * rows)
            runs = 2 * rows // PIECE
            keys = kv_ref[at, head(kv)]
            values = kv_ref[at, head(KVH + kv)]
            key_sum = value_sum = None
            for j in range(groups):
                part = slice(j * rows, (j + 1) * rows)
                h = kv * groups + j
                queries, grads = q_rows[part, :], grad_rows[part, :]
                scores = dot_transposed(keys, queries)
                weights = jnp.exp2(scores * (scale * log2_e) - lse_ref[h : h + 1, :])
                weights = mask_keys(weights, query_bases, key_bases, step * runs, 0.0)
                weight_grads = dot_transposed(values, grads)
                score_grads = (weights * (weight_grads - deltas[:, part])).astype(bf16)
                value_part = dot(weights.astype(bf16), grads)
                key_part = dot(score_grads, queries)
                key_sum = key_part if key_sum is None else key_sum + key_part
                value_sum = value_part if value_sum is None else value_sum + value_part
                q_sums[part, :] += lax.dot_general(
                    score_grads, keys, (((0,), (0,)), ((), ())), preferred_element_type=f32
                )
            key_sum = (key_sum * scale).astype(bf16)
            value_sum = value_sum.astype(bf16)
            to = pl.ds(pl.multiple_of(step * rows, rows), rows)
            for ref, mine in ((kv_own_ref, slice(0, rows)), (kv_other_ref, slice(rows, 2 * rows))):
                ref[to, head(kv)] = key_sum[mine, :]
                ref[to, head(KVH + kv)] = value_sum[mine, :]

        for j in range(groups):
            part = q_sums[j * rows : (j + 1) * rows, :] * scale
            q_grad_ref[:, head(kv * groups + j)] = (
                part * cosine[...] - swap_halves(part) * sine[...]
            ).astype(bf16)


def attend_back(queries, key_value, grads, attended, lse, query_bases, key_bases, cosine, sine):
    rows, total = queries.shape[0], key_value.shape[0]
    groups = HEADS // KVH
    return kernel_call(
        attend_back_kernel,
        "attend_back",
        (
            shape_of((rows, D), bf16),
            shape_of((total // 2, 2 * KVW), bf16),
            shape_of((total // 2, 2 * KVW), bf16),
        ),
        (query_bases, key_bases, queries, key_value, grads, attended, lse, cosine, sine),
        in_specs=[smem] * 2 + [vmem] * 7,
        scratch_shapes=[
            pltpu.VMEM((groups * rows, HD), bf16),
            pltpu.VMEM((groups * rows, HD), bf16),
            pltpu.VMEM((1, groups * rows), f32),
            pltpu.VMEM((groups * rows, HD), f32),
        ],
    )


def input_kernel(
    tokens, gain, w_qkv, query_grad, cosine, sine, residual_grad, own, *refs
):
    got, (kv_ref, input_ref, gain_ref, bias_ref) = refs[:-4], refs[-4:]
    rows = own[...].astype(f32)
    for piece in got:
        rows = rows + piece[...].astype(f32)
    for j in range(KVH):
        part = rows[:, head(j)]
        kv_ref[:, head(j)] = (part * cosine[...] - swap_halves(part) * sine[...]).astype(bf16)
    kv_ref[:, KVW:] = rows[:, KVW:].astype(bf16)
    kv_grad = kv_ref[...]
    q_grad = query_grad[...]
    bias_ref[:, :D] = jnp.sum(q_grad.astype(f32), axis=0, keepdims=True)
    bias_ref[:, D:] = jnp.sum(kv_grad.astype(f32), axis=0, keepdims=True)
    normed_grad = dot_transposed(q_grad, w_qkv[:, :D]) + dot_transposed(kv_grad, w_qkv[:, D:])
    inputs = tokens[...].astype(f32)
    scale = rms_scale(inputs)
    unit = inputs * scale
    gain_ref[...] = jnp.sum(normed_grad * unit, axis=0, keepdims=True)
    weighted = normed_grad * gain[...]
    input_ref[...] = residual_grad[...] + scale * (
        weighted - unit * jnp.mean(weighted * unit, axis=-1, keepdims=True)
    )


def input_back(tokens, gain, w_qkv, query_grad, cosine, sine, residual_grad, own, got):
    rows = tokens.shape[0]
    return kernel_call(
        input_kernel,
        "input_back",
        (
            shape_of((rows, 2 * KVW), bf16),
            shape_of((rows, D), f32),
            shape_of((1, D), f32),
            shape_of((1, D + 2 * KVW), f32),
        ),
        (tokens, gain, w_qkv, query_grad, cosine, sine, residual_grad, own, *got),
        megabytes=58,
    )


def split_kernel(sides, values, *outs, cuts, bits):
    blocks = values.shape[0]
    for i, ((lo, hi), bit) in enumerate(zip(cuts, bits)):
        for out, side in ((outs[2 * i], sides[i]), (outs[2 * i + 1], 1 - sides[i])):
            for o in range(blocks // (2 * bit)):
                for j in range(bit):
                    out[o * bit + j] = values[(2 * o + side) * bit + j, :, lo:hi]


def split_columns(values, sides, cuts, bits):
    blocks, rows, _ = values.shape
    outs = kernel_call(
        functools.partial(split_kernel, cuts=cuts, bits=bits),
        "split_columns",
        tuple(shape_of((blocks // 2, rows, hi - lo), bf16) for lo, hi in cuts for _ in range(2)),
        (sides, values),
        in_specs=[smem, vmem],
    )
    return [(outs[2 * i], outs[2 * i + 1]) for i in range(len(cuts))]


def weight_grad_kernel(sides, left, *refs, count, inners, based):
    rights, refs = refs[:count], refs[count:]
    bases, outs = refs[: count * based], refs[count * based :]
    turned = left[...].reshape(-1, left.shape[-1]).T
    for i, right in enumerate(rights):
        result = dot(turned, right[...].reshape(-1, right.shape[-1]))
        if based:
            result = result + bases[i][...]
        if not inners:
            outs[i][...] = result.astype(outs[i].dtype)
            continue
        stays, goes = outs[2 * i], outs[2 * i + 1]
        rows = stays.shape[2]
        result = result.astype(bf16)
        for side, refs_of in ((0, (stays, goes)), (1, (goes, stays))):

            @pl.when(sides[i] == side)
            def _():
                for o in range(stays.shape[0]):
                    for bit in range(2):
                        for j in range(inners[i]):
                            block = (o * 2 + bit) * inners[i] + j
                            refs_of[bit][o, j] = result[block * rows : (block + 1) * rows]


def weight_grad(
    left, rights, slots=(0, 1), bases=(), split=None, rows=0, part=(0, 1), kind=bf16
):
    n_slots, tokens, m = left.shape
    n_slots = n_slots // slots[1]
    m = m // part[1]
    block = 3 * HD if m % (3 * HD) == 0 else HD
    steps = m // block
    first = part[0] * steps
    whole = pl.Buffered(buffer_count=1)
    sides, inners = split if split else (jnp.zeros((1,), jnp.int32), ())
    out_shape, out_specs = [], []
    for i, right in enumerate(rights):
        n = right.shape[-1]
        if not inners:
            out_shape.append(shape_of((m, n), kind))
            out_specs.append(pl.BlockSpec((block, n), lambda i: (i, 0)))
            continue
        outer = block // (2 * inners[i] * rows)
        for _ in range(2):
            out_shape.append(shape_of((steps * outer, inners[i], rows, n), bf16))
            out_specs.append(pl.BlockSpec((outer, inners[i], rows, n), lambda i: (i, 0, 0, 0)))
    outs = kernel_call(
        functools.partial(
            weight_grad_kernel, count=len(rights), inners=inners, based=int(bool(bases))
        ),
        "weight_grad",
        tuple(out_shape),
        (sides, left, *rights, *bases),
        megabytes=32,
        grid=(steps,),
        in_specs=[
            smem,
            pl.BlockSpec((n_slots, tokens, block), lambda i: (slots[0], 0, i + first)),
        ]
        + [
            vmem
            if slots == (0, 1)
            else pl.BlockSpec(
                (n_slots, tokens, right.shape[-1]),
                lambda i: (slots[0], 0, 0),
                pipeline_mode=whole,
            )
            for right in rights
        ]
        + [pl.BlockSpec((block, base.shape[1]), lambda i: (i + first, 0)) for base in bases],
        out_specs=tuple(out_specs),
    )
    if not inners:
        return outs
    outs = [out.reshape((-1,) + out.shape[2:]) for out in outs]
    return [(outs[2 * i], outs[2 * i + 1]) for i in range(len(rights))]


def stack_kernel(*refs, cuts):
    pieces, outs = refs[: -len(cuts)], refs[-len(cuts) :]
    for i, piece in enumerate(pieces):
        for out, (lo, hi) in zip(outs, cuts):
            out[i] = piece[:, lo:hi]


def stack_columns(pieces, cuts):
    return kernel_call(
        functools.partial(stack_kernel, cuts=cuts),
        "stack_columns",
        tuple(shape_of((len(pieces), pieces[0].shape[0], hi - lo), bf16) for lo, hi in cuts),
        tuple(pieces),
    )


def cut_kernel(core, values, kept_ref, sent_ref, *, n_dp, own, padded):
    kept_ref[...] = jnp.zeros_like(kept_ref)
    sent_ref[...] = jnp.zeros_like(sent_ref)
    for side, refs in ((0, (kept_ref, sent_ref)), (1, (sent_ref, kept_ref))):

        @pl.when(core[0] == side)
        def _():
            for s in range(2 * kept_ref.shape[0]):
                for d in range(n_dp):
                    start = (s * n_dp + d) * own
                    refs[s % 2][s // 2, 0, :, d * padded : d * padded + own] = values[
                        0, :, start : start + own
                    ].astype(bf16)


def cut_hidden(values, core, n_chips, n_dp, padded):
    two, rows, ff = values.shape
    own = ff // (2 * n_chips * n_dp)
    dims = (n_chips, two, rows, n_dp * padded)
    return kernel_call(
        functools.partial(cut_kernel, n_dp=n_dp, own=own, padded=padded),
        "cut_hidden",
        (shape_of(dims, bf16),) * 2,
        (core, values),
        grid=(two,),
        in_specs=[smem, pl.BlockSpec((1, rows, ff), lambda g: (g, 0, 0))],
        out_specs=(pl.BlockSpec((n_chips, 1, rows, n_dp * padded), lambda g: (0, g, 0, 0)),) * 2,
    )


def turn_kernel(chip, *refs, n_chips):
    ins, outs = refs[: len(refs) - n_chips], refs[len(refs) - n_chips :]
    per_side = len(ins) // 2
    for t, out in enumerate(outs):
        at = lax.rem(chip[0] + t, n_chips)
        for side in range(2):
            if per_side == 1:
                out[side] = ins[side][at]
            else:
                for g in range(2):
                    out[side, g] = ins[2 * side + g][at]


def turn_pairs(kept, got, chip, n_chips):
    rows, width = kept[0].shape[-2:]
    return kernel_call(
        functools.partial(turn_kernel, n_chips=n_chips),
        "turn_pairs",
        (shape_of((2, 2, rows, width), bf16),) * n_chips,
        (chip, *kept, *got),
        in_specs=[smem] + [vmem] * (len(kept) + len(got)),
    )


def add_kernel(*refs):
    *ins, out = refs
    total = ins[0][...].astype(f32)
    for ref in ins[1:]:
        total = total + ref[...].astype(f32)
    out[...] = total.astype(bf16)


def add(*arrays):
    return kernel_call(add_kernel, "add", shape_of(arrays[0].shape, bf16), arrays)


def add_turn_kernel(chip, kept, got, *outs):
    n = kept.shape[0]
    for t, out in enumerate(outs):
        at = lax.rem(chip[0] + t, n)
        out[...] = (kept[at].astype(f32) + got[at].astype(f32)).astype(bf16)


def add_turn(kept, got, chip):
    n = kept.shape[0]
    return kernel_call(
        add_turn_kernel,
        "add_turn",
        (shape_of(kept.shape[1:], bf16),) * n,
        (chip, kept, got),
        in_specs=[smem, vmem, vmem],
    )


def add_halve_kernel(mine, *refs):
    parts, (stays, goes) = refs[:-2], refs[-2:]
    count = len(parts) // 2
    at = 0
    for kept, got in zip(parts[:count], parts[count:]):
        for o in range(kept.shape[0]):
            for out, side in ((stays, mine[0]), (goes, 1 - mine[0])):
                out[at] = (kept[o, side].astype(f32) + got[o, side].astype(f32)).astype(bf16)
            at += 1


def add_halve(kept, got, mine, outer):
    rows, width = kept[0].shape[1:]
    blocks = sum(part.shape[0] for part in kept)
    inner = blocks // (2 * outer)
    half = shape_of((outer, inner, rows, width), bf16)
    stays, goes = kernel_call(
        add_halve_kernel,
        "add_halve",
        (half, half),
        (mine, *[part.reshape(-1, 2, inner, rows, width) for part in (*kept, *got)]),
        in_specs=[smem] + [vmem] * (len(kept) + len(got)),
        megabytes=40,
    )
    return stays.reshape(-1, rows, width), goes.reshape(-1, rows, width)


def add_halve_columns_kernel(mine, *refs, cuts):
    parts, (stays, goes) = refs[:-2], refs[-2:]
    count = len(parts) // 2
    lo = 0
    for kept, got, (first, last) in zip(parts[:count], parts[count:], cuts):
        hi = lo + last - first
        for o in range(kept.shape[0]):
            for out, side in ((stays, mine[0]), (goes, 1 - mine[0])):
                total = kept[o, side, :, :, first:last].astype(f32) + got[
                    o, side, :, :, first:last
                ].astype(f32)
                out[o, :, :, lo:hi] = total.astype(bf16)
        lo = hi


def add_halve_columns(kept, got, cuts, mine, outer):
    blocks, rows, _ = kept[0].shape
    inner = blocks // (2 * outer)
    width = sum(last - first for first, last in cuts)
    half = shape_of((outer, inner, rows, width), bf16)
    stays, goes = kernel_call(
        functools.partial(add_halve_columns_kernel, cuts=cuts),
        "add_halve",
        (half, half),
        (mine, *[part.reshape(outer, 2, inner, rows, -1) for part in (*kept, *got)]),
        in_specs=[smem] + [vmem] * (len(kept) + len(got)),
        megabytes=44,
    )
    return stays.reshape(-1, rows, width), goes.reshape(-1, rows, width)


def adamw_update(master, moment_one, moment_two, gradient, step_rate, decay_weight):
    first_new = beta_one * moment_one + (1.0 - beta_one) * gradient
    second_new = beta_two * moment_two + (1.0 - beta_two) * gradient * gradient
    first_hat = first_new / (1.0 - beta_one**STEP)
    second_hat = second_new / (1.0 - beta_two**STEP)
    master_new = master - step_rate * (
        first_hat / (jnp.sqrt(second_hat) + adam_eps) + decay_weight * master
    )
    return (first_new, second_new, master_new)


def adamw_kernel(where, master, first, second, *refs, n_dp, own, padded, rate, decay):
    pieces, (first_ref, second_ref, master_ref, slots, joined) = refs[:-5], refs[-5:]
    for t, piece in enumerate(pieces):
        for o in range(2):
            slots[where[2 * t + o]] = piece[o, 0]
    for s in range(slots.shape[0]):
        for d in range(n_dp):
            start = (s * n_dp + d) * own
            joined[:, start : start + own] = slots[
                s, :, d * padded : d * padded + own
            ].astype(f32)
    first_ref[0], second_ref[0], master_ref[0] = adamw_update(
        master[0], first[0], second[0], joined[...], rate, decay
    )


def adamw_hidden(master, first, second, pieces, where, n_dp, padded, rate, decay):
    two, rows, ff = master.shape
    n_seq = 2 * len(pieces)
    own = ff // (n_seq * n_dp)
    block = pl.BlockSpec((1, rows, ff), lambda g: (g, 0, 0))
    part = pl.BlockSpec((2, 1, rows, n_dp * padded), lambda g: (0, g, 0, 0))
    return kernel_call(
        functools.partial(
            adamw_kernel, n_dp=n_dp, own=own, padded=padded, rate=rate, decay=decay
        ),
        "adamw_hidden",
        (shape_of(master.shape, f32),) * 3,
        (where, master, first, second, *pieces),
        megabytes=44,
        grid=(two,),
        in_specs=[smem] + [block] * 3 + [part] * len(pieces),
        out_specs=(block,) * 3,
        scratch_shapes=[
            pltpu.VMEM((n_seq, rows, n_dp * padded), bf16),
            pltpu.VMEM((rows, ff), f32),
        ],
    )


def assemble_kernel(where, *refs, splits, counts):
    ins, outs, sems = refs[: len(counts)], refs[len(counts) : -1], refs[-1]
    copies = []
    entry = 0
    for ref, (column, count) in zip(ins, counts):
        for i in range(count):
            for out, start, width in splits[column]:
                copies.append(
                    pltpu.make_async_copy(
                        ref.at[i, :, pl.ds(start, width)],
                        outs[out[0]].at[where[entry], :, pl.ds(out[1], width)],
                        sems.at[len(copies)],
                    )
                )
            entry += 1
    for copy in copies:
        copy.start()
    for copy in copies:
        copy.wait()


def assemble(pieces, where, splits, out_widths):
    counts = [(column, array.shape[0]) for array, column in pieces]
    rows = pieces[0][0].shape[1]
    blocks = sum(count for column, count in counts if column == 0)
    n_copies = sum(count * len(splits[column]) for column, count in counts)
    return kernel_call(
        functools.partial(assemble_kernel, splits=splits, counts=counts),
        "assemble",
        tuple(shape_of((blocks, rows, w), bf16) for w in out_widths),
        (where.astype(jnp.int32), *[array for array, _ in pieces]),
        in_specs=[smem] + [anywhere] * len(pieces),
        out_specs=(vmem,) * len(out_widths),
        scratch_shapes=[pltpu.SemaphoreType.DMA((n_copies,))],
    )


def seq_perm(values, chips, flip):
    count = lax.axis_size("seq")
    return lax.ppermute(
        values, "seq", [(i, ((i + 2 * chips) % count) ^ flip) for i in range(count)]
    )


def dp_perm(values, bit):
    return lax.ppermute(values, "dp", [(i, i ^ bit) for i in range(lax.axis_size("dp"))])


def dp_bits():
    return [1 << i for i in range(lax.axis_size("dp").bit_length() - 1)]


def pick(values, index, axis):
    return lax.dynamic_index_in_dim(values, index, axis, keepdims=False)


def places_of():
    n_chips = lax.axis_size("seq") // 2
    seq_at = lax.axis_index("seq")
    return n_chips, seq_at // 2, seq_at % 2, lax.axis_size("dp"), lax.axis_index("dp")


def swap(values):
    return seq_perm(values, 0, 1)


def sent_pieces(values):
    return [values] + [seq_perm(values, t, 0) for t in range(1, lax.axis_size("seq") // 2)]


def shards(
    tokens,
    cotangent,
    positions,
    qkv_master,
    qkv_first,
    qkv_second,
    out_master,
    out_first,
    out_second,
    gate_up_master,
    gate_up_first,
    gate_up_second,
    down_master,
    down_first,
    down_second,
    small_master,
    small_first,
    small_second,
):
    n_chips, chip_at, core_at, n_dp, dp_at = places_of()
    n_seq = 2 * n_chips
    n_all = n_seq * n_dp
    bits = dp_bits()
    rows_own, qkv_width = qkv_master.shape
    half = qkv_width // 2
    small_own = small_master.shape[0]
    ff_dev = down_master.shape[0]
    ff_pad = -(-ff_dev // 16) * 16
    ff_own = n_dp * ff_pad
    inputs = tokens[0]
    upstream = cotangent[0]
    tok_rows = inputs.shape[0]
    seq_length = positions.shape[1]
    shifts = list(range(1, n_chips))

    ring_chips = [(chip_at - t) % n_chips for t in range(n_chips)]
    ring_order = jnp.stack(
        [chip * 2 + (core_at ^ flip) for chip in ring_chips for flip in range(2)]
    ).astype(jnp.int32)
    bases = positions[0, ::PIECE].reshape(n_seq, tok_rows // PIECE)
    key_bases = jnp.take(bases, ring_order, axis=0)
    query_bases = key_bases[0]
    key_bases = key_bases.reshape(-1)
    own_places = lax.dynamic_slice_in_dim(
        positions[0], (chip_at * 2 + core_at) * tok_rows, tok_rows, 0
    )
    cosine, sine = rotary_tables(own_places)

    small_block = jnp.pad(
        small_master.astype(bf16), (0, rows_own * HD - small_own)
    ).reshape(rows_own, HD)
    packed = jnp.concatenate([small_block, qkv_master.astype(bf16)], axis=1)
    qkv_ring = sent_pieces(packed)
    core_side = core_at.reshape(1).astype(jnp.int32)
    chip_side = chip_at.reshape(1).astype(jnp.int32)
    bit_sides = {bit: ((dp_at // bit) % 2).reshape(1).astype(jnp.int32) for bit in bits}
    cut_kept, cut_sent = cut_hidden(gate_up_master, core_side, n_chips, n_dp, ff_pad)
    to_send = turn_pairs([cut_kept], [swap(cut_sent)], chip_side, n_chips)
    qkv_ring, to_send, cosine, sine = fence(qkv_ring, to_send, cosine, sine)

    def exchange(shift):
        return seq_perm(to_send[shift], shift, 0)

    w_out = lax.all_gather(
        after(out_master.astype(bf16), *to_send), ("seq", "dp"), axis=0, tiled=True
    )

    columns = ((0, HD + half), (HD + half, HD + qkv_width))
    orders = (bits, bits[::-1])
    held = list(stack_columns(qkv_ring, columns))
    flips = [[0], [0]]
    gate_up_pieces = {0: to_send[0]}
    groups = [shifts[:1], shifts[-1:], shifts[1:-1]] if n_chips > 2 else [shifts, [], []]
    for stage in range(len(bits)):
        got = [dp_perm(h, order[stage]) for h, order in zip(held, orders)]
        if stage == len(bits) - 1:
            swapped = [swap(h) for h in held]
        for shift in groups[min(stage, 1)] if stage < 2 else []:
            gate_up_pieces[shift] = exchange(shift)
        got, held, gate_up_pieces = fence(got, held, gate_up_pieces)
        flips = [f + [k ^ order[stage] for k in f] for f, order in zip(flips, orders)]
        if stage < len(bits) - 1:
            held = [jnp.concatenate([h, g], axis=0) for h, g in zip(held, got)]
    (swapped,) = fence(swapped)
    for shift in groups[2]:
        gate_up_pieces[shift] = exchange(shift)
    down_share = jnp.pad(down_master.astype(bf16), ((0, ff_pad - ff_dev), (0, 0)))
    w_down = lax.all_gather(after(down_share, *got), "dp", axis=0, tiled=True)
    got_swapped = [swap(g) for g in got]
    pieces, where = [], []
    for column in range(2):
        for flip, part, ks in (
            (0, held[column], flips[column][: n_dp // 2]),
            (0, got[column], flips[column][n_dp // 2 :]),
            (1, swapped[column], flips[column][: n_dp // 2]),
            (1, got_swapped[column], flips[column][n_dp // 2 :]),
        ):
            pieces.append((part, column))
            where += [
                (chip * 2 + (core_at ^ flip)) * n_dp + (dp_at ^ k) for k in ks for chip in ring_chips
            ]
    w_qkv, small_blocks = assemble(
        pieces,
        jnp.stack(where),
        ((((1, 0), 0, HD), ((0, 0), HD, half)), (((0, half), 0, half),)),
        (qkv_width, HD),
    )
    w_qkv = w_qkv.reshape(D, qkv_width)
    small_params = small_blocks.reshape(n_all, rows_own * HD)[:, :small_own].reshape(1, -1)
    small_params = small_params.astype(f32)
    gain_one = small_params[:, :D]
    gain_two = small_params[:, D : 2 * D]
    qkv_bias = small_params[:, 2 * D :]
    normed_one, key_value = project_kv(inputs, w_qkv, gain_one, qkv_bias, cosine, sine)
    for shift in groups[2]:
        gate_up_pieces[shift] = after(gate_up_pieces[shift], key_value)
    gate_up_held = [
        jnp.concatenate([gate_up_pieces[t] for t in ts], axis=0)
        for ts in (range(n_chips // 2), range(n_chips // 2, n_chips))
    ]
    normed_one, key_value, gate_up_held = fence(normed_one, key_value, gate_up_held)

    kv_ring = sent_pieces(key_value)
    gate_up_parts = [
        [held, dp_perm(held, order[0])] for held, order in zip(gate_up_held, orders)
    ]
    gate_up_flips = [[0, order[0]] for order in orders]
    queries = project_q(normed_one, w_qkv, qkv_bias, cosine, sine)
    kv_swapped = [swap(kv_ring[0])] + [swap(after(piece, queries)) for piece in kv_ring[1:]]
    kv_ring, kv_swapped, gate_up_parts, queries, upstream = fence(
        kv_ring, kv_swapped, gate_up_parts, queries, upstream
    )

    def cross(start, stop, stage):
        for parts, flips_of, order in zip(gate_up_parts, gate_up_flips, orders):
            parts += [dp_perm(piece, order[stage]) for piece in parts[start:stop]]
            flips_of += [k ^ order[stage] for k in flips_of[start:stop]]

    upstream_ring = [upstream, seq_perm(upstream, 1, 0)]
    cross(0, 1 if len(bits) == 2 else 2, 1)
    attended, logsum, key_value_all = attend(
        queries, [piece for pair in zip(kv_ring, kv_swapped) for piece in pair], query_bases, key_bases
    )
    gate_up_parts, upstream_ring, attended, logsum, key_value_all = fence(
        gate_up_parts, upstream_ring, attended, logsum, key_value_all
    )

    def ring_step(pieces):
        return pieces + [seq_perm(pieces[-1], 1, 0)] if len(pieces) < n_chips else pieces

    upstream_ring = ring_step(upstream_ring)
    if len(bits) == 2:
        cross(1, 2, 1)
    else:
        cross(0, 4, 2)
    upstream_swapped = [swap(piece) for piece in upstream_ring[:2]]
    residual, normed_two, attended_low = out_project(inputs, attended, w_out, gain_two)
    normed_ring, normed_swapped = [normed_two], [swap(normed_two)]
    gate_up_parts, upstream_ring, upstream_swapped, normed_ring, normed_swapped, residual = fence(
        gate_up_parts, upstream_ring, upstream_swapped, normed_ring, normed_swapped, residual
    )

    pieces, where = [], []
    for column, (parts, flips_of) in enumerate(zip(gate_up_parts, gate_up_flips)):
        slots = ring_order[:n_chips] if column == 0 else ring_order[n_chips:]
        for part, k in zip(parts, flips_of):
            pieces.append((part.reshape(-1, rows_own, ff_own), 0))
            block = slots * n_dp + (dp_at ^ k)
            where.append(jnp.stack([block, n_all + block], axis=1).reshape(-1))
    (w_gate_up,) = assemble(
        pieces, jnp.concatenate(where), ((((0, 0), 0, ff_own),),), (ff_own,)
    )
    w_gate_up = w_gate_up.reshape(2, D, ff_own)
    out_pairs, kept = [], ()
    running = None
    for slot in range(n_chips):
        sent = None if running is None else seq_perm(running, 1, 0)
        normed_ring = ring_step(normed_ring)
        upstream_ring = ring_step(upstream_ring)
        out_own, out_other, grad_own, grad_other, *kept = feed_forward(
            (normed_ring[slot], normed_swapped[slot]),
            (upstream_ring[slot], upstream_swapped[slot]),
            w_gate_up,
            w_down,
            slot,
            n_chips,
            kept,
        )
        grad_swapped = swap(grad_other)
        if slot + 1 < n_chips:
            normed_swapped = normed_swapped + [swap(after(normed_ring[slot + 1], grad_own))]
        if slot + 2 < n_chips and len(upstream_swapped) < slot + 3:
            upstream_swapped = upstream_swapped + [swap(after(upstream_ring[slot + 2], grad_own))]
        if slot == 0:
            grad_first = (grad_own, grad_swapped)
        elif sent is None:
            running = add(grad_own, grad_swapped)
        else:
            running = add(grad_own, grad_swapped, after(sent, grad_own))
        running, normed_ring, normed_swapped, upstream_ring, upstream_swapped, kept = fence(
            running, normed_ring, normed_swapped, upstream_ring, upstream_swapped, kept
        )
        out_pairs = out_pairs + [(out_own, out_other)]
        if 1 < slot:
            out_pairs[slot - 1] = (out_pairs[slot - 1][0], swap(out_pairs[slot - 1][1]))
        if slot == 2:
            ring_first = add(*out_pairs[1])

    grad_ring = jnp.zeros_like(grad_first[0]) if running is None else seq_perm(running, 1, 0)
    normed_all, ffn_all, hidden_all, gate_grads_all, up_grads_all = kept
    first_split = (
        jnp.concatenate([bit_sides[order[0]] for order in orders]),
        tuple(order[0] for order in orders),
    )
    halves = [
        weight_grad(
            normed_all,
            (gate_grads_all, up_grads_all),
            split=first_split,
            rows=rows_own,
            part=(part, 2),
        )
        for part in range(2)
    ]
    out_running = seq_perm(ring_first, 1, 0)
    out_running = add(after(out_running, *halves[0][0]), *out_pairs[2])
    grad_ring, halves, out_pairs, out_running = fence(grad_ring, halves, out_pairs, out_running)

    got_one = [dp_perm(goes, order[0]) for (_, goes), order in zip(halves[0], orders)]
    out_running = seq_perm(out_running, 1, 0)
    out_pairs[-1] = (out_pairs[-1][0], swap(out_pairs[-1][1]))
    residual_grads, branch_grads, attended_grads, gain_two_grad = norm_back(
        grad_ring, *grad_first, residual, upstream, gain_two, w_out
    )
    query_pre, kv_grad_own, kv_grad_other = attend_back(
        queries,
        key_value_all,
        attended_grads,
        attended,
        logsum,
        query_bases,
        key_bases,
        cosine,
        sine,
    )
    got_one, kv_grad_own, kv_grad_other, query_pre, branch_grads, out_running, out_pairs = fence(
        got_one, kv_grad_own, kv_grad_other, query_pre, branch_grads, out_running, out_pairs
    )
    own_parts = kv_grad_own.reshape(n_chips, tok_rows, 2 * KVW)
    other_parts = swap(kv_grad_other).reshape(n_chips, tok_rows, 2 * KVW)
    kv_sum = add_turn(own_parts, other_parts, jnp.zeros_like(chip_side))
    kv_sum, halves, query_pre, branch_grads, kept = fence(
        kv_sum, halves, query_pre, branch_grads, kept
    )

    def next_split(kept_parts, got, done_bits, left_bits):
        rest = [bit for bit in bits[::-1] if bit not in done_bits]
        bit = left_bits[0]
        lead = sum(part.shape[0] for part in kept_parts) // 2 ** len(rest)
        return add_halve(kept_parts, got, bit_sides[bit], lead * 2 ** rest.index(bit))

    kv_got = [seq_perm(kv_sum[t], n_chips - t, 0) for t in range(1, n_chips)]
    got_two = [dp_perm(goes, order[0]) for (_, goes), order in zip(halves[1], orders)]
    by_core = (core_side, (n_dp,))
    (query_split,) = weight_grad(normed_one[None], (query_pre[None],), split=by_core, rows=rows_own)
    (out_split,) = weight_grad(
        attended_low[None], (branch_grads[None],), split=by_core, rows=rows_own
    )
    (down_grad,) = weight_grad(kept[2], (kept[1],))
    out_running = add(out_running, *out_pairs[3])
    kv_got, got_two, query_split, out_split, down_grad, out_running = fence(
        kv_got, got_two, query_split, out_split, down_grad, out_running
    )

    out_running = seq_perm(out_running, 1, 0)
    gate_up_split = [
        next_split([one[0], two[0]], [got, other], order[:1], order[1:])
        for one, two, got, other, order in zip(*halves, got_one, got_two, orders)
    ]
    gate_up_sums = [dp_perm(goes, order[1]) for (_, goes), order in zip(gate_up_split, orders)]
    both = [(split[0], swap(split[1])) for split in (query_split, out_split)]
    key_value_pre, input_grads, gain_one_grad, bias_grad = input_back(
        inputs,
        gain_one,
        w_qkv,
        query_pre,
        cosine,
        sine,
        residual_grads,
        kv_sum[0],
        kv_got,
    )
    down_split = split_columns(
        down_grad.reshape(n_dp, ff_pad, D),
        first_split[0],
        ((0, D // 2), (D // 2, D)),
        tuple(order[0] for order in orders),
    )
    ((kv_stays, kv_goes),) = weight_grad(
        normed_one[None], (key_value_pre[None],), split=by_core, rows=rows_own
    )
    (
        gate_up_split,
        gate_up_sums,
        down_split,
        both,
        input_grads,
        kv_stays,
        kv_goes,
        out_running,
        small_parts,
    ) = fence(
        gate_up_split,
        gate_up_sums,
        down_split,
        both,
        input_grads,
        kv_stays,
        kv_goes,
        out_running,
        (gain_one_grad, gain_two_grad, bias_grad),
    )

    down_got = [dp_perm(goes, order[0]) for (_, goes), order in zip(down_split, orders)]
    ready = []
    for split, got, order in zip(gate_up_split, gate_up_sums, orders):
        kept_part = split[0]
        for i in range(2, len(order)):
            kept_part, goes = next_split([kept_part], [got], order[:i], order[i:])
            got = dp_perm(goes, order[i])
        ready.append(add_halve([kept_part], [got], core_side, n_chips))
    to_send = turn_pairs(
        [kept_part for kept_part, _ in ready],
        [swap(sent) for _, sent in ready],
        chip_side,
        n_chips,
    )
    small_grad = jnp.concatenate(small_parts, axis=1).astype(bf16)
    small_grad = jnp.pad(
        small_grad.reshape(n_all, small_own), ((0, 0), (0, rows_own * HD - small_own))
    ).reshape(n_chips, 2, n_dp, rows_own, HD)
    kv_stays = jnp.concatenate(
        [pick(small_grad, core_at, 1).reshape(-1, rows_own, HD), kv_stays], axis=2
    )
    kv_goes = jnp.concatenate(
        [pick(small_grad, 1 - core_at, 1).reshape(-1, rows_own, HD), kv_goes], axis=2
    )
    kv_got = swap(kv_goes)
    rest_cuts = (((0, D), (0, 3 * HD)), ((0, D), (3 * HD, HD + 2 * KVW)))
    rest = [
        add_halve_columns(
            [kept_part, kv_stays],
            [got, kv_got],
            cuts,
            bit_sides[order[0]],
            n_chips * n_dp // (2 * order[0]),
        )
        for (kept_part, got), cuts, order in zip(both, rest_cuts, orders)
    ]
    to_send, rest, out_running, down_got = fence(to_send, rest, out_running, down_got)

    gate_up_owned = {0: to_send[0]}
    rest_got = [dp_perm(goes, order[0]) for (_, goes), order in zip(rest, orders)]
    for shift in groups[0] + groups[2]:
        gate_up_owned[shift] = exchange(shift)
    if len(bits) > 1:
        down_split = [
            next_split([kept_part], [got], order[:1], order[1:])
            for (kept_part, _), got, order in zip(down_split, down_got, orders)
        ]
    out_pairs[0] = (out_pairs[0][0], swap(out_pairs[0][1]))
    gate_up_owned, rest_got, down_split, out_pairs = fence(
        gate_up_owned, rest_got, down_split, out_pairs
    )

    for shift in groups[1]:
        gate_up_owned[shift] = exchange(shift)
    rest_send = []
    for (kept_part, _), got, order in zip(rest, rest_got, orders):
        for i in range(1, len(order)):
            kept_part, goes = next_split([kept_part], [got], order[:i], order[i:])
            got = dp_perm(goes, order[i])
        rest_send.append(add_turn(kept_part, got, chip_side))
    gate_up_owned, rest_send, down_split = fence(gate_up_owned, rest_send, down_split)

    rest_send = [
        jnp.concatenate([parts[t] for parts in rest_send], axis=1) for t in range(n_chips)
    ]
    rest_ring = [rest_send[0]] + [seq_perm(rest_send[shift], shift, 0) for shift in shifts]
    down_owned = []
    for (kept_part, goes), got, order in zip(down_split, down_got, orders):
        for i in range(1, len(order)):
            if i > 1:
                kept_part, goes = next_split([kept_part], [got], order[:i], order[i:])
            got = dp_perm(goes, order[i])
        down_owned.append(kept_part[0, :ff_dev].astype(f32) + got[0, :ff_dev].astype(f32))
    down_owned = jnp.concatenate(down_owned, axis=1)
    down_new = adamw_update(down_master, down_first, down_second, down_owned, 0.026, 0.1)
    rest_ring, down_new = fence(rest_ring, down_new)
    total = sum(piece.astype(f32) for piece in rest_ring)
    for t in range(4, n_chips):
        out_running = seq_perm(add(out_running, *out_pairs[t]), 1, 0)
    outputs = residual + out_pairs[0][0].astype(f32) + out_pairs[0][1].astype(f32)
    outputs = outputs + out_running.astype(f32)
    outputs = outputs.astype(bf16)
    gate_up_new = adamw_hidden(
        gate_up_master,
        gate_up_first,
        gate_up_second,
        [gate_up_owned[t] for t in range(n_chips)],
        ring_order,
        n_dp,
        ff_pad,
        0.064,
        0.1,
    )
    wide = D + 3 * HD
    query_owned, out_owned = total[:, :D], total[:, wide : wide + D]
    small_owned = total[:, D : D + HD]
    qkv_owned = jnp.concatenate(
        [query_owned, total[:, D + HD : wide], total[:, wide + D :]], axis=1
    )
    small_owned = small_owned.reshape(-1)[:small_own]

    qkv_new = adamw_update(qkv_master, qkv_first, qkv_second, qkv_owned, 0.09, 0.1)
    out_new = adamw_update(out_master, out_first, out_second, out_owned, 0.18, 0.1)
    small_new = adamw_update(small_master, small_first, small_second, small_owned, 0.6, 0.0)
    return (
        outputs[None],
        input_grads[None],
        *qkv_new,
        *out_new,
        *gate_up_new,
        *down_new,
        *small_new,
    )


def solution(mesh):
    in_specs = (
        P("dp", "seq", None),
        P("dp", "seq", None),
        P("dp", None),
        P(("seq", "dp"), None),
        P(("seq", "dp"), None),
        P(("seq", "dp"), None),
        P(("seq", "dp"), None),
        P(("seq", "dp"), None),
        P(("seq", "dp"), None),
        P(None, ("seq", "dp"), None),
        P(None, ("seq", "dp"), None),
        P(None, ("seq", "dp"), None),
        P(("seq", "dp"), None),
        P(("seq", "dp"), None),
        P(("seq", "dp"), None),
        P(("seq", "dp")),
        P(("seq", "dp")),
        P(("seq", "dp")),
    )
    out_specs = (
        P("dp", "seq", None),
        P("dp", "seq", None),
        P(("seq", "dp"), None),
        P(("seq", "dp"), None),
        P(("seq", "dp"), None),
        P(("seq", "dp"), None),
        P(("seq", "dp"), None),
        P(("seq", "dp"), None),
        P(None, ("seq", "dp"), None),
        P(None, ("seq", "dp"), None),
        P(None, ("seq", "dp"), None),
        P(("seq", "dp"), None),
        P(("seq", "dp"), None),
        P(("seq", "dp"), None),
        P(("seq", "dp")),
        P(("seq", "dp")),
        P(("seq", "dp")),
    )
    return jax.shard_map(shards, mesh=mesh, in_specs=in_specs, out_specs=out_specs, check_vma=False)
```
